32 devices in a mesh: graph: 2 (over core), edge: 16 (over z, y, x).
Axes of the slice: x: 2, y: 2, z: 4, core: 2. Of those that a mesh axis runs over, the one named last changes fastest.
Arguments:
- states: bfloat16 [2, 2048, 128], P(None, ('graph', 'edge')), may hold values from -6 to 6
- edge_feats: bfloat16 [2, 16, 32768], P(None, None, ('graph', 'edge')), may hold values from -6 to 6
- source_index: int32 [2, 32768], P(None, ('graph', 'edge')), may hold values from 0 to 1023, as said below
- target_index: int32 [2, 32768], P(None, ('graph', 'edge')), may hold values from 0 to 1023, as said below
- w_edge_in: bfloat16 [16, 128], replicated, may hold values from -1.5 to 1.5
- b_edge_in: float32 [128], replicated, may hold values from -3 to 3
- w_edge_out: bfloat16 [128, 16384], replicated, may hold values from -0.01953125 to 0.01953125
- b_edge_out: float32 [16384], replicated, may hold values from -0.125 to 0.125
- w_input: bfloat16 [128, 384], replicated, may hold values from -0.5 to 0.5
- w_hidden: bfloat16 [128, 384], replicated, may hold values from -0.5 to 0.5
- b_input: float32 [384], replicated, may hold values from -3 to 3
- b_hidden: float32 [384], replicated, may hold values from -3 to 3
- cotangent: bfloat16 [2, 2048, 128], P(None, ('graph', 'edge')), may hold values from -6 to 6
Outputs:
- new_states: bfloat16 [2, 2048, 128], P(None, ('graph', 'edge'))
- state_grad: bfloat16 [2, 2048, 128], P(None, ('graph', 'edge'))
- feat_grad: bfloat16 [2, 16, 32768], P(None, None, ('graph', 'edge'))
- w_edge_in_grad: float32 [16, 128], replicated
- b_edge_in_grad: float32 [128], replicated
- w_edge_out_grad: float32 [128, 16384], replicated
- b_edge_out_grad: float32 [16384], replicated
- w_input_grad: float32 [128, 384], replicated
- w_hidden_grad: float32 [128, 384], replicated
- b_input_grad: float32 [384], replicated
- b_hidden_grad: float32 [384], replicated
The draws below stay inside these ranges and needn't reach their ends.
Inputs may be any that keep to these rules, and one draw needn't show every extreme that they name: `source_index`: atom numbers within the edge's group: an edge of group g reads rows g * 1024 + index of the state arrays. Source and target of an edge lie in the same molecule; each device's 64 rows of a group hold whole molecules, runs of consecutive atom numbers taken cyclically within those rows, one of min(100, 32) atoms and the others of at most 18. Among the 1024 edges of one device in one micro-batch, at most 128 have their target atom among the rows of any one device, and exactly 128 for each device that they reach. `target_index`: same numbering and molecules as source_index; the same bound of 128 edges of one device with target atoms on one device holds for source atoms.
All inputs are finite; a program needn't handle non-finite values.
Results may differ from the reference program's by a relative error of at most 0.015.
Values may be sent and summed in bfloat16 or wider, within the bound.
No kernel may reach another device: no remote copies, remote signals or barrier semaphores. Data moves between devices by JAX's collectives and lax.ppermute only.
A program may use at most 128 MiB of HBM per device.

```python
import math
import jax
import jax.numpy as jnp
from jax import lax

H = 128
EH = 128
EF = 16
MB = 2
EDGE_DEV = 1024
NODE_DEV = 64
NODES = 1024
EDGES = 16384
N_GRAPH = 2
N_EDGE = 16


def edge_pairs(key):
    group_count = MB * N_GRAPH
    row_count = group_count * N_EDGE
    slot_cap = max(2, 2 * EDGE_DEV // N_EDGE)
    owners_each = EDGE_DEV // slot_cap
    sub_keys = jax.random.split(key, 4)
    perm_keys = jax.random.split(sub_keys[0], row_count)
    orders = jax.vmap(lambda one_key: jax.random.permutation(one_key, N_EDGE))(perm_keys).astype(jnp.int32)
    owner = jnp.repeat(orders[:, :owners_each], slot_cap, axis=1)
    rot_table = jax.random.randint(sub_keys[1], (group_count, N_EDGE), 0, NODE_DEV)
    group_row = jnp.arange(row_count, dtype=jnp.int32) // N_EDGE
    rotation = jnp.take_along_axis(rot_table[group_row], owner, 1)
    local_first = jax.random.randint(sub_keys[2], (row_count, EDGE_DEV), 0, NODE_DEV)
    big_size = min(100, NODE_DEV // 2)
    shifted = (local_first - rotation) % NODE_DEV
    mol_start = jnp.where(shifted < big_size, 0, big_size + (shifted - big_size) // 18 * 18)
    mol_size = jnp.where(shifted < big_size, big_size, jnp.minimum(18, NODE_DEV - mol_start))
    offset_draw = jax.random.randint(sub_keys[3], (row_count, EDGE_DEV), 0, 1 << 20) % jnp.maximum(mol_size - 1, 1)
    partner = mol_start + (shifted - mol_start + 1 + offset_draw) % mol_size
    local_second = (partner + rotation) % NODE_DEV
    first_node = owner * NODE_DEV + local_first
    second_node = owner * NODE_DEV + local_second
    odd_slot = (jnp.arange(EDGE_DEV) % 2 == 1)[None, :]
    source = jnp.where(odd_slot, second_node, first_node).astype(jnp.int32)
    target = jnp.where(odd_slot, first_node, second_node).astype(jnp.int32)
    return (source.reshape(MB, N_GRAPH * EDGES), target.reshape(MB, N_GRAPH * EDGES))


def draw_source_index(key, part):
    both_sides = edge_pairs(key)
    return both_sides[0]


def draw_target_index(key, part):
    both_sides = edge_pairs(key)
    return both_sides[1]


def block_scale(rng, extent, cuts, smallest, top_value):
    def one(position, blocks):
        steps = jax.random.uniform(jax.random.fold_in(jax.random.fold_in(rng, 6), position), (blocks,), jnp.float32, smallest / len(cuts), top_value / len(cuts))
        return jnp.repeat(jnp.exp(steps), extent[position] // blocks).reshape((-1,) + (1,) * (len(extent) - position - 1))

    factor_of = one(*cuts[0])
    for cut in cuts[1:]:
        factor_of = factor_of * one(*cut)
    return factor_of


def gaussian(stream_key, shape, scale, reach, cuts=(), kind=jnp.bfloat16):
    entries = scale * jax.random.normal(stream_key, shape, jnp.float32)
    if cuts:
        entries = entries * block_scale(stream_key, shape, cuts, -0.22, 0.18)
    return jnp.clip(entries, -reach, reach).astype(kind)


def setup_inputs(seed: int = 0) -> dict:
    key_list = jax.random.split(jax.random.key(seed), 14)
    states = gaussian(key_list[0], (MB, N_GRAPH * NODES, H), 1.0, 6.0, ((1, 32),))
    edge_feats = gaussian(key_list[1], (MB, EF, N_GRAPH * EDGES), 1.0, 6.0, ((2, 32),))
    source_index = draw_source_index(jax.random.fold_in(key_list[13], 71), 0)
    target_index = draw_target_index(jax.random.fold_in(key_list[13], 71), 0)
    w_edge_in = gaussian(key_list[4], (EF, EH), EF ** -0.5, 1.5)
    b_edge_in = gaussian(key_list[5], (EH,), 0.5, 3.0, (), jnp.float32)
    w_edge_out = gaussian(key_list[6], (EH, H * H), (6 * EH * H) ** -0.5, 0.01953125)
    b_edge_out = gaussian(key_list[7], (H * H,), 0.02, 0.125, (), jnp.float32)
    w_input = gaussian(key_list[8], (H, 3 * H), H ** -0.5, 0.5)
    w_hidden = gaussian(key_list[9], (H, 3 * H), H ** -0.5, 0.5)
    b_input = gaussian(key_list[10], (3 * H,), 0.5, 3.0, (), jnp.float32)
    b_hidden = gaussian(key_list[11], (3 * H,), 0.5, 3.0, (), jnp.float32)
    cotangent = gaussian(key_list[12], (MB, N_GRAPH * NODES, H), 1.0, 6.0, ((1, 32),))
    return dict(states=states, edge_feats=edge_feats, source_index=source_index, target_index=target_index, w_edge_in=w_edge_in, b_edge_in=b_edge_in, w_edge_out=w_edge_out, b_edge_out=b_edge_out, w_input=w_input, w_hidden=w_hidden, b_input=b_input, b_hidden=b_hidden, cotangent=cotangent)


@jax.custom_vjp
def low(v):
    return lax.optimization_barrier(v.astype(jnp.bfloat16)).astype(jnp.float32)

@jax.custom_vjp
def low_back(v):
    return v

def low_keep(v):
    return (low(v), None)

def low_pass(kept, grad):
    return (grad,)

def back_keep(v):
    return (v, None)

def back_low(kept, grad):
    return (low(grad),)
low.defvjp(low_keep, low_pass)
low_back.defvjp(back_keep, back_low)

def dense_f32(first_arg, second_arg):
    return jnp.dot(first_arg, second_arg, precision=lax.Precision.HIGHEST, preferred_element_type=jnp.float32)

def forward(params, states, feats, source, target):
    w_edge_in, b_edge_in, w_edge_out, b_edge_out, w_input, w_hidden, b_input, b_hidden = params
    state_width = states.shape[1]
    edge_count = source.shape[0]
    block_rows = math.gcd(edge_count, 512)
    pre_act = low_back(dense_f32(feats.T, w_edge_in) + b_edge_in)
    hidden = low(jax.nn.silu(pre_act))
    hid_blocks = hidden.reshape(edge_count // block_rows, block_rows, hidden.shape[1])
    src_blocks = source.reshape(edge_count // block_rows, block_rows)
    current = states
    for step_no in range(2):
        levels = low(current)

        def block_messages(pieces):
            hid_block, src_block = pieces
            matrices = low(low_back(dense_f32(hid_block, w_edge_out) + b_edge_out))
            matrices = matrices.reshape(block_rows, state_width, state_width)
            return jnp.einsum('eij,ej->ei', matrices, levels[src_block], precision=lax.Precision.HIGHEST)
        pieces = lax.map(jax.checkpoint(block_messages), (hid_blocks, src_blocks))
        summed = jax.ops.segment_sum(pieces.reshape(edge_count, state_width), target, num_segments=states.shape[0])
        mail_low = low(low_back(summed))
        from_mail = low_back(dense_f32(mail_low, w_input) + b_input)
        from_state = low_back(dense_f32(levels, w_hidden) + b_hidden)
        reset = jax.nn.sigmoid(from_mail[:, :state_width] + from_state[:, :state_width])
        update = jax.nn.sigmoid(from_mail[:, state_width:2 * state_width] + from_state[:, state_width:2 * state_width])
        candidate = jnp.tanh(from_mail[:, 2 * state_width:] + reset * from_state[:, 2 * state_width:])
        current = (1.0 - update) * candidate + update * current
    return current

def reference(states, edge_feats, source_index, target_index, w_edge_in, b_edge_in, w_edge_out, b_edge_out, w_input, w_hidden, b_input, b_hidden, cotangent):
    params = tuple((p_arr.astype(jnp.float32) for p_arr in (w_edge_in, b_edge_in, w_edge_out, b_edge_out, w_input, w_hidden, b_input, b_hidden)))
    totals = tuple((jnp.zeros(p_arr.shape, jnp.float32) for p_arr in params))
    new_list, grad_list, feat_list = ([], [], [])
    for batch_no in range(MB):
        new_parts, grad_parts, feat_parts = ([], [], [])
        for group_no in range(N_GRAPH):
            node_lo = group_no * NODES
            edge_lo = group_no * EDGES
            source = source_index[batch_no, edge_lo:edge_lo + EDGES]
            target = target_index[batch_no, edge_lo:edge_lo + EDGES]

            def run_group(p_all, s_all, f_all):
                return forward(p_all, s_all, f_all, source, target)
            result, pullback = jax.vjp(run_group, params, states[batch_no, node_lo:node_lo + NODES].astype(jnp.float32), edge_feats[batch_no, :, edge_lo:edge_lo + EDGES].astype(jnp.float32))
            d_params, d_states, d_feats = pullback(cotangent[batch_no, node_lo:node_lo + NODES].astype(jnp.float32))
            totals = tuple((acc + new for acc, new in zip(totals, d_params)))
            new_parts.append(result.astype(jnp.bfloat16))
            grad_parts.append(d_states.astype(jnp.bfloat16))
            feat_parts.append(d_feats.astype(jnp.bfloat16))
        new_list.append(jnp.concatenate(new_parts, 0))
        grad_list.append(jnp.concatenate(grad_parts, 0))
        feat_list.append(jnp.concatenate(feat_parts, 1))
    return (jnp.stack(new_list), jnp.stack(grad_list), jnp.stack(feat_list), totals[0], totals[1], totals[2], totals[3], totals[4], totals[5], totals[6], totals[7])
```

```python
import functools

import jax
import jax.numpy as jnp
from jax import lax
from jax.experimental import pallas as pl
from jax.experimental.pallas import tpu as pltpu
from jax.sharding import PartitionSpec as P

F32 = jnp.float32
BF16 = jnp.bfloat16
LANES = 128
GROUP = 12
PARAMS = pltpu.CompilerParams(vmem_limit_bytes=60 * 1024 * 1024)


def dot(first, second, dims=((1,), (0,))):
    return lax.dot_general(first, second, (dims, ((), ())), preferred_element_type=F32)


def dot_nt(first, second):
    return dot(first, second, ((1,), (1,)))


def row_ids(shape):
    return lax.broadcasted_iota(jnp.int32, shape, 0)


def col_ids(shape):
    return lax.broadcasted_iota(jnp.int32, shape, 1)


def full_call(kernel, out_shape, scratch=(), **more):
    return pl.pallas_call(
        kernel,
        out_shape=out_shape,
        scratch_shapes=scratch,
        compiler_params=PARAMS,
        **more,
    )


def ranks_of(owner, owners):
    hits = (row_ids((owners, owner.shape[1])) == owner).astype(F32)
    before = (row_ids((LANES, LANES)) < col_ids((LANES, LANES))).astype(BF16)
    seen = jnp.zeros((owners, 1), F32)
    ranks = []
    for start in range(0, owner.shape[1], LANES):
        part = hits[:, start : start + LANES]
        place = dot(part.astype(BF16), before) + seen
        ranks.append(jnp.sum(part * place, axis=0, keepdims=True))
        seen = seen + jnp.sum(part, axis=1, keepdims=True)
    return hits, jnp.concatenate(ranks, axis=1)


def route_kernel(own_rows, src_ref, dst_ref, feat_ref, out_ref):
    owners, batches, rows, cap = out_ref.shape
    edges = src_ref.shape[2]
    shift = own_rows.bit_length() - 1
    for batch in range(batches):
        source, target = src_ref[batch], dst_ref[batch]
        owner = source >> shift
        hits, rank = ranks_of(owner, owners)
        spots = (row_ids((cap, edges)) == rank.astype(jnp.int32)).astype(BF16)
        line = row_ids((16, edges))
        first = owner << shift
        extra = jnp.where(line == 0, source - first, jnp.where(line == 1, target - first, 1))
        extra = jnp.where(line < 3, extra, 0).astype(F32)
        load = jnp.concatenate([feat_ref[batch].astype(F32), extra], axis=0)
        for part in range(owners):
            masked = (load * hits[part : part + 1]).astype(BF16)
            out_ref[part, batch] = dot_nt(masked, spots).astype(BF16)


def unroute_kernel(own_rows, src_ref, back_ref, out_ref):
    owners, batches, rows, cap = back_ref.shape
    edges = src_ref.shape[2]
    shift = own_rows.bit_length() - 1
    for batch in range(batches):
        hits, rank = ranks_of(src_ref[batch] >> shift, owners)
        spots = (row_ids((cap, edges)) == rank.astype(jnp.int32)).astype(BF16)
        total = jnp.zeros((rows, edges), F32)
        for part in range(owners):
            total = total + dot(back_ref[part, batch], spots) * hits[part : part + 1]
        out_ref[batch] = total.astype(BF16)


def edge_piece(edge_ref, piece, batch):
    return jnp.concatenate([edge_ref[2 * piece, batch], edge_ref[2 * piece + 1, batch]], axis=1)


def pair_masks(block):
    marks = block[16:32].astype(F32)
    source = marks[0:1].astype(jnp.int32)
    target = marks[1:2].astype(jnp.int32)
    held = marks[2:3] > 0.5
    code = ((target >> 3) & 3) * 128 + (target >> 5) * 64 + source
    code = jnp.where(held, code, -1)
    pairs = (row_ids((512, block.shape[1])) == code).astype(BF16)
    low = row_ids((8, block.shape[1])) == (target & 7)
    return pairs, low


def pre_of(block, w_in_ref, b_in_ref):
    return dot(w_in_ref[...], block) + b_in_ref[...]


def gates_of(mail_low, level, w_x, w_h, b_x, b_h):
    width = level.shape[1]
    from_mail = dot(mail_low, w_x[...]) + b_x[...]
    from_state = dot(level, w_h[...]) + b_h[...]
    reset = jax.nn.sigmoid(from_mail[:, :width] + from_state[:, :width])
    update = jax.nn.sigmoid(from_mail[:, width : 2 * width] + from_state[:, width : 2 * width])
    state_part = from_state[:, 2 * width :]
    candidate = jnp.tanh(from_mail[:, 2 * width :] + reset * state_part)
    return reset, update, candidate, state_part


def doubled(level):
    blank = jnp.zeros_like(level)
    return jnp.concatenate(
        [jnp.concatenate([level, blank], axis=1), jnp.concatenate([blank, level], axis=1)], axis=0
    )


def main_kernel(
    edge_ref,
    state_ref,
    cot_ref,
    w_in_ref,
    b_in_ref,
    w_ref,
    w_x,
    w_h,
    b_x,
    b_h,
    new_ref,
    grad_ref,
    dw_ref,
    dg_ref,
    hid_ref,
    acc_ref,
    g_ref,
    gt_ref,
    p_ref,
    part_ref,
):
    pieces = edge_ref.shape[0] // 2
    batches = edge_ref.shape[1]
    units = w_ref.shape[1] // LANES
    hidden_units = hid_ref.shape[0]
    own = state_ref.shape[0] // batches
    half = own // 2
    span = GROUP * half
    wide = GROUP * LANES
    chunks = units // GROUP

    for batch in range(batches):
        acc_ref[...] = jnp.zeros_like(acc_ref)

        def add_piece(piece, carry):
            block = edge_piece(edge_ref, piece, batch)
            pairs, low = pair_masks(block)
            pre = pre_of(block, w_in_ref, b_in_ref)
            hid_ref[...] = (pre * jax.nn.sigmoid(pre)).astype(BF16).astype(F32)
            ones = jnp.where(low, 1.0, 0.0)
            parts = []
            for unit in range(0, hidden_units, 2):
                two = [jnp.where(low, hid_ref[unit + k : unit + k + 1], 0.0) for k in range(2)]
                parts.append(jnp.concatenate(two, axis=0).astype(BF16))
            parts.append(jnp.concatenate([ones, ones], axis=0).astype(BF16))
            parts.append(jnp.zeros((8 * (units - hidden_units - 2), block.shape[1]), BF16))
            acc_ref[...] += dot_nt(jnp.concatenate(parts, axis=0), pairs)
            return carry

        lax.fori_loop(0, pieces, add_piece, 0)

        def place_four(step, carry):
            rows = []
            for k in range(4):
                for part in range(4):
                    start = pl.multiple_of(step * 32 + k * 8, 8)
                    rows.append(acc_ref[pl.ds(start, 8), part * LANES : (part + 1) * LANES])
            tile = jnp.concatenate(rows, axis=0)
            at = pl.ds(pl.multiple_of(step * LANES, LANES), LANES)
            g_ref[batch, at, :] = tile.astype(BF16)
            gt_ref[batch, :, at] = tile.T.astype(BF16)
            return carry

        lax.fori_loop(0, units // 4, place_four, 0)

    def forward(step, level):
        two = [doubled(level[batch * own : (batch + 1) * own]) for batch in range(batches)]

        def chunk(number, mail):
            for batch in range(batches):
                rows = pl.ds(pl.multiple_of(number * span, LANES), span)
                out = dot(g_ref[batch, rows, :], two[batch]).astype(BF16)
                for unit in range(GROUP):
                    for part in range(2):
                        base = (step * batches + batch) * own + part * half
                        lane = pl.multiple_of(number * wide + unit * LANES, LANES)
                        p_ref[base : base + half, pl.ds(lane, LANES)] = out[
                            unit * half : (unit + 1) * half, part * LANES : (part + 1) * LANES
                        ]
            lanes = pl.ds(pl.multiple_of(number * wide, LANES), wide)
            base = step * batches * own
            return mail + dot_nt(p_ref[base : base + batches * own, lanes], w_ref[:, lanes])

        return lax.fori_loop(0, chunks, chunk, jnp.zeros((batches * own, LANES), F32))

    def backward(level, d_mail, last):
        two = [doubled(level[batch * own : (batch + 1) * own]) for batch in range(batches)]

        def chunk(number, sums):
            lanes = pl.ds(pl.multiple_of(number * wide, LANES), wide)
            pulled = dot(d_mail, w_ref[:, lanes]).astype(BF16)
            out = []
            for batch in range(batches):
                rows = []
                for unit in range(GROUP):
                    tile = pulled[batch * own : (batch + 1) * own, unit * LANES : (unit + 1) * LANES]
                    rows.append(jnp.concatenate([tile[:half], tile[half:]], axis=1))
                tall = jnp.concatenate(rows, axis=0)
                at = pl.ds(pl.multiple_of(number * span, LANES), span)
                out.append(sums[batch] + dot(gt_ref[batch, :, at], tall))
                d_pair = dot_nt(tall, two[batch])
                if not last:
                    part_ref[batch, at, :] = d_pair
                else:
                    d_pair = d_pair + part_ref[batch, at, :]
                    for unit in range(0, GROUP, 2):
                        for part in range(half // 8):
                            pair = [
                                d_pair[(unit + k) * half + part * 8 : (unit + k) * half + part * 8 + 8]
                                for k in range(2)
                            ]
                            start = pl.multiple_of(number * (GROUP * 8) + unit * 8, 16)
                            dg_ref[batch, pl.ds(start, 16), part * LANES : (part + 1) * LANES] = (
                                jnp.concatenate(pair, axis=0).astype(BF16)
                            )
            return tuple(out)

        zero = jnp.zeros((LANES, 2 * LANES), F32)
        sums = lax.fori_loop(0, chunks, chunk, (zero,) * batches)
        return jnp.concatenate(
            [one[:own, :LANES] + one[own:, LANES:] for one in sums], axis=0
        )

    weights = (w_x, w_h, b_x, b_h)
    level_zero = state_ref[...]
    state_zero = level_zero.astype(F32)
    mail_zero = forward(0, level_zero).astype(BF16)
    gates_zero = gates_of(mail_zero, level_zero, *weights)
    state_one = (1.0 - gates_zero[1]) * gates_zero[2] + gates_zero[1] * state_zero
    level_one = state_one.astype(BF16)
    mail_one = forward(1, level_one).astype(BF16)
    gates_one = gates_of(mail_one, level_one, *weights)
    new_ref[...] = ((1.0 - gates_one[1]) * gates_one[2] + gates_one[1] * state_one).astype(BF16)

    def gru_back(d_next, gates, current):
        reset, update, candidate, state_part = gates
        d_cand = d_next * (1.0 - update) * (1.0 - candidate * candidate)
        d_reset = d_cand * state_part * reset * (1.0 - reset)
        d_update = d_next * (current - candidate) * update * (1.0 - update)
        dg_mail = jnp.concatenate([d_reset, d_update, d_cand], axis=1).astype(BF16)
        dg_state = jnp.concatenate([d_reset, d_update, d_cand * reset], axis=1).astype(BF16)
        d_mail = dot_nt(dg_mail, w_x[...]).astype(BF16)
        d_current = d_next * update + dot_nt(dg_state, w_h[...])
        return dg_mail, dg_state, d_mail, d_current

    dgm_one, dgs_one, dm_one, d_state = gru_back(cot_ref[...].astype(F32), gates_one, state_one)
    d_state = d_state + backward(level_one, dm_one, False)
    dgm_zero, dgs_zero, dm_zero, d_state = gru_back(d_state, gates_zero, state_zero)
    d_state = d_state + backward(level_zero, dm_zero, True)
    grad_ref[...] = d_state.astype(BF16)

    dm_all = jnp.concatenate([dm_zero.astype(F32).T, dm_one.astype(F32).T], axis=1).astype(BF16)

    def grad_chunk(number, carry):
        lanes = pl.ds(pl.multiple_of(number * wide, LANES), wide)
        dw_ref[:, lanes] = dot(dm_all, p_ref[:, lanes]).astype(BF16)
        return carry

    lax.fori_loop(0, chunks, grad_chunk, 0)

    def both(first, second):
        return jnp.concatenate([first.astype(F32), second.astype(F32)], axis=0)

    mails, levels = both(mail_zero, mail_one), both(level_zero, level_one)
    dgm, dgs = both(dgm_zero, dgm_one), both(dgs_zero, dgs_one)
    width = dgm.shape[1]
    base = (hidden_units + 1) * LANES
    dw_ref[:, base : base + width] = dot(mails.T.astype(BF16), dgm.astype(BF16)).astype(BF16)
    dw_ref[:, base + width : base + 2 * width] = dot(
        levels.T.astype(BF16), dgs.astype(BF16)
    ).astype(BF16)
    sums = [jnp.sum(one, axis=0, keepdims=True) for one in (dgm, dgs)]
    rows = [one[:, k : k + LANES] for one in sums for k in range(0, width, LANES)]
    line = row_ids((dw_ref.shape[0], LANES))
    tail = jnp.zeros((dw_ref.shape[0], LANES), F32)
    for k, row in enumerate(rows):
        tail = jnp.where(line == k, row, tail)
    dw_ref[:, base + 2 * width : base + 2 * width + LANES] = tail.astype(BF16)
    if dw_ref.shape[1] > base + 2 * width + LANES:
        rest = dw_ref.shape[1] - (base + 2 * width + LANES)
        dw_ref[:, base + 2 * width + LANES :] = jnp.zeros((dw_ref.shape[0], rest), BF16)


def edge_kernel(edge_ref, dg_ref, w_in_ref, b_in_ref, w_out_ref, feat_ref, win_ref):
    pieces = edge_ref.shape[0] // 2
    batches = edge_ref.shape[1]
    hidden_units = w_in_ref.shape[0]

    def one_piece(piece, batch, total):
        block = edge_piece(edge_ref, piece, batch)
        pairs, low = pair_masks(block)
        pre = pre_of(block, w_in_ref, b_in_ref)
        sig = jax.nn.sigmoid(pre)
        spread = dot(dg_ref[batch, : 8 * hidden_units], pairs)
        spread = spread.reshape(hidden_units, 8, block.shape[1])
        d_hidden = jnp.sum(jnp.where(low[None], spread, 0.0), axis=1)
        d_pre = (d_hidden * sig * (1.0 + pre * (1.0 - sig))).astype(BF16)
        feats = dot(w_out_ref[...], d_pre).astype(BF16)
        feat_ref[2 * piece, batch] = feats[:, :LANES]
        feat_ref[2 * piece + 1, batch] = feats[:, LANES:]
        return total + dot_nt(block, d_pre)

    total = jnp.zeros((32, hidden_units), F32)
    for batch in range(batches):
        total = lax.fori_loop(
            0, pieces, lambda piece, acc: one_piece(piece, batch, acc), total
        )
    win_ref[...] = total.astype(BF16)


def body(
    states,
    edge_feats,
    source_index,
    target_index,
    w_edge_in,
    b_edge_in,
    w_edge_out,
    b_edge_out,
    w_input,
    w_hidden,
    b_input,
    b_hidden,
    cotangent,
):
    batches, own, width = states.shape
    edges = source_index.shape[1]
    owners = lax.axis_size("edge")
    cores = lax.axis_size("graph")
    cap = max(2, 2 * edges // owners)
    feat_count, units = w_edge_in.shape
    source = source_index.reshape(batches, 1, edges)
    target = target_index.reshape(batches, 1, edges)

    sent = full_call(
        functools.partial(route_kernel, own),
        jax.ShapeDtypeStruct((owners, batches, 32, cap), BF16),
    )(source, target, edge_feats)
    edge_data = lax.all_to_all(sent, "edge", 0, 0, tiled=True)
    merge = max(1, LANES // cap)
    if merge > 1:
        edge_data = edge_data.reshape(owners // merge, merge, batches, 32, cap)
        edge_data = edge_data.transpose(0, 2, 3, 1, 4).reshape(
            owners // merge, batches, 32, merge * cap
        )

    padded = (units + 2 + GROUP - 1) // GROUP * GROUP
    bias = b_edge_out.reshape(width, width)
    bias_high = lax.reduce_precision(bias, 8, 7)
    w_tall = jnp.concatenate(
        [
            w_edge_out.reshape(units, width, width).transpose(1, 0, 2).reshape(width, units * width),
            bias_high.astype(BF16),
            (bias - bias_high).astype(BF16),
            jnp.zeros((width, (padded - units - 2) * width), BF16),
        ],
        axis=1,
    )
    w_in_t = jnp.pad(w_edge_in.T, ((0, 0), (0, 32 - feat_count)))
    b_in = b_edge_in.reshape(units, 1)

    z_parts = owners // 4
    blocks = units + max(8, z_parts)
    pairs = own // 2
    new_states, state_grad, d_wide, d_pairs = full_call(
        main_kernel,
        (
            jax.ShapeDtypeStruct((batches * own, width), BF16),
            jax.ShapeDtypeStruct((batches * own, width), BF16),
            jax.ShapeDtypeStruct((width, blocks * width), BF16),
            jax.ShapeDtypeStruct((batches, padded * 8, 512), BF16),
        ),
        (
            pltpu.VMEM((units, 2 * LANES), F32),
            pltpu.VMEM((padded * 8, 512), F32),
            pltpu.VMEM((batches, padded * pairs, LANES), BF16),
            pltpu.VMEM((batches, LANES, padded * pairs), BF16),
            pltpu.VMEM((2 * batches * own, padded * width), BF16),
            pltpu.VMEM((batches, padded * pairs, LANES), F32),
        ),
    )(
        edge_data,
        states.reshape(batches * own, width),
        cotangent.reshape(batches * own, width),
        w_in_t,
        b_in,
        w_tall,
        w_input,
        w_hidden,
        b_input.reshape(1, -1),
        b_hidden.reshape(1, -1),
    )

    core = lax.axis_index("graph")
    swap = [(0, 1), (1, 0)]
    halves = d_wide.reshape(cores, width // cores, blocks * width)
    kept = lax.dynamic_index_in_dim(halves, core, 0, False)
    given = lax.dynamic_index_in_dim(halves, 1 - core, 0, False)
    got = lax.ppermute(given, "graph", swap)
    chip_sum = (kept.astype(F32) + got.astype(F32)).astype(BF16)
    share = chip_sum.reshape(4, width // cores // 4, z_parts, blocks // z_parts * width)
    share = share.transpose(0, 2, 1, 3).reshape(owners, width // cores // 4, -1)
    parts = lax.all_to_all(share, "edge", 0, 0, tiled=True)
    mine = jnp.sum(parts.astype(F32), axis=0).astype(BF16)
    mine = mine.reshape(width // cores // 4, blocks // z_parts, width)

    d_feats, d_first = full_call(
        edge_kernel,
        (
            jax.ShapeDtypeStruct(
                (edge_data.shape[0], batches, feat_count, edge_data.shape[3]), BF16
            ),
            jax.ShapeDtypeStruct((32, units), BF16),
        ),
    )(edge_data, d_pairs, w_in_t, b_in, w_edge_in)
    if merge > 1:
        d_feats = d_feats.reshape(owners // merge, batches, feat_count, merge, cap)
        d_feats = d_feats.transpose(0, 3, 1, 2, 4)
    d_feats = d_feats.reshape(owners, batches * feat_count, cap)
    spread = jnp.broadcast_to(
        d_first.reshape(1, 32 * units // cap, cap), (owners, 32 * units // cap, cap)
    )
    back = lax.all_to_all(jnp.concatenate([d_feats, spread], axis=1), "edge", 0, 0, tiled=True)
    d_edges = back[:, : batches * feat_count].reshape(owners, batches, feat_count, cap)
    first_parts = back[:, batches * feat_count :].reshape(owners, 32, units)
    first_sum = jnp.sum(first_parts.astype(F32), axis=0)
    first_sum = first_sum + lax.ppermute(first_sum, "graph", swap)
    feat_grad = full_call(
        functools.partial(unroute_kernel, own),
        jax.ShapeDtypeStruct((batches, feat_count, edges), BF16),
    )(source, d_edges)

    every = lax.all_gather(mine, "edge", axis=0, tiled=False)
    every = every.reshape(4, z_parts, width // cores // 4, blocks // z_parts, width)
    every = every.transpose(0, 2, 1, 3, 4).reshape(width // cores, blocks, width)
    other = lax.ppermute(every, "graph", swap)
    whole = jnp.where(
        core == 0,
        jnp.concatenate([every, other], axis=0),
        jnp.concatenate([other, every], axis=0),
    )
    d_out = whole[:, :units].transpose(1, 0, 2).reshape(units, width * width).astype(F32)
    small = whole[:, units:].astype(F32)
    bias_rows = small[:, 7].reshape(-1)
    return (
        new_states.reshape(batches, own, width),
        state_grad.reshape(batches, own, width),
        feat_grad,
        first_sum[:feat_count],
        first_sum[feat_count + 2],
        d_out,
        small[:, 0].reshape(-1),
        small[:, 1:4].reshape(width, 3 * width),
        small[:, 4:7].reshape(width, 3 * width),
        bias_rows[: 3 * width],
        bias_rows[3 * width : 6 * width],
    )


def solution(mesh):
    spread = ("graph", "edge")
    rows = P(None, spread, None)
    edges = P(None, spread)
    feats = P(None, None, spread)
    in_specs = (rows, feats, edges, edges) + (P(),) * 8 + (rows,)
    out_specs = (rows, rows, feats) + (P(),) * 8
    return jax.shard_map(
        body,
        mesh=mesh,
        in_specs=in_specs,
        out_specs=out_specs,
        check_vma=False,
    )
```

```python
import functools

import jax
import jax.numpy as jnp
from jax import lax
from jax.experimental import pallas as pl
from jax.experimental.pallas import tpu as pltpu
from jax.sharding import PartitionSpec as P

F32 = jnp.float32
BF16 = jnp.bfloat16
LANES = 128
GROUP = 12
PARAMS = pltpu.CompilerParams(vmem_limit_bytes=60 * 1024 * 1024)


def dot(first, second, dims=((1,), (0,))):
    return lax.dot_general(first, second, (dims, ((), ())), preferred_element_type=F32)


def dot_nt(first, second):
    return dot(first, second, ((1,), (1,)))


def row_ids(shape):
    return lax.broadcasted_iota(jnp.int32, shape, 0)


def col_ids(shape):
    return lax.broadcasted_iota(jnp.int32, shape, 1)


def full_call(kernel, out_shape, scratch=(), **more):
    return pl.pallas_call(
        kernel,
        out_shape=out_shape,
        scratch_shapes=scratch,
        compiler_params=PARAMS,
        **more,
    )


def ranks_of(owner, owners):
    hits = (row_ids((owners, owner.shape[1])) == owner).astype(F32)
    before = (row_ids((LANES, LANES)) < col_ids((LANES, LANES))).astype(BF16)
    seen = jnp.zeros((owners, 1), F32)
    ranks = []
    for start in range(0, owner.shape[1], LANES):
        part = hits[:, start : start + LANES]
        place = dot(part.astype(BF16), before) + seen
        ranks.append(jnp.sum(part * place, axis=0, keepdims=True))
        seen = seen + jnp.sum(part, axis=1, keepdims=True)
    return hits, jnp.concatenate(ranks, axis=1)


def route_kernel(own_rows, src_ref, dst_ref, feat_ref, out_ref):
    owners, batches, rows, cap = out_ref.shape
    edges = src_ref.shape[1]
    shift = own_rows.bit_length() - 1
    for batch in range(batches):
        source, target = src_ref[batch : batch + 1], dst_ref[batch : batch + 1]
        owner = source >> shift
        hits, rank = ranks_of(owner, owners)
        spots = (row_ids((cap, edges)) == rank.astype(jnp.int32)).astype(BF16)
        line = row_ids((16, edges))
        first = owner << shift
        extra = jnp.where(line == 0, source - first, jnp.where(line == 1, target - first, 1))
        extra = jnp.where(line < 3, extra, 0).astype(F32)
        load = jnp.concatenate([feat_ref[batch].astype(F32), extra], axis=0)
        for part in range(owners):
            masked = (load * hits[part : part + 1]).astype(BF16)
            out_ref[part, batch] = dot_nt(masked, spots).astype(BF16)


def unroute_kernel(own_rows, src_ref, back_ref, out_ref):
    owners, batches, rows, cap = back_ref.shape
    edges = src_ref.shape[1]
    shift = own_rows.bit_length() - 1
    for batch in range(batches):
        hits, rank = ranks_of(src_ref[batch : batch + 1] >> shift, owners)
        spots = (row_ids((cap, edges)) == rank.astype(jnp.int32)).astype(BF16)
        total = jnp.zeros((rows, edges), F32)
        for part in range(owners):
            total = total + dot(back_ref[part, batch], spots) * hits[part : part + 1]
        out_ref[batch] = total.astype(BF16)


def edge_piece(edge_ref, piece, batch):
    return jnp.concatenate([edge_ref[2 * piece, batch], edge_ref[2 * piece + 1, batch]], axis=1)


def pair_masks(block):
    marks = block[16:32].astype(F32)
    source = marks[0:1].astype(jnp.int32)
    target = marks[1:2].astype(jnp.int32)
    held = marks[2:3] > 0.5
    code = ((target >> 3) & 3) * 128 + (target >> 5) * 64 + source
    code = jnp.where(held, code, -1)
    pairs = (row_ids((512, block.shape[1])) == code).astype(BF16)
    low = row_ids((8, block.shape[1])) == (target & 7)
    return pairs, low


def pre_of(block, w_in_ref, b_in_ref):
    return dot(w_in_ref[...], block) + b_in_ref[...]


def gates_of(mail_low, level, w_x, w_h, b_x, b_h):
    width = level.shape[1]
    from_mail = dot(mail_low, w_x[...]) + b_x[...]
    from_state = dot(level, w_h[...]) + b_h[...]
    reset = jax.nn.sigmoid(from_mail[:, :width] + from_state[:, :width])
    update = jax.nn.sigmoid(from_mail[:, width : 2 * width] + from_state[:, width : 2 * width])
    state_part = from_state[:, 2 * width :]
    candidate = jnp.tanh(from_mail[:, 2 * width :] + reset * state_part)
    return reset, update, candidate, state_part


def doubled(level):
    blank = jnp.zeros_like(level)
    return jnp.concatenate(
        [jnp.concatenate([level, blank], axis=1), jnp.concatenate([blank, level], axis=1)], axis=0
    )


def main_kernel(
    core_ref,
    edge_ref,
    state_ref,
    cot_ref,
    w_in_ref,
    b_in_ref,
    w_ref,
    bias_ref,
    w_x,
    w_h,
    b_x,
    b_h,
    new_ref,
    grad_ref,
    kept_ref,
    given_ref,
    dg_ref,
    hid_ref,
    acc_ref,
    g_ref,
    gt_ref,
    p_ref,
    part_ref,
    tail_ref,
):
    pieces = edge_ref.shape[0] // 2
    batches = edge_ref.shape[1]
    hidden_units = hid_ref.shape[0]
    units = acc_ref.shape[0] // 8
    own = state_ref.shape[0] // batches
    half = own // 2
    span = GROUP * half
    wide = GROUP * LANES
    chunks = units // GROUP

    tail_ref[...] = jnp.zeros_like(tail_ref)
    high = bias_ref[...].astype(BF16)
    tail_ref[0] = high
    tail_ref[1] = (bias_ref[...] - high.astype(F32)).astype(BF16)

    def weights_of(number):
        blocks = []
        for unit in range(number * GROUP, (number + 1) * GROUP):
            blocks.append(w_ref[unit] if unit < hidden_units else tail_ref[unit - hidden_units])
        return jnp.concatenate(blocks, axis=1)

    for batch in range(batches):
        acc_ref[...] = jnp.zeros_like(acc_ref)

        def add_piece(piece, carry):
            block = edge_piece(edge_ref, piece, batch)
            pairs, low = pair_masks(block)
            pre = pre_of(block, w_in_ref, b_in_ref)
            hid_ref[...] = (pre * jax.nn.sigmoid(pre)).astype(BF16).astype(F32)
            ones = jnp.where(low, 1.0, 0.0)
            parts = []
            for unit in range(0, hidden_units, 2):
                two = [jnp.where(low, hid_ref[unit + k : unit + k + 1], 0.0) for k in range(2)]
                parts.append(jnp.concatenate(two, axis=0).astype(BF16))
            parts.append(jnp.concatenate([ones, ones], axis=0).astype(BF16))
            parts.append(jnp.zeros((8 * (units - hidden_units - 2), block.shape[1]), BF16))
            acc_ref[...] += dot_nt(jnp.concatenate(parts, axis=0), pairs)
            return carry

        lax.fori_loop(0, pieces, add_piece, 0)

        def place(step, carry):
            for four in range(3):
                rows = []
                for k in range(4):
                    for part in range(4):
                        start = pl.multiple_of(step * 96 + four * 32 + k * 8, 8)
                        rows.append(acc_ref[pl.ds(start, 8), part * LANES : (part + 1) * LANES])
                tile = jnp.concatenate(rows, axis=0).astype(BF16)
                at = pl.ds(pl.multiple_of((step * 3 + four) * LANES, LANES), LANES)
                g_ref[batch, at, :] = tile
                gt_ref[batch, :, at] = tile.T
            return carry

        lax.fori_loop(0, units // 12, place, 0)

    def forward(step, level):
        two = [doubled(level[batch * own : (batch + 1) * own]) for batch in range(batches)]
        mail = jnp.zeros((batches * own, LANES), F32)
        base = step * batches * own
        for number in range(chunks):
            for batch in range(batches):
                out = dot(g_ref[batch, number * span : (number + 1) * span, :], two[batch])
                out = out.astype(BF16)
                for unit in range(GROUP):
                    lane = number * wide + unit * LANES
                    for part in range(2):
                        row = base + batch * own + part * half
                        p_ref[row : row + half, lane : lane + LANES] = out[
                            unit * half : (unit + 1) * half, part * LANES : (part + 1) * LANES
                        ]
            rows = p_ref[base : base + batches * own, number * wide : (number + 1) * wide]
            mail = mail + dot_nt(rows, weights_of(number))
        return mail

    def backward(level, d_mail, last):
        two = [doubled(level[batch * own : (batch + 1) * own]) for batch in range(batches)]
        sums = [jnp.zeros((LANES, 2 * LANES), F32) for batch in range(batches)]
        for number in range(chunks):
            pulled = dot(d_mail, weights_of(number)).astype(BF16)
            at = slice(number * span, (number + 1) * span)
            for batch in range(batches):
                rows = []
                for unit in range(GROUP):
                    tile = pulled[batch * own : (batch + 1) * own, unit * LANES : (unit + 1) * LANES]
                    rows.append(jnp.concatenate([tile[:half], tile[half:]], axis=1))
                tall = jnp.concatenate(rows, axis=0)
                sums[batch] = sums[batch] + dot(gt_ref[batch, :, at], tall)
                d_pair = dot_nt(tall, two[batch])
                if not last:
                    part_ref[batch, at, :] = d_pair
                    continue
                d_pair = d_pair + part_ref[batch, at, :]
                for unit in range(0, GROUP, 2):
                    row = (number * GROUP + unit) * 8
                    for part in range(half // 8):
                        pair = [
                            d_pair[(unit + k) * half + part * 8 : (unit + k) * half + part * 8 + 8]
                            for k in range(2)
                        ]
                        dg_ref[batch, row : row + 16, part * LANES : (part + 1) * LANES] = (
                            jnp.concatenate(pair, axis=0).astype(BF16)
                        )
        return jnp.concatenate([one[:own, :LANES] + one[own:, LANES:] for one in sums], axis=0)

    weights = (w_x, w_h, b_x, b_h)
    level_zero = state_ref[...]
    state_zero = level_zero.astype(F32)
    mail_zero = forward(0, level_zero).astype(BF16)
    gates_zero = gates_of(mail_zero, level_zero, *weights)
    state_one = (1.0 - gates_zero[1]) * gates_zero[2] + gates_zero[1] * state_zero
    level_one = state_one.astype(BF16)
    mail_one = forward(1, level_one).astype(BF16)
    gates_one = gates_of(mail_one, level_one, *weights)
    new_ref[...] = ((1.0 - gates_one[1]) * gates_one[2] + gates_one[1] * state_one).astype(BF16)

    def gru_back(d_next, gates, current):
        reset, update, candidate, state_part = gates
        d_cand = d_next * (1.0 - update) * (1.0 - candidate * candidate)
        d_reset = d_cand * state_part * reset * (1.0 - reset)
        d_update = d_next * (current - candidate) * update * (1.0 - update)
        dg_mail = jnp.concatenate([d_reset, d_update, d_cand], axis=1).astype(BF16)
        dg_state = jnp.concatenate([d_reset, d_update, d_cand * reset], axis=1).astype(BF16)
        d_mail = dot_nt(dg_mail, w_x[...]).astype(BF16)
        d_current = d_next * update + dot_nt(dg_state, w_h[...])
        return dg_mail, dg_state, d_mail, d_current

    dgm_one, dgs_one, dm_one, d_state = gru_back(cot_ref[...].astype(F32), gates_one, state_one)
    d_state = d_state + backward(level_one, dm_one, False)
    dgm_zero, dgs_zero, dm_zero, d_state = gru_back(d_state, gates_zero, state_zero)
    d_state = d_state + backward(level_zero, dm_zero, True)
    grad_ref[...] = d_state.astype(BF16)

    def both(first, second):
        return jnp.concatenate([first.astype(F32), second.astype(F32)], axis=0)

    dms = both(dm_zero, dm_one).T.astype(BF16)
    mails, levels = both(mail_zero, mail_one), both(level_zero, level_one)
    dgm, dgs = both(dgm_zero, dgm_one), both(dgs_zero, dgs_one)
    width = dgm.shape[1]
    sums = [jnp.sum(one, axis=0, keepdims=True) for one in (dgm, dgs)]
    lines = [one[:, k : k + LANES] for one in sums for k in range(0, width, LANES)]
    line = row_ids((2 * own, LANES))
    bias_rows = jnp.zeros((2 * own, LANES), F32)
    for k, row in enumerate(lines):
        bias_rows = jnp.where(line == k, row, bias_rows)
    small = jnp.concatenate(
        [
            dot(dms, p_ref[:, hidden_units * LANES : (hidden_units + 1) * LANES]),
            dot(mails.T.astype(BF16), dgm.astype(BF16)),
            dot(levels.T.astype(BF16), dgs.astype(BF16)),
            bias_rows,
        ],
        axis=1,
    )

    first = core_ref[0] == 0
    swapped = jnp.concatenate([dms[own:], dms[:own]], axis=0)
    dms = jnp.where(first, dms.astype(F32), swapped.astype(F32)).astype(BF16)
    small = jnp.where(first, small, jnp.concatenate([small[own:], small[:own]], axis=0)).astype(BF16)
    rows_in, groups, tall, wide_out = kept_ref.shape
    taken = wide_out - LANES
    for group in range(groups):
        out = dot(dms, p_ref[:, group * taken : (group + 1) * taken]).astype(BF16)
        stream, part = divmod(group, groups // 2)
        extra = small[:, (stream * 4 + part) * LANES : (stream * 4 + part + 1) * LANES]
        if part >= 4:
            extra = jnp.zeros((2 * own, LANES), BF16)
        for row in range(rows_in):
            for ref, start in ((kept_ref, row * tall), (given_ref, (rows_in + row) * tall)):
                ref[row, group, :, :taken] = out[start : start + tall]
                ref[row, group, :, taken:] = extra[start : start + tall]


def edge_kernel(edge_ref, dg_ref, w_in_ref, b_in_ref, w_out_ref, feat_ref, win_ref):
    pieces = edge_ref.shape[0] // 2
    batches = edge_ref.shape[1]
    hidden_units = w_in_ref.shape[0]

    def one_piece(piece, batch, total):
        block = edge_piece(edge_ref, piece, batch)
        pairs, low = pair_masks(block)
        pre = pre_of(block, w_in_ref, b_in_ref)
        sig = jax.nn.sigmoid(pre)
        spread = dot(dg_ref[batch, : 8 * hidden_units], pairs)
        spread = spread.reshape(hidden_units, 8, block.shape[1])
        d_hidden = jnp.sum(jnp.where(low[None], spread, 0.0), axis=1)
        d_pre = (d_hidden * sig * (1.0 + pre * (1.0 - sig))).astype(BF16)
        feats = dot(w_out_ref[...], d_pre).astype(BF16)
        feat_ref[2 * piece, batch] = feats[:, :LANES]
        feat_ref[2 * piece + 1, batch] = feats[:, LANES:]
        return total + dot_nt(block, d_pre)

    total = jnp.zeros((32, hidden_units), F32)
    for batch in range(batches):
        total = lax.fori_loop(
            0, pieces, lambda piece, acc: one_piece(piece, batch, acc), total
        )
    win_ref[...] = total.astype(BF16)


def place_kernel(streams, carried, *refs):
    count = len(streams)
    at_ref, pieces = refs[0], refs[1 : 1 + count]
    outs = refs[1 + count + carried : 6 + count + carried]
    big, little, sems = refs[6 + count + carried :]
    d_w, d_bias, d_x, d_h, d_rows = outs
    parts, tall, blocks, lanes = pieces[0].shape
    main = blocks - 1
    copies = []
    for k, (stream, piece) in enumerate(zip(streams, pieces)):
        for part in range(parts):
            for row in range(tall):
                big[k, part * main : (part + 1) * main, row * lanes : (row + 1) * lanes] = piece[
                    part, row, :main
                ].astype(F32)
        for part in range(4):
            little[k, :, part * lanes : (part + 1) * lanes] = piece[part, :, main].astype(F32)
        high = parts * main
        to = pl.ds(pl.multiple_of(at_ref[k] * (tall * lanes), LANES), tall * lanes)
        rows = pl.ds(pl.multiple_of(at_ref[k] * tall, 8), tall)
        cut = (1 if stream == 0 else 3) * lanes
        left, right = (d_bias, d_x) if stream == 0 else (d_h, d_rows)
        moves = (
            (big.at[k], d_w.at[stream * high : (stream + 1) * high, to]),
            (little.at[k, :, :cut], left.at[rows, :]),
            (little.at[k, :, cut:], right.at[rows, :]),
        )
        for sem, (source, target) in enumerate(moves):
            copy = pltpu.make_async_copy(source, target, sems.at[k, sem])
            copy.start()
            copies.append(copy)
    for copy in copies:
        copy.wait()


def place_pieces(at, pieces, streams, shapes, before=()):
    count = len(pieces)
    parts, tall, blocks, lanes = pieces[0].shape
    vmem = pl.BlockSpec(memory_space=pltpu.VMEM)
    hbm = pl.BlockSpec(memory_space=pl.ANY)
    return pl.pallas_call(
        functools.partial(place_kernel, streams, len(before)),
        out_shape=shapes,
        in_specs=[pl.BlockSpec(memory_space=pltpu.SMEM)] + [vmem] * count + [hbm] * len(before),
        out_specs=[hbm] * len(shapes),
        scratch_shapes=(
            pltpu.VMEM((count, parts * (blocks - 1), tall * lanes), F32),
            pltpu.VMEM((count, tall, 4 * lanes), F32),
            pltpu.SemaphoreType.DMA((count, 3)),
        ),
        input_output_aliases={1 + count + k: k for k in range(len(before))},
        compiler_params=PARAMS,
    )(at, *pieces, *before)


def body(
    states,
    edge_feats,
    source_index,
    target_index,
    w_edge_in,
    b_edge_in,
    w_edge_out,
    b_edge_out,
    w_input,
    w_hidden,
    b_input,
    b_hidden,
    cotangent,
):
    batches, own, width = states.shape
    edges = source_index.shape[1]
    owners = lax.axis_size("edge")
    cap = max(2, 2 * edges // owners)
    feat_count, units = w_edge_in.shape

    sent = full_call(
        functools.partial(route_kernel, own),
        jax.ShapeDtypeStruct((owners, batches, 32, cap), BF16),
    )(source_index, target_index, edge_feats)
    edge_data = lax.all_to_all(sent, "edge", 0, 0, tiled=True)
    merge = max(1, LANES // cap)
    if merge > 1:
        edge_data = edge_data.reshape(owners // merge, merge, batches, 32, cap)
        edge_data = edge_data.transpose(0, 2, 3, 1, 4).reshape(
            owners // merge, batches, 32, merge * cap
        )

    w_mats = w_edge_out.reshape(units, width, width)
    padded = (units + 2 + GROUP - 1) // GROUP * GROUP
    w_in_t = jnp.pad(w_edge_in.T, ((0, 0), (0, 32 - feat_count)))
    b_in = b_edge_in.reshape(units, 1)

    z_parts = owners // 4
    taken = units // (2 * z_parts)
    tall = width // 8
    pairs = own // 2
    core = lax.axis_index("graph")
    spot = lax.axis_index("edge")
    half_shape = jax.ShapeDtypeStruct((4, 2 * z_parts, tall, (taken + 1) * width), BF16)
    new_states, state_grad, kept, given, d_pairs = full_call(
        main_kernel,
        (
            jax.ShapeDtypeStruct((batches * own, width), BF16),
            jax.ShapeDtypeStruct((batches * own, width), BF16),
            half_shape,
            half_shape,
            jax.ShapeDtypeStruct((batches, padded * 8, 512), BF16),
        ),
        (
            pltpu.VMEM((units, 2 * LANES), F32),
            pltpu.VMEM((padded * 8, 512), F32),
            pltpu.VMEM((batches, padded * pairs, LANES), BF16),
            pltpu.VMEM((batches, LANES, padded * pairs), BF16),
            pltpu.VMEM((2 * batches * own, padded * width), BF16),
            pltpu.VMEM((batches, padded * pairs, LANES), F32),
            pltpu.VMEM((padded - units, width, width), BF16),
        ),
        in_specs=[pl.BlockSpec(memory_space=pltpu.SMEM)]
        + [pl.BlockSpec(memory_space=pltpu.VMEM)] * 11,
    )(
        core.reshape(1),
        edge_data,
        states.reshape(batches * own, width),
        cotangent.reshape(batches * own, width),
        w_in_t,
        b_in,
        w_mats,
        b_edge_out.reshape(width, width),
        w_input,
        w_hidden,
        b_input.reshape(1, -1),
        b_hidden.reshape(1, -1),
    )

    swap = [(0, 1), (1, 0)]
    bits = (spot & 1, (spot >> 1) & 1)
    place = spot >> 2

    def to_core(value):
        return lax.ppermute(value, "graph", swap)

    def to_chip(value, flip):
        return lax.ppermute(value, "edge", [(k, k ^ flip) for k in range(owners)])

    def pick(value, number):
        return lax.dynamic_index_in_dim(value, number, 0, False)

    got = to_core(given)
    chip = [one.reshape(2, 2, 2, z_parts, tall, (taken + 1) * width) for one in (kept, got)]

    def added(terms, number):
        return sum(pick(one, number).astype(F32) for one in terms)

    gathered = []
    for stream in range(2):
        high, low = bits[stream], bits[1 - stream]
        terms = [one[:, :, stream] for one in chip]
        terms = [pick(one, high) for one in terms] + [
            to_chip(added(terms, 1 - high).astype(BF16), 1 << stream)
        ]
        terms = [pick(one, low) for one in terms] + [
            to_chip(added(terms, 1 - low).astype(BF16), 2 >> stream)
        ]
        far = [
            to_chip(added(terms, place ^ step).astype(BF16), 4 * step) for step in range(1, z_parts)
        ]
        mine = added(terms, place) + sum(one.astype(F32) for one in far)
        gathered.append(mine.astype(BF16).reshape(tall, taken + 1, width))

    d_feats, d_first = full_call(
        edge_kernel,
        (
            jax.ShapeDtypeStruct(
                (edge_data.shape[0], batches, feat_count, edge_data.shape[3]), BF16
            ),
            jax.ShapeDtypeStruct((32, units), BF16),
        ),
    )(edge_data, d_pairs, w_in_t, b_in, w_edge_in)
    if merge > 1:
        d_feats = d_feats.reshape(owners // merge, batches, feat_count, merge, cap)
        d_feats = d_feats.transpose(0, 3, 1, 2, 4)
    d_feats = d_feats.reshape(owners, batches * feat_count, cap)
    spread = jnp.broadcast_to(
        d_first.reshape(1, 32 * units // cap, cap), (owners, 32 * units // cap, cap)
    )
    back = lax.all_to_all(jnp.concatenate([d_feats, spread], axis=1), "edge", 0, 0, tiled=True)
    d_edges = back[:, : batches * feat_count].reshape(owners, batches, feat_count, cap)
    first_parts = back[:, batches * feat_count :].reshape(owners, 32, units)
    first_sum = jnp.sum(first_parts.astype(F32), axis=0)
    first_sum = first_sum + lax.ppermute(first_sum, "graph", swap)
    feat_grad = full_call(
        functools.partial(unroute_kernel, own),
        jax.ShapeDtypeStruct((batches, feat_count, edges), BF16),
    )(source_index, d_edges)

    early, late, early_at, late_at = [], [], [], []
    for stream in range(2):
        high, low = bits[stream], bits[1 - stream]
        mine = gathered[stream]
        column = jnp.zeros((z_parts,) + mine.shape, BF16)
        column = lax.dynamic_update_index_in_dim(column, mine, place, 0)
        for step in range(1, z_parts):
            column = lax.dynamic_update_index_in_dim(
                column, to_chip(mine, 4 * step), place ^ step, 0
            )
        near = to_chip(column, 2 >> stream)
        far = [to_chip(one, 1 << stream) for one in (column, near)]
        for one, flip in ((column, 0), (near, 1)):
            early += [one, to_core(one)]
            early_at += [side * 4 + high * 2 + (low ^ flip) for side in (core, 1 - core)]
        for one, flip in zip(far, (0, 1)):
            late += [one, to_core(one)]
            late_at += [side * 4 + (1 - high) * 2 + (low ^ flip) for side in (core, 1 - core)]
    shapes = tuple(
        jax.ShapeDtypeStruct(shape, F32)
        for shape in (
            (units, width * width),
            (width, width),
            (width, 3 * width),
            (width, 3 * width),
            (width, width),
        )
    )
    streams = (0,) * 4 + (1,) * 4
    outs = place_pieces(jnp.stack(early_at), early, streams, shapes)
    outs = place_pieces(jnp.stack(late_at), late, streams, shapes, outs)
    d_w, d_bias, d_x, d_h, d_rows = outs
    rows = d_rows[:8].reshape(-1)
    return (
        new_states.reshape(batches, own, width),
        state_grad.reshape(batches, own, width),
        feat_grad,
        first_sum[:feat_count],
        first_sum[feat_count + 2],
        d_w,
        d_bias.reshape(-1),
        d_x,
        d_h,
        rows[: 3 * width],
        rows[3 * width : 6 * width],
    )


def solution(mesh):
    spread = ("graph", "edge")
    rows = P(None, spread, None)
    edges = P(None, spread)
    feats = P(None, None, spread)
    in_specs = (rows, feats, edges, edges) + (P(),) * 8 + (rows,)
    out_specs = (rows, rows, feats) + (P(),) * 8
    return jax.shard_map(
        body,
        mesh=mesh,
        in_specs=in_specs,
        out_specs=out_specs,
        check_vma=False,
    )
```

```python
import functools

import jax
import jax.numpy as jnp
from jax import lax
from jax.experimental import pallas as pl
from jax.experimental.pallas import tpu as pltpu
from jax.sharding import PartitionSpec as P

F32 = jnp.float32
BF16 = jnp.bfloat16
LANES = 128
GROUP = 12
PARAMS = pltpu.CompilerParams(vmem_limit_bytes=60 * 1024 * 1024)


def dot(first, second, dims=((1,), (0,))):
    return lax.dot_general(first, second, (dims, ((), ())), preferred_element_type=F32)


def dot_nt(first, second):
    return dot(first, second, ((1,), (1,)))


def row_ids(shape):
    return lax.broadcasted_iota(jnp.int32, shape, 0)


def col_ids(shape):
    return lax.broadcasted_iota(jnp.int32, shape, 1)


def full_call(kernel, out_shape, scratch=(), **more):
    return pl.pallas_call(
        kernel,
        out_shape=out_shape,
        scratch_shapes=scratch,
        compiler_params=PARAMS,
        **more,
    )


def ranks_of(owner, owners):
    hits = (row_ids((owners, owner.shape[1])) == owner).astype(F32)
    before = (row_ids((LANES, LANES)) < col_ids((LANES, LANES))).astype(BF16)
    seen = jnp.zeros((owners, 1), F32)
    ranks = []
    for start in range(0, owner.shape[1], LANES):
        part = hits[:, start : start + LANES]
        place = dot(part.astype(BF16), before) + seen
        ranks.append(jnp.sum(part * place, axis=0, keepdims=True))
        seen = seen + jnp.sum(part, axis=1, keepdims=True)
    return hits, jnp.concatenate(ranks, axis=1)


def route_kernel(own_rows, src_ref, dst_ref, feat_ref, out_ref):
    owners, batches, rows, cap = out_ref.shape
    edges = src_ref.shape[1]
    shift = own_rows.bit_length() - 1
    for batch in range(batches):
        source, target = src_ref[batch : batch + 1], dst_ref[batch : batch + 1]
        owner = source >> shift
        hits, rank = ranks_of(owner, owners)
        spots = (row_ids((cap, edges)) == rank.astype(jnp.int32)).astype(BF16)
        line = row_ids((16, edges))
        first = owner << shift
        extra = jnp.where(line == 0, source - first, jnp.where(line == 1, target - first, 1))
        extra = jnp.where(line < 3, extra, 0).astype(F32)
        load = jnp.concatenate([feat_ref[batch].astype(F32), extra], axis=0)
        for part in range(owners):
            masked = (load * hits[part : part + 1]).astype(BF16)
            out_ref[part, batch] = dot_nt(masked, spots).astype(BF16)


def unroute_kernel(own_rows, src_ref, back_ref, out_ref):
    owners, batches, rows, cap = back_ref.shape
    edges = src_ref.shape[1]
    shift = own_rows.bit_length() - 1
    for batch in range(batches):
        hits, rank = ranks_of(src_ref[batch : batch + 1] >> shift, owners)
        spots = (row_ids((cap, edges)) == rank.astype(jnp.int32)).astype(BF16)
        total = jnp.zeros((rows, edges), F32)
        for part in range(owners):
            total = total + dot(back_ref[part, batch], spots) * hits[part : part + 1]
        out_ref[batch] = total.astype(BF16)


def edge_piece(edge_ref, piece, batch):
    return jnp.concatenate([edge_ref[2 * piece, batch], edge_ref[2 * piece + 1, batch]], axis=1)


def pair_masks(block):
    marks = block[16:32].astype(F32)
    source = marks[0:1].astype(jnp.int32)
    target = marks[1:2].astype(jnp.int32)
    held = marks[2:3] > 0.5
    code = ((target >> 3) & 3) * 128 + (target >> 5) * 64 + source
    code = jnp.where(held, code, -1)
    pairs = (row_ids((512, block.shape[1])) == code).astype(BF16)
    low = row_ids((8, block.shape[1])) == (target & 7)
    return pairs, low


def first_layer(w_in_ref, b_in_ref):
    bias = jnp.broadcast_to(b_in_ref[...].reshape(1, -1), (8, b_in_ref.shape[0]))
    return w_in_ref[...].astype(F32).T.astype(BF16), bias.T[:, :1]


def gates_of(mail_low, level, w_x, w_h, b_x, b_h):
    width = level.shape[1]
    from_mail = dot(mail_low, w_x[...]) + b_x[...].reshape(1, -1)
    from_state = dot(level, w_h[...]) + b_h[...].reshape(1, -1)
    reset = jax.nn.sigmoid(from_mail[:, :width] + from_state[:, :width])
    update = jax.nn.sigmoid(from_mail[:, width : 2 * width] + from_state[:, width : 2 * width])
    state_part = from_state[:, 2 * width :]
    candidate = jnp.tanh(from_mail[:, 2 * width :] + reset * state_part)
    return reset, update, candidate, state_part


def doubled(level):
    blank = jnp.zeros_like(level)
    return jnp.concatenate(
        [jnp.concatenate([level, blank], axis=1), jnp.concatenate([blank, level], axis=1)], axis=0
    )


def main_kernel(
    core_ref,
    edge_ref,
    state_ref,
    cot_ref,
    w_in_ref,
    b_in_ref,
    w_ref,
    bias_ref,
    w_x,
    w_h,
    b_x,
    b_h,
    new_ref,
    grad_ref,
    kept_a,
    kept_b,
    given_a,
    given_b,
    dg_ref,
    hid_ref,
    acc_ref,
    g_ref,
    gt_ref,
    p_ref,
    part_ref,
    tail_ref,
):
    pieces = edge_ref.shape[0] // 2
    batches = edge_ref.shape[1]
    hidden_units = hid_ref.shape[0]
    units = acc_ref.shape[0] // 8
    own = state_ref.shape[0] // batches
    half = own // 2
    span = GROUP * half
    wide = GROUP * LANES
    chunks = units // GROUP

    tail_ref[...] = jnp.zeros_like(tail_ref)
    high = bias_ref[...].astype(BF16)
    tail_ref[0] = high
    tail_ref[1] = (bias_ref[...] - high.astype(F32)).astype(BF16)

    def weights_of(number):
        blocks = []
        for unit in range(number * GROUP, (number + 1) * GROUP):
            blocks.append(w_ref[unit] if unit < hidden_units else tail_ref[unit - hidden_units])
        return jnp.concatenate(blocks, axis=1)

    w_in, b_in = first_layer(w_in_ref, b_in_ref)

    for batch in range(batches):
        acc_ref[...] = jnp.zeros_like(acc_ref)

        def add_piece(piece, carry):
            block = edge_piece(edge_ref, piece, batch)
            pairs, low = pair_masks(block)
            pre = dot(w_in, block[:16]) + b_in
            hid_ref[...] = (pre * jax.nn.sigmoid(pre)).astype(BF16).astype(F32)
            ones = jnp.where(low, 1.0, 0.0)
            parts = []
            for unit in range(0, hidden_units, 2):
                two = [jnp.where(low, hid_ref[unit + k : unit + k + 1], 0.0) for k in range(2)]
                parts.append(jnp.concatenate(two, axis=0).astype(BF16))
            parts.append(jnp.concatenate([ones, ones], axis=0).astype(BF16))
            parts.append(jnp.zeros((8 * (units - hidden_units - 2), block.shape[1]), BF16))
            acc_ref[...] += dot_nt(jnp.concatenate(parts, axis=0), pairs)
            return carry

        lax.fori_loop(0, pieces, add_piece, 0)

        def place(step, carry):
            for four in range(3):
                rows = []
                for k in range(4):
                    for part in range(4):
                        start = pl.multiple_of(step * 96 + four * 32 + k * 8, 8)
                        rows.append(acc_ref[pl.ds(start, 8), part * LANES : (part + 1) * LANES])
                tile = jnp.concatenate(rows, axis=0).astype(BF16)
                at = pl.ds(pl.multiple_of((step * 3 + four) * LANES, LANES), LANES)
                g_ref[batch, at, :] = tile
                gt_ref[batch, :, at] = tile.T
            return carry

        lax.fori_loop(0, units // 12, place, 0)

    def forward(step, level):
        two = [doubled(level[batch * own : (batch + 1) * own]) for batch in range(batches)]
        mail = jnp.zeros((batches * own, LANES), F32)
        base = step * batches * own
        for number in range(chunks):
            for batch in range(batches):
                out = dot(g_ref[batch, number * span : (number + 1) * span, :], two[batch])
                out = out.astype(BF16)
                for unit in range(GROUP):
                    lane = number * wide + unit * LANES
                    for part in range(2):
                        row = base + batch * own + part * half
                        p_ref[row : row + half, lane : lane + LANES] = out[
                            unit * half : (unit + 1) * half, part * LANES : (part + 1) * LANES
                        ]
            rows = p_ref[base : base + batches * own, number * wide : (number + 1) * wide]
            mail = mail + dot_nt(rows, weights_of(number))
        return mail

    def backward(level, d_mail, last):
        two = [doubled(level[batch * own : (batch + 1) * own]) for batch in range(batches)]
        sums = [jnp.zeros((LANES, 2 * LANES), F32) for batch in range(batches)]
        for number in range(chunks):
            pulled = dot(d_mail, weights_of(number)).astype(BF16)
            at = slice(number * span, (number + 1) * span)
            for batch in range(batches):
                rows = []
                for unit in range(GROUP):
                    tile = pulled[batch * own : (batch + 1) * own, unit * LANES : (unit + 1) * LANES]
                    rows.append(jnp.concatenate([tile[:half], tile[half:]], axis=1))
                tall = jnp.concatenate(rows, axis=0)
                sums[batch] = sums[batch] + dot(gt_ref[batch, :, at], tall)
                d_pair = dot_nt(tall, two[batch])
                if not last:
                    part_ref[batch, at, :] = d_pair
                    continue
                d_pair = d_pair + part_ref[batch, at, :]
                for unit in range(0, GROUP, 2):
                    row = (number * GROUP + unit) * 8
                    for part in range(half // 8):
                        pair = [
                            d_pair[(unit + k) * half + part * 8 : (unit + k) * half + part * 8 + 8]
                            for k in range(2)
                        ]
                        dg_ref[batch, row : row + 16, part * LANES : (part + 1) * LANES] = (
                            jnp.concatenate(pair, axis=0).astype(BF16)
                        )
        return jnp.concatenate([one[:own, :LANES] + one[own:, LANES:] for one in sums], axis=0)

    weights = (w_x, w_h, b_x, b_h)
    level_zero = state_ref[...]
    state_zero = level_zero.astype(F32)
    mail_zero = forward(0, level_zero).astype(BF16)
    gates_zero = gates_of(mail_zero, level_zero, *weights)
    state_one = (1.0 - gates_zero[1]) * gates_zero[2] + gates_zero[1] * state_zero
    level_one = state_one.astype(BF16)
    mail_one = forward(1, level_one).astype(BF16)
    gates_one = gates_of(mail_one, level_one, *weights)
    new_ref[...] = ((1.0 - gates_one[1]) * gates_one[2] + gates_one[1] * state_one).astype(BF16)

    def gru_back(d_next, gates, current):
        reset, update, candidate, state_part = gates
        d_cand = d_next * (1.0 - update) * (1.0 - candidate * candidate)
        d_reset = d_cand * state_part * reset * (1.0 - reset)
        d_update = d_next * (current - candidate) * update * (1.0 - update)
        dg_mail = jnp.concatenate([d_reset, d_update, d_cand], axis=1).astype(BF16)
        dg_state = jnp.concatenate([d_reset, d_update, d_cand * reset], axis=1).astype(BF16)
        d_mail = dot_nt(dg_mail, w_x[...]).astype(BF16)
        d_current = d_next * update + dot_nt(dg_state, w_h[...])
        return dg_mail, dg_state, d_mail, d_current

    dgm_one, dgs_one, dm_one, d_state = gru_back(cot_ref[...].astype(F32), gates_one, state_one)
    d_state = d_state + backward(level_one, dm_one, False)
    dgm_zero, dgs_zero, dm_zero, d_state = gru_back(d_state, gates_zero, state_zero)
    d_state = d_state + backward(level_zero, dm_zero, True)
    grad_ref[...] = d_state.astype(BF16)

    def both(first, second):
        return jnp.concatenate([first.astype(F32), second.astype(F32)], axis=0)

    dms = both(dm_zero, dm_one).T.astype(BF16)
    mails, levels = both(mail_zero, mail_one), both(level_zero, level_one)
    dgm, dgs = both(dgm_zero, dgm_one), both(dgs_zero, dgs_one)
    width = dgm.shape[1]
    sums = [jnp.sum(one, axis=0, keepdims=True) for one in (dgm, dgs)]
    lines = [one[:, k : k + LANES] for one in sums for k in range(0, width, LANES)]
    line = row_ids((2 * own, LANES))
    bias_rows = jnp.zeros((2 * own, LANES), F32)
    for k, row in enumerate(lines):
        bias_rows = jnp.where(line == k, row, bias_rows)
    small = jnp.concatenate(
        [
            dot(dms, p_ref[:, hidden_units * LANES : (hidden_units + 1) * LANES]),
            dot(mails.T.astype(BF16), dgm.astype(BF16)),
            dot(levels.T.astype(BF16), dgs.astype(BF16)),
            bias_rows,
        ],
        axis=1,
    )

    first = core_ref[0] == 0
    swapped = jnp.concatenate([dms[own:], dms[:own]], axis=0)
    dms = jnp.where(first, dms.astype(F32), swapped.astype(F32)).astype(BF16)
    small = jnp.where(first, small, jnp.concatenate([small[own:], small[:own]], axis=0)).astype(BF16)
    rows_in, groups, tall, wide_out = kept_a.shape
    taken = wide_out - LANES
    for stream, (kept, given) in enumerate(((kept_a, given_a), (kept_b, given_b))):
        for group in range(groups):
            start = (stream * groups + group) * taken
            out = dot(dms, p_ref[:, start : start + taken]).astype(BF16)
            extra = small[:, (stream * 4 + group) * LANES : (stream * 4 + group + 1) * LANES]
            if group >= 4:
                extra = jnp.zeros((2 * own, LANES), BF16)
            for row in range(rows_in):
                for ref, at in ((kept, row * tall), (given, (rows_in + row) * tall)):
                    ref[row, group, :, :taken] = out[at : at + tall]
                    ref[row, group, :, taken:] = extra[at : at + tall]


def edge_kernel(batch, edge_ref, dg_ref, w_in_ref, b_in_ref, feat_ref, win_ref):
    hidden_units = w_in_ref.shape[1]
    w_in, b_in = first_layer(w_in_ref, b_in_ref)

    def one_piece(piece, total):
        block = edge_piece(edge_ref, piece, batch)
        pairs, low = pair_masks(block)
        pre = dot(w_in, block[:16]) + b_in
        sig = jax.nn.sigmoid(pre)
        spread = dot(dg_ref[batch, : 8 * hidden_units], pairs)
        spread = spread.reshape(hidden_units, 8, block.shape[1])
        d_hidden = jnp.sum(jnp.where(low[None], spread, 0.0), axis=1)
        d_pre = (d_hidden * sig * (1.0 + pre * (1.0 - sig))).astype(BF16)
        feats = dot(w_in_ref[...], d_pre).astype(BF16)
        feat_ref[2 * piece] = feats[:, :LANES]
        feat_ref[2 * piece + 1] = feats[:, LANES:]
        return total + dot_nt(block, d_pre)

    win_ref[...] = lax.fori_loop(
        0, edge_ref.shape[0] // 2, one_piece, jnp.zeros((32, hidden_units), F32)
    )


def spread_kernel(part_ref, out_ref, rows_ref):
    parts, streams, tall, wide = part_ref.shape
    main = wide // LANES - 1
    for stream in range(streams):
        total = part_ref[0, stream].astype(F32)
        for part in range(1, parts):
            total = total + part_ref[part, stream].astype(F32)
        for block in range(main):
            rows_ref[pl.ds(block, tall, stride=main), :] = total[:, block * LANES : (block + 1) * LANES]
        rows_ref[tall * main :, :] = total[:, main * LANES :]
        rows = rows_ref[...].astype(BF16)
        for part in range(parts):
            out_ref[part, stream] = rows


def place_kernel(tall, streams, carried, *refs):
    count = len(streams)
    at_ref, pieces = refs[0], refs[1 : 1 + count]
    outs = refs[1 + count + carried : 6 + count + carried]
    big, little, sems = refs[6 + count + carried :]
    d_w, d_bias, d_x, d_h, d_rows = outs
    parts, _, rows_in, lanes = pieces[0].shape
    main = rows_in // tall - 1
    high = parts * main
    copies = []
    for piece, held in zip(pieces, streams):
        for k, stream in enumerate(held):
            slot = len(copies) // 3
            for part in range(parts):
                for row in range(tall):
                    big[slot, part * main : (part + 1) * main, row * lanes : (row + 1) * lanes] = (
                        piece[part, k, row * main : (row + 1) * main].astype(F32)
                    )
            for part in range(4):
                little[slot, :, part * lanes : (part + 1) * lanes] = piece[part, k, tall * main :].astype(F32)
            to = pl.ds(pl.multiple_of(at_ref[slot] * (tall * lanes), LANES), tall * lanes)
            rows = pl.ds(pl.multiple_of(at_ref[slot] * tall, 8), tall)
            cut = (1 if stream == 0 else 3) * lanes
            left, right = (d_bias, d_x) if stream == 0 else (d_h, d_rows)
            moves = (
                (big.at[slot], d_w.at[stream * high : (stream + 1) * high, to]),
                (little.at[slot, :, :cut], left.at[rows, :]),
                (little.at[slot, :, cut:], right.at[rows, :]),
            )
            for sem, (source, target) in enumerate(moves):
                copy = pltpu.make_async_copy(source, target, sems.at[slot, sem])
                copy.start()
                copies.append(copy)
    for copy in copies:
        copy.wait()


def cost(micros):
    return pl.CostEstimate(
        flops=int(micros * 1e9), bytes_accessed=int(micros * 3e6), transcendentals=0
    )


def place_pieces(tall, at, pieces, streams, shapes, before=()):
    count = len(pieces)
    slots = sum(len(held) for held in streams)
    parts, _, rows_in, lanes = pieces[0].shape
    high = parts * (rows_in // tall - 1)
    vmem = pl.BlockSpec(memory_space=pltpu.VMEM)
    hbm = pl.BlockSpec(memory_space=pl.ANY)
    return pl.pallas_call(
        functools.partial(place_kernel, tall, streams, len(before)),
        out_shape=shapes,
        in_specs=[pl.BlockSpec(memory_space=pltpu.SMEM)] + [vmem] * count + [hbm] * len(before),
        out_specs=[hbm] * len(shapes),
        scratch_shapes=(
            pltpu.VMEM((slots, high, tall * lanes), F32),
            pltpu.VMEM((slots, tall, 4 * lanes), F32),
            pltpu.SemaphoreType.DMA((slots, 3)),
        ),
        input_output_aliases={1 + count + k: k for k in range(len(before))},
        cost_estimate=cost(0.5 * slots),
        compiler_params=PARAMS,
    )(at, *pieces, *before)


def body(
    states,
    edge_feats,
    source_index,
    target_index,
    w_edge_in,
    b_edge_in,
    w_edge_out,
    b_edge_out,
    w_input,
    w_hidden,
    b_input,
    b_hidden,
    cotangent,
):
    batches, own, width = states.shape
    edges = source_index.shape[1]
    owners = lax.axis_size("edge")
    cap = max(2, 2 * edges // owners)
    feat_count, units = w_edge_in.shape

    sent = full_call(
        functools.partial(route_kernel, own),
        jax.ShapeDtypeStruct((owners, batches, 32, cap), BF16),
    )(source_index, target_index, edge_feats)
    edge_data = lax.all_to_all(sent, "edge", 0, 0, tiled=True)
    merge = max(1, LANES // cap)
    if merge > 1:
        edge_data = edge_data.reshape(owners // merge, merge, batches, 32, cap)
        edge_data = edge_data.transpose(0, 2, 3, 1, 4).reshape(
            owners // merge, batches, 32, merge * cap
        )

    w_mats = w_edge_out.reshape(units, width, width)
    padded = (units + 2 + GROUP - 1) // GROUP * GROUP

    z_parts = owners // 4
    taken = units // (2 * z_parts)
    tall = width // 8
    pairs = own // 2
    core = lax.axis_index("graph")
    spot = lax.axis_index("edge")
    half_shape = jax.ShapeDtypeStruct((4, z_parts, tall, (taken + 1) * width), BF16)
    new_states, state_grad, kept_a, kept_b, given_a, given_b, d_pairs = full_call(
        main_kernel,
        (
            jax.ShapeDtypeStruct((batches * own, width), BF16),
            jax.ShapeDtypeStruct((batches * own, width), BF16),
            half_shape,
            half_shape,
            half_shape,
            half_shape,
            jax.ShapeDtypeStruct((batches, padded * 8, 512), BF16),
        ),
        (
            pltpu.VMEM((units, 2 * LANES), F32),
            pltpu.VMEM((padded * 8, 512), F32),
            pltpu.VMEM((batches, padded * pairs, LANES), BF16),
            pltpu.VMEM((batches, LANES, padded * pairs), BF16),
            pltpu.VMEM((2 * batches * own, padded * width), BF16),
            pltpu.VMEM((batches, padded * pairs, LANES), F32),
            pltpu.VMEM((padded - units, width, width), BF16),
        ),
        in_specs=[pl.BlockSpec(memory_space=pltpu.SMEM)]
        + [pl.BlockSpec(memory_space=pltpu.VMEM)] * 11,
    )(
        core.reshape(1),
        edge_data,
        states.reshape(batches * own, width),
        cotangent.reshape(batches * own, width),
        w_edge_in,
        b_edge_in,
        w_mats,
        b_edge_out.reshape(width, width),
        w_input,
        w_hidden,
        b_input,
        b_hidden,
    )

    swap = [(0, 1), (1, 0)]
    bits = (spot & 1, (spot >> 1) & 1)
    place = spot >> 2

    def to_core(value):
        return lax.ppermute(value, "graph", swap)

    def to_chip(value, flip):
        return lax.ppermute(value, "edge", [(k, k ^ flip) for k in range(owners)])

    def to_column(value):
        groups = [[first + 4 * part for part in range(z_parts)] for first in range(4)]
        return lax.all_to_all(value, "edge", 0, 0, axis_index_groups=groups, tiled=True)

    def pick(value, number):
        return lax.dynamic_index_in_dim(value, number, 0, False)

    def added(terms):
        return sum(one.astype(F32) for one in terms)

    chip = [(kept, to_core(given)) for kept, given in ((kept_a, given_a), (kept_b, given_b))]
    columns, sent_high, sent_low = [], [], []
    for stream in range(2):
        high, low = bits[stream], bits[1 - stream]
        terms = [one.reshape(2, 2, z_parts, tall, (taken + 1) * width) for one in chip[stream]]
        give = added([pick(one, 1 - high) for one in terms]).astype(BF16)
        sent_high.append(give)
        terms = [pick(one, high) for one in terms] + [to_chip(give, 1 << stream)]
        give = added([pick(one, 1 - low) for one in terms]).astype(BF16)
        sent_low.append(give)
        terms = [pick(one, low) for one in terms] + [to_chip(give, 2 >> stream)]
        columns.append(added(terms).astype(BF16))
    column = to_column(jnp.stack(columns, axis=1))
    column = full_call(
        spread_kernel,
        jax.ShapeDtypeStruct((z_parts, 2, tall * (taken + 1), width), BF16),
        (pltpu.VMEM((tall * (taken + 1), width), F32),),
        cost_estimate=cost(1),
    )(column)
    summed = column
    column = to_column(column)

    d_feats, d_first = [], []
    for batch in range(batches):
        d_pairs = lax.optimization_barrier([d_pairs] + (sent_low if batch else sent_high))[0]
        feats, first = full_call(
            functools.partial(edge_kernel, batch),
            (
                jax.ShapeDtypeStruct((edge_data.shape[0], feat_count, edge_data.shape[3]), BF16),
                jax.ShapeDtypeStruct((32, units), F32),
            ),
            cost_estimate=cost(6.5),
        )(edge_data, d_pairs, w_edge_in, b_edge_in)
        d_feats.append(feats)
        d_first.append(first)
    d_feats = jnp.stack(d_feats, axis=1)
    d_first = sum(d_first).astype(BF16)
    if merge > 1:
        d_feats = d_feats.reshape(owners // merge, batches, feat_count, merge, cap)
        d_feats = d_feats.transpose(0, 3, 1, 2, 4)
    d_feats = d_feats.reshape(owners, batches * feat_count, cap)
    spread = jnp.broadcast_to(
        d_first.reshape(1, 32 * units // cap, cap), (owners, 32 * units // cap, cap)
    )
    spread, _ = lax.optimization_barrier((jnp.concatenate([d_feats, spread], axis=1), summed))
    back = lax.all_to_all(spread, "edge", 0, 0, tiled=True)
    d_edges = back[:, : batches * feat_count].reshape(owners, batches, feat_count, cap)
    first_parts = back[:, batches * feat_count :].reshape(owners, 32, units)
    first_sum = jnp.sum(first_parts.astype(F32), axis=0)
    first_sum = first_sum + lax.ppermute(first_sum, "graph", swap)
    feat_grad = full_call(
        functools.partial(unroute_kernel, own),
        jax.ShapeDtypeStruct((batches, feat_count, edges), BF16),
        cost_estimate=cost(3),
    )(source_index, d_edges)

    along_x, along_y = to_chip(column, 1), to_chip(column, 2)
    far_a, far_b = to_chip(along_y[:, :1], 1), to_chip(along_x[:, 1:], 2)

    def spots(flip_x, flip_y, streams):
        x, y = bits[0] ^ flip_x, bits[1] ^ flip_y
        inner = (x * 2 + y, y * 2 + x)
        return [side * 4 + inner[stream] for side in (core, 1 - core) for stream in streams]

    shapes = tuple(
        jax.ShapeDtypeStruct(shape, F32)
        for shape in (
            (units, width * width),
            (width, width),
            (width, 3 * width),
            (width, 3 * width),
            (width, width),
        )
    )
    outs = ()
    for wave in (
        ((column, 0, 0, (0, 1)),),
        ((along_x, 1, 0, (0, 1)), (along_y, 0, 1, (0, 1))),
        ((far_a, 1, 1, (0,)), (far_b, 1, 1, (1,))),
    ):
        at, pieces, streams = [], [], []
        for piece, flip_x, flip_y, held in wave:
            at += spots(flip_x, flip_y, held)
            pieces += [piece, to_core(piece)]
            streams += [held, held]
        outs = place_pieces(tall, jnp.stack(at), pieces, streams, shapes, outs)
    d_w, d_bias, d_x, d_h, d_rows = outs
    rows = d_rows[:8].reshape(-1)
    return (
        new_states.reshape(batches, own, width),
        state_grad.reshape(batches, own, width),
        feat_grad,
        first_sum[:feat_count],
        first_sum[feat_count + 2],
        d_w,
        d_bias.reshape(-1),
        d_x,
        d_h,
        rows[: 3 * width],
        rows[3 * width : 6 * width],
    )


def solution(mesh):
    spread = ("graph", "edge")
    rows = P(None, spread, None)
    edges = P(None, spread)
    feats = P(None, None, spread)
    in_specs = (rows, feats, edges, edges) + (P(),) * 8 + (rows,)
    out_specs = (rows, rows, feats) + (P(),) * 8
    return jax.shard_map(
        body,
        mesh=mesh,
        in_specs=in_specs,
        out_specs=out_specs,
        check_vma=False,
    )
```

```python
import functools

import jax
import jax.numpy as jnp
from jax import lax
from jax.experimental import pallas as pl
from jax.experimental.pallas import tpu as pltpu
from jax.sharding import PartitionSpec as P

F32 = jnp.float32
BF16 = jnp.bfloat16
LANES = 128
GROUP = 12
PARAMS = pltpu.CompilerParams(vmem_limit_bytes=60 * 1024 * 1024)


def dot(first, second, dims=((1,), (0,))):
    return lax.dot_general(first, second, (dims, ((), ())), preferred_element_type=F32)


def dot_nt(first, second):
    return dot(first, second, ((1,), (1,)))


def row_ids(shape):
    return lax.broadcasted_iota(jnp.int32, shape, 0)


def col_ids(shape):
    return lax.broadcasted_iota(jnp.int32, shape, 1)


def full_call(kernel, out_shape, scratch=(), **more):
    return pl.pallas_call(
        kernel,
        out_shape=out_shape,
        scratch_shapes=scratch,
        compiler_params=PARAMS,
        **more,
    )


def ranks_of(owner, owners):
    hits = (row_ids((owners, owner.shape[1])) == owner).astype(F32)
    before = (row_ids((LANES, LANES)) < col_ids((LANES, LANES))).astype(BF16)
    seen = jnp.zeros((owners, 1), F32)
    ranks = []
    for start in range(0, owner.shape[1], LANES):
        part = hits[:, start : start + LANES]
        place = dot(part.astype(BF16), before) + seen
        ranks.append(jnp.sum(part * place, axis=0, keepdims=True))
        seen = seen + jnp.sum(part, axis=1, keepdims=True)
    return hits, jnp.concatenate(ranks, axis=1)


def route_kernel(own_rows, src_ref, dst_ref, feat_ref, out_ref):
    owners, batches, rows, cap = out_ref.shape
    edges = src_ref.shape[1]
    shift = own_rows.bit_length() - 1
    for batch in range(batches):
        source, target = src_ref[batch : batch + 1], dst_ref[batch : batch + 1]
        owner = source >> shift
        hits, rank = ranks_of(owner, owners)
        spots = (row_ids((cap, edges)) == rank.astype(jnp.int32)).astype(BF16)
        line = row_ids((16, edges))
        first = owner << shift
        extra = jnp.where(line == 0, source - first, jnp.where(line == 1, target - first, 1))
        extra = jnp.where(line < 3, extra, 0).astype(F32)
        load = jnp.concatenate([feat_ref[batch].astype(F32), extra], axis=0)
        for part in range(owners):
            masked = (load * hits[part : part + 1]).astype(BF16)
            out_ref[part, batch] = dot_nt(masked, spots).astype(BF16)


def unroute_kernel(own_rows, src_ref, back_ref, out_ref):
    owners, batches, rows, cap = back_ref.shape
    edges = src_ref.shape[1]
    shift = own_rows.bit_length() - 1
    for batch in range(batches):
        hits, rank = ranks_of(src_ref[batch : batch + 1] >> shift, owners)
        spots = (row_ids((cap, edges)) == rank.astype(jnp.int32)).astype(BF16)
        total = jnp.zeros((rows, edges), F32)
        for part in range(owners):
            total = total + dot(back_ref[part, batch], spots) * hits[part : part + 1]
        out_ref[batch] = total.astype(BF16)


def edge_piece(order_ref, edge_ref, piece, batch):
    two = [edge_ref[order_ref[batch, 2 * piece + k], batch] for k in range(2)]
    return jnp.concatenate(two, axis=1)


def order_blocks(edge_ref, order_ref):
    blocks, batches = edge_ref.shape[:2]
    for batch in range(batches):
        front, back = jnp.int32(0), jnp.int32(blocks - 1)
        for block in range(blocks):
            held = jnp.max(edge_ref[block, batch, 16:32].astype(F32)[2:3]) > 0.5
            order_ref[batch, jnp.where(held, front, back)] = jnp.int32(block)
            step = held.astype(jnp.int32)
            front, back = front + step, back - (1 - step)
        order_ref[batch, blocks] = front


def pair_masks(block):
    marks = block[16:32].astype(F32)
    source = marks[0:1].astype(jnp.int32)
    target = marks[1:2].astype(jnp.int32)
    held = marks[2:3] > 0.5
    code = ((target >> 3) & 3) * 128 + (target >> 5) * 64 + source
    code = jnp.where(held, code, -1)
    pairs = (row_ids((512, block.shape[1])) == code).astype(BF16)
    low = row_ids((8, block.shape[1])) == (target & 7)
    return pairs, low


def first_layer(w_in_ref, b_in_ref):
    bias = jnp.broadcast_to(b_in_ref[...].reshape(1, -1), (8, b_in_ref.shape[0]))
    return w_in_ref[...].astype(F32).T.astype(BF16), bias.T[:, :1]


def gates_of(mail_low, level, w_x, w_h, b_x, b_h):
    width = level.shape[1]
    from_mail = dot(mail_low, w_x[...]) + b_x[...].reshape(1, -1)
    from_state = dot(level, w_h[...]) + b_h[...].reshape(1, -1)
    reset = jax.nn.sigmoid(from_mail[:, :width] + from_state[:, :width])
    update = jax.nn.sigmoid(from_mail[:, width : 2 * width] + from_state[:, width : 2 * width])
    state_part = from_state[:, 2 * width :]
    candidate = jnp.tanh(from_mail[:, 2 * width :] + reset * state_part)
    return reset, update, candidate, state_part


def doubled(level):
    blank = jnp.zeros_like(level)
    return jnp.concatenate(
        [jnp.concatenate([level, blank], axis=1), jnp.concatenate([blank, level], axis=1)], axis=0
    )


def main_kernel(
    core_ref,
    edge_ref,
    state_ref,
    cot_ref,
    w_in_ref,
    b_in_ref,
    w_ref,
    bias_ref,
    w_x,
    w_h,
    b_x,
    b_h,
    new_ref,
    grad_ref,
    kept_a,
    kept_b,
    given_a,
    given_b,
    dg_ref,
    order_ref,
    hid_ref,
    acc_ref,
    g_ref,
    gt_ref,
    p_ref,
    part_ref,
    tail_ref,
):
    blocks, batches = edge_ref.shape[:2]
    hidden_units = hid_ref.shape[0]
    units = acc_ref.shape[0] // 8
    own = state_ref.shape[0] // batches
    half = own // 2
    span = GROUP * half
    wide = GROUP * LANES
    chunks = units // GROUP
    order_blocks(edge_ref, order_ref)

    tail_ref[...] = jnp.zeros_like(tail_ref)
    high = bias_ref[...].astype(BF16)
    tail_ref[0] = high
    tail_ref[1] = (bias_ref[...] - high.astype(F32)).astype(BF16)

    def weights_of(number):
        blocks = []
        for unit in range(number * GROUP, (number + 1) * GROUP):
            blocks.append(w_ref[unit] if unit < hidden_units else tail_ref[unit - hidden_units])
        return jnp.concatenate(blocks, axis=1)

    w_in, b_in = first_layer(w_in_ref, b_in_ref)

    for batch in range(batches):
        acc_ref[...] = jnp.zeros_like(acc_ref)

        def add_piece(piece, carry):
            block = edge_piece(order_ref, edge_ref, piece, batch)
            pairs, low = pair_masks(block)
            pre = dot(w_in, block[:16]) + b_in
            hid_ref[...] = (pre * jax.nn.sigmoid(pre)).astype(BF16).astype(F32)
            ones = jnp.where(low, 1.0, 0.0)
            parts = []
            for unit in range(0, hidden_units, 2):
                two = [jnp.where(low, hid_ref[unit + k : unit + k + 1], 0.0) for k in range(2)]
                parts.append(jnp.concatenate(two, axis=0).astype(BF16))
            parts.append(jnp.concatenate([ones, ones], axis=0).astype(BF16))
            parts.append(jnp.zeros((8 * (units - hidden_units - 2), block.shape[1]), BF16))
            acc_ref[...] += dot_nt(jnp.concatenate(parts, axis=0), pairs)
            return carry

        lax.fori_loop(0, (order_ref[batch, blocks] + 1) // 2, add_piece, 0)

        def place(step, carry):
            for four in range(3):
                rows = []
                for k in range(4):
                    for part in range(4):
                        start = pl.multiple_of(step * 96 + four * 32 + k * 8, 8)
                        rows.append(acc_ref[pl.ds(start, 8), part * LANES : (part + 1) * LANES])
                tile = jnp.concatenate(rows, axis=0).astype(BF16)
                at = pl.ds(pl.multiple_of((step * 3 + four) * LANES, LANES), LANES)
                g_ref[batch, at, :] = tile
                gt_ref[batch, :, at] = tile.T
            return carry

        lax.fori_loop(0, units // 12, place, 0)

    def forward(step, level):
        two = [doubled(level[batch * own : (batch + 1) * own]) for batch in range(batches)]
        mail = jnp.zeros((batches * own, LANES), F32)
        base = step * batches * own
        for number in range(chunks):
            for batch in range(batches):
                out = dot(g_ref[batch, number * span : (number + 1) * span, :], two[batch])
                out = out.astype(BF16)
                for unit in range(GROUP):
                    lane = number * wide + unit * LANES
                    for part in range(2):
                        row = base + batch * own + part * half
                        p_ref[row : row + half, lane : lane + LANES] = out[
                            unit * half : (unit + 1) * half, part * LANES : (part + 1) * LANES
                        ]
            rows = p_ref[base : base + batches * own, number * wide : (number + 1) * wide]
            mail = mail + dot_nt(rows, weights_of(number))
        return mail

    def backward(level, d_mail, last):
        two = [doubled(level[batch * own : (batch + 1) * own]) for batch in range(batches)]
        sums = [jnp.zeros((LANES, 2 * LANES), F32) for batch in range(batches)]
        for number in range(chunks):
            pulled = dot(d_mail, weights_of(number)).astype(BF16)
            at = slice(number * span, (number + 1) * span)
            for batch in range(batches):
                rows = []
                for unit in range(GROUP):
                    tile = pulled[batch * own : (batch + 1) * own, unit * LANES : (unit + 1) * LANES]
                    rows.append(jnp.concatenate([tile[:half], tile[half:]], axis=1))
                tall = jnp.concatenate(rows, axis=0)
                sums[batch] = sums[batch] + dot(gt_ref[batch, :, at], tall)
                d_pair = dot_nt(tall, two[batch])
                if not last:
                    part_ref[batch, at, :] = d_pair
                    continue
                d_pair = d_pair + part_ref[batch, at, :]
                for unit in range(0, GROUP, 2):
                    row = (number * GROUP + unit) * 8
                    for part in range(half // 8):
                        pair = [
                            d_pair[(unit + k) * half + part * 8 : (unit + k) * half + part * 8 + 8]
                            for k in range(2)
                        ]
                        dg_ref[batch, row : row + 16, part * LANES : (part + 1) * LANES] = (
                            jnp.concatenate(pair, axis=0).astype(BF16)
                        )
        return jnp.concatenate([one[:own, :LANES] + one[own:, LANES:] for one in sums], axis=0)

    weights = (w_x, w_h, b_x, b_h)
    level_zero = state_ref[...]
    state_zero = level_zero.astype(F32)
    mail_zero = forward(0, level_zero).astype(BF16)
    gates_zero = gates_of(mail_zero, level_zero, *weights)
    state_one = (1.0 - gates_zero[1]) * gates_zero[2] + gates_zero[1] * state_zero
    level_one = state_one.astype(BF16)
    mail_one = forward(1, level_one).astype(BF16)
    gates_one = gates_of(mail_one, level_one, *weights)
    new_ref[...] = ((1.0 - gates_one[1]) * gates_one[2] + gates_one[1] * state_one).astype(BF16)

    def gru_back(d_next, gates, current):
        reset, update, candidate, state_part = gates
        d_cand = d_next * (1.0 - update) * (1.0 - candidate * candidate)
        d_reset = d_cand * state_part * reset * (1.0 - reset)
        d_update = d_next * (current - candidate) * update * (1.0 - update)
        dg_mail = jnp.concatenate([d_reset, d_update, d_cand], axis=1).astype(BF16)
        dg_state = jnp.concatenate([d_reset, d_update, d_cand * reset], axis=1).astype(BF16)
        d_mail = dot_nt(dg_mail, w_x[...]).astype(BF16)
        d_current = d_next * update + dot_nt(dg_state, w_h[...])
        return dg_mail, dg_state, d_mail, d_current

    dgm_one, dgs_one, dm_one, d_state = gru_back(cot_ref[...].astype(F32), gates_one, state_one)
    d_state = d_state + backward(level_one, dm_one, False)
    dgm_zero, dgs_zero, dm_zero, d_state = gru_back(d_state, gates_zero, state_zero)
    d_state = d_state + backward(level_zero, dm_zero, True)
    grad_ref[...] = d_state.astype(BF16)

    def both(first, second):
        return jnp.concatenate([first.astype(F32), second.astype(F32)], axis=0)

    dms = both(dm_zero, dm_one).T.astype(BF16)
    mails, levels = both(mail_zero, mail_one), both(level_zero, level_one)
    dgm, dgs = both(dgm_zero, dgm_one), both(dgs_zero, dgs_one)
    width = dgm.shape[1]
    sums = [jnp.sum(one, axis=0, keepdims=True) for one in (dgm, dgs)]
    lines = [one[:, k : k + LANES] for one in sums for k in range(0, width, LANES)]
    line = row_ids((2 * own, LANES))
    bias_rows = jnp.zeros((2 * own, LANES), F32)
    for k, row in enumerate(lines):
        bias_rows = jnp.where(line == k, row, bias_rows)
    small = jnp.concatenate(
        [
            dot(dms, p_ref[:, hidden_units * LANES : (hidden_units + 1) * LANES]),
            dot(mails.T.astype(BF16), dgm.astype(BF16)),
            dot(levels.T.astype(BF16), dgs.astype(BF16)),
            bias_rows,
        ],
        axis=1,
    )

    first = core_ref[0] == 0
    swapped = jnp.concatenate([dms[own:], dms[:own]], axis=0)
    dms = jnp.where(first, dms.astype(F32), swapped.astype(F32)).astype(BF16)
    small = jnp.where(first, small, jnp.concatenate([small[own:], small[:own]], axis=0)).astype(BF16)
    start = 0
    for stream, (kept, given) in enumerate(((kept_a, given_a), (kept_b, given_b))):
        rows_in, groups, tall, wide_out = kept.shape
        taken = wide_out - LANES
        for group in range(groups):
            out = dot(dms, p_ref[:, start : start + taken]).astype(BF16)
            start += taken
            extra = small[:, (stream * 4 + group) * LANES : (stream * 4 + group + 1) * LANES]
            for row in range(rows_in):
                for ref, at in ((kept, row * tall), (given, (rows_in + row) * tall)):
                    ref[row, group, :, :taken] = out[at : at + tall]
                    ref[row, group, :, taken:] = extra[at : at + tall]


def edge_kernel(order_ref, edge_ref, dg_ref, w_in_ref, b_in_ref, feat_ref, win_ref):
    blocks, batches = edge_ref.shape[:2]
    hidden_units = w_in_ref.shape[1]
    w_in, b_in = first_layer(w_in_ref, b_in_ref)
    fold = (col_ids((hidden_units, 8 * hidden_units)) >> 3) == row_ids(
        (hidden_units, 8 * hidden_units)
    )
    fold = fold.astype(F32).astype(BF16)
    feat_ref[...] = jnp.zeros_like(feat_ref)

    def one_piece(piece, batch, total):
        block = edge_piece(order_ref, edge_ref, piece, batch)
        pairs, low = pair_masks(block)
        pre = dot(w_in, block[:16]) + b_in
        sig = jax.nn.sigmoid(pre)
        spread = dot(dg_ref[batch, : 8 * hidden_units], pairs)
        spread = spread.reshape(hidden_units, 8, block.shape[1])
        spread = jnp.where(low[None], spread, 0.0).reshape(8 * hidden_units, block.shape[1])
        d_hidden = dot(fold, spread.astype(BF16))
        d_pre = (d_hidden * sig * (1.0 + pre * (1.0 - sig))).astype(BF16)
        feats = dot(w_in_ref[...], d_pre).astype(BF16)
        for k in range(2):
            at = order_ref[batch, 2 * piece + k]
            feat_ref[at, batch] = feats[:, k * LANES : (k + 1) * LANES]
        return total + dot_nt(block, d_pre)

    total = jnp.zeros((32, hidden_units), F32)
    for batch in range(batches):
        total = lax.fori_loop(
            0,
            (order_ref[batch, blocks] + 1) // 2,
            lambda piece, acc: one_piece(piece, batch, acc),
            total,
        )
    win_ref[...] = total.astype(BF16)


def rows_kernel(wide_ref, out_ref, rows_ref):
    tall, wide = wide_ref.shape
    main = wide // LANES - 1
    total = wide_ref[...].astype(F32)
    for block in range(main):
        rows_ref[pl.ds(block, tall, stride=main), :] = total[:, block * LANES : (block + 1) * LANES]
    rows_ref[tall * main :, :] = total[:, main * LANES :]
    out_ref[...] = rows_ref[...].astype(BF16)


def rows_of(value):
    tall, wide = value.shape
    shape = (tall * (wide // LANES), LANES)
    return full_call(
        rows_kernel,
        jax.ShapeDtypeStruct(shape, BF16),
        (pltpu.VMEM(shape, F32),),
        cost_estimate=cost(1),
    )(value)


def place_kernel(tall, streams, carried, *refs):
    count = len(streams)
    at_ref, pieces = refs[0], refs[1 : 1 + count]
    outs = refs[1 + count + carried : 6 + count + carried]
    bigs = refs[6 + count + carried : 8 + count + carried]
    little, sems = refs[8 + count + carried :]
    d_w, d_bias, d_x, d_h, d_rows = outs
    used = [0, 0]
    copies = []
    for k, (stream, piece) in enumerate(zip(streams, pieces)):
        chunks, rows_in, lanes = piece.shape
        main = rows_in // tall - 1
        base = 0 if stream == 0 else d_w.shape[0] - 4 * main
        for chunk in range(chunks):
            slot = len(copies) // 2
            big = bigs[stream].at[used[stream]]
            used[stream] += 1
            rows = piece[chunk].astype(F32)
            for row in range(tall):
                big[:, row * lanes : (row + 1) * lanes] = rows[row * main : (row + 1) * main]
            little[slot] = rows[tall * main :]
            code = at_ref[k] ^ chunk
            line, part = code >> 2, code & 3
            at = pl.ds(pl.multiple_of(line * tall, 8), tall)
            big_copy = pltpu.make_async_copy(
                big,
                d_w.at[
                    pl.ds(pl.multiple_of(base + part * main, 8), main),
                    pl.ds(pl.multiple_of(line * (tall * lanes), LANES), tall * lanes),
                ],
                sems.at[slot, 0],
            )
            big_copy.start()
            alone, left, right = (0, d_bias, d_x) if stream == 0 else (3, d_rows, d_h)
            lane = (part - 1 if stream == 0 else part) * lanes
            one = pltpu.make_async_copy(little.at[slot], left.at[at, :], sems.at[slot, 1])
            wide = pl.ds(pl.multiple_of(jnp.maximum(jnp.minimum(lane, 2 * lanes), 0), LANES), lanes)
            other = pltpu.make_async_copy(little.at[slot], right.at[at, wide], sems.at[slot, 1])
            pl.when(part == alone)(one.start)
            pl.when(part != alone)(other.start)
            copies += [big_copy, one]
    for copy in copies:
        copy.wait()


def cost(micros):
    return pl.CostEstimate(
        flops=int(micros * 1e9), bytes_accessed=int(micros * 3e6), transcendentals=0
    )


def place_pieces(tall, at, pieces, streams, shapes, before=()):
    count = len(pieces)
    lanes = pieces[0].shape[2]
    slots = sum(piece.shape[0] for piece in pieces)
    bigs = []
    for stream in range(2):
        held = [piece for piece, one in zip(pieces, streams) if one == stream]
        main = held[0].shape[1] // tall - 1
        bigs.append(
            pltpu.VMEM((sum(piece.shape[0] for piece in held), main, tall * lanes), F32)
        )
    vmem = pl.BlockSpec(memory_space=pltpu.VMEM)
    hbm = pl.BlockSpec(memory_space=pl.ANY)
    return pl.pallas_call(
        functools.partial(place_kernel, tall, streams, len(before)),
        out_shape=shapes,
        in_specs=[pl.BlockSpec(memory_space=pltpu.SMEM)] + [vmem] * count + [hbm] * len(before),
        out_specs=[hbm] * len(shapes),
        scratch_shapes=(
            *bigs,
            pltpu.VMEM((slots, tall, lanes), F32),
            pltpu.SemaphoreType.DMA((slots, 2)),
        ),
        input_output_aliases={1 + count + k: k for k in range(len(before))},
        cost_estimate=cost(slots / 8),
        compiler_params=PARAMS,
    )(at, *pieces, *before)


def body(
    states,
    edge_feats,
    source_index,
    target_index,
    w_edge_in,
    b_edge_in,
    w_edge_out,
    b_edge_out,
    w_input,
    w_hidden,
    b_input,
    b_hidden,
    cotangent,
):
    batches, own, width = states.shape
    edges = source_index.shape[1]
    owners = lax.axis_size("edge")
    cap = max(2, 2 * edges // owners)
    feat_count, units = w_edge_in.shape

    sent = full_call(
        functools.partial(route_kernel, own),
        jax.ShapeDtypeStruct((owners, batches, 32, cap), BF16),
    )(source_index, target_index, edge_feats)
    edge_data = lax.all_to_all(sent, "edge", 0, 0, tiled=True)
    merge = max(1, LANES // cap)
    if merge > 1:
        edge_data = edge_data.reshape(owners // merge, merge, batches, 32, cap)
        edge_data = edge_data.transpose(0, 2, 3, 1, 4).reshape(
            owners // merge, batches, 32, merge * cap
        )

    w_mats = w_edge_out.reshape(units, width, width)
    padded = (units + 2 + GROUP - 1) // GROUP * GROUP

    tall = width // 8
    pairs = own // 2
    blocks = edge_data.shape[0]
    core = lax.axis_index("graph")
    spot = lax.axis_index("edge")
    halves = [
        jax.ShapeDtypeStruct((4, 4, tall, (main + 1) * width), BF16)
        for main in (units // 16 * 3, units // 16)
    ]
    smem = pl.BlockSpec(memory_space=pltpu.SMEM)
    vmem = pl.BlockSpec(memory_space=pltpu.VMEM)
    new_states, state_grad, kept_a, kept_b, given_a, given_b, d_pairs, order = full_call(
        main_kernel,
        (
            jax.ShapeDtypeStruct((batches * own, width), BF16),
            jax.ShapeDtypeStruct((batches * own, width), BF16),
            *halves,
            *halves,
            jax.ShapeDtypeStruct((batches, padded * 8, 512), BF16),
            jax.ShapeDtypeStruct((batches, blocks + 1), jnp.int32),
        ),
        (
            pltpu.VMEM((units, 2 * LANES), F32),
            pltpu.VMEM((padded * 8, 512), F32),
            pltpu.VMEM((batches, padded * pairs, LANES), BF16),
            pltpu.VMEM((batches, LANES, padded * pairs), BF16),
            pltpu.VMEM((2 * batches * own, padded * width), BF16),
            pltpu.VMEM((batches, padded * pairs, LANES), F32),
            pltpu.VMEM((padded - units, width, width), BF16),
        ),
        in_specs=[smem] + [vmem] * 11,
        out_specs=[vmem] * 7 + [smem],
    )(
        core.reshape(1),
        edge_data,
        states.reshape(batches * own, width),
        cotangent.reshape(batches * own, width),
        w_edge_in,
        b_edge_in,
        w_mats,
        b_edge_out.reshape(width, width),
        w_input,
        w_hidden,
        b_input,
        b_hidden,
    )

    orders = (((0, 1, 2, 3), (2, 0, 1, 3)), ((1, 2, 0, 3), (1, 2, 0, 3)))
    cores = lax.axis_size("graph")

    def to_core(value):
        return lax.ppermute(value, "graph", [(0, 1), (1, 0)])

    def swap(value, masks):
        moves = []
        for side in range(cores):
            first = side * owners
            moves += [(first + k, first + (k ^ masks[side])) for k in range(owners)]
        return lax.ppermute(value, ("graph", "edge"), moves)

    def swap_step(value, stream, step):
        return swap(value, [1 << orders[stream][side][step] for side in range(cores)])

    def bit(stream, side, step):
        first, second = [(spot >> orders[stream][k][step]) & 1 for k in range(2)]
        return jnp.where(side == 0, first, second)

    def pick(value, number):
        return lax.dynamic_index_in_dim(value, number, 0, False)

    def added(terms):
        return sum(one.astype(F32) for one in terms)

    def after(value, *others):
        return lax.optimization_barrier((value, *others))[0]

    def edge_grads(pairs_in):
        return pl.pallas_call(
            edge_kernel,
            out_shape=(
                jax.ShapeDtypeStruct((blocks, batches, feat_count, edge_data.shape[3]), BF16),
                jax.ShapeDtypeStruct((32, units), BF16),
            ),
            in_specs=[smem] + [vmem] * 4,
            cost_estimate=cost(9),
            compiler_params=PARAMS,
        )(order, edge_data, pairs_in, w_edge_in, b_edge_in)

    chip = [(kept, to_core(given)) for kept, given in ((kept_a, given_a), (kept_b, given_b))]
    terms = [[one.reshape((2,) * 4 + one.shape[2:]) for one in pair] for pair in chip]
    for step in range(4):
        gives = []
        for stream in range(2):
            number = bit(stream, core, step)
            give = added([pick(one, 1 - number) for one in terms[stream]]).astype(BF16)
            gives.append(give)
            terms[stream] = [pick(one, number) for one in terms[stream]]
        for stream in range(2):
            terms[stream].append(swap_step(gives[stream], stream, step))
        if step == 0:
            d_feats, d_first = edge_grads(after(d_pairs, *gives))
            for stream in range(2):
                terms[stream][-1] = after(terms[stream][-1], d_first)
    mine = []
    for stream in range(2):
        total = added(terms[stream]).astype(BF16)
        for extra in range(4, owners.bit_length() - 1):
            total = added([total, swap(total, [1 << extra] * cores)]).astype(BF16)
        mine.append(rows_of(total)[None])

    if merge > 1:
        d_feats = d_feats.reshape(owners // merge, batches, feat_count, merge, cap)
        d_feats = d_feats.transpose(0, 3, 1, 2, 4)
    d_feats = d_feats.reshape(owners, batches * feat_count, cap)
    spread = jnp.broadcast_to(
        d_first.reshape(1, 32 * units // cap, cap), (owners, 32 * units // cap, cap)
    )
    spread = after(jnp.concatenate([d_feats, spread], axis=1), *mine)
    back = lax.all_to_all(spread, "edge", 0, 0, tiled=True)
    d_edges = back[:, : batches * feat_count].reshape(owners, batches, feat_count, cap)
    first_parts = back[:, batches * feat_count :].reshape(owners, 32, units)
    first_sum = jnp.sum(first_parts.astype(F32), axis=0)
    first_sum = first_sum + to_core(first_sum)
    feat_grad = full_call(
        functools.partial(unroute_kernel, own),
        jax.ShapeDtypeStruct((batches, feat_count, edges), BF16),
        cost_estimate=cost(3),
    )(source_index, d_edges)

    near, far = [], []
    for stream in range(2):
        held = mine[stream]
        for step in (3, 2, 1):
            held = jnp.concatenate([held, swap_step(held, stream, step)], axis=0)
        near.append(held)
    for stream in range(2):
        far.append(swap_step(near[stream], stream, 0))

    shapes = tuple(
        jax.ShapeDtypeStruct(shape, F32)
        for shape in (
            (units, width * width),
            (width, width),
            (width, 3 * width),
            (width, 3 * width),
            (width, width),
        )
    )
    outs = ()
    for flip, wave in enumerate((near, far)):
        at, pieces, streams = [], [], []
        for stream, piece in enumerate(wave):
            for side, one in ((core, piece), (1 - core, to_core(piece))):
                code = side
                for step in range(4):
                    code = code * 2 + (bit(stream, side, step) ^ (flip if step == 0 else 0))
                at.append(code)
                pieces.append(one)
                streams.append(stream)
        outs = place_pieces(tall, jnp.stack(at), pieces, tuple(streams), shapes, outs)
    d_w, d_bias, d_x, d_h, d_rows = outs
    rows = d_rows[:8].reshape(-1)
    return (
        new_states.reshape(batches, own, width),
        state_grad.reshape(batches, own, width),
        feat_grad,
        first_sum[:feat_count],
        first_sum[feat_count + 2],
        d_w,
        d_bias.reshape(-1),
        d_x,
        d_h,
        rows[: 3 * width],
        rows[3 * width : 6 * width],
    )


def solution(mesh):
    spread = ("graph", "edge")
    rows = P(None, spread, None)
    edges = P(None, spread)
    feats = P(None, None, spread)
    in_specs = (rows, feats, edges, edges) + (P(),) * 8 + (rows,)
    out_specs = (rows, rows, feats) + (P(),) * 8
    return jax.shard_map(
        body,
        mesh=mesh,
        in_specs=in_specs,
        out_specs=out_specs,
        check_vma=False,
    )
```

```python
import functools

import jax
import jax.numpy as jnp
from jax import lax
from jax.experimental import pallas as pl
from jax.experimental.pallas import tpu as pltpu
from jax.sharding import PartitionSpec as P

F32 = jnp.float32
BF16 = jnp.bfloat16
LANES = 128
GROUP = 12
PARAMS = pltpu.CompilerParams(vmem_limit_bytes=60 * 1024 * 1024)


def dot(first, second, dims=((1,), (0,))):
    return lax.dot_general(first, second, (dims, ((), ())), preferred_element_type=F32)


def dot_nt(first, second):
    return dot(first, second, ((1,), (1,)))


def row_ids(shape):
    return lax.broadcasted_iota(jnp.int32, shape, 0)


def col_ids(shape):
    return lax.broadcasted_iota(jnp.int32, shape, 1)


def full_call(kernel, out_shape, scratch=(), **more):
    return pl.pallas_call(
        kernel,
        out_shape=out_shape,
        scratch_shapes=scratch,
        compiler_params=PARAMS,
        **more,
    )


def ranks_of(owner, owners):
    hits = (row_ids((owners, owner.shape[1])) == owner).astype(F32)
    before = (row_ids((LANES, LANES)) < col_ids((LANES, LANES))).astype(BF16)
    seen = jnp.zeros((owners, 1), F32)
    ranks = []
    for start in range(0, owner.shape[1], LANES):
        part = hits[:, start : start + LANES]
        place = dot(part.astype(BF16), before) + seen
        ranks.append(jnp.sum(part * place, axis=0, keepdims=True))
        seen = seen + jnp.sum(part, axis=1, keepdims=True)
    return hits, jnp.concatenate(ranks, axis=1)


def route_kernel(own_rows, src_ref, dst_ref, feat_ref, out_ref):
    owners, batches, rows, cap = out_ref.shape
    edges = src_ref.shape[1]
    shift = own_rows.bit_length() - 1
    for batch in range(batches):
        source, target = src_ref[batch : batch + 1], dst_ref[batch : batch + 1]
        owner = source >> shift
        hits, rank = ranks_of(owner, owners)
        spots = (row_ids((cap, edges)) == rank.astype(jnp.int32)).astype(BF16)
        line = row_ids((16, edges))
        first = owner << shift
        extra = jnp.where(line == 0, source - first, jnp.where(line == 1, target - first, 1))
        extra = jnp.where(line < 3, extra, 0).astype(F32)
        load = jnp.concatenate([feat_ref[batch].astype(F32), extra], axis=0)
        masked = [(load * hits[part : part + 1]).astype(BF16) for part in range(owners)]
        out = dot_nt(jnp.concatenate(masked, axis=0), spots).astype(BF16)
        for part in range(owners):
            out_ref[part, batch] = out[part * rows : (part + 1) * rows]


def unroute_kernel(own_rows, src_ref, back_ref, out_ref):
    owners, batches, rows, cap = back_ref.shape
    edges = src_ref.shape[1]
    shift = own_rows.bit_length() - 1
    for batch in range(batches):
        hits, rank = ranks_of(src_ref[batch : batch + 1] >> shift, owners)
        spots = (row_ids((cap, edges)) == rank.astype(jnp.int32)).astype(BF16)
        parts = [back_ref[part, batch] for part in range(owners)]
        spread = dot(jnp.concatenate(parts, axis=0), spots)
        total = jnp.zeros((rows, edges), F32)
        for part in range(owners):
            total = total + spread[part * rows : (part + 1) * rows] * hits[part : part + 1]
        out_ref[batch] = total.astype(BF16)


def edge_piece(order_ref, edge_ref, piece, batch):
    two = [edge_ref[order_ref[batch, 2 * piece + k], batch] for k in range(2)]
    return jnp.concatenate(two, axis=1)


def order_blocks(edge_ref, order_ref):
    blocks, batches = edge_ref.shape[:2]
    for batch in range(batches):
        front, back = jnp.int32(0), jnp.int32(blocks - 1)
        for block in range(blocks):
            held = jnp.max(edge_ref[block, batch, 16:32].astype(F32)[2:3]) > 0.5
            order_ref[batch, jnp.where(held, front, back)] = jnp.int32(block)
            step = held.astype(jnp.int32)
            front, back = front + step, back - (1 - step)
        order_ref[batch, blocks] = front


def pair_masks(block):
    marks = block[16:32].astype(F32)
    source = marks[0:1].astype(jnp.int32)
    target = marks[1:2].astype(jnp.int32)
    held = marks[2:3] > 0.5
    code = ((target >> 3) & 3) * 128 + (target >> 5) * 64 + source
    code = jnp.where(held, code, -1)
    pairs = (row_ids((512, block.shape[1])) == code).astype(BF16)
    low = row_ids((8, block.shape[1])) == (target & 7)
    return pairs, low


def first_layer(w_in_ref, b_in_ref):
    bias = jnp.broadcast_to(b_in_ref[...].reshape(1, -1), (8, b_in_ref.shape[0]))
    return w_in_ref[...].astype(F32).T.astype(BF16), bias.T[:, :1]


def gates_of(mail_low, level, w_x, w_h, b_x, b_h):
    width = level.shape[1]
    from_mail = dot(mail_low, w_x[...]) + b_x[...].reshape(1, -1)
    from_state = dot(level, w_h[...]) + b_h[...].reshape(1, -1)
    reset = jax.nn.sigmoid(from_mail[:, :width] + from_state[:, :width])
    update = jax.nn.sigmoid(from_mail[:, width : 2 * width] + from_state[:, width : 2 * width])
    state_part = from_state[:, 2 * width :]
    candidate = jnp.tanh(from_mail[:, 2 * width :] + reset * state_part)
    return reset, update, candidate, state_part


def doubled(level):
    blank = jnp.zeros_like(level)
    return jnp.concatenate(
        [jnp.concatenate([level, blank], axis=1), jnp.concatenate([blank, level], axis=1)], axis=0
    )


def main_kernel(
    core_ref,
    edge_ref,
    state_ref,
    cot_ref,
    w_in_ref,
    b_in_ref,
    w_ref,
    bias_ref,
    w_x,
    w_h,
    b_x,
    b_h,
    new_ref,
    grad_ref,
    kept_ref,
    given_ref,
    dg_ref,
    order_ref,
    rows_ref,
    hid_ref,
    acc_ref,
    g_ref,
    gt_ref,
    p_ref,
    part_ref,
    tail_ref,
):
    blocks, batches = edge_ref.shape[:2]
    hidden_units = hid_ref.shape[0]
    units = acc_ref.shape[0] // 8
    own = state_ref.shape[0] // batches
    half = own // 2
    span = GROUP * half
    wide = GROUP * LANES
    chunks = units // GROUP
    order_blocks(edge_ref, order_ref)

    tail_ref[...] = jnp.zeros_like(tail_ref)
    high = bias_ref[...].astype(BF16)
    tail_ref[0] = high
    tail_ref[1] = (bias_ref[...] - high.astype(F32)).astype(BF16)

    def weights_of(number):
        blocks = []
        for unit in range(number * GROUP, (number + 1) * GROUP):
            blocks.append(w_ref[unit] if unit < hidden_units else tail_ref[unit - hidden_units])
        return jnp.concatenate(blocks, axis=1)

    w_in, b_in = first_layer(w_in_ref, b_in_ref)

    for batch in range(batches):
        acc_ref[...] = jnp.zeros_like(acc_ref)

        def add_piece(piece, carry):
            block = edge_piece(order_ref, edge_ref, piece, batch)
            pairs, low = pair_masks(block)
            pre = dot(w_in, block[:16]) + b_in
            hid_ref[...] = (pre * jax.nn.sigmoid(pre)).astype(BF16).astype(F32)
            ones = jnp.where(low, 1.0, 0.0)
            parts = []
            for unit in range(0, hidden_units, 2):
                two = [jnp.where(low, hid_ref[unit + k : unit + k + 1], 0.0) for k in range(2)]
                parts.append(jnp.concatenate(two, axis=0).astype(BF16))
            parts.append(jnp.concatenate([ones, ones], axis=0).astype(BF16))
            parts.append(jnp.zeros((8 * (units - hidden_units - 2), block.shape[1]), BF16))
            acc_ref[...] += dot_nt(jnp.concatenate(parts, axis=0), pairs)
            return carry

        lax.fori_loop(0, (order_ref[batch, blocks] + 1) // 2, add_piece, 0)

        def place(step, carry):
            for four in range(3):
                rows = []
                for k in range(4):
                    for part in range(4):
                        start = pl.multiple_of(step * 96 + four * 32 + k * 8, 8)
                        rows.append(acc_ref[pl.ds(start, 8), part * LANES : (part + 1) * LANES])
                tile = jnp.concatenate(rows, axis=0).astype(BF16)
                at = pl.ds(pl.multiple_of((step * 3 + four) * LANES, LANES), LANES)
                g_ref[batch, at, :] = tile
                gt_ref[batch, :, at] = tile.T
            return carry

        lax.fori_loop(0, units // 12, place, 0)

    def forward(step, level):
        two = [doubled(level[batch * own : (batch + 1) * own]) for batch in range(batches)]
        mail = jnp.zeros((batches * own, LANES), F32)
        base = step * batches * own
        for number in range(chunks):
            for batch in range(batches):
                out = dot(g_ref[batch, number * span : (number + 1) * span, :], two[batch])
                out = out.astype(BF16)
                for unit in range(GROUP):
                    lane = number * wide + unit * LANES
                    for part in range(2):
                        row = base + batch * own + part * half
                        p_ref[row : row + half, lane : lane + LANES] = out[
                            unit * half : (unit + 1) * half, part * LANES : (part + 1) * LANES
                        ]
            rows = p_ref[base : base + batches * own, number * wide : (number + 1) * wide]
            mail = mail + dot_nt(rows, weights_of(number))
        return mail

    def backward(level, d_mail, last):
        two = [doubled(level[batch * own : (batch + 1) * own]) for batch in range(batches)]
        sums = [jnp.zeros((LANES, 2 * LANES), F32) for batch in range(batches)]
        for number in range(chunks):
            pulled = dot(d_mail, weights_of(number)).astype(BF16)
            at = slice(number * span, (number + 1) * span)
            for batch in range(batches):
                rows = []
                for unit in range(GROUP):
                    tile = pulled[batch * own : (batch + 1) * own, unit * LANES : (unit + 1) * LANES]
                    rows.append(jnp.concatenate([tile[:half], tile[half:]], axis=1))
                tall = jnp.concatenate(rows, axis=0)
                sums[batch] = sums[batch] + dot(gt_ref[batch, :, at], tall)
                d_pair = dot_nt(tall, two[batch])
                if not last:
                    part_ref[batch, at, :] = d_pair
                    continue
                d_pair = d_pair + part_ref[batch, at, :]
                for unit in range(0, GROUP, 2):
                    row = (number * GROUP + unit) * 8
                    for part in range(half // 8):
                        pair = [
                            d_pair[(unit + k) * half + part * 8 : (unit + k) * half + part * 8 + 8]
                            for k in range(2)
                        ]
                        dg_ref[batch, row : row + 16, part * LANES : (part + 1) * LANES] = (
                            jnp.concatenate(pair, axis=0).astype(BF16)
                        )
        return jnp.concatenate([one[:own, :LANES] + one[own:, LANES:] for one in sums], axis=0)

    weights = (w_x, w_h, b_x, b_h)
    level_zero = state_ref[...]
    state_zero = level_zero.astype(F32)
    mail_zero = forward(0, level_zero).astype(BF16)
    gates_zero = gates_of(mail_zero, level_zero, *weights)
    state_one = (1.0 - gates_zero[1]) * gates_zero[2] + gates_zero[1] * state_zero
    level_one = state_one.astype(BF16)
    mail_one = forward(1, level_one).astype(BF16)
    gates_one = gates_of(mail_one, level_one, *weights)
    new_ref[...] = ((1.0 - gates_one[1]) * gates_one[2] + gates_one[1] * state_one).astype(BF16)

    def gru_back(d_next, gates, current):
        reset, update, candidate, state_part = gates
        d_cand = d_next * (1.0 - update) * (1.0 - candidate * candidate)
        d_reset = d_cand * state_part * reset * (1.0 - reset)
        d_update = d_next * (current - candidate) * update * (1.0 - update)
        dg_mail = jnp.concatenate([d_reset, d_update, d_cand], axis=1).astype(BF16)
        dg_state = jnp.concatenate([d_reset, d_update, d_cand * reset], axis=1).astype(BF16)
        d_mail = dot_nt(dg_mail, w_x[...]).astype(BF16)
        d_current = d_next * update + dot_nt(dg_state, w_h[...])
        return dg_mail, dg_state, d_mail, d_current

    dgm_one, dgs_one, dm_one, d_state = gru_back(cot_ref[...].astype(F32), gates_one, state_one)
    d_state = d_state + backward(level_one, dm_one, False)
    dgm_zero, dgs_zero, dm_zero, d_state = gru_back(d_state, gates_zero, state_zero)
    d_state = d_state + backward(level_zero, dm_zero, True)
    grad_ref[...] = d_state.astype(BF16)

    def both(first, second):
        return jnp.concatenate([first.astype(F32), second.astype(F32)], axis=0)

    dms = both(dm_zero, dm_one).T.astype(BF16)
    mails, levels = both(mail_zero, mail_one), both(level_zero, level_one)
    dgm, dgs = both(dgm_zero, dgm_one), both(dgs_zero, dgs_one)
    width = dgm.shape[1]
    for k, one in enumerate((dgm, dgs)):
        total = jnp.sum(one, axis=0, keepdims=True)
        for part in range(3):
            row = 3 * k + part
            rows_ref[row : row + 1, :] = total[:, part * LANES : (part + 1) * LANES]
    rows_ref[6:, :] = jnp.zeros((rows_ref.shape[0] - 6, LANES), F32)
    small = jnp.concatenate(
        [
            dot(dms, p_ref[:, hidden_units * LANES : (hidden_units + 1) * LANES]),
            dot(mails.T.astype(BF16), dgm.astype(BF16)),
            dot(levels.T.astype(BF16), dgs.astype(BF16)),
            jnp.zeros((2 * own, LANES), F32),
        ],
        axis=1,
    )

    first = core_ref[0] == 0
    swapped = jnp.concatenate([dms[own:], dms[:own]], axis=0)
    dms = jnp.where(first, dms.astype(F32), swapped.astype(F32)).astype(BF16)
    small = jnp.where(first, small, jnp.concatenate([small[own:], small[:own]], axis=0)).astype(BF16)
    rows_in, groups, tall, wide_out = kept_ref.shape
    taken = wide_out - 2 * LANES
    for group in range(groups):
        out = dot(dms, p_ref[:, group * taken : (group + 1) * taken]).astype(BF16)
        extra = small[:, group * 2 * LANES : (group + 1) * 2 * LANES]
        for row in range(rows_in):
            for ref, at in ((kept_ref, row * tall), (given_ref, (rows_in + row) * tall)):
                ref[row, group, :, :taken] = out[at : at + tall]
                ref[row, group, :, taken:] = extra[at : at + tall]


def edge_kernel(order_ref, edge_ref, dg_ref, rows_ref, w_in_ref, b_in_ref, feat_ref, win_ref):
    blocks, batches = edge_ref.shape[:2]
    hidden_units = w_in_ref.shape[1]
    w_in, b_in = first_layer(w_in_ref, b_in_ref)
    fold = (col_ids((hidden_units, 8 * hidden_units)) >> 3) == row_ids(
        (hidden_units, 8 * hidden_units)
    )
    fold = fold.astype(F32).astype(BF16)
    feat_ref[...] = jnp.zeros_like(feat_ref)

    def one_piece(piece, batch, total):
        block = edge_piece(order_ref, edge_ref, piece, batch)
        pairs, low = pair_masks(block)
        pre = dot(w_in, block[:16]) + b_in
        sig = jax.nn.sigmoid(pre)
        spread = dot(dg_ref[batch, : 8 * hidden_units], pairs)
        spread = spread.reshape(hidden_units, 8, block.shape[1])
        spread = jnp.where(low[None], spread, 0.0).reshape(8 * hidden_units, block.shape[1])
        d_hidden = dot(fold, spread.astype(BF16))
        d_pre = (d_hidden * sig * (1.0 + pre * (1.0 - sig))).astype(BF16)
        feats = dot(w_in_ref[...], d_pre).astype(BF16)
        for k in range(2):
            at = order_ref[batch, 2 * piece + k]
            feat_ref[at, batch] = feats[:, k * LANES : (k + 1) * LANES]
        return total + dot_nt(block, d_pre)

    total = jnp.zeros((32, hidden_units), F32)
    for batch in range(batches):
        total = lax.fori_loop(
            0,
            (order_ref[batch, blocks] + 1) // 2,
            lambda piece, acc: one_piece(piece, batch, acc),
            total,
        )
    win_ref[...] = total.astype(BF16)
    win_ref[24:, :] = rows_ref[...].astype(BF16)


def rows_kernel(wide_ref, out_ref, rows_ref):
    tall, wide = wide_ref.shape
    main = wide // LANES - 2
    total = wide_ref[...].astype(F32)
    for block in range(main):
        rows_ref[pl.ds(block, tall, stride=main), :] = total[:, block * LANES : (block + 1) * LANES]
    for k in range(2):
        start = tall * (main + k)
        rows_ref[start : start + tall, :] = total[:, (main + k) * LANES : (main + k + 1) * LANES]
    out_ref[...] = rows_ref[...].astype(BF16)


def rows_of(value):
    tall, wide = value.shape
    shape = (tall * (wide // LANES), LANES)
    return full_call(
        rows_kernel,
        jax.ShapeDtypeStruct(shape, BF16),
        (pltpu.VMEM(shape, F32),),
        cost_estimate=cost(1),
    )(value)


def place_kernel(tall, count, carried, *refs):
    at_ref, pieces = refs[0], refs[1 : 1 + count]
    outs = refs[1 + count + carried : 6 + count + carried]
    big_ref, little_ref, sems = refs[6 + count + carried :]
    d_w, d_bias, d_x, d_h, d_rest = outs
    waits = []
    slot = 0
    for k, piece in enumerate(pieces):
        chunks, rows_in, lanes = piece.shape
        main = rows_in // tall - 2
        for chunk in range(chunks):
            code = at_ref[k] ^ chunk
            line, part = code >> 2, code & 3
            at = pl.ds(pl.multiple_of(line * tall, 8), tall)
            rows = piece[chunk].astype(F32)
            for row in range(tall):
                big_ref[slot, :, row * lanes : (row + 1) * lanes] = rows[row * main : (row + 1) * main]
            copy = pltpu.make_async_copy(
                big_ref.at[slot],
                d_w.at[
                    pl.ds(pl.multiple_of(part * main, 8), main),
                    pl.ds(pl.multiple_of(line * (tall * lanes), LANES), tall * lanes),
                ],
                sems.at[slot, 0],
            )
            copy.start()
            waits.append(copy)

            for side in range(2):
                start = tall * (main + side)
                little_ref[slot, side] = rows[start : start + tall]

                def move(target, lane):
                    lane = jnp.maximum(lane, 0) * lanes
                    to = pl.ds(pl.multiple_of(jnp.minimum(lane, target.shape[1] - lanes), LANES), lanes)
                    return pltpu.make_async_copy(
                        little_ref.at[slot, side], target.at[at, to], sems.at[slot, 1 + side]
                    )

                block = 2 * part + side
                to_x, to_h = move(d_x, block - 1), move(d_h, block - 4)
                alone = move((d_bias, d_rest)[side], 0)
                lone = block == 7 * side
                pl.when(lone)(alone.start)
                pl.when((block > 0) & (block < 4))(to_x.start)
                pl.when((block > 3) & (block < 7))(to_h.start)
                waits.append(alone)
            slot += 1
    for copy in waits:
        copy.wait()


def cost(micros):
    return pl.CostEstimate(
        flops=int(micros * 1e9), bytes_accessed=int(micros * 3e6), transcendentals=0
    )


def place_pieces(tall, at, pieces, shapes, before=()):
    count = len(pieces)
    chunks, rows_in, lanes = pieces[0].shape
    slots = count * chunks
    vmem = pl.BlockSpec(memory_space=pltpu.VMEM)
    hbm = pl.BlockSpec(memory_space=pl.ANY)
    return pl.pallas_call(
        functools.partial(place_kernel, tall, count, len(before)),
        out_shape=shapes,
        in_specs=[pl.BlockSpec(memory_space=pltpu.SMEM)] + [vmem] * count + [hbm] * len(before),
        out_specs=[hbm] * len(shapes),
        scratch_shapes=(
            pltpu.VMEM((slots, rows_in // tall - 2, tall * lanes), F32),
            pltpu.VMEM((slots, 2, tall, lanes), F32),
            pltpu.SemaphoreType.DMA((slots, 3)),
        ),
        input_output_aliases={1 + count + k: k for k in range(len(before))},
        cost_estimate=cost(slots / 4),
        compiler_params=PARAMS,
    )(at, *pieces, *before)


def body(
    states,
    edge_feats,
    source_index,
    target_index,
    w_edge_in,
    b_edge_in,
    w_edge_out,
    b_edge_out,
    w_input,
    w_hidden,
    b_input,
    b_hidden,
    cotangent,
):
    batches, own, width = states.shape
    edges = source_index.shape[1]
    owners = lax.axis_size("edge")
    cap = max(2, 2 * edges // owners)
    feat_count, units = w_edge_in.shape

    sent = full_call(
        functools.partial(route_kernel, own),
        jax.ShapeDtypeStruct((owners, batches, 32, cap), BF16),
    )(source_index, target_index, edge_feats)
    edge_data = lax.all_to_all(sent, "edge", 0, 0, tiled=True)
    merge = max(1, LANES // cap)
    if merge > 1:
        edge_data = edge_data.reshape(owners // merge, merge, batches, 32, cap)
        edge_data = edge_data.transpose(0, 2, 3, 1, 4).reshape(
            owners // merge, batches, 32, merge * cap
        )

    w_mats = w_edge_out.reshape(units, width, width)
    padded = (units + 2 + GROUP - 1) // GROUP * GROUP

    tall = width // 8
    pairs = own // 2
    blocks = edge_data.shape[0]
    core = lax.axis_index("graph")
    spot = lax.axis_index("edge")
    half_shape = jax.ShapeDtypeStruct((4, 4, tall, (units // 4 + 2) * width), BF16)
    smem = pl.BlockSpec(memory_space=pltpu.SMEM)
    vmem = pl.BlockSpec(memory_space=pltpu.VMEM)
    new_states, state_grad, kept, given, d_pairs, order, bias_rows = full_call(
        main_kernel,
        (
            jax.ShapeDtypeStruct((batches * own, width), BF16),
            jax.ShapeDtypeStruct((batches * own, width), BF16),
            half_shape,
            half_shape,
            jax.ShapeDtypeStruct((batches, padded * 8, 512), BF16),
            jax.ShapeDtypeStruct((batches, blocks + 1), jnp.int32),
            jax.ShapeDtypeStruct((8, width), F32),
        ),
        (
            pltpu.VMEM((units, 2 * LANES), F32),
            pltpu.VMEM((padded * 8, 512), F32),
            pltpu.VMEM((batches, padded * pairs, LANES), BF16),
            pltpu.VMEM((batches, LANES, padded * pairs), BF16),
            pltpu.VMEM((2 * batches * own, padded * width), BF16),
            pltpu.VMEM((batches, padded * pairs, LANES), F32),
            pltpu.VMEM((padded - units, width, width), BF16),
        ),
        in_specs=[smem] + [vmem] * 11,
        out_specs=[vmem] * 5 + [smem, vmem],
    )(
        core.reshape(1),
        edge_data,
        states.reshape(batches * own, width),
        cotangent.reshape(batches * own, width),
        w_edge_in,
        b_edge_in,
        w_mats,
        b_edge_out.reshape(width, width),
        w_input,
        w_hidden,
        b_input,
        b_hidden,
    )

    orders = ((0, 1, 2, 3), (2, 0, 1, 3))
    cores = lax.axis_size("graph")

    def to_core(value):
        return lax.ppermute(value, "graph", [(0, 1), (1, 0)])

    def swap(value, masks):
        moves = []
        for side in range(cores):
            first = side * owners
            moves += [(first + k, first + (k ^ masks[side])) for k in range(owners)]
        return lax.ppermute(value, ("graph", "edge"), moves)

    def swap_step(value, step):
        return swap(value, [1 << orders[side][step] for side in range(cores)])

    def bit(side, step):
        first, second = [(spot >> orders[k][step]) & 1 for k in range(2)]
        return jnp.where(side == 0, first, second)

    def pick(value, number):
        return lax.dynamic_index_in_dim(value, number, 0, False)

    def added(terms):
        return sum(one.astype(F32) for one in terms)

    def after(value, *others):
        return lax.optimization_barrier((value, *others))[0]

    def edge_grads(pairs_in):
        return pl.pallas_call(
            edge_kernel,
            out_shape=(
                jax.ShapeDtypeStruct((blocks, batches, feat_count, edge_data.shape[3]), BF16),
                jax.ShapeDtypeStruct((32, units), BF16),
            ),
            in_specs=[smem] + [vmem] * 5,
            cost_estimate=cost(9),
            compiler_params=PARAMS,
        )(order, edge_data, pairs_in, bias_rows, w_edge_in, b_edge_in)

    terms = [one.reshape((2,) * 4 + one.shape[2:]) for one in (kept, to_core(given))]
    for step in range(4):
        number = bit(core, step)
        give = added([pick(one, 1 - number) for one in terms]).astype(BF16)
        got = swap_step(give, step)
        if step == 0:
            d_feats, d_first = edge_grads(after(d_pairs, give))
            got = after(got, d_first)
        terms = [pick(one, number) for one in terms] + [got]
    total = added(terms).astype(BF16)
    for extra in range(4, owners.bit_length() - 1):
        total = added([total, swap(total, [1 << extra] * cores)]).astype(BF16)
    held = rows_of(total)[None]

    for step in (3, 2):
        held = jnp.concatenate([held, swap_step(held, step)], axis=0)
    near, far = swap_step(held, 1), swap_step(held, 0)
    last = swap_step(near, 0)

    if merge > 1:
        d_feats = d_feats.reshape(owners // merge, batches, feat_count, merge, cap)
        d_feats = d_feats.transpose(0, 3, 1, 2, 4)
    d_feats = d_feats.reshape(owners, batches * feat_count, cap)
    spread = jnp.broadcast_to(
        d_first.reshape(1, 32 * units // cap, cap), (owners, 32 * units // cap, cap)
    )
    spread = after(jnp.concatenate([d_feats, spread], axis=1), held)
    back = lax.all_to_all(spread, "edge", 0, 0, tiled=True)
    d_edges = back[:, : batches * feat_count].reshape(owners, batches, feat_count, cap)
    first_parts = back[:, batches * feat_count :].reshape(owners, 32, units)
    first_sum = jnp.sum(first_parts.astype(F32), axis=0)
    first_sum = first_sum + to_core(first_sum)
    feat_grad = full_call(
        functools.partial(unroute_kernel, own),
        jax.ShapeDtypeStruct((batches, feat_count, edges), BF16),
        cost_estimate=cost(3),
    )(source_index, d_edges)

    shapes = tuple(
        jax.ShapeDtypeStruct(shape, F32)
        for shape in (
            (units, width * width),
            (width, width),
            (width, 3 * width),
            (width, 3 * width),
            (width, width),
        )
    )
    outs = ()
    for number, wave in enumerate((((held, 0),), ((near, 4), (far, 8)), ((last, 12),))):
        at, pieces = [], []
        ready = (outs, tuple(piece for piece, _ in wave), back, feat_grad, first_sum)
        ready = lax.optimization_barrier(ready[: (2, 3, 5)[number]])
        outs, wave = ready[0], zip(ready[1], [flips for _, flips in wave])
        for piece, flips in wave:
            for side, one in ((core, piece), (1 - core, to_core(piece))):
                code = side
                for step in range(4):
                    code = code * 2 + bit(side, step)
                at.append(code ^ flips)
                pieces.append(one)
        outs = place_pieces(tall, jnp.stack(at), pieces, shapes, outs)
    d_w, d_bias, d_x, d_h, _ = outs
    return (
        new_states.reshape(batches, own, width),
        state_grad.reshape(batches, own, width),
        feat_grad,
        first_sum[:feat_count],
        first_sum[feat_count + 2],
        d_w,
        d_bias.reshape(-1),
        d_x,
        d_h,
        first_sum[24:27].reshape(-1),
        first_sum[27:30].reshape(-1),
    )


def solution(mesh):
    spread = ("graph", "edge")
    rows = P(None, spread, None)
    edges = P(None, spread)
    feats = P(None, None, spread)
    in_specs = (rows, feats, edges, edges) + (P(),) * 8 + (rows,)
    out_specs = (rows, rows, feats) + (P(),) * 8
    return jax.shard_map(
        body,
        mesh=mesh,
        in_specs=in_specs,
        out_specs=out_specs,
        check_vma=False,
    )
```

```python
import functools

import jax
import jax.numpy as jnp
from jax import lax
from jax.experimental import pallas as pl
from jax.experimental.pallas import tpu as pltpu
from jax.sharding import PartitionSpec as P

F32 = jnp.float32
BF16 = jnp.bfloat16
LANES = 128
GROUP = 12
PARAMS = pltpu.CompilerParams(vmem_limit_bytes=60 * 1024 * 1024)


def dot(first, second, dims=((1,), (0,))):
    return lax.dot_general(first, second, (dims, ((), ())), preferred_element_type=F32)


def dot_nt(first, second):
    return dot(first, second, ((1,), (1,)))


def row_ids(shape):
    return lax.broadcasted_iota(jnp.int32, shape, 0)


def col_ids(shape):
    return lax.broadcasted_iota(jnp.int32, shape, 1)


def full_call(kernel, out_shape, scratch=(), **more):
    return pl.pallas_call(
        kernel,
        out_shape=out_shape,
        scratch_shapes=scratch,
        compiler_params=PARAMS,
        **more,
    )


def ranks_of(owner, owners):
    hits = (row_ids((owners, owner.shape[1])) == owner).astype(F32)
    before = (row_ids((LANES, LANES)) < col_ids((LANES, LANES))).astype(BF16)
    seen = jnp.zeros((owners, 1), F32)
    ranks = []
    for start in range(0, owner.shape[1], LANES):
        part = hits[:, start : start + LANES]
        place = dot(part.astype(BF16), before) + seen
        ranks.append(jnp.sum(part * place, axis=0, keepdims=True))
        seen = seen + jnp.sum(part, axis=1, keepdims=True)
    return hits, jnp.concatenate(ranks, axis=1)


def route_kernel(own_rows, src_ref, dst_ref, feat_ref, out_ref):
    owners, rows, cap = out_ref.shape
    batches, feats, edges = feat_ref.shape
    shift = own_rows.bit_length() - 1
    marks = [jnp.zeros((16, cap), F32)] * owners
    for batch in range(batches):
        source, target = src_ref[batch : batch + 1], dst_ref[batch : batch + 1]
        owner = source >> shift
        hits, rank = ranks_of(owner, owners)
        spots = (row_ids((cap, edges)) == rank.astype(jnp.int32)).astype(BF16)
        line = row_ids((16, edges)) - 3 * batch
        first = owner << shift
        extra = jnp.where(line == 0, source - first, jnp.where(line == 1, target - first, 1))
        extra = jnp.where((line >= 0) & (line < 3), extra, 0).astype(F32)
        load = jnp.concatenate([feat_ref[batch].astype(F32), extra], axis=0)
        masked = [(load * hits[part : part + 1]).astype(BF16) for part in range(owners)]
        out = dot_nt(jnp.concatenate(masked, axis=0), spots)
        for part in range(owners):
            tile = out[part * (feats + 16) : (part + 1) * (feats + 16)]
            out_ref[part, batch * feats : (batch + 1) * feats] = tile[:feats].astype(BF16)
            marks[part] = marks[part] + tile[feats:]
    for part in range(owners):
        out_ref[part, batches * feats :] = marks[part].astype(BF16)


def unroute_kernel(own_rows, src_ref, back_ref, out_ref):
    owners, batches, rows, cap = back_ref.shape
    edges = src_ref.shape[1]
    shift = own_rows.bit_length() - 1
    for batch in range(batches):
        hits, rank = ranks_of(src_ref[batch : batch + 1] >> shift, owners)
        spots = (row_ids((cap, edges)) == rank.astype(jnp.int32)).astype(BF16)
        parts = [back_ref[part, batch] for part in range(owners)]
        spread = dot(jnp.concatenate(parts, axis=0), spots)
        total = jnp.zeros((rows, edges), F32)
        for part in range(owners):
            total = total + spread[part * rows : (part + 1) * rows] * hits[part : part + 1]
        out_ref[batch] = total.astype(BF16)


def edge_piece(batches, order_ref, edge_ref, piece, batch):
    two = [edge_ref[order_ref[batch, 2 * piece + k]] for k in range(2)]
    block = jnp.concatenate(two, axis=1)
    feats, marks = block[batch * 16 : (batch + 1) * 16], block[batches * 16 :].astype(F32)
    source = marks[3 * batch : 3 * batch + 1].astype(jnp.int32)
    target = marks[3 * batch + 1 : 3 * batch + 2].astype(jnp.int32)
    held = marks[3 * batch + 2 : 3 * batch + 3]
    code = ((target >> 3) & 3) * 128 + (target >> 5) * 64 + source
    code = jnp.where(held > 0.5, code, -1)
    pairs = (row_ids((512, block.shape[1])) == code).astype(BF16)
    low = row_ids((8, block.shape[1])) == (target & 7)
    return feats, held, pairs, low


def order_blocks(batches, edge_ref, order_ref):
    blocks = edge_ref.shape[0]
    for batch in range(batches):
        front, back = jnp.int32(0), jnp.int32(blocks - 1)
        row = 3 * batch + 2
        for block in range(blocks):
            marks = edge_ref[block, batches * 16 :].astype(F32)
            held = jnp.max(marks[row : row + 1]) > 0.5
            order_ref[batch, jnp.where(held, front, back)] = jnp.int32(block)
            step = held.astype(jnp.int32)
            front, back = front + step, back - (1 - step)
        order_ref[batch, blocks] = front


def first_layer(w_in_ref, b_in_ref):
    bias = jnp.broadcast_to(b_in_ref[...].reshape(1, -1), (8, b_in_ref.shape[0]))
    return w_in_ref[...].astype(F32).T.astype(BF16), bias.T[:, :1]


def gates_of(mail_low, level, w_x, w_h, b_x, b_h):
    width = level.shape[1]
    from_mail = dot(mail_low, w_x[...]) + b_x[...].reshape(1, -1)
    from_state = dot(level, w_h[...]) + b_h[...].reshape(1, -1)
    reset = jax.nn.sigmoid(from_mail[:, :width] + from_state[:, :width])
    update = jax.nn.sigmoid(from_mail[:, width : 2 * width] + from_state[:, width : 2 * width])
    state_part = from_state[:, 2 * width :]
    candidate = jnp.tanh(from_mail[:, 2 * width :] + reset * state_part)
    return reset, update, candidate, state_part


def doubled(level):
    blank = jnp.zeros_like(level)
    return jnp.concatenate(
        [jnp.concatenate([level, blank], axis=1), jnp.concatenate([blank, level], axis=1)], axis=0
    )


def bias_blocks(bias_ref, tail_ref):
    tail_ref[...] = jnp.zeros_like(tail_ref)
    high = bias_ref[...].astype(BF16)
    tail_ref[0] = high
    tail_ref[1] = (bias_ref[...] - high.astype(F32)).astype(BF16)


def weights_of(w_ref, tail_ref, number):
    units = w_ref.shape[0]
    blocks = []
    for unit in range(number * GROUP, (number + 1) * GROUP):
        blocks.append(w_ref[unit] if unit < units else tail_ref[unit - units])
    return jnp.concatenate(blocks, axis=1)


def pulled_rows(pulled, half):
    rows = []
    for start in range(0, pulled.shape[1], LANES):
        tile = pulled[:, start : start + LANES]
        rows.append(jnp.concatenate([tile[:half], tile[half:]], axis=1))
    return jnp.concatenate(rows, axis=0)


def main_kernel(
    where_ref,
    edge_ref,
    state_ref,
    cot_ref,
    w_in_ref,
    b_in_ref,
    w_far,
    bias_ref,
    w_x,
    w_h,
    b_x,
    b_h,
    new_ref,
    kept_first,
    kept_last,
    given_first,
    given_last,
    gt_ref,
    level_ref,
    dm_ref,
    base_ref,
    order_ref,
    rows_ref,
    hid_ref,
    acc_ref,
    g_ref,
    p_ref,
    w_ref,
    tail_ref,
    sem,
):
    fetch = pltpu.make_async_copy(w_far, w_ref, sem)
    fetch.start()
    blocks = edge_ref.shape[0]
    batches = g_ref.shape[0]
    hidden_units = hid_ref.shape[0]
    units = acc_ref.shape[0] // 8
    own = state_ref.shape[0] // batches
    half = own // 2
    span = GROUP * half
    wide = GROUP * LANES
    chunks = units // GROUP
    order_blocks(batches, edge_ref, order_ref)
    bias_blocks(bias_ref, tail_ref)
    w_in, b_in = first_layer(w_in_ref, b_in_ref)

    for batch in range(batches):
        acc_ref[...] = jnp.zeros_like(acc_ref)

        def add_piece(piece, carry):
            feats, held, pairs, low = edge_piece(batches, order_ref, edge_ref, piece, batch)
            pre = dot(w_in, feats) + b_in
            hid_ref[...] = (pre * jax.nn.sigmoid(pre)).astype(BF16).astype(F32)
            ones = jnp.where(low, 1.0, 0.0)
            parts = []
            for unit in range(0, hidden_units, 2):
                two = [jnp.where(low, hid_ref[unit + k : unit + k + 1], 0.0) for k in range(2)]
                parts.append(jnp.concatenate(two, axis=0).astype(BF16))
            parts.append(jnp.concatenate([ones, ones], axis=0).astype(BF16))
            parts.append(jnp.zeros((8 * (units - hidden_units - 2), pre.shape[1]), BF16))
            acc_ref[...] += dot_nt(jnp.concatenate(parts, axis=0), pairs)
            return carry

        lax.fori_loop(0, (order_ref[batch, blocks] + 1) // 2, add_piece, 0)

        def place(step, carry):
            for four in range(3):
                rows = []
                for k in range(4):
                    for part in range(4):
                        start = pl.multiple_of(step * 96 + four * 32 + k * 8, 8)
                        rows.append(acc_ref[pl.ds(start, 8), part * LANES : (part + 1) * LANES])
                tile = jnp.concatenate(rows, axis=0).astype(BF16)
                at = pl.ds(pl.multiple_of((step * 3 + four) * LANES, LANES), LANES)
                g_ref[batch, at, :] = tile
                gt_ref[batch, :, at] = tile.T
            return carry

        lax.fori_loop(0, units // 12, place, 0)

    def forward(step, level):
        two = [doubled(level[batch * own : (batch + 1) * own]) for batch in range(batches)]
        mail = jnp.zeros((batches * own, LANES), F32)
        base = step * batches * own
        for number in range(chunks):
            for batch in range(batches):
                out = dot(g_ref[batch, number * span : (number + 1) * span, :], two[batch])
                out = out.astype(BF16)
                for unit in range(GROUP):
                    lane = number * wide + unit * LANES
                    for part in range(2):
                        row = base + batch * own + part * half
                        p_ref[row : row + half, lane : lane + LANES] = out[
                            unit * half : (unit + 1) * half, part * LANES : (part + 1) * LANES
                        ]
            rows = p_ref[base : base + batches * own, number * wide : (number + 1) * wide]
            mail = mail + dot_nt(rows, weights_of(w_ref, tail_ref, number))
        return mail

    def backward(d_mail):
        sums = [jnp.zeros((LANES, 2 * LANES), F32) for batch in range(batches)]
        for number in range(chunks):
            pulled = dot(d_mail, weights_of(w_ref, tail_ref, number)).astype(BF16)
            at = slice(number * span, (number + 1) * span)
            for batch in range(batches):
                tall = pulled_rows(pulled[batch * own : (batch + 1) * own], half)
                sums[batch] = sums[batch] + dot(gt_ref[batch, :, at], tall)
        return jnp.concatenate([one[:own, :LANES] + one[own:, LANES:] for one in sums], axis=0)

    weights = (w_x, w_h, b_x, b_h)
    level_zero = state_ref[...]
    state_zero = level_zero.astype(F32)
    fetch.wait()
    mail_zero = forward(0, level_zero).astype(BF16)
    gates_zero = gates_of(mail_zero, level_zero, *weights)
    state_one = (1.0 - gates_zero[1]) * gates_zero[2] + gates_zero[1] * state_zero
    level_one = state_one.astype(BF16)
    mail_one = forward(1, level_one).astype(BF16)
    gates_one = gates_of(mail_one, level_one, *weights)
    new_ref[...] = ((1.0 - gates_one[1]) * gates_one[2] + gates_one[1] * state_one).astype(BF16)

    def gru_back(d_next, gates, current):
        reset, update, candidate, state_part = gates
        d_cand = d_next * (1.0 - update) * (1.0 - candidate * candidate)
        d_reset = d_cand * state_part * reset * (1.0 - reset)
        d_update = d_next * (current - candidate) * update * (1.0 - update)
        dg_mail = jnp.concatenate([d_reset, d_update, d_cand], axis=1).astype(BF16)
        dg_state = jnp.concatenate([d_reset, d_update, d_cand * reset], axis=1).astype(BF16)
        d_mail = dot_nt(dg_mail, w_x[...]).astype(BF16)
        d_current = d_next * update + dot_nt(dg_state, w_h[...])
        return dg_mail, dg_state, d_mail, d_current

    dgm_one, dgs_one, dm_one, d_state = gru_back(cot_ref[...].astype(F32), gates_one, state_one)
    d_state = d_state + backward(dm_one)
    dgm_zero, dgs_zero, dm_zero, d_state = gru_back(d_state, gates_zero, state_zero)
    base_ref[...] = d_state
    level_ref[...] = jnp.concatenate([level_zero, level_one], axis=1)
    dm_ref[...] = jnp.concatenate([dm_zero, dm_one], axis=1)

    def both(first, second):
        return jnp.concatenate([first.astype(F32), second.astype(F32)], axis=0)

    dms = both(dm_zero, dm_one).T
    mails, levels = both(mail_zero, mail_one), both(level_zero, level_one)
    dgm, dgs = both(dgm_zero, dgm_one), both(dgs_zero, dgs_one)
    width = dgm.shape[1]
    rows_ref[...] = jnp.zeros_like(rows_ref)
    for k, one in enumerate((dgm, dgs)):
        total = jnp.sum(one, axis=0, keepdims=True)
        for part in range(3):
            row = 24 + 3 * k + part
            rows_ref[row : row + 1, :] = total[:, part * LANES : (part + 1) * LANES]
    small = jnp.concatenate(
        [
            dot(dms.astype(BF16), p_ref[:, hidden_units * LANES : (hidden_units + 1) * LANES]),
            dot(mails.T.astype(BF16), dgm.astype(BF16)),
            dot(levels.T.astype(BF16), dgs.astype(BF16)),
            jnp.zeros((2 * own, LANES), F32),
        ],
        axis=1,
    )

    def sorted_rows(value):
        rows = value.shape[0] // 2
        upper, lower = value[:rows], value[rows:]
        halves = [jnp.where(where_ref[0] == k, upper, lower) for k in range(2)]
        parts = []
        for k, one in enumerate(halves):
            first, second = one[: rows // 2], one[rows // 2 :]
            parts += [jnp.where(where_ref[1 + k] == side, second, first) for side in range(2)]
        return jnp.concatenate(parts, axis=0).astype(BF16)

    dms, small = sorted_rows(dms), sorted_rows(small)
    rows_in, groups, tall, wide_out = kept_first.shape
    taken = wide_out - 2 * LANES
    for group in range(groups):
        out = dot(dms, p_ref[:, group * taken : (group + 1) * taken]).astype(BF16)
        extra = small[:, group * 2 * LANES : (group + 1) * 2 * LANES]
        at = 0
        for ref in (kept_first, kept_last, given_first, given_last):
            for row in range(rows_in):
                ref[row, group, :, :taken] = out[at : at + tall]
                ref[row, group, :, taken:] = extra[at : at + tall]
                at += tall


def edge_kernel(
    batch,
    order_ref,
    edge_ref,
    gt_ref,
    level_ref,
    dm_ref,
    base_ref,
    w_in_ref,
    b_in_ref,
    w_ref,
    bias_ref,
    before_ref,
    grad_ref,
    feat_ref,
    win_ref,
    tail_ref,
    dg_ref,
):
    blocks = edge_ref.shape[0]
    batches = gt_ref.shape[0]
    hidden_units = w_in_ref.shape[1]
    chunks = (hidden_units + tail_ref.shape[0]) // GROUP
    own, width = grad_ref.shape
    half = own // 2
    mine = slice(batch * own, (batch + 1) * own)
    bias_blocks(bias_ref, tail_ref)

    pulls = [dm_ref[mine, step * width : (step + 1) * width] for step in range(2)]
    levels = [doubled(level_ref[mine, step * width : (step + 1) * width]) for step in range(2)]
    levels = jnp.concatenate(levels, axis=1)
    total = jnp.zeros((2 * own, 2 * width), F32)
    both = jnp.concatenate(pulls, axis=0)
    for number in range(chunks):
        pulled = dot(both, weights_of(w_ref, tail_ref, number)).astype(BF16)
        talls = [pulled_rows(pulled[k * own : (k + 1) * own], half) for k in range(2)]
        at = slice(number * GROUP * half, (number + 1) * GROUP * half)
        total = total + dot(gt_ref[batch, :, at], talls[0])
        d_pair = dot_nt(jnp.concatenate(talls, axis=1), levels)
        for unit in range(0, GROUP, 2):
            row = (number * GROUP + unit) * 8
            for part in range(half // 8):
                pair = [
                    d_pair[(unit + k) * half + part * 8 : (unit + k) * half + part * 8 + 8]
                    for k in range(2)
                ]
                dg_ref[row : row + 16, part * LANES : (part + 1) * LANES] = jnp.concatenate(
                    pair, axis=0
                ).astype(BF16)
    grad = base_ref[mine] + total[:own, :width] + total[own:, width:]
    grad_ref[...] = grad.astype(BF16)

    w_in, b_in = first_layer(w_in_ref, b_in_ref)
    fold = (col_ids((hidden_units, 8 * hidden_units)) >> 3) == row_ids(
        (hidden_units, 8 * hidden_units)
    )
    fold = fold.astype(F32).astype(BF16)
    feat_ref[...] = jnp.zeros_like(feat_ref)

    def one_piece(piece, sums):
        feats, held, pairs, low = edge_piece(batches, order_ref, edge_ref, piece, batch)
        pre = dot(w_in, feats) + b_in
        sig = jax.nn.sigmoid(pre)
        spread = dot(dg_ref[: 8 * hidden_units], pairs)
        spread = spread.reshape(hidden_units, 8, pre.shape[1])
        spread = jnp.where(low[None], spread, 0.0).reshape(8 * hidden_units, pre.shape[1])
        d_hidden = dot(fold, spread.astype(BF16))
        d_pre = (d_hidden * sig * (1.0 + pre * (1.0 - sig))).astype(BF16)
        out = dot(w_in_ref[...], d_pre).astype(BF16)
        for k in range(2):
            feat_ref[order_ref[batch, 2 * piece + k]] = out[:, k * LANES : (k + 1) * LANES]
        ones = jnp.where(row_ids((16, pre.shape[1])) == 0, held, 0.0).astype(BF16)
        return sums + dot_nt(jnp.concatenate([feats, ones], axis=0), d_pre)

    win_ref[...] = lax.fori_loop(
        0, (order_ref[batch, blocks] + 1) // 2, one_piece, before_ref[...]
    )


def rows_kernel(wide_ref, out_ref, rows_ref):
    tall, wide = wide_ref.shape
    main = wide // LANES - 2
    total = wide_ref[...].astype(F32)
    for block in range(main):
        rows_ref[pl.ds(block, tall, stride=main), :] = total[:, block * LANES : (block + 1) * LANES]
    for k in range(2):
        start = tall * (main + k)
        rows_ref[start : start + tall, :] = total[:, (main + k) * LANES : (main + k + 1) * LANES]
    out_ref[...] = rows_ref[...].astype(BF16)


def rows_of(value):
    tall, wide = value.shape
    shape = (tall * (wide // LANES), LANES)
    return full_call(
        rows_kernel,
        jax.ShapeDtypeStruct(shape, BF16),
        (pltpu.VMEM(shape, F32),),
        cost_estimate=cost(1),
    )(value)


def place_kernel(tall, count, carried, *refs):
    at_ref, pieces = refs[0], refs[1 : 1 + count]
    outs = refs[1 + count + carried : 6 + count + carried]
    big_ref, little_ref, sems = refs[6 + count + carried :]
    d_w, d_bias, d_x, d_h, d_rest = outs
    waits = []
    slot = 0
    for k, piece in enumerate(pieces):
        chunks, rows_in, lanes = piece.shape
        main = rows_in // tall - 2
        for chunk in range(chunks):
            code = at_ref[k] ^ chunk
            line, part = code >> 2, code & 3
            at = pl.ds(pl.multiple_of(line * tall, 8), tall)
            rows = piece[chunk].astype(F32)
            for row in range(tall):
                big_ref[slot, :, row * lanes : (row + 1) * lanes] = rows[row * main : (row + 1) * main]
            copy = pltpu.make_async_copy(
                big_ref.at[slot],
                d_w.at[
                    pl.ds(pl.multiple_of(part * main, 8), main),
                    pl.ds(pl.multiple_of(line * (tall * lanes), LANES), tall * lanes),
                ],
                sems.at[slot, 0],
            )
            copy.start()
            waits.append(copy)

            for side in range(2):
                start = tall * (main + side)
                little_ref[slot, side] = rows[start : start + tall]

                def move(target, lane):
                    lane = jnp.maximum(lane, 0) * lanes
                    to = pl.ds(pl.multiple_of(jnp.minimum(lane, target.shape[1] - lanes), LANES), lanes)
                    return pltpu.make_async_copy(
                        little_ref.at[slot, side], target.at[at, to], sems.at[slot, 1 + side]
                    )

                block = 2 * part + side
                to_x, to_h = move(d_x, block - 1), move(d_h, block - 4)
                alone = move((d_bias, d_rest)[side], 0)
                lone = block == 7 * side
                pl.when(lone)(alone.start)
                pl.when((block > 0) & (block < 4))(to_x.start)
                pl.when((block > 3) & (block < 7))(to_h.start)
                waits.append(alone)
            slot += 1
    for copy in waits:
        copy.wait()


def cost(micros):
    return pl.CostEstimate(
        flops=int(micros * 1e9), bytes_accessed=int(micros * 3e6), transcendentals=0
    )


def place_pieces(tall, at, pieces, shapes, before=()):
    count = len(pieces)
    chunks, rows_in, lanes = pieces[0].shape
    slots = count * chunks
    vmem = pl.BlockSpec(memory_space=pltpu.VMEM)
    hbm = pl.BlockSpec(memory_space=pl.ANY)
    return pl.pallas_call(
        functools.partial(place_kernel, tall, count, len(before)),
        out_shape=shapes,
        in_specs=[pl.BlockSpec(memory_space=pltpu.SMEM)] + [vmem] * count + [hbm] * len(before),
        out_specs=[hbm] * len(shapes),
        scratch_shapes=(
            pltpu.VMEM((slots, rows_in // tall - 2, tall * lanes), F32),
            pltpu.VMEM((slots, 2, tall, lanes), F32),
            pltpu.SemaphoreType.DMA((slots, 3)),
        ),
        input_output_aliases={1 + count + k: k for k in range(len(before))},
        cost_estimate=cost(slots / 4),
        compiler_params=PARAMS,
    )(at, *pieces, *before)


def body(
    states,
    edge_feats,
    source_index,
    target_index,
    w_edge_in,
    b_edge_in,
    w_edge_out,
    b_edge_out,
    w_input,
    w_hidden,
    b_input,
    b_hidden,
    cotangent,
):
    batches, own, width = states.shape
    edges = source_index.shape[1]
    owners = lax.axis_size("edge")
    cap = max(2, 2 * edges // owners)
    feat_count, units = w_edge_in.shape

    sent = full_call(
        functools.partial(route_kernel, own),
        jax.ShapeDtypeStruct((owners, batches * feat_count + 16, cap), BF16),
    )(source_index, target_index, edge_feats)
    edge_data = lax.all_to_all(sent, "edge", 0, 0, tiled=True)
    merge = max(1, LANES // cap)
    if merge > 1:
        edge_data = edge_data.reshape(owners // merge, merge, -1, cap).transpose(0, 2, 1, 3)
        edge_data = edge_data.reshape(owners // merge, -1, merge * cap)

    w_mats = w_edge_out.reshape(units, width, width)
    padded = (units + 2 + GROUP - 1) // GROUP * GROUP

    tall = width // 8
    pairs = own // 2
    blocks = edge_data.shape[0]
    core = lax.axis_index("graph")
    spot = lax.axis_index("edge")
    orders = ((0, 1, 2, 3), (2, 0, 1, 3))

    def bit(side, step):
        first, second = [(spot >> orders[k][step]) & 1 for k in range(2)]
        return jnp.where(side == 0, first, second)

    where = jnp.stack([core, bit(core, 0), bit(1 - core, 0)])
    smem = pl.BlockSpec(memory_space=pltpu.SMEM)
    vmem = pl.BlockSpec(memory_space=pltpu.VMEM)
    bias = b_edge_out.reshape(width, width)
    quarter = jax.ShapeDtypeStruct((2, 4, tall, (units // 4 + 2) * width), BF16)
    new_states, *sums, gt, levels, d_mails, base, order, first = full_call(
        main_kernel,
        (
            jax.ShapeDtypeStruct((batches * own, width), BF16),
            *[quarter] * 4,
            jax.ShapeDtypeStruct((batches, LANES, padded * pairs), BF16),
            jax.ShapeDtypeStruct((batches * own, 2 * width), BF16),
            jax.ShapeDtypeStruct((batches * own, 2 * width), BF16),
            jax.ShapeDtypeStruct((batches * own, width), F32),
            jax.ShapeDtypeStruct((batches, blocks + 1), jnp.int32),
            jax.ShapeDtypeStruct((32, width), F32),
        ),
        (
            pltpu.VMEM((units, 2 * LANES), F32),
            pltpu.VMEM((padded * 8, 512), F32),
            pltpu.VMEM((batches, padded * pairs, LANES), BF16),
            pltpu.VMEM((2 * batches * own, padded * width), BF16),
            pltpu.VMEM((units, width, width), BF16),
            pltpu.VMEM((padded - units, width, width), BF16),
            pltpu.SemaphoreType.DMA(()),
        ),
        in_specs=[smem] + [vmem] * 5 + [pl.BlockSpec(memory_space=pl.ANY)] + [vmem] * 5,
        out_specs=[vmem] * 9 + [smem, vmem],
    )(
        where,
        edge_data,
        states.reshape(batches * own, width),
        cotangent.reshape(batches * own, width),
        w_edge_in,
        b_edge_in,
        w_mats,
        bias,
        w_input,
        w_hidden,
        b_input,
        b_hidden,
    )

    cores = lax.axis_size("graph")

    def to_core(value):
        return lax.ppermute(value, "graph", [(0, 1), (1, 0)])

    def swap(value, masks):
        moves = []
        for side in range(cores):
            first = side * owners
            moves += [(first + k, first + (k ^ masks[side])) for k in range(owners)]
        return lax.ppermute(value, ("graph", "edge"), moves)

    def swap_step(value, step):
        return swap(value, [1 << orders[side][step] for side in range(cores)])

    def pick(value, number):
        return lax.dynamic_index_in_dim(value, number, 0, False)

    def added(terms):
        return sum(one.astype(F32) for one in terms)

    def after(value, *others):
        return lax.optimization_barrier((value, *others))[0]

    def edge_grads(batch, gt_in, first):
        return full_call(
            functools.partial(edge_kernel, batch),
            (
                jax.ShapeDtypeStruct((own, width), BF16),
                jax.ShapeDtypeStruct((blocks, feat_count, edge_data.shape[2]), BF16),
                jax.ShapeDtypeStruct((32, units), F32),
            ),
            (
                pltpu.VMEM((padded - units, width, width), BF16),
                pltpu.VMEM((padded * 8, 512), BF16),
            ),
            in_specs=[smem] + [vmem] * 10,
            cost_estimate=cost(9),
        )(
            order, edge_data, gt_in, levels, d_mails, base,
            w_edge_in, b_edge_in, w_mats, bias, first,
        )

    kept_first, kept_last, given_first, given_last = sums
    got_first, got_last = to_core(given_first), to_core(given_last)
    give = added([kept_first, got_first]).astype(BF16)
    terms = [kept_last, got_last]
    state_grad, d_feats = [], []
    for step in range(4):
        if step > 0:
            number = bit(core, step)
            give = added([pick(one, 1 - number) for one in terms]).astype(BF16)
            terms = [pick(one, number) for one in terms]
        got = swap_step(give, step)
        if step < batches:
            grad, feats, first = edge_grads(step, after(gt, give), first)
            got = after(got, first)
            state_grad.append(grad)
            d_feats.append(feats)
        if step == 2:
            fourth = give
        terms.append(got)
        if step == 0:
            terms = [one.reshape((2, 2, 2) + one.shape[2:]) for one in terms]
    total = added(terms).astype(BF16)
    for extra in range(4, owners.bit_length() - 1):
        total = added([total, swap(total, [1 << extra] * cores)]).astype(BF16)
    held = rows_of(total)[None]

    if merge > 1:
        d_feats = [
            one.reshape(blocks, feat_count, merge, cap).transpose(0, 2, 1, 3).reshape(owners, -1, cap)
            for one in d_feats
        ]
    spread = first.astype(BF16).reshape(1, -1, cap)
    spread = jnp.broadcast_to(spread, (owners,) + spread.shape[1:])
    spread = after(jnp.concatenate(d_feats + [spread], axis=1), fourth)
    back = lax.all_to_all(spread, "edge", 0, 0, tiled=True)
    d_edges = back[:, : batches * feat_count].reshape(owners, batches, feat_count, cap)
    first_parts = back[:, batches * feat_count :].reshape(owners, 32, units)
    first_sum = jnp.sum(first_parts.astype(F32), axis=0)
    first_sum = first_sum + to_core(first_sum)
    feat_grad = full_call(
        functools.partial(unroute_kernel, own),
        jax.ShapeDtypeStruct((batches, feat_count, edges), BF16),
        cost_estimate=cost(3),
    )(source_index, d_edges)

    for step in (3, 2):
        got = swap_step(held, step)
        if step == 3:
            got = after(got, feat_grad)
        held = jnp.concatenate([held, got], axis=0)
    near, far = swap_step(held, 1), swap_step(held, 0)
    last = swap_step(near, 0)

    shapes = tuple(
        jax.ShapeDtypeStruct(shape, F32)
        for shape in (
            (units, width * width),
            (width, width),
            (width, 3 * width),
            (width, 3 * width),
            (width, width),
        )
    )
    outs = ()
    for number, wave in enumerate((((held, 0),), ((near, 4), (far, 8)), ((last, 12),))):
        at, pieces = [], []
        ready = (outs, tuple(piece for piece, _ in wave), first_sum)
        ready = lax.optimization_barrier(ready[: (2, 3, 2)[number]])
        outs, wave = ready[0], zip(ready[1], [flips for _, flips in wave])
        for piece, flips in wave:
            for side, one in ((core, piece), (1 - core, to_core(piece))):
                code = side
                for step in range(4):
                    code = code * 2 + bit(side, step)
                at.append(code ^ flips)
                pieces.append(one)
        outs = place_pieces(tall, jnp.stack(at), pieces, shapes, outs)
    d_w, d_bias, d_x, d_h, _ = outs
    return (
        new_states.reshape(batches, own, width),
        jnp.stack(state_grad),
        feat_grad,
        first_sum[:feat_count],
        first_sum[feat_count],
        d_w,
        d_bias.reshape(-1),
        d_x,
        d_h,
        first_sum[24:27].reshape(-1),
        first_sum[27:30].reshape(-1),
    )


def solution(mesh):
    spread = ("graph", "edge")
    rows = P(None, spread, None)
    edges = P(None, spread)
    feats = P(None, None, spread)
    in_specs = (rows, feats, edges, edges) + (P(),) * 8 + (rows,)
    out_specs = (rows, rows, feats) + (P(),) * 8
    return jax.shard_map(
        body,
        mesh=mesh,
        in_specs=in_specs,
        out_specs=out_specs,
        check_vma=False,
    )
```

```python
import functools

import jax
import jax.numpy as jnp
from jax import lax
from jax.experimental import pallas as pl
from jax.experimental.pallas import tpu as pltpu
from jax.sharding import PartitionSpec as P

F32 = jnp.float32
BF16 = jnp.bfloat16
LANES = 128
GROUP = 12
MIB = 1024 * 1024


def dot(first, second, dims=((1,), (0,))):
    return lax.dot_general(first, second, (dims, ((), ())), preferred_element_type=F32)


def dot_nt(first, second):
    return dot(first, second, ((1,), (1,)))


def row_ids(shape):
    return lax.broadcasted_iota(jnp.int32, shape, 0)


def col_ids(shape):
    return lax.broadcasted_iota(jnp.int32, shape, 1)


def full_call(kernel, out_shape, scratch=(), limit=16, **more):
    return pl.pallas_call(
        kernel,
        out_shape=out_shape,
        scratch_shapes=scratch,
        compiler_params=pltpu.CompilerParams(vmem_limit_bytes=limit * MIB),
        **more,
    )


def ranks_of(owner, owners):
    hits = (row_ids((owners, owner.shape[1])) == owner).astype(F32)
    before = (row_ids((LANES, LANES)) < col_ids((LANES, LANES))).astype(BF16)
    seen = jnp.zeros((owners, 1), F32)
    ranks = []
    for start in range(0, owner.shape[1], LANES):
        part = hits[:, start : start + LANES]
        place = dot(part.astype(BF16), before) + seen
        ranks.append(jnp.sum(part * place, axis=0, keepdims=True))
        seen = seen + jnp.sum(part, axis=1, keepdims=True)
    return hits, jnp.concatenate(ranks, axis=1)


def route_kernel(own_rows, src_ref, dst_ref, feat_ref, out_ref):
    owners, rows, cap = out_ref.shape
    batches, feats, edges = feat_ref.shape
    shift = own_rows.bit_length() - 1
    marks = [jnp.zeros((16, cap), F32)] * owners
    for batch in range(batches):
        source, target = src_ref[batch : batch + 1], dst_ref[batch : batch + 1]
        owner = source >> shift
        hits, rank = ranks_of(owner, owners)
        spots = (row_ids((cap, edges)) == rank.astype(jnp.int32)).astype(BF16)
        line = row_ids((16, edges)) - 3 * batch
        first = owner << shift
        extra = jnp.where(line == 0, source - first, jnp.where(line == 1, target - first, 1))
        extra = jnp.where((line >= 0) & (line < 3), extra, 0).astype(F32)
        load = jnp.concatenate([feat_ref[batch].astype(F32), extra], axis=0)
        masked = [(load * hits[part : part + 1]).astype(BF16) for part in range(owners)]
        out = dot_nt(jnp.concatenate(masked, axis=0), spots)
        for part in range(owners):
            tile = out[part * (feats + 16) : (part + 1) * (feats + 16)]
            out_ref[part, batch * feats : (batch + 1) * feats] = tile[:feats].astype(BF16)
            marks[part] = marks[part] + tile[feats:]
    for part in range(owners):
        out_ref[part, batches * feats :] = marks[part].astype(BF16)


def unroute_kernel(own_rows, src_ref, back_ref, out_ref):
    owners, batches, rows, cap = back_ref.shape
    edges = src_ref.shape[1]
    shift = own_rows.bit_length() - 1
    for batch in range(batches):
        hits, rank = ranks_of(src_ref[batch : batch + 1] >> shift, owners)
        spots = (row_ids((cap, edges)) == rank.astype(jnp.int32)).astype(BF16)
        parts = [back_ref[part, batch] for part in range(owners)]
        spread = dot(jnp.concatenate(parts, axis=0), spots)
        total = jnp.zeros((rows, edges), F32)
        for part in range(owners):
            total = total + spread[part * rows : (part + 1) * rows] * hits[part : part + 1]
        out_ref[batch] = total.astype(BF16)


def edge_piece(batches, order_ref, edge_ref, piece, batch):
    two = [edge_ref[order_ref[batch, 2 * piece + k]] for k in range(2)]
    block = jnp.concatenate(two, axis=1)
    feats, marks = block[batch * 16 : (batch + 1) * 16], block[batches * 16 :].astype(F32)
    source = marks[3 * batch : 3 * batch + 1].astype(jnp.int32)
    target = marks[3 * batch + 1 : 3 * batch + 2].astype(jnp.int32)
    held = marks[3 * batch + 2 : 3 * batch + 3]
    code = ((target >> 3) & 3) * 128 + (target >> 5) * 64 + source
    code = jnp.where(held > 0.5, code, -1)
    pairs = (row_ids((512, block.shape[1])) == code).astype(BF16)
    low = row_ids((8, block.shape[1])) == (target & 7)
    return feats, held, pairs, low


def order_blocks(batches, edge_ref, order_ref):
    blocks = edge_ref.shape[0]
    for batch in range(batches):
        front, back = jnp.int32(0), jnp.int32(blocks - 1)
        row = 3 * batch + 2
        for block in range(blocks):
            marks = edge_ref[block, batches * 16 :].astype(F32)
            held = jnp.max(marks[row : row + 1]) > 0.5
            order_ref[batch, jnp.where(held, front, back)] = jnp.int32(block)
            step = held.astype(jnp.int32)
            front, back = front + step, back - (1 - step)
        order_ref[batch, blocks] = front


def first_layer(w_in_ref, b_in_ref):
    bias = jnp.broadcast_to(b_in_ref[...].reshape(1, -1), (8, b_in_ref.shape[0]))
    return w_in_ref[...].astype(F32).T.astype(BF16), bias.T[:, :1]


def gates_of(mail_low, level, w_x, w_h, b_x, b_h):
    width = level.shape[1]
    from_mail = dot(mail_low, w_x[...]) + b_x[...].reshape(1, -1)
    from_state = dot(level, w_h[...]) + b_h[...].reshape(1, -1)
    reset = jax.nn.sigmoid(from_mail[:, :width] + from_state[:, :width])
    update = jax.nn.sigmoid(from_mail[:, width : 2 * width] + from_state[:, width : 2 * width])
    state_part = from_state[:, 2 * width :]
    candidate = jnp.tanh(from_mail[:, 2 * width :] + reset * state_part)
    return reset, update, candidate, state_part


def doubled(level):
    blank = jnp.zeros_like(level)
    return jnp.concatenate(
        [jnp.concatenate([level, blank], axis=1), jnp.concatenate([blank, level], axis=1)], axis=0
    )


def bias_blocks(bias_ref, tail_ref):
    tail_ref[...] = jnp.zeros_like(tail_ref)
    high = bias_ref[...].astype(BF16)
    tail_ref[0] = high
    tail_ref[1] = (bias_ref[...] - high.astype(F32)).astype(BF16)


def weights_of(w_ref, tail_ref, number):
    units = w_ref.shape[0]
    blocks = []
    for unit in range(number * GROUP, (number + 1) * GROUP):
        blocks.append(w_ref[unit] if unit < units else tail_ref[unit - units])
    return jnp.concatenate(blocks, axis=1)


def pulled_rows(pulled, half):
    rows = []
    for start in range(0, pulled.shape[1], LANES):
        tile = pulled[:, start : start + LANES]
        rows.append(jnp.concatenate([tile[:half], tile[half:]], axis=1))
    return jnp.concatenate(rows, axis=0)


def main_kernel(
    where_ref,
    edge_ref,
    state_ref,
    cot_ref,
    w_in_ref,
    b_in_ref,
    w_far,
    bias_ref,
    w_x,
    w_h,
    b_x,
    b_h,
    new_ref,
    kept_first,
    kept_last,
    given_first,
    given_last,
    gt_ref,
    level_ref,
    dm_ref,
    base_ref,
    order_ref,
    rows_ref,
    hid_ref,
    acc_ref,
    g_ref,
    p_ref,
    w_ref,
    tail_ref,
    sem,
):
    fetch = pltpu.make_async_copy(w_far, w_ref, sem)
    fetch.start()
    blocks = edge_ref.shape[0]
    batches = g_ref.shape[0]
    hidden_units = hid_ref.shape[0]
    units = acc_ref.shape[0] // 8
    own = state_ref.shape[0] // batches
    half = own // 2
    span = GROUP * half
    wide = GROUP * LANES
    chunks = units // GROUP
    order_blocks(batches, edge_ref, order_ref)
    bias_blocks(bias_ref, tail_ref)
    w_in, b_in = first_layer(w_in_ref, b_in_ref)

    for batch in range(batches):
        acc_ref[...] = jnp.zeros_like(acc_ref)

        def add_piece(piece, carry):
            feats, held, pairs, low = edge_piece(batches, order_ref, edge_ref, piece, batch)
            pre = dot(w_in, feats) + b_in
            hid_ref[...] = (pre * jax.nn.sigmoid(pre)).astype(BF16).astype(F32)
            ones = jnp.where(low, 1.0, 0.0)
            parts = []
            for unit in range(0, hidden_units, 2):
                two = [jnp.where(low, hid_ref[unit + k : unit + k + 1], 0.0) for k in range(2)]
                parts.append(jnp.concatenate(two, axis=0).astype(BF16))
            parts.append(jnp.concatenate([ones, ones], axis=0).astype(BF16))
            parts.append(jnp.zeros((8 * (units - hidden_units - 2), pre.shape[1]), BF16))
            acc_ref[...] += dot_nt(jnp.concatenate(parts, axis=0), pairs)
            return carry

        lax.fori_loop(0, (order_ref[batch, blocks] + 1) // 2, add_piece, 0)

        def place(step, carry):
            for four in range(3):
                rows = []
                for k in range(4):
                    for part in range(4):
                        start = pl.multiple_of(step * 96 + four * 32 + k * 8, 8)
                        rows.append(acc_ref[pl.ds(start, 8), part * LANES : (part + 1) * LANES])
                tile = jnp.concatenate(rows, axis=0).astype(BF16)
                at = pl.ds(pl.multiple_of((step * 3 + four) * LANES, LANES), LANES)
                g_ref[batch, at, :] = tile
                gt_ref[batch, :, at] = tile.T
            return carry

        lax.fori_loop(0, units // 12, place, 0)

    def forward(step, level):
        two = [doubled(level[batch * own : (batch + 1) * own]) for batch in range(batches)]
        mail = jnp.zeros((batches * own, LANES), F32)
        base = step * batches * own
        for number in range(chunks):
            for batch in range(batches):
                out = dot(g_ref[batch, number * span : (number + 1) * span, :], two[batch])
                out = out.astype(BF16)
                for unit in range(GROUP):
                    lane = number * wide + unit * LANES
                    for part in range(2):
                        row = base + batch * own + part * half
                        p_ref[row : row + half, lane : lane + LANES] = out[
                            unit * half : (unit + 1) * half, part * LANES : (part + 1) * LANES
                        ]
            rows = p_ref[base : base + batches * own, number * wide : (number + 1) * wide]
            mail = mail + dot_nt(rows, weights_of(w_ref, tail_ref, number))
        return mail

    def backward(d_mail):
        sums = [jnp.zeros((LANES, 2 * LANES), F32) for batch in range(batches)]
        for number in range(chunks):
            pulled = dot(d_mail, weights_of(w_ref, tail_ref, number)).astype(BF16)
            at = slice(number * span, (number + 1) * span)
            for batch in range(batches):
                tall = pulled_rows(pulled[batch * own : (batch + 1) * own], half)
                sums[batch] = sums[batch] + dot(gt_ref[batch, :, at], tall)
        return jnp.concatenate([one[:own, :LANES] + one[own:, LANES:] for one in sums], axis=0)

    weights = (w_x, w_h, b_x, b_h)
    level_zero = state_ref[...]
    state_zero = level_zero.astype(F32)
    fetch.wait()
    mail_zero = forward(0, level_zero).astype(BF16)
    gates_zero = gates_of(mail_zero, level_zero, *weights)
    state_one = (1.0 - gates_zero[1]) * gates_zero[2] + gates_zero[1] * state_zero
    level_one = state_one.astype(BF16)
    mail_one = forward(1, level_one).astype(BF16)
    gates_one = gates_of(mail_one, level_one, *weights)
    new_ref[...] = ((1.0 - gates_one[1]) * gates_one[2] + gates_one[1] * state_one).astype(BF16)

    def gru_back(d_next, gates, current):
        reset, update, candidate, state_part = gates
        d_cand = d_next * (1.0 - update) * (1.0 - candidate * candidate)
        d_reset = d_cand * state_part * reset * (1.0 - reset)
        d_update = d_next * (current - candidate) * update * (1.0 - update)
        dg_mail = jnp.concatenate([d_reset, d_update, d_cand], axis=1).astype(BF16)
        dg_state = jnp.concatenate([d_reset, d_update, d_cand * reset], axis=1).astype(BF16)
        d_mail = dot_nt(dg_mail, w_x[...]).astype(BF16)
        d_current = d_next * update + dot_nt(dg_state, w_h[...])
        return dg_mail, dg_state, d_mail, d_current

    dgm_one, dgs_one, dm_one, d_state = gru_back(cot_ref[...].astype(F32), gates_one, state_one)
    d_state = d_state + backward(dm_one)
    dgm_zero, dgs_zero, dm_zero, d_state = gru_back(d_state, gates_zero, state_zero)
    base_ref[...] = d_state
    level_ref[...] = jnp.concatenate([level_zero, level_one], axis=1)
    dm_ref[...] = jnp.concatenate([dm_zero, dm_one], axis=1)

    def both(first, second):
        return jnp.concatenate([first.astype(F32), second.astype(F32)], axis=0)

    dms = both(dm_zero, dm_one).T
    mails, levels = both(mail_zero, mail_one), both(level_zero, level_one)
    dgm, dgs = both(dgm_zero, dgm_one), both(dgs_zero, dgs_one)
    width = dgm.shape[1]
    rows_ref[...] = jnp.zeros_like(rows_ref)
    for k, one in enumerate((dgm, dgs)):
        total = jnp.sum(one, axis=0, keepdims=True)
        for part in range(3):
            row = 24 + 3 * k + part
            rows_ref[row : row + 1, :] = total[:, part * LANES : (part + 1) * LANES]
    small = jnp.concatenate(
        [
            dot(dms.astype(BF16), p_ref[:, hidden_units * LANES : (hidden_units + 1) * LANES]),
            dot(mails.T.astype(BF16), dgm.astype(BF16)),
            dot(levels.T.astype(BF16), dgs.astype(BF16)),
            jnp.zeros((2 * own, LANES), F32),
        ],
        axis=1,
    )

    def sorted_rows(value):
        rows = value.shape[0] // 2
        upper, lower = value[:rows], value[rows:]
        halves = [jnp.where(where_ref[0] == k, upper, lower) for k in range(2)]
        parts = []
        for k, one in enumerate(halves):
            first, second = one[: rows // 2], one[rows // 2 :]
            parts += [jnp.where(where_ref[1 + k] == side, second, first) for side in range(2)]
        return jnp.concatenate(parts, axis=0).astype(BF16)

    dms, small = sorted_rows(dms), sorted_rows(small)
    rows_in, groups, tall, wide_out = kept_first.shape
    taken = wide_out - 2 * LANES
    for group in range(groups):
        out = dot(dms, p_ref[:, group * taken : (group + 1) * taken]).astype(BF16)
        extra = small[:, group * 2 * LANES : (group + 1) * 2 * LANES]
        at = 0
        for ref in (kept_first, kept_last, given_first, given_last):
            for row in range(rows_in):
                ref[row, group, :, :taken] = out[at : at + tall]
                ref[row, group, :, taken:] = extra[at : at + tall]
                at += tall


def edge_kernel(
    batch,
    order_ref,
    edge_ref,
    gt_far,
    level_ref,
    dm_ref,
    base_ref,
    w_in_ref,
    b_in_ref,
    w_far,
    bias_ref,
    before_ref,
    grad_ref,
    feat_ref,
    win_ref,
    tail_ref,
    dg_ref,
    w_ref,
    gt_ref,
    sems,
):
    blocks = edge_ref.shape[0]
    batches = order_ref.shape[0]
    hidden_units = w_in_ref.shape[1]
    chunks = (hidden_units + tail_ref.shape[0]) // GROUP
    fetches = []
    for number in range(chunks):
        some = pl.ds(number * GROUP, min(GROUP, hidden_units - number * GROUP))
        lanes = pl.ds(number * GROUP * LANES // 4, GROUP * LANES // 4)
        fetches += [
            pltpu.make_async_copy(w_far.at[some], w_ref.at[some], sems.at[number, 0]),
            pltpu.make_async_copy(
                gt_far.at[batch, :, lanes], gt_ref.at[:, lanes], sems.at[number, 1]
            ),
        ]
    for fetch in fetches:
        fetch.start()
    own, width = grad_ref.shape
    half = own // 2
    mine = slice(batch * own, (batch + 1) * own)
    bias_blocks(bias_ref, tail_ref)

    pulls = [dm_ref[mine, step * width : (step + 1) * width] for step in range(2)]
    levels = [doubled(level_ref[mine, step * width : (step + 1) * width]) for step in range(2)]
    levels = jnp.concatenate(levels, axis=1)
    total = jnp.zeros((2 * own, 2 * width), F32)
    both = jnp.concatenate(pulls, axis=0)
    for number in range(chunks):
        fetches[2 * number].wait()
        fetches[2 * number + 1].wait()
        pulled = dot(both, weights_of(w_ref, tail_ref, number)).astype(BF16)
        talls = [pulled_rows(pulled[k * own : (k + 1) * own], half) for k in range(2)]
        at = slice(number * GROUP * half, (number + 1) * GROUP * half)
        total = total + dot(gt_ref[:, at], talls[0])
        d_pair = dot_nt(jnp.concatenate(talls, axis=1), levels)
        for unit in range(0, GROUP, 2):
            row = (number * GROUP + unit) * 8
            for part in range(half // 8):
                pair = [
                    d_pair[(unit + k) * half + part * 8 : (unit + k) * half + part * 8 + 8]
                    for k in range(2)
                ]
                dg_ref[row : row + 16, part * LANES : (part + 1) * LANES] = jnp.concatenate(
                    pair, axis=0
                ).astype(BF16)
    grad = base_ref[mine] + total[:own, :width] + total[own:, width:]
    grad_ref[...] = grad.astype(BF16)

    w_in, b_in = first_layer(w_in_ref, b_in_ref)
    fold = (col_ids((hidden_units, 8 * hidden_units)) >> 3) == row_ids(
        (hidden_units, 8 * hidden_units)
    )
    fold = fold.astype(F32).astype(BF16)
    feat_ref[...] = jnp.zeros_like(feat_ref)

    def one_piece(piece, sums):
        feats, held, pairs, low = edge_piece(batches, order_ref, edge_ref, piece, batch)
        pre = dot(w_in, feats) + b_in
        sig = jax.nn.sigmoid(pre)
        spread = dot(dg_ref[: 8 * hidden_units], pairs)
        spread = spread.reshape(hidden_units, 8, pre.shape[1])
        spread = jnp.where(low[None], spread, 0.0).reshape(8 * hidden_units, pre.shape[1])
        d_hidden = dot(fold, spread.astype(BF16))
        d_pre = (d_hidden * sig * (1.0 + pre * (1.0 - sig))).astype(BF16)
        out = dot(w_in_ref[...], d_pre).astype(BF16)
        for k in range(2):
            feat_ref[order_ref[batch, 2 * piece + k]] = out[:, k * LANES : (k + 1) * LANES]
        ones = jnp.where(row_ids((16, pre.shape[1])) == 0, held, 0.0).astype(BF16)
        return sums + dot_nt(jnp.concatenate([feats, ones], axis=0), d_pre)

    win_ref[...] = lax.fori_loop(
        0, (order_ref[batch, blocks] + 1) // 2, one_piece, before_ref[...]
    )


def add_kernel(first_ref, second_ref, out_ref):
    out_ref[...] = (first_ref[...].astype(F32) + second_ref[...].astype(F32)).astype(BF16)


def rows_kernel(first_ref, second_ref, out_ref, rows_ref):
    parts, tall, wide = first_ref.shape
    main = wide // LANES - 2
    for part in range(parts):
        total = first_ref[part].astype(F32) + second_ref[part].astype(F32)
        for block in range(main):
            rows_ref[pl.ds(block, tall, stride=main), :] = total[
                :, block * LANES : (block + 1) * LANES
            ]
        for k in range(2):
            start = tall * (main + k)
            rows_ref[start : start + tall, :] = total[:, (main + k) * LANES : (main + k + 1) * LANES]
        out_ref[part] = rows_ref[...].astype(BF16)


def rows_of(first, second):
    parts, tall, wide = first.shape
    shape = (tall * (wide // LANES), LANES)
    return full_call(
        rows_kernel,
        jax.ShapeDtypeStruct((parts,) + shape, BF16),
        (pltpu.VMEM(shape, F32),),
        cost_estimate=cost(1),
    )(first, second)


def place_kernel(tall, count, carried, *refs):
    at_ref, pieces = refs[0], refs[1 : 1 + count]
    outs = refs[1 + count + carried : 6 + count + carried]
    big_ref, little_ref, sems = refs[6 + count + carried :]
    d_w, d_bias, d_x, d_h, d_rest = outs
    waits = []
    slot = 0
    for k, piece in enumerate(pieces):
        chunks, rows_in, lanes = piece.shape
        main = rows_in // tall - 2
        for chunk in range(chunks):
            code = at_ref[k] ^ chunk
            line, part = code >> 2, code & 3
            at = pl.ds(pl.multiple_of(line * tall, 8), tall)
            rows = piece[chunk].astype(F32)
            for row in range(tall):
                big_ref[slot, :, row * lanes : (row + 1) * lanes] = rows[row * main : (row + 1) * main]
            copy = pltpu.make_async_copy(
                big_ref.at[slot],
                d_w.at[
                    pl.ds(pl.multiple_of(part * main, 8), main),
                    pl.ds(pl.multiple_of(line * (tall * lanes), LANES), tall * lanes),
                ],
                sems.at[slot, 0],
            )
            copy.start()
            waits.append(copy)

            for side in range(2):
                start = tall * (main + side)
                little_ref[slot, side] = rows[start : start + tall]

                def move(target, lane):
                    lane = jnp.maximum(lane, 0) * lanes
                    to = pl.ds(pl.multiple_of(jnp.minimum(lane, target.shape[1] - lanes), LANES), lanes)
                    return pltpu.make_async_copy(
                        little_ref.at[slot, side], target.at[at, to], sems.at[slot, 1 + side]
                    )

                block = 2 * part + side
                to_x, to_h = move(d_x, block - 1), move(d_h, block - 4)
                alone = move((d_bias, d_rest)[side], 0)
                lone = block == 7 * side
                pl.when(lone)(alone.start)
                pl.when((block > 0) & (block < 4))(to_x.start)
                pl.when((block > 3) & (block < 7))(to_h.start)
                waits.append(alone)
            slot += 1
    for copy in waits:
        copy.wait()


def cost(micros):
    return pl.CostEstimate(
        flops=int(micros * 1e9), bytes_accessed=int(micros * 3e6), transcendentals=0
    )


def place_pieces(tall, at, pieces, shapes, before=()):
    count = len(pieces)
    chunks, rows_in, lanes = pieces[0].shape
    slots = count * chunks
    vmem = pl.BlockSpec(memory_space=pltpu.VMEM)
    hbm = pl.BlockSpec(memory_space=pl.ANY)
    return pl.pallas_call(
        functools.partial(place_kernel, tall, count, len(before)),
        out_shape=shapes,
        in_specs=[pl.BlockSpec(memory_space=pltpu.SMEM)] + [vmem] * count + [hbm] * len(before),
        out_specs=[hbm] * len(shapes),
        scratch_shapes=(
            pltpu.VMEM((slots, rows_in // tall - 2, tall * lanes), F32),
            pltpu.VMEM((slots, 2, tall, lanes), F32),
            pltpu.SemaphoreType.DMA((slots, 3)),
        ),
        input_output_aliases={1 + count + k: k for k in range(len(before))},
        cost_estimate=cost(slots / 4),
        compiler_params=pltpu.CompilerParams(vmem_limit_bytes=16 * MIB),
    )(at, *pieces, *before)


def body(
    states,
    edge_feats,
    source_index,
    target_index,
    w_edge_in,
    b_edge_in,
    w_edge_out,
    b_edge_out,
    w_input,
    w_hidden,
    b_input,
    b_hidden,
    cotangent,
):
    batches, own, width = states.shape
    edges = source_index.shape[1]
    owners = lax.axis_size("edge")
    cap = max(2, 2 * edges // owners)
    feat_count, units = w_edge_in.shape

    sent = full_call(
        functools.partial(route_kernel, own),
        jax.ShapeDtypeStruct((owners, batches * feat_count + 16, cap), BF16),
    )(source_index, target_index, edge_feats)
    edge_data = lax.all_to_all(sent, "edge", 0, 0, tiled=True)
    merge = max(1, LANES // cap)
    if merge > 1:
        edge_data = edge_data.reshape(owners // merge, merge, -1, cap).transpose(0, 2, 1, 3)
        edge_data = edge_data.reshape(owners // merge, -1, merge * cap)

    w_mats = w_edge_out.reshape(units, width, width)
    padded = (units + 2 + GROUP - 1) // GROUP * GROUP

    tall = width // 8
    pairs = own // 2
    blocks = edge_data.shape[0]
    core = lax.axis_index("graph")
    spot = lax.axis_index("edge")
    orders = ((0, 1, 2, 3), (2, 0, 1, 3))

    def bit(side, step):
        first, second = [(spot >> orders[k][step]) & 1 for k in range(2)]
        return jnp.where(side == 0, first, second)

    where = jnp.stack([core, bit(core, 0), bit(1 - core, 0)])
    smem = pl.BlockSpec(memory_space=pltpu.SMEM)
    vmem = pl.BlockSpec(memory_space=pltpu.VMEM)
    far = pl.BlockSpec(memory_space=pl.ANY)
    bias = b_edge_out.reshape(width, width)
    quarter = jax.ShapeDtypeStruct((2, 4, tall, (units // 4 + 2) * width), BF16)
    new_states, *sums, gt, levels, d_mails, base, order, first = full_call(
        main_kernel,
        (
            jax.ShapeDtypeStruct((batches * own, width), BF16),
            *[quarter] * 4,
            jax.ShapeDtypeStruct((batches, LANES, padded * pairs), BF16),
            jax.ShapeDtypeStruct((batches * own, 2 * width), BF16),
            jax.ShapeDtypeStruct((batches * own, 2 * width), BF16),
            jax.ShapeDtypeStruct((batches * own, width), F32),
            jax.ShapeDtypeStruct((batches, blocks + 1), jnp.int32),
            jax.ShapeDtypeStruct((32, width), F32),
        ),
        (
            pltpu.VMEM((units, 2 * LANES), F32),
            pltpu.VMEM((padded * 8, 512), F32),
            pltpu.VMEM((batches, padded * pairs, LANES), BF16),
            pltpu.VMEM((2 * batches * own, padded * width), BF16),
            pltpu.VMEM((units, width, width), BF16),
            pltpu.VMEM((padded - units, width, width), BF16),
            pltpu.SemaphoreType.DMA(()),
        ),
        limit=36,
        in_specs=[smem] + [vmem] * 5 + [far] + [vmem] * 5,
        out_specs=[vmem] * 9 + [smem, vmem],
    )(
        where,
        edge_data,
        states.reshape(batches * own, width),
        cotangent.reshape(batches * own, width),
        w_edge_in,
        b_edge_in,
        w_mats,
        bias,
        w_input,
        w_hidden,
        b_input,
        b_hidden,
    )

    cores = lax.axis_size("graph")

    def to_core(value):
        return lax.ppermute(value, "graph", [(0, 1), (1, 0)])

    def swap(value, masks):
        moves = []
        for side in range(cores):
            first = side * owners
            moves += [(first + k, first + (k ^ masks[side])) for k in range(owners)]
        return lax.ppermute(value, ("graph", "edge"), moves)

    def swap_step(value, step):
        return swap(value, [1 << orders[side][step] for side in range(cores)])

    def pick(value, number):
        return lax.dynamic_index_in_dim(value, number, 0, False)

    def added(terms):
        return sum(one.astype(F32) for one in terms)

    def after(value, *others):
        return lax.optimization_barrier((value, *others))[0]

    def edge_grads(batch, gt_in, first):
        return full_call(
            functools.partial(edge_kernel, batch),
            (
                jax.ShapeDtypeStruct((own, width), BF16),
                jax.ShapeDtypeStruct((blocks, feat_count, edge_data.shape[2]), BF16),
                jax.ShapeDtypeStruct((32, units), F32),
            ),
            (
                pltpu.VMEM((padded - units, width, width), BF16),
                pltpu.VMEM((padded * 8, 512), BF16),
                pltpu.VMEM((units, width, width), BF16),
                pltpu.VMEM((LANES, padded * pairs), BF16),
                pltpu.SemaphoreType.DMA((padded // GROUP, 2)),
            ),
            limit=20,
            in_specs=[smem, vmem, far] + [vmem] * 5 + [far] + [vmem] * 2,
            cost_estimate=cost(9),
        )(
            order, edge_data, gt_in, levels, d_mails, base,
            w_edge_in, b_edge_in, w_mats, bias, first,
        )

    def edge_payload(first, feats):
        if merge > 1:
            feats = [
                one.reshape(blocks, feat_count, merge, cap)
                .transpose(0, 2, 1, 3)
                .reshape(owners, -1, cap)
                for one in feats
            ]
        spread = first.astype(BF16).reshape(1, -1, cap)
        spread = jnp.broadcast_to(spread, (owners,) + spread.shape[1:])
        return jnp.concatenate(feats + [spread], axis=1)

    kept_first, kept_last, given_first, given_last = sums
    got_first, got_last = to_core(given_first), to_core(given_last)
    give = full_call(
        add_kernel, jax.ShapeDtypeStruct(kept_first.shape, BF16), cost_estimate=cost(1)
    )(kept_first, got_first)
    terms = [kept_last, got_last]
    state_grad, d_feats = [], []
    for step in range(3):
        if step > 0:
            number = bit(core, step)
            give = added([pick(one, 1 - number) for one in terms]).astype(BF16)
            terms = [pick(one, number) for one in terms]
        got = swap_step(give, step)
        if step < batches:
            grad, feats, first = edge_grads(step, after(gt, give), first)
            got = after(got, first)
            state_grad.append(grad)
            d_feats.append(feats)
        if step == 2:
            spread = edge_payload(after(first, give), d_feats)
            got = after(got, spread)
        terms.append(got)
        if step == 0:
            terms = [one.reshape((2, 2, 2) + one.shape[2:]) for one in terms]
    total = added(terms).astype(BF16)
    for extra in range(3, owners.bit_length() - 1):
        got = swap(total, [1 << extra] * cores)
        if extra < owners.bit_length() - 2:
            total = added([total, got]).astype(BF16)

    back = lax.all_to_all(after(spread, total), "edge", 0, 0, tiled=True)
    d_edges = back[:, : batches * feat_count].reshape(owners, batches, feat_count, cap)
    feat_grad = full_call(
        functools.partial(unroute_kernel, own),
        jax.ShapeDtypeStruct((batches, feat_count, edges), BF16),
        cost_estimate=cost(3),
    )(source_index, d_edges)

    held = rows_of(total, after(got, feat_grad))
    held = jnp.concatenate([held, swap_step(held, 2)], axis=0)
    near, across = swap_step(held, 1), swap_step(held, 0)
    last = swap_step(near, 0)
    first_parts = after(back, held)[:, batches * feat_count :].reshape(owners, 32, units)
    first_sum = jnp.sum(first_parts.astype(F32), axis=0)
    first_sum = first_sum + to_core(first_sum)

    shapes = tuple(
        jax.ShapeDtypeStruct(shape, F32)
        for shape in (
            (units, width * width),
            (width, width),
            (width, 3 * width),
            (width, 3 * width),
            (width, width),
        )
    )
    outs = ()
    for number, wave in enumerate((((held, 0),), ((near, 4), (across, 8)), ((last, 12),))):
        at, pieces = [], []
        ready = (outs, tuple(piece for piece, _ in wave), first_sum)
        ready = lax.optimization_barrier(ready[: (2, 3, 2)[number]])
        outs, wave = ready[0], zip(ready[1], [flips for _, flips in wave])
        for piece, flips in wave:
            for side, one in ((core, piece), (1 - core, to_core(piece))):
                code = side
                for step in range(3):
                    code = code * 2 + bit(side, step)
                at.append((code * 2) ^ flips)
                pieces.append(one)
        outs = place_pieces(tall, jnp.stack(at), pieces, shapes, outs)
    d_w, d_bias, d_x, d_h, _ = outs
    return (
        new_states.reshape(batches, own, width),
        jnp.stack(state_grad),
        feat_grad,
        first_sum[:feat_count],
        first_sum[feat_count],
        d_w,
        d_bias.reshape(-1),
        d_x,
        d_h,
        first_sum[24:27].reshape(-1),
        first_sum[27:30].reshape(-1),
    )


def solution(mesh):
    spread = ("graph", "edge")
    rows = P(None, spread, None)
    edges = P(None, spread)
    feats = P(None, None, spread)
    in_specs = (rows, feats, edges, edges) + (P(),) * 8 + (rows,)
    out_specs = (rows, rows, feats) + (P(),) * 8
    return jax.shard_map(
        body,
        mesh=mesh,
        in_specs=in_specs,
        out_specs=out_specs,
        check_vma=False,
    )
```

```python
import functools

import jax
import jax.numpy as jnp
from jax import lax
from jax.experimental import pallas as pl
from jax.experimental.pallas import tpu as pltpu
from jax.sharding import PartitionSpec as P

F32 = jnp.float32
BF16 = jnp.bfloat16
LANES = 128
PIECE = 4
GROUP = 12
MIB = 1024 * 1024


def dot(first, second, dims=((1,), (0,))):
    return lax.dot_general(first, second, (dims, ((), ())), preferred_element_type=F32)


def dot_nt(first, second):
    return dot(first, second, ((1,), (1,)))


def row_ids(shape):
    return lax.broadcasted_iota(jnp.int32, shape, 0)


def col_ids(shape):
    return lax.broadcasted_iota(jnp.int32, shape, 1)


def full_call(kernel, out_shape, scratch=(), limit=16, **more):
    return pl.pallas_call(
        kernel,
        out_shape=out_shape,
        scratch_shapes=scratch,
        compiler_params=pltpu.CompilerParams(vmem_limit_bytes=limit * MIB),
        **more,
    )


def ranks_of(owner, owners):
    hits = (row_ids((owners, owner.shape[1])) == owner).astype(F32)
    before = (row_ids((LANES, LANES)) < col_ids((LANES, LANES))).astype(BF16)
    seen = jnp.zeros((owners, 1), F32)
    ranks = []
    for start in range(0, owner.shape[1], LANES):
        part = hits[:, start : start + LANES]
        place = dot(part.astype(BF16), before) + seen
        ranks.append(jnp.sum(part * place, axis=0, keepdims=True))
        seen = seen + jnp.sum(part, axis=1, keepdims=True)
    return hits, jnp.concatenate(ranks, axis=1)


def route_kernel(own_rows, src_ref, dst_ref, feat_ref, out_ref):
    owners, rows, cap = out_ref.shape
    batches, feats, edges = feat_ref.shape
    shift = own_rows.bit_length() - 1
    marks = [jnp.zeros((16, cap), F32)] * owners
    for batch in range(batches):
        source, target = src_ref[batch : batch + 1], dst_ref[batch : batch + 1]
        owner = source >> shift
        hits, rank = ranks_of(owner, owners)
        spots = (row_ids((cap, edges)) == rank.astype(jnp.int32)).astype(BF16)
        line = row_ids((16, edges)) - 3 * batch
        first = owner << shift
        extra = jnp.where(line == 0, source - first, jnp.where(line == 1, target - first, 1))
        extra = jnp.where((line >= 0) & (line < 3), extra, 0).astype(F32)
        load = jnp.concatenate([feat_ref[batch].astype(F32), extra], axis=0)
        masked = [(load * hits[part : part + 1]).astype(BF16) for part in range(owners)]
        out = dot_nt(jnp.concatenate(masked, axis=0), spots)
        for part in range(owners):
            tile = out[part * (feats + 16) : (part + 1) * (feats + 16)]
            out_ref[part, batch * feats : (batch + 1) * feats] = tile[:feats].astype(BF16)
            marks[part] = marks[part] + tile[feats:]
    for part in range(owners):
        out_ref[part, batches * feats :] = marks[part].astype(BF16)


def unroute_kernel(own_rows, src_ref, back_ref, out_ref):
    owners, batches, rows, cap = back_ref.shape
    edges = src_ref.shape[1]
    shift = own_rows.bit_length() - 1
    for batch in range(batches):
        hits, rank = ranks_of(src_ref[batch : batch + 1] >> shift, owners)
        spots = (row_ids((cap, edges)) == rank.astype(jnp.int32)).astype(BF16)
        parts = [back_ref[part, batch] for part in range(owners)]
        spread = dot(jnp.concatenate(parts, axis=0), spots)
        total = jnp.zeros((rows, edges), F32)
        for part in range(owners):
            total = total + spread[part * rows : (part + 1) * rows] * hits[part : part + 1]
        out_ref[batch] = total.astype(BF16)


def edge_piece(batches, order_ref, edge_ref, piece, batch):
    some = [edge_ref[order_ref[batch, PIECE * piece + k]] for k in range(PIECE)]
    block = jnp.concatenate(some, axis=1)
    feats, marks = block[batch * 16 : (batch + 1) * 16], block[batches * 16 :].astype(F32)
    source = marks[3 * batch : 3 * batch + 1].astype(jnp.int32)
    target = marks[3 * batch + 1 : 3 * batch + 2].astype(jnp.int32)
    held = marks[3 * batch + 2 : 3 * batch + 3]
    code = ((target >> 3) & 3) * 128 + (target >> 5) * 64 + source
    code = jnp.where(held > 0.5, code, -1)
    pairs = (row_ids((512, block.shape[1])) == code).astype(BF16)
    low = row_ids((8, block.shape[1])) == (target & 7)
    return feats, held, pairs, low


def order_blocks(batches, edge_ref, order_ref):
    blocks = edge_ref.shape[0]
    for batch in range(batches):
        front, back = jnp.int32(0), jnp.int32(blocks - 1)
        row = 3 * batch + 2
        for block in range(blocks):
            marks = edge_ref[block, batches * 16 :].astype(F32)
            held = jnp.max(marks[row : row + 1]) > 0.5
            order_ref[batch, jnp.where(held, front, back)] = jnp.int32(block)
            step = held.astype(jnp.int32)
            front, back = front + step, back - (1 - step)
        order_ref[batch, blocks] = front


def first_layer(w_in_ref, b_in_ref):
    bias = jnp.broadcast_to(b_in_ref[...].reshape(1, -1), (8, b_in_ref.shape[0]))
    return w_in_ref[...].astype(F32).T.astype(BF16), bias.T[:, :1]


def gates_of(mail_low, level, w_x, w_h, b_x, b_h):
    width = level.shape[1]
    from_mail = dot(mail_low, w_x[...]) + b_x[...].reshape(1, -1)
    from_state = dot(level, w_h[...]) + b_h[...].reshape(1, -1)
    reset = jax.nn.sigmoid(from_mail[:, :width] + from_state[:, :width])
    update = jax.nn.sigmoid(from_mail[:, width : 2 * width] + from_state[:, width : 2 * width])
    state_part = from_state[:, 2 * width :]
    candidate = jnp.tanh(from_mail[:, 2 * width :] + reset * state_part)
    return reset, update, candidate, state_part


def doubled(level):
    blank = jnp.zeros_like(level)
    return jnp.concatenate(
        [jnp.concatenate([level, blank], axis=1), jnp.concatenate([blank, level], axis=1)], axis=0
    )


def bias_blocks(bias_ref, tail_ref):
    tail_ref[...] = jnp.zeros_like(tail_ref)
    high = bias_ref[...].astype(BF16)
    tail_ref[0] = high
    tail_ref[1] = (bias_ref[...] - high.astype(F32)).astype(BF16)


def weights_of(w_ref, tail_ref, number):
    units = w_ref.shape[0]
    blocks = []
    for unit in range(number * GROUP, (number + 1) * GROUP):
        blocks.append(w_ref[unit] if unit < units else tail_ref[unit - units])
    return jnp.concatenate(blocks, axis=1)


def pulled_rows(pulled, half):
    rows = []
    for start in range(0, pulled.shape[1], LANES):
        tile = pulled[:, start : start + LANES]
        rows.append(jnp.concatenate([tile[:half], tile[half:]], axis=1))
    return jnp.concatenate(rows, axis=0)


def main_kernel(
    where_ref,
    edge_ref,
    state_ref,
    cot_ref,
    w_in_ref,
    b_in_ref,
    w_far,
    bias_ref,
    w_x,
    w_h,
    b_x,
    b_h,
    new_ref,
    kept_first,
    kept_last,
    given_first,
    given_last,
    gt_ref,
    level_ref,
    dm_ref,
    base_ref,
    order_ref,
    rows_ref,
    hid_ref,
    acc_ref,
    g_ref,
    p_ref,
    w_ref,
    tail_ref,
    sem,
):
    fetch = pltpu.make_async_copy(w_far, w_ref, sem)
    fetch.start()
    blocks = edge_ref.shape[0]
    batches = g_ref.shape[0]
    hidden_units = hid_ref.shape[0]
    units = acc_ref.shape[0] // 8
    own = state_ref.shape[0] // batches
    half = own // 2
    span = GROUP * half
    wide = GROUP * LANES
    chunks = units // GROUP
    order_blocks(batches, edge_ref, order_ref)
    bias_blocks(bias_ref, tail_ref)
    w_in, b_in = first_layer(w_in_ref, b_in_ref)

    for batch in range(batches):
        acc_ref[...] = jnp.zeros_like(acc_ref)

        def add_piece(piece, carry):
            feats, held, pairs, low = edge_piece(batches, order_ref, edge_ref, piece, batch)
            pre = dot(w_in, feats) + b_in
            hid_ref[...] = (pre * jax.nn.sigmoid(pre)).astype(BF16).astype(F32)
            ones = jnp.where(low, 1.0, 0.0)
            parts = []
            for unit in range(0, hidden_units, 2):
                two = [jnp.where(low, hid_ref[unit + k : unit + k + 1], 0.0) for k in range(2)]
                parts.append(jnp.concatenate(two, axis=0).astype(BF16))
            parts.append(jnp.concatenate([ones, ones], axis=0).astype(BF16))
            parts.append(jnp.zeros((8 * (units - hidden_units - 2), pre.shape[1]), BF16))
            acc_ref[...] += dot_nt(jnp.concatenate(parts, axis=0), pairs)
            return carry

        lax.fori_loop(0, (order_ref[batch, blocks] + PIECE - 1) // PIECE, add_piece, 0)

        def place(step, carry):
            for four in range(3):
                rows = []
                for k in range(4):
                    for part in range(4):
                        start = pl.multiple_of(step * 96 + four * 32 + k * 8, 8)
                        rows.append(acc_ref[pl.ds(start, 8), part * LANES : (part + 1) * LANES])
                tile = jnp.concatenate(rows, axis=0).astype(BF16)
                at = pl.ds(pl.multiple_of((step * 3 + four) * LANES, LANES), LANES)
                g_ref[batch, at, :] = tile
                gt_ref[batch, :, at] = tile.T
            return carry

        lax.fori_loop(0, units // 12, place, 0)

    def forward(step, level):
        two = [doubled(level[batch * own : (batch + 1) * own]) for batch in range(batches)]
        mail = jnp.zeros((batches * own, LANES), F32)
        base = step * batches * own
        for number in range(chunks):
            for batch in range(batches):
                out = dot(g_ref[batch, number * span : (number + 1) * span, :], two[batch])
                out = out.astype(BF16)
                for unit in range(GROUP):
                    lane = number * wide + unit * LANES
                    for part in range(2):
                        row = base + batch * own + part * half
                        p_ref[row : row + half, lane : lane + LANES] = out[
                            unit * half : (unit + 1) * half, part * LANES : (part + 1) * LANES
                        ]
            rows = p_ref[base : base + batches * own, number * wide : (number + 1) * wide]
            mail = mail + dot_nt(rows, weights_of(w_ref, tail_ref, number))
        return mail

    def backward(d_mail):
        sums = [jnp.zeros((LANES, 2 * LANES), F32) for batch in range(batches)]
        for number in range(chunks):
            pulled = dot(d_mail, weights_of(w_ref, tail_ref, number)).astype(BF16)
            at = slice(number * span, (number + 1) * span)
            for batch in range(batches):
                tall = pulled_rows(pulled[batch * own : (batch + 1) * own], half)
                sums[batch] = sums[batch] + dot(gt_ref[batch, :, at], tall)
        return jnp.concatenate([one[:own, :LANES] + one[own:, LANES:] for one in sums], axis=0)

    weights = (w_x, w_h, b_x, b_h)
    level_zero = state_ref[...]
    state_zero = level_zero.astype(F32)
    fetch.wait()
    mail_zero = forward(0, level_zero).astype(BF16)
    gates_zero = gates_of(mail_zero, level_zero, *weights)
    state_one = (1.0 - gates_zero[1]) * gates_zero[2] + gates_zero[1] * state_zero
    level_one = state_one.astype(BF16)
    mail_one = forward(1, level_one).astype(BF16)
    gates_one = gates_of(mail_one, level_one, *weights)
    new_ref[...] = ((1.0 - gates_one[1]) * gates_one[2] + gates_one[1] * state_one).astype(BF16)

    def gru_back(d_next, gates, current):
        reset, update, candidate, state_part = gates
        d_cand = d_next * (1.0 - update) * (1.0 - candidate * candidate)
        d_reset = d_cand * state_part * reset * (1.0 - reset)
        d_update = d_next * (current - candidate) * update * (1.0 - update)
        dg_mail = jnp.concatenate([d_reset, d_update, d_cand], axis=1).astype(BF16)
        dg_state = jnp.concatenate([d_reset, d_update, d_cand * reset], axis=1).astype(BF16)
        d_mail = dot_nt(dg_mail, w_x[...]).astype(BF16)
        d_current = d_next * update + dot_nt(dg_state, w_h[...])
        return dg_mail, dg_state, d_mail, d_current

    dgm_one, dgs_one, dm_one, d_state = gru_back(cot_ref[...].astype(F32), gates_one, state_one)
    d_state = d_state + backward(dm_one)
    dgm_zero, dgs_zero, dm_zero, d_state = gru_back(d_state, gates_zero, state_zero)
    base_ref[...] = d_state
    level_ref[...] = jnp.concatenate([level_zero, level_one], axis=1)
    dm_ref[...] = jnp.concatenate([dm_zero, dm_one], axis=1)

    def both(first, second):
        return jnp.concatenate([first.astype(F32), second.astype(F32)], axis=0)

    dms = both(dm_zero, dm_one).T
    mails, levels = both(mail_zero, mail_one), both(level_zero, level_one)
    dgm, dgs = both(dgm_zero, dgm_one), both(dgs_zero, dgs_one)
    width = dgm.shape[1]
    rows_ref[...] = jnp.zeros_like(rows_ref)
    for k, one in enumerate((dgm, dgs)):
        total = jnp.sum(one, axis=0, keepdims=True)
        for part in range(3):
            row = 24 + 3 * k + part
            rows_ref[row : row + 1, :] = total[:, part * LANES : (part + 1) * LANES]
    small = jnp.concatenate(
        [
            dot(dms.astype(BF16), p_ref[:, hidden_units * LANES : (hidden_units + 1) * LANES]),
            dot(mails.T.astype(BF16), dgm.astype(BF16)),
            dot(levels.T.astype(BF16), dgs.astype(BF16)),
            jnp.zeros((2 * own, LANES), F32),
        ],
        axis=1,
    )

    def sorted_rows(value):
        rows = value.shape[0] // 2
        upper, lower = value[:rows], value[rows:]
        halves = [jnp.where(where_ref[0] == k, upper, lower) for k in range(2)]
        parts = []
        for k, one in enumerate(halves):
            first, second = one[: rows // 2], one[rows // 2 :]
            parts += [jnp.where(where_ref[1 + k] == side, second, first) for side in range(2)]
        return jnp.concatenate(parts, axis=0).astype(BF16)

    dms, small = sorted_rows(dms), sorted_rows(small)
    rows_in, groups, tall, wide_out = kept_first.shape
    taken = wide_out - 2 * LANES
    for group in range(groups):
        out = dot(dms, p_ref[:, group * taken : (group + 1) * taken]).astype(BF16)
        extra = small[:, group * 2 * LANES : (group + 1) * 2 * LANES]
        at = 0
        for ref in (kept_first, kept_last, given_first, given_last):
            for row in range(rows_in):
                ref[row, group, :, :taken] = out[at : at + tall]
                ref[row, group, :, taken:] = extra[at : at + tall]
                at += tall


def edge_kernel(
    batch,
    order_ref,
    edge_ref,
    gt_far,
    level_ref,
    dm_ref,
    base_ref,
    w_in_ref,
    b_in_ref,
    w_far,
    bias_ref,
    before_ref,
    feat_before,
    grad_ref,
    feat_ref,
    win_ref,
    tail_ref,
    dg_ref,
    w_ref,
    gt_ref,
    sems,
):
    blocks = edge_ref.shape[0]
    batches = order_ref.shape[0]
    hidden_units = w_in_ref.shape[1]
    chunks = (hidden_units + tail_ref.shape[0]) // GROUP
    fetches = []
    for number in range(chunks):
        some = pl.ds(number * GROUP, min(GROUP, hidden_units - number * GROUP))
        lanes = pl.ds(number * GROUP * LANES // 4, GROUP * LANES // 4)
        fetches += [
            pltpu.make_async_copy(w_far.at[some], w_ref.at[some], sems.at[number, 0]),
            pltpu.make_async_copy(
                gt_far.at[batch, :, lanes], gt_ref.at[:, lanes], sems.at[number, 1]
            ),
        ]
    for fetch in fetches:
        fetch.start()
    own, width = grad_ref.shape
    half = own // 2
    mine = slice(batch * own, (batch + 1) * own)
    bias_blocks(bias_ref, tail_ref)

    pulls = [dm_ref[mine, step * width : (step + 1) * width] for step in range(2)]
    levels = [doubled(level_ref[mine, step * width : (step + 1) * width]) for step in range(2)]
    levels = jnp.concatenate(levels, axis=1)
    total = jnp.zeros((2 * own, 2 * width), F32)
    both = jnp.concatenate(pulls, axis=0)
    for number in range(chunks):
        fetches[2 * number].wait()
        fetches[2 * number + 1].wait()
        pulled = dot(both, weights_of(w_ref, tail_ref, number)).astype(BF16)
        talls = [pulled_rows(pulled[k * own : (k + 1) * own], half) for k in range(2)]
        at = slice(number * GROUP * half, (number + 1) * GROUP * half)
        total = total + dot(gt_ref[:, at], talls[0])
        d_pair = dot_nt(jnp.concatenate(talls, axis=1), levels)
        for unit in range(0, GROUP, 2):
            row = (number * GROUP + unit) * 8
            for part in range(half // 8):
                pair = [
                    d_pair[(unit + k) * half + part * 8 : (unit + k) * half + part * 8 + 8]
                    for k in range(2)
                ]
                dg_ref[row : row + 16, part * LANES : (part + 1) * LANES] = jnp.concatenate(
                    pair, axis=0
                ).astype(BF16)
    grad = base_ref[mine] + total[:own, :width] + total[own:, width:]
    grad_ref[...] = grad.astype(BF16)

    w_in, b_in = first_layer(w_in_ref, b_in_ref)
    fold = (col_ids((hidden_units, 8 * hidden_units)) >> 3) == row_ids(
        (hidden_units, 8 * hidden_units)
    )
    fold = fold.astype(F32).astype(BF16)
    feat_ref[...] = jnp.zeros_like(feat_ref)
    if batch > 0:
        feat_ref[:, : batch * 16] = feat_before[...]

    def one_piece(piece, sums):
        feats, held, pairs, low = edge_piece(batches, order_ref, edge_ref, piece, batch)
        pre = dot(w_in, feats) + b_in
        sig = jax.nn.sigmoid(pre)
        spread = dot(dg_ref[: 8 * hidden_units], pairs)
        spread = spread.reshape(hidden_units, 8, pre.shape[1])
        spread = jnp.where(low[None], spread, 0.0).reshape(8 * hidden_units, pre.shape[1])
        d_hidden = dot(fold, spread.astype(BF16))
        d_pre = (d_hidden * sig * (1.0 + pre * (1.0 - sig))).astype(BF16)
        out = dot(w_in_ref[...], d_pre).astype(BF16)
        for k in range(PIECE):
            at = order_ref[batch, PIECE * piece + k]
            feat_ref[at, batch * 16 :] = out[:, k * LANES : (k + 1) * LANES]
        ones = jnp.where(row_ids((16, pre.shape[1])) == 0, held, 0.0).astype(BF16)
        return sums + dot_nt(jnp.concatenate([feats, ones], axis=0), d_pre)

    win_ref[...] = lax.fori_loop(
        0, (order_ref[batch, blocks] + PIECE - 1) // PIECE, one_piece, before_ref[...]
    )


def add_kernel(first_ref, second_ref, out_ref):
    out_ref[...] = (first_ref[...].astype(F32) + second_ref[...].astype(F32)).astype(BF16)


def rows_kernel(first_ref, second_ref, out_ref, rows_ref):
    parts, tall, wide = first_ref.shape
    main = wide // LANES - 2
    for part in range(parts):
        total = first_ref[part].astype(F32) + second_ref[part].astype(F32)
        for block in range(main):
            rows_ref[pl.ds(block, tall, stride=main), :] = total[
                :, block * LANES : (block + 1) * LANES
            ]
        for k in range(2):
            start = tall * (main + k)
            rows_ref[start : start + tall, :] = total[:, (main + k) * LANES : (main + k + 1) * LANES]
        out_ref[part] = rows_ref[...].astype(BF16)


def rows_of(first, second):
    parts, tall, wide = first.shape
    shape = (tall * (wide // LANES), LANES)
    return full_call(
        rows_kernel,
        jax.ShapeDtypeStruct((parts,) + shape, BF16),
        (pltpu.VMEM(shape, F32),),
        cost_estimate=cost(1),
    )(first, second)


def place_kernel(tall, count, carried, *refs):
    at_ref, pieces = refs[0], refs[1 : 1 + count]
    outs = refs[1 + count + carried : 6 + count + carried]
    big_ref, little_ref, sems = refs[6 + count + carried :]
    d_w, d_bias, d_x, d_h, d_rest = outs
    waits = []
    slot = 0
    for k, piece in enumerate(pieces):
        chunks, rows_in, lanes = piece.shape
        main = rows_in // tall - 2
        for chunk in range(chunks):
            code = at_ref[k] ^ chunk
            line, part = code >> 2, code & 3
            at = pl.ds(pl.multiple_of(line * tall, 8), tall)
            rows = piece[chunk].astype(F32)
            for row in range(tall):
                big_ref[slot, :, row * lanes : (row + 1) * lanes] = rows[row * main : (row + 1) * main]
            copy = pltpu.make_async_copy(
                big_ref.at[slot],
                d_w.at[
                    pl.ds(pl.multiple_of(part * main, 8), main),
                    pl.ds(pl.multiple_of(line * (tall * lanes), LANES), tall * lanes),
                ],
                sems.at[slot, 0],
            )
            copy.start()
            waits.append(copy)

            for side in range(2):
                start = tall * (main + side)
                little_ref[slot, side] = rows[start : start + tall]

                def move(target, lane):
                    lane = jnp.maximum(lane, 0) * lanes
                    to = pl.ds(pl.multiple_of(jnp.minimum(lane, target.shape[1] - lanes), LANES), lanes)
                    return pltpu.make_async_copy(
                        little_ref.at[slot, side], target.at[at, to], sems.at[slot, 1 + side]
                    )

                block = 2 * part + side
                to_x, to_h = move(d_x, block - 1), move(d_h, block - 4)
                alone = move((d_bias, d_rest)[side], 0)
                lone = block == 7 * side
                pl.when(lone)(alone.start)
                pl.when((block > 0) & (block < 4))(to_x.start)
                pl.when((block > 3) & (block < 7))(to_h.start)
                waits.append(alone)
            slot += 1
    for copy in waits:
        copy.wait()


def cost(micros):
    return pl.CostEstimate(
        flops=int(micros * 1e9), bytes_accessed=int(micros * 3e6), transcendentals=0
    )


def place_pieces(tall, at, pieces, shapes, before=()):
    count = len(pieces)
    chunks, rows_in, lanes = pieces[0].shape
    slots = count * chunks
    vmem = pl.BlockSpec(memory_space=pltpu.VMEM)
    hbm = pl.BlockSpec(memory_space=pl.ANY)
    return pl.pallas_call(
        functools.partial(place_kernel, tall, count, len(before)),
        out_shape=shapes,
        in_specs=[pl.BlockSpec(memory_space=pltpu.SMEM)] + [vmem] * count + [hbm] * len(before),
        out_specs=[hbm] * len(shapes),
        scratch_shapes=(
            pltpu.VMEM((slots, rows_in // tall - 2, tall * lanes), F32),
            pltpu.VMEM((slots, 2, tall, lanes), F32),
            pltpu.SemaphoreType.DMA((slots, 3)),
        ),
        input_output_aliases={1 + count + k: k for k in range(len(before))},
        cost_estimate=cost(slots / 4),
        compiler_params=pltpu.CompilerParams(vmem_limit_bytes=16 * MIB),
    )(at, *pieces, *before)


def body(
    states,
    edge_feats,
    source_index,
    target_index,
    w_edge_in,
    b_edge_in,
    w_edge_out,
    b_edge_out,
    w_input,
    w_hidden,
    b_input,
    b_hidden,
    cotangent,
):
    batches, own, width = states.shape
    edges = source_index.shape[1]
    owners = lax.axis_size("edge")
    cap = max(2, 2 * edges // owners)
    feat_count, units = w_edge_in.shape

    sent = full_call(
        functools.partial(route_kernel, own),
        jax.ShapeDtypeStruct((owners, batches * feat_count + 16, cap), BF16),
        limit=60,
    )(source_index, target_index, edge_feats)
    edge_data = lax.all_to_all(sent, "edge", 0, 0, tiled=True)
    merge = max(1, LANES // cap)
    if merge > 1:
        edge_data = edge_data.reshape(owners // merge, merge, -1, cap).transpose(0, 2, 1, 3)
        edge_data = edge_data.reshape(owners // merge, -1, merge * cap)

    w_mats = w_edge_out.reshape(units, width, width)
    padded = (units + 2 + GROUP - 1) // GROUP * GROUP

    tall = width // 8
    pairs = own // 2
    blocks = edge_data.shape[0]
    core = lax.axis_index("graph")
    spot = lax.axis_index("edge")
    orders = ((0, 1, 2, 3), (2, 0, 1, 3))

    def bit(side, step):
        first, second = [(spot >> orders[k][step]) & 1 for k in range(2)]
        return jnp.where(side == 0, first, second)

    where = jnp.stack([core, bit(core, 0), bit(1 - core, 0)])
    smem = pl.BlockSpec(memory_space=pltpu.SMEM)
    vmem = pl.BlockSpec(memory_space=pltpu.VMEM)
    far = pl.BlockSpec(memory_space=pl.ANY)
    bias = b_edge_out.reshape(width, width)
    quarter = jax.ShapeDtypeStruct((2, 4, tall, (units // 4 + 2) * width), BF16)
    new_states, *sums, gt, levels, d_mails, base, order, first = full_call(
        main_kernel,
        (
            jax.ShapeDtypeStruct((batches * own, width), BF16),
            *[quarter] * 4,
            jax.ShapeDtypeStruct((batches, LANES, padded * pairs), BF16),
            jax.ShapeDtypeStruct((batches * own, 2 * width), BF16),
            jax.ShapeDtypeStruct((batches * own, 2 * width), BF16),
            jax.ShapeDtypeStruct((batches * own, width), F32),
            jax.ShapeDtypeStruct((batches, blocks + 1), jnp.int32),
            jax.ShapeDtypeStruct((32, width), F32),
        ),
        (
            pltpu.VMEM((units, PIECE * LANES), F32),
            pltpu.VMEM((padded * 8, 512), F32),
            pltpu.VMEM((batches, padded * pairs, LANES), BF16),
            pltpu.VMEM((2 * batches * own, padded * width), BF16),
            pltpu.VMEM((units, width, width), BF16),
            pltpu.VMEM((padded - units, width, width), BF16),
            pltpu.SemaphoreType.DMA(()),
        ),
        limit=60,
        in_specs=[smem] + [vmem] * 5 + [far] + [vmem] * 5,
        out_specs=[vmem] * 9 + [smem, vmem],
    )(
        where,
        edge_data,
        states.reshape(batches * own, width),
        cotangent.reshape(batches * own, width),
        w_edge_in,
        b_edge_in,
        w_mats,
        bias,
        w_input,
        w_hidden,
        b_input,
        b_hidden,
    )

    cores = lax.axis_size("graph")

    def to_core(value):
        return lax.ppermute(value, "graph", [(0, 1), (1, 0)])

    def swap(value, masks):
        moves = []
        for side in range(cores):
            first = side * owners
            moves += [(first + k, first + (k ^ masks[side])) for k in range(owners)]
        return lax.ppermute(value, ("graph", "edge"), moves)

    def swap_step(value, step):
        return swap(value, [1 << orders[side][step] for side in range(cores)])

    def pick(value, number):
        return lax.dynamic_index_in_dim(value, number, 0, False)

    def added(terms):
        return sum(one.astype(F32) for one in terms)

    def after(value, *others):
        return lax.optimization_barrier((value, *others))[0]

    def edge_grads(batch, gt_in, first, feats):
        return full_call(
            functools.partial(edge_kernel, batch),
            (
                jax.ShapeDtypeStruct((own, width), BF16),
                jax.ShapeDtypeStruct((blocks, (batch + 1) * feat_count, LANES), BF16),
                jax.ShapeDtypeStruct((32, units), F32),
            ),
            (
                pltpu.VMEM((padded - units, width, width), BF16),
                pltpu.VMEM((padded * 8, 512), BF16),
                pltpu.VMEM((units, width, width), BF16),
                pltpu.VMEM((LANES, padded * pairs), BF16),
                pltpu.SemaphoreType.DMA((padded // GROUP, 2)),
            ),
            limit=60,
            in_specs=[smem, vmem, far] + [vmem] * 5 + [far] + [vmem] * 3,
            cost_estimate=cost(9),
        )(
            order, edge_data, gt_in, levels, d_mails, base,
            w_edge_in, b_edge_in, w_mats, bias, first, feats,
        )

    kept_first, kept_last, given_first, given_last = sums
    got_first, got_last = to_core(given_first), to_core(given_last)
    give = full_call(
        add_kernel, jax.ShapeDtypeStruct(kept_first.shape, BF16), cost_estimate=cost(1)
    )(kept_first, got_first)
    terms = [kept_last, got_last]
    state_grad, d_feats = [], jnp.zeros((8, LANES), BF16)
    for step in range(3):
        if step > 0:
            number = bit(core, step)
            give = added([pick(one, 1 - number) for one in terms]).astype(BF16)
            terms = [pick(one, number) for one in terms]
        got = swap_step(give, step)
        if step < batches:
            grad, d_feats, first = edge_grads(step, after(gt, give), first, d_feats)
            got = after(got, first)
            state_grad.append(grad)
        if step == 2:
            back = d_feats
            if merge > 1:
                back = back.reshape(blocks, -1, merge, cap).transpose(0, 2, 1, 3)
            back = after(back.reshape(owners, -1, cap), give)
            back = lax.all_to_all(back, "edge", 0, 0, tiled=True)
            got = after(got, back)
        terms.append(got)
        if step == 0:
            terms = [one.reshape((2, 2, 2) + one.shape[2:]) for one in terms]
    total = added(terms).astype(BF16)
    for extra in range(3, owners.bit_length() - 1):
        masks = [1 << extra] * cores
        got, more = lax.optimization_barrier((swap(total, masks), swap(first, masks)))
        first = first + more
        if extra < owners.bit_length() - 2:
            total = added([total, got]).astype(BF16)
    feat_grad = full_call(
        functools.partial(unroute_kernel, own),
        jax.ShapeDtypeStruct((batches, feat_count, edges), BF16),
        cost_estimate=cost(3),
    )(source_index, after(back, total).reshape(owners, batches, feat_count, cap))

    held = rows_of(total, after(got, feat_grad))

    def both(big, small, step):
        return lax.optimization_barrier((swap_step(big, step), swap_step(small, step)))

    got, more = both(held, first, 2)
    first = first + more
    held = jnp.concatenate([held, got], axis=0)
    across = swap_step(held, 0)
    near, more = both(held, first, 1)
    first = first + more
    last, more = swap_step(near, 0), swap_step(first, 0)

    shapes = tuple(
        jax.ShapeDtypeStruct(shape, F32)
        for shape in (
            (units, width * width),
            (width, width),
            (width, 3 * width),
            (width, 3 * width),
            (width, width),
        )
    )
    outs = ()
    for wave in (((held, 0),), ((near, 4), (across, 8)), ((last, 12),)):
        at, pieces = [], []
        extra = more if wave[0][0] is last else ()
        ready = lax.optimization_barrier((outs, tuple(piece for piece, _ in wave), extra))
        outs, wave, more_in = ready[0], zip(ready[1], [flips for _, flips in wave]), ready[2]
        for piece, flips in wave:
            for side, one in ((core, piece), (1 - core, to_core(piece))):
                code = side
                for step in range(3):
                    code = code * 2 + bit(side, step)
                at.append((code * 2) ^ flips)
                pieces.append(one)
        outs = place_pieces(tall, jnp.stack(at), pieces, shapes, outs)
    first = first + more_in
    first_sum = first + to_core(first)
    d_w, d_bias, d_x, d_h, _ = outs
    return (
        new_states.reshape(batches, own, width),
        jnp.stack(state_grad),
        feat_grad,
        first_sum[:feat_count],
        first_sum[feat_count],
        d_w,
        d_bias.reshape(-1),
        d_x,
        d_h,
        first_sum[24:27].reshape(-1),
        first_sum[27:30].reshape(-1),
    )


def solution(mesh):
    spread = ("graph", "edge")
    rows = P(None, spread, None)
    edges = P(None, spread)
    feats = P(None, None, spread)
    in_specs = (rows, feats, edges, edges) + (P(),) * 8 + (rows,)
    out_specs = (rows, rows, feats) + (P(),) * 8
    return jax.shard_map(
        body,
        mesh=mesh,
        in_specs=in_specs,
        out_specs=out_specs,
        check_vma=False,
    )
```

```python
import functools

import jax
import jax.numpy as jnp
from jax import lax
from jax.experimental import pallas as pl
from jax.experimental.pallas import tpu as pltpu
from jax.sharding import PartitionSpec as P

F32 = jnp.float32
BF16 = jnp.bfloat16
LANES = 128
PIECE = 4
GROUP = 12
MIB = 1024 * 1024


def dot(first, second, dims=((1,), (0,))):
    return lax.dot_general(first, second, (dims, ((), ())), preferred_element_type=F32)


def dot_nt(first, second):
    return dot(first, second, ((1,), (1,)))


def row_ids(shape):
    return lax.broadcasted_iota(jnp.int32, shape, 0)


def col_ids(shape):
    return lax.broadcasted_iota(jnp.int32, shape, 1)


def full_call(kernel, out_shape, scratch=(), limit=16, **more):
    return pl.pallas_call(
        kernel,
        out_shape=out_shape,
        scratch_shapes=scratch,
        compiler_params=pltpu.CompilerParams(vmem_limit_bytes=limit * MIB),
        **more,
    )


def ranks_of(owner, owners):
    hits = (row_ids((owners, owner.shape[1])) == owner).astype(F32)
    before = (row_ids((LANES, LANES)) < col_ids((LANES, LANES))).astype(BF16)
    seen = jnp.zeros((owners, 1), F32)
    ranks = []
    for start in range(0, owner.shape[1], LANES):
        part = hits[:, start : start + LANES]
        place = dot(part.astype(BF16), before) + seen
        ranks.append(jnp.sum(part * place, axis=0, keepdims=True))
        seen = seen + jnp.sum(part, axis=1, keepdims=True)
    return hits, jnp.concatenate(ranks, axis=1)


def route_kernel(own_rows, src_ref, dst_ref, feat_ref, out_ref):
    owners, rows, cap = out_ref.shape
    batches, feats, edges = feat_ref.shape
    shift = own_rows.bit_length() - 1
    marks = [jnp.zeros((16, cap), F32)] * owners
    for batch in range(batches):
        source, target = src_ref[batch : batch + 1], dst_ref[batch : batch + 1]
        owner = source >> shift
        hits, rank = ranks_of(owner, owners)
        spots = (row_ids((cap, edges)) == rank.astype(jnp.int32)).astype(BF16)
        line = row_ids((16, edges)) - 3 * batch
        first = owner << shift
        extra = jnp.where(line == 0, source - first, jnp.where(line == 1, target - first, 1))
        extra = jnp.where((line >= 0) & (line < 3), extra, 0).astype(F32)
        load = jnp.concatenate([feat_ref[batch].astype(F32), extra], axis=0)
        masked = [(load * hits[part : part + 1]).astype(BF16) for part in range(owners)]
        out = dot_nt(jnp.concatenate(masked, axis=0), spots)
        for part in range(owners):
            tile = out[part * (feats + 16) : (part + 1) * (feats + 16)]
            out_ref[part, batch * feats : (batch + 1) * feats] = tile[:feats].astype(BF16)
            marks[part] = marks[part] + tile[feats:]
    for part in range(owners):
        out_ref[part, batches * feats :] = marks[part].astype(BF16)


def unroute_kernel(own_rows, src_ref, back_ref, out_ref):
    owners, batches, rows, cap = back_ref.shape
    edges = src_ref.shape[1]
    shift = own_rows.bit_length() - 1
    for batch in range(batches):
        hits, rank = ranks_of(src_ref[batch : batch + 1] >> shift, owners)
        spots = (row_ids((cap, edges)) == rank.astype(jnp.int32)).astype(BF16)
        parts = [back_ref[part, batch] for part in range(owners)]
        spread = dot(jnp.concatenate(parts, axis=0), spots)
        total = jnp.zeros((rows, edges), F32)
        for part in range(owners):
            total = total + spread[part * rows : (part + 1) * rows] * hits[part : part + 1]
        out_ref[batch] = total.astype(BF16)


def edge_piece(batches, order_ref, edge_ref, piece, batch):
    some = [edge_ref[order_ref[batch, PIECE * piece + k]] for k in range(PIECE)]
    block = jnp.concatenate(some, axis=1)
    feats, marks = block[batch * 16 : (batch + 1) * 16], block[batches * 16 :].astype(F32)
    source = marks[3 * batch : 3 * batch + 1].astype(jnp.int32)
    target = marks[3 * batch + 1 : 3 * batch + 2].astype(jnp.int32)
    held = marks[3 * batch + 2 : 3 * batch + 3]
    code = ((target >> 3) & 3) * 128 + (target >> 5) * 64 + source
    code = jnp.where(held > 0.5, code, -1)
    pairs = (row_ids((512, block.shape[1])) == code).astype(BF16)
    low = row_ids((8, block.shape[1])) == (target & 7)
    return feats, held, pairs, low


def order_blocks(batches, edge_ref, order_ref):
    blocks = edge_ref.shape[0]
    for batch in range(batches):
        front, back = jnp.int32(0), jnp.int32(blocks - 1)
        row = 3 * batch + 2
        for block in range(blocks):
            marks = edge_ref[block, batches * 16 :].astype(F32)
            held = jnp.max(marks[row : row + 1]) > 0.5
            order_ref[batch, jnp.where(held, front, back)] = jnp.int32(block)
            step = held.astype(jnp.int32)
            front, back = front + step, back - (1 - step)
        order_ref[batch, blocks] = front


def first_layer(w_in_ref, b_in_ref):
    bias = jnp.broadcast_to(b_in_ref[...].reshape(1, -1), (8, b_in_ref.shape[0]))
    return w_in_ref[...].astype(F32).T.astype(BF16), bias.T[:, :1]


def gates_of(mail_low, level, w_x, w_h, b_x, b_h):
    width = level.shape[1]
    from_mail = dot(mail_low, w_x[...]) + b_x[...].reshape(1, -1)
    from_state = dot(level, w_h[...]) + b_h[...].reshape(1, -1)
    reset = jax.nn.sigmoid(from_mail[:, :width] + from_state[:, :width])
    update = jax.nn.sigmoid(from_mail[:, width : 2 * width] + from_state[:, width : 2 * width])
    state_part = from_state[:, 2 * width :]
    candidate = jnp.tanh(from_mail[:, 2 * width :] + reset * state_part)
    return reset, update, candidate, state_part


def doubled(level):
    blank = jnp.zeros_like(level)
    return jnp.concatenate(
        [jnp.concatenate([level, blank], axis=1), jnp.concatenate([blank, level], axis=1)], axis=0
    )


def bias_blocks(bias_ref, tail_ref):
    tail_ref[...] = jnp.zeros_like(tail_ref)
    high = bias_ref[...].astype(BF16)
    tail_ref[0] = high
    tail_ref[1] = (bias_ref[...] - high.astype(F32)).astype(BF16)


def weights_of(w_ref, tail_ref, number):
    units = w_ref.shape[0]
    blocks = []
    for unit in range(number * GROUP, (number + 1) * GROUP):
        blocks.append(w_ref[unit] if unit < units else tail_ref[unit - units])
    return jnp.concatenate(blocks, axis=1)


def pulled_rows(pulled, half):
    rows = []
    for start in range(0, pulled.shape[1], LANES):
        tile = pulled[:, start : start + LANES]
        rows.append(jnp.concatenate([tile[:half], tile[half:]], axis=1))
    return jnp.concatenate(rows, axis=0)


def main_kernel(
    where_ref,
    edge_ref,
    state_ref,
    cot_ref,
    w_in_ref,
    b_in_ref,
    w_far,
    bias_ref,
    w_x,
    w_h,
    b_x,
    b_h,
    new_ref,
    kept_first,
    kept_last,
    given_first,
    given_last,
    gt_far,
    level_ref,
    dm_ref,
    base_ref,
    order_ref,
    rows_ref,
    hid_ref,
    acc_ref,
    g_ref,
    p_ref,
    w_ref,
    tail_ref,
    gt_ref,
    sum_ref,
    sum_sems,
    sems,
):
    fetch = pltpu.make_async_copy(w_far, w_ref, sems.at[0])
    fetch.start()
    blocks = edge_ref.shape[0]
    batches = g_ref.shape[0]
    hidden_units = hid_ref.shape[0]
    units = acc_ref.shape[0] // 8
    own = state_ref.shape[0] // batches
    half = own // 2
    span = GROUP * half
    wide = GROUP * LANES
    chunks = units // GROUP
    order_blocks(batches, edge_ref, order_ref)
    bias_blocks(bias_ref, tail_ref)
    w_in, b_in = first_layer(w_in_ref, b_in_ref)

    for batch in range(batches):
        acc_ref[...] = jnp.zeros_like(acc_ref)

        def add_piece(piece, carry):
            feats, held, pairs, low = edge_piece(batches, order_ref, edge_ref, piece, batch)
            pre = dot(w_in, feats) + b_in
            hid_ref[...] = (pre * jax.nn.sigmoid(pre)).astype(BF16).astype(F32)
            ones = jnp.where(low, 1.0, 0.0)
            parts = []
            for unit in range(0, hidden_units, 2):
                two = [jnp.where(low, hid_ref[unit + k : unit + k + 1], 0.0) for k in range(2)]
                parts.append(jnp.concatenate(two, axis=0).astype(BF16))
            parts.append(jnp.concatenate([ones, ones], axis=0).astype(BF16))
            parts.append(jnp.zeros((8 * (units - hidden_units - 2), pre.shape[1]), BF16))
            acc_ref[...] += dot_nt(jnp.concatenate(parts, axis=0), pairs)
            return carry

        lax.fori_loop(0, (order_ref[batch, blocks] + PIECE - 1) // PIECE, add_piece, 0)

        def place(step, carry):
            for four in range(3):
                rows = []
                for k in range(4):
                    for part in range(4):
                        start = pl.multiple_of(step * 96 + four * 32 + k * 8, 8)
                        rows.append(acc_ref[pl.ds(start, 8), part * LANES : (part + 1) * LANES])
                tile = jnp.concatenate(rows, axis=0).astype(BF16)
                at = pl.ds(pl.multiple_of((step * 3 + four) * LANES, LANES), LANES)
                g_ref[batch, at, :] = tile
                gt_ref[batch, :, at] = tile.T
            return carry

        lax.fori_loop(0, units // 12, place, 0)

    def forward(step, level):
        two = [doubled(level[batch * own : (batch + 1) * own]) for batch in range(batches)]
        mail = jnp.zeros((batches * own, LANES), F32)
        base = step * batches * own
        for number in range(chunks):
            for batch in range(batches):
                out = dot(g_ref[batch, number * span : (number + 1) * span, :], two[batch])
                out = out.astype(BF16)
                for unit in range(GROUP):
                    lane = number * wide + unit * LANES
                    for part in range(2):
                        row = base + batch * own + part * half
                        p_ref[row : row + half, lane : lane + LANES] = out[
                            unit * half : (unit + 1) * half, part * LANES : (part + 1) * LANES
                        ]
            rows = p_ref[base : base + batches * own, number * wide : (number + 1) * wide]
            mail = mail + dot_nt(rows, weights_of(w_ref, tail_ref, number))
        return mail

    def backward(d_mail):
        sums = [jnp.zeros((LANES, 2 * LANES), F32) for batch in range(batches)]
        for number in range(chunks):
            pulled = dot(d_mail, weights_of(w_ref, tail_ref, number)).astype(BF16)
            at = slice(number * span, (number + 1) * span)
            for batch in range(batches):
                tall = pulled_rows(pulled[batch * own : (batch + 1) * own], half)
                sums[batch] = sums[batch] + dot(gt_ref[batch, :, at], tall)
        return jnp.concatenate([one[:own, :LANES] + one[own:, LANES:] for one in sums], axis=0)

    weights = (w_x, w_h, b_x, b_h)
    level_zero = state_ref[...]
    state_zero = level_zero.astype(F32)
    leave = pltpu.make_async_copy(gt_ref, gt_far, sems.at[1])
    leave.start()
    fetch.wait()
    mail_zero = forward(0, level_zero).astype(BF16)
    gates_zero = gates_of(mail_zero, level_zero, *weights)
    state_one = (1.0 - gates_zero[1]) * gates_zero[2] + gates_zero[1] * state_zero
    level_one = state_one.astype(BF16)
    mail_one = forward(1, level_one).astype(BF16)
    gates_one = gates_of(mail_one, level_one, *weights)
    new_ref[...] = ((1.0 - gates_one[1]) * gates_one[2] + gates_one[1] * state_one).astype(BF16)

    def gru_back(d_next, gates, current):
        reset, update, candidate, state_part = gates
        d_cand = d_next * (1.0 - update) * (1.0 - candidate * candidate)
        d_reset = d_cand * state_part * reset * (1.0 - reset)
        d_update = d_next * (current - candidate) * update * (1.0 - update)
        dg_mail = jnp.concatenate([d_reset, d_update, d_cand], axis=1).astype(BF16)
        dg_state = jnp.concatenate([d_reset, d_update, d_cand * reset], axis=1).astype(BF16)
        d_mail = dot_nt(dg_mail, w_x[...]).astype(BF16)
        d_current = d_next * update + dot_nt(dg_state, w_h[...])
        return dg_mail, dg_state, d_mail, d_current

    dgm_one, dgs_one, dm_one, d_state = gru_back(cot_ref[...].astype(F32), gates_one, state_one)
    d_state = d_state + backward(dm_one)
    dgm_zero, dgs_zero, dm_zero, d_state = gru_back(d_state, gates_zero, state_zero)
    base_ref[...] = d_state
    level_ref[...] = jnp.concatenate([level_zero, level_one], axis=1)
    dm_ref[...] = jnp.concatenate([dm_zero, dm_one], axis=1)

    def both(first, second):
        return jnp.concatenate([first.astype(F32), second.astype(F32)], axis=0)

    dms = both(dm_zero, dm_one).T
    mails, levels = both(mail_zero, mail_one), both(level_zero, level_one)
    dgm, dgs = both(dgm_zero, dgm_one), both(dgs_zero, dgs_one)
    width = dgm.shape[1]
    rows_ref[...] = jnp.zeros_like(rows_ref)
    for k, one in enumerate((dgm, dgs)):
        total = jnp.sum(one, axis=0, keepdims=True)
        for part in range(3):
            row = 24 + 3 * k + part
            rows_ref[row : row + 1, :] = total[:, part * LANES : (part + 1) * LANES]
    small = jnp.concatenate(
        [
            dot(dms.astype(BF16), p_ref[:, hidden_units * LANES : (hidden_units + 1) * LANES]),
            dot(mails.T.astype(BF16), dgm.astype(BF16)),
            dot(levels.T.astype(BF16), dgs.astype(BF16)),
            jnp.zeros((2 * own, LANES), F32),
        ],
        axis=1,
    )

    def sorted_rows(value):
        rows = value.shape[0] // 2
        upper, lower = value[:rows], value[rows:]
        halves = [jnp.where(where_ref[0] == k, upper, lower) for k in range(2)]
        parts = []
        for k, one in enumerate(halves):
            first, second = one[: rows // 2], one[rows // 2 :]
            parts += [jnp.where(where_ref[1 + k] == side, second, first) for side in range(2)]
        return jnp.concatenate(parts, axis=0).astype(BF16)

    dms, small = sorted_rows(dms), sorted_rows(small)
    rows_in, groups, tall, wide_out = kept_first.shape
    taken = wide_out - 2 * LANES
    moves = []
    for group in range(groups):
        out = dot(dms, p_ref[:, group * taken : (group + 1) * taken]).astype(BF16)
        extra = small[:, group * 2 * LANES : (group + 1) * 2 * LANES]
        for k, ref in enumerate((given_first, kept_first, given_last, kept_last)):
            for row in range(rows_in):
                at = ((2, 0, 3, 1)[k] * rows_in + row) * tall
                sum_ref[k, row, group, :, :taken] = out[at : at + tall]
                sum_ref[k, row, group, :, taken:] = extra[at : at + tall]
                moves.append(
                    pltpu.make_async_copy(
                        sum_ref.at[k, row, group], ref.at[row, group], sum_sems.at[k, row, group]
                    )
                )
                moves[-1].start()
    for move in moves:
        move.wait()
    leave.wait()


def edge_kernel(
    batch,
    order_ref,
    edge_ref,
    gt_far,
    level_ref,
    dm_ref,
    base_ref,
    w_in_ref,
    b_in_ref,
    w_far,
    bias_ref,
    before_ref,
    feat_before,
    grad_ref,
    feat_ref,
    win_ref,
    tail_ref,
    dg_ref,
    w_ref,
    gt_ref,
    sems,
):
    blocks = edge_ref.shape[0]
    batches = order_ref.shape[0]
    hidden_units = w_in_ref.shape[1]
    chunks = (hidden_units + tail_ref.shape[0]) // GROUP
    fetches = []
    for number in range(chunks):
        some = pl.ds(number * GROUP, min(GROUP, hidden_units - number * GROUP))
        lanes = pl.ds(number * GROUP * LANES // 4, GROUP * LANES // 4)
        fetches += [
            pltpu.make_async_copy(w_far.at[some], w_ref.at[some], sems.at[number, 0]),
            pltpu.make_async_copy(
                gt_far.at[batch, :, lanes], gt_ref.at[:, lanes], sems.at[number, 1]
            ),
        ]
    for fetch in fetches:
        fetch.start()
    own, width = grad_ref.shape
    half = own // 2
    mine = slice(batch * own, (batch + 1) * own)
    bias_blocks(bias_ref, tail_ref)

    pulls = [dm_ref[mine, step * width : (step + 1) * width] for step in range(2)]
    levels = [doubled(level_ref[mine, step * width : (step + 1) * width]) for step in range(2)]
    levels = jnp.concatenate(levels, axis=1)
    total = jnp.zeros((2 * own, 2 * width), F32)
    both = jnp.concatenate(pulls, axis=0)
    for number in range(chunks):
        fetches[2 * number].wait()
        fetches[2 * number + 1].wait()
        pulled = dot(both, weights_of(w_ref, tail_ref, number)).astype(BF16)
        talls = [pulled_rows(pulled[k * own : (k + 1) * own], half) for k in range(2)]
        at = slice(number * GROUP * half, (number + 1) * GROUP * half)
        total = total + dot(gt_ref[:, at], talls[0])
        d_pair = dot_nt(jnp.concatenate(talls, axis=1), levels)
        for unit in range(0, GROUP, 2):
            row = (number * GROUP + unit) * 8
            for part in range(half // 8):
                pair = [
                    d_pair[(unit + k) * half + part * 8 : (unit + k) * half + part * 8 + 8]
                    for k in range(2)
                ]
                dg_ref[row : row + 16, part * LANES : (part + 1) * LANES] = jnp.concatenate(
                    pair, axis=0
                ).astype(BF16)
    grad = base_ref[mine] + total[:own, :width] + total[own:, width:]
    grad_ref[...] = grad.astype(BF16)

    w_in, b_in = first_layer(w_in_ref, b_in_ref)
    fold = (col_ids((hidden_units, 8 * hidden_units)) >> 3) == row_ids(
        (hidden_units, 8 * hidden_units)
    )
    fold = fold.astype(F32).astype(BF16)
    feat_ref[...] = jnp.zeros_like(feat_ref)
    if batch > 0:
        feat_ref[:, : batch * 16] = feat_before[...]

    def one_piece(piece, sums):
        feats, held, pairs, low = edge_piece(batches, order_ref, edge_ref, piece, batch)
        pre = dot(w_in, feats) + b_in
        sig = jax.nn.sigmoid(pre)
        spread = dot(dg_ref[: 8 * hidden_units], pairs)
        spread = spread.reshape(hidden_units, 8, pre.shape[1])
        spread = jnp.where(low[None], spread, 0.0).reshape(8 * hidden_units, pre.shape[1])
        d_hidden = dot(fold, spread.astype(BF16))
        d_pre = (d_hidden * sig * (1.0 + pre * (1.0 - sig))).astype(BF16)
        out = dot(w_in_ref[...], d_pre).astype(BF16)
        for k in range(PIECE):
            at = order_ref[batch, PIECE * piece + k]
            feat_ref[at, batch * 16 :] = out[:, k * LANES : (k + 1) * LANES]
        ones = jnp.where(row_ids((16, pre.shape[1])) == 0, held, 0.0).astype(BF16)
        return sums + dot_nt(jnp.concatenate([feats, ones], axis=0), d_pre)

    win_ref[...] = lax.fori_loop(
        0, (order_ref[batch, blocks] + PIECE - 1) // PIECE, one_piece, before_ref[...]
    )


def add_kernel(first_ref, second_ref, out_ref):
    out_ref[...] = (first_ref[...].astype(F32) + second_ref[...].astype(F32)).astype(BF16)


def rows_kernel(first_ref, second_ref, out_ref, rows_ref):
    parts, tall, wide = first_ref.shape
    main = wide // LANES - 2
    for part in range(parts):
        total = first_ref[part].astype(F32) + second_ref[part].astype(F32)
        for block in range(main):
            rows_ref[pl.ds(block, tall, stride=main), :] = total[
                :, block * LANES : (block + 1) * LANES
            ]
        for k in range(2):
            start = tall * (main + k)
            rows_ref[start : start + tall, :] = total[:, (main + k) * LANES : (main + k + 1) * LANES]
        out_ref[part] = rows_ref[...].astype(BF16)


def rows_of(first, second):
    parts, tall, wide = first.shape
    shape = (tall * (wide // LANES), LANES)
    return full_call(
        rows_kernel,
        jax.ShapeDtypeStruct((parts,) + shape, BF16),
        (pltpu.VMEM(shape, F32),),
        cost_estimate=cost(1),
    )(first, second)


def place_kernel(tall, count, carried, *refs):
    at_ref, pieces = refs[0], refs[1 : 1 + count]
    outs = refs[1 + count + carried : 6 + count + carried]
    big_ref, little_ref, sems = refs[6 + count + carried :]
    d_w, d_bias, d_x, d_h, d_rest = outs
    waits = []
    slot = 0
    for k, piece in enumerate(pieces):
        chunks, rows_in, lanes = piece.shape
        main = rows_in // tall - 2
        for chunk in range(chunks):
            code = at_ref[k] ^ chunk
            line, part = code >> 2, code & 3
            at = pl.ds(pl.multiple_of(line * tall, 8), tall)
            rows = piece[chunk].astype(F32)
            for row in range(tall):
                big_ref[slot, :, row * lanes : (row + 1) * lanes] = rows[row * main : (row + 1) * main]
            copy = pltpu.make_async_copy(
                big_ref.at[slot],
                d_w.at[
                    pl.ds(pl.multiple_of(part * main, 8), main),
                    pl.ds(pl.multiple_of(line * (tall * lanes), LANES), tall * lanes),
                ],
                sems.at[slot, 0],
            )
            copy.start()
            waits.append(copy)

            for side in range(2):
                start = tall * (main + side)
                little_ref[slot, side] = rows[start : start + tall]

                def move(target, lane):
                    lane = jnp.maximum(lane, 0) * lanes
                    to = pl.ds(pl.multiple_of(jnp.minimum(lane, target.shape[1] - lanes), LANES), lanes)
                    return pltpu.make_async_copy(
                        little_ref.at[slot, side], target.at[at, to], sems.at[slot, 1 + side]
                    )

                block = 2 * part + side
                to_x, to_h = move(d_x, block - 1), move(d_h, block - 4)
                alone = move((d_bias, d_rest)[side], 0)
                lone = block == 7 * side
                pl.when(lone)(alone.start)
                pl.when((block > 0) & (block < 4))(to_x.start)
                pl.when((block > 3) & (block < 7))(to_h.start)
                waits.append(alone)
            slot += 1
    for copy in waits:
        copy.wait()


def cost(micros):
    return pl.CostEstimate(
        flops=int(micros * 1e9), bytes_accessed=int(micros * 3e6), transcendentals=0
    )


def place_pieces(tall, at, pieces, shapes, before=()):
    count = len(pieces)
    chunks, rows_in, lanes = pieces[0].shape
    slots = count * chunks
    vmem = pl.BlockSpec(memory_space=pltpu.VMEM)
    hbm = pl.BlockSpec(memory_space=pl.ANY)
    return pl.pallas_call(
        functools.partial(place_kernel, tall, count, len(before)),
        out_shape=shapes,
        in_specs=[pl.BlockSpec(memory_space=pltpu.SMEM)] + [vmem] * count + [hbm] * len(before),
        out_specs=[hbm] * len(shapes),
        scratch_shapes=(
            pltpu.VMEM((slots, rows_in // tall - 2, tall * lanes), F32),
            pltpu.VMEM((slots, 2, tall, lanes), F32),
            pltpu.SemaphoreType.DMA((slots, 3)),
        ),
        input_output_aliases={1 + count + k: k for k in range(len(before))},
        cost_estimate=cost(slots / 4),
        compiler_params=pltpu.CompilerParams(vmem_limit_bytes=16 * MIB),
    )(at, *pieces, *before)


def body(
    states,
    edge_feats,
    source_index,
    target_index,
    w_edge_in,
    b_edge_in,
    w_edge_out,
    b_edge_out,
    w_input,
    w_hidden,
    b_input,
    b_hidden,
    cotangent,
):
    batches, own, width = states.shape
    edges = source_index.shape[1]
    owners = lax.axis_size("edge")
    cap = max(2, 2 * edges // owners)
    feat_count, units = w_edge_in.shape

    sent = full_call(
        functools.partial(route_kernel, own),
        jax.ShapeDtypeStruct((owners, batches * feat_count + 16, cap), BF16),
        limit=60,
    )(source_index, target_index, edge_feats)
    edge_data = lax.all_to_all(sent, "edge", 0, 0, tiled=True)
    merge = max(1, LANES // cap)
    if merge > 1:
        edge_data = edge_data.reshape(owners // merge, merge, -1, cap).transpose(0, 2, 1, 3)
        edge_data = edge_data.reshape(owners // merge, -1, merge * cap)

    w_mats = w_edge_out.reshape(units, width, width)
    padded = (units + 2 + GROUP - 1) // GROUP * GROUP

    tall = width // 8
    pairs = own // 2
    blocks = edge_data.shape[0]
    core = lax.axis_index("graph")
    spot = lax.axis_index("edge")
    orders = ((0, 1, 2, 3), (2, 0, 1, 3))

    def bit(side, step):
        first, second = [(spot >> orders[k][step]) & 1 for k in range(2)]
        return jnp.where(side == 0, first, second)

    where = jnp.stack([core, bit(core, 0), bit(1 - core, 0)])
    smem = pl.BlockSpec(memory_space=pltpu.SMEM)
    vmem = pl.BlockSpec(memory_space=pltpu.VMEM)
    far = pl.BlockSpec(memory_space=pltpu.HBM)
    bias = b_edge_out.reshape(width, width)
    quarter = jax.ShapeDtypeStruct((2, 4, tall, (units // 4 + 2) * width), BF16)
    new_states, *sums, gt, levels, d_mails, base, order, first = full_call(
        main_kernel,
        (
            jax.ShapeDtypeStruct((batches * own, width), BF16),
            *[quarter] * 4,
            jax.ShapeDtypeStruct((batches, LANES, padded * pairs), BF16),
            jax.ShapeDtypeStruct((batches * own, 2 * width), BF16),
            jax.ShapeDtypeStruct((batches * own, 2 * width), BF16),
            jax.ShapeDtypeStruct((batches * own, width), F32),
            jax.ShapeDtypeStruct((batches, blocks + 1), jnp.int32),
            jax.ShapeDtypeStruct((32, width), F32),
        ),
        (
            pltpu.VMEM((units, PIECE * LANES), F32),
            pltpu.VMEM((padded * 8, 512), F32),
            pltpu.VMEM((batches, padded * pairs, LANES), BF16),
            pltpu.VMEM((2 * batches * own, padded * width), BF16),
            pltpu.VMEM((units, width, width), BF16),
            pltpu.VMEM((padded - units, width, width), BF16),
            pltpu.VMEM((batches, LANES, padded * pairs), BF16),
            pltpu.VMEM((4,) + quarter.shape, BF16),
            pltpu.SemaphoreType.DMA((4,) + quarter.shape[:2]),
            pltpu.SemaphoreType.DMA((2,)),
        ),
        limit=60,
        in_specs=[smem] + [vmem] * 5 + [far] + [vmem] * 5,
        out_specs=[vmem] + [far] * 5 + [vmem] * 3 + [smem, vmem],
    )(
        where,
        edge_data,
        states.reshape(batches * own, width),
        cotangent.reshape(batches * own, width),
        w_edge_in,
        b_edge_in,
        w_mats,
        bias,
        w_input,
        w_hidden,
        b_input,
        b_hidden,
    )

    cores = lax.axis_size("graph")

    def to_core(value):
        return lax.ppermute(value, "graph", [(0, 1), (1, 0)])

    def swap(value, masks):
        moves = []
        for side in range(cores):
            first = side * owners
            moves += [(first + k, first + (k ^ masks[side])) for k in range(owners)]
        return lax.ppermute(value, ("graph", "edge"), moves)

    def swap_step(value, step):
        return swap(value, [1 << orders[side][step] for side in range(cores)])

    def pick(value, number):
        return lax.dynamic_index_in_dim(value, number, 0, False)

    def added(terms):
        return sum(one.astype(F32) for one in terms)

    def after(value, *others):
        return lax.optimization_barrier((value, *others))[0]

    def edge_grads(batch, gt_in, first, feats):
        return full_call(
            functools.partial(edge_kernel, batch),
            (
                jax.ShapeDtypeStruct((own, width), BF16),
                jax.ShapeDtypeStruct((blocks, (batch + 1) * feat_count, LANES), BF16),
                jax.ShapeDtypeStruct((32, units), F32),
            ),
            (
                pltpu.VMEM((padded - units, width, width), BF16),
                pltpu.VMEM((padded * 8, 512), BF16),
                pltpu.VMEM((units, width, width), BF16),
                pltpu.VMEM((LANES, padded * pairs), BF16),
                pltpu.SemaphoreType.DMA((padded // GROUP, 2)),
            ),
            limit=60,
            in_specs=[smem, vmem, far] + [vmem] * 5 + [far] + [vmem] * 3,
            cost_estimate=cost(9),
        )(
            order, edge_data, gt_in, levels, d_mails, base,
            w_edge_in, b_edge_in, w_mats, bias, first, feats,
        )

    kept_first, kept_last, given_first, given_last = sums
    got_first, got_last = to_core(given_first), to_core(given_last)
    give = full_call(
        add_kernel, jax.ShapeDtypeStruct(kept_first.shape, BF16), cost_estimate=cost(1)
    )(kept_first, got_first)
    terms = [kept_last, got_last]
    state_grad, d_feats = [], b_edge_in
    for step in range(3):
        if step > 0:
            number = bit(core, step)
            give = added([pick(one, 1 - number) for one in terms]).astype(BF16)
            terms = [pick(one, number) for one in terms]
        got = swap_step(give, step)
        if step < batches:
            grad, d_feats, first = edge_grads(step, after(gt, give), first, d_feats)
            got = after(got, first)
            state_grad.append(grad)
        terms.append(got)
        if step == 0:
            terms = [one.reshape((2, 2, 2) + one.shape[2:]) for one in terms]
    total = added(terms).astype(BF16)
    for extra in range(3, owners.bit_length() - 1):
        masks = [1 << extra] * cores
        got, more = lax.optimization_barrier((swap(total, masks), swap(first, masks)))
        first = first + more
        if extra < owners.bit_length() - 2:
            total = added([total, got]).astype(BF16)
    held = rows_of(total, got)

    def both(big, small, step):
        return lax.optimization_barrier((swap_step(big, step), swap_step(small, step)))

    got, more = both(held, first, 2)
    first = first + more
    held = jnp.concatenate([held, got], axis=0)
    across = swap_step(held, 0)
    back = d_feats
    if merge > 1:
        back = back.reshape(blocks, -1, merge, cap).transpose(0, 2, 1, 3)
    back = after(back.reshape(owners, -1, cap), held)
    back = lax.all_to_all(back, "edge", 0, 0, tiled=True)

    near, more = both(held, first, 1)
    near = after(near, back)
    first = first + more
    last, more = swap_step(near, 0), swap_step(first, 0)

    feat_grad = full_call(
        functools.partial(unroute_kernel, own),
        jax.ShapeDtypeStruct((batches, feat_count, edges), BF16),
        cost_estimate=cost(3),
    )(source_index, back.reshape(owners, batches, feat_count, cap))

    shapes = tuple(
        jax.ShapeDtypeStruct(shape, F32)
        for shape in (
            (units, width * width),
            (width, width),
            (width, 3 * width),
            (width, 3 * width),
            (width, width),
        )
    )
    outs = ()
    for wave in (((held, 0),), ((near, 4), (across, 8)), ((last, 12),)):
        at, pieces = [], []
        extra = (more, feat_grad) if wave[0][0] is last else ()
        ready = lax.optimization_barrier((outs, tuple(piece for piece, _ in wave), extra))
        outs, wave, extra = ready[0], zip(ready[1], [flips for _, flips in wave]), ready[2]
        for piece, flips in wave:
            for side, one in ((core, piece), (1 - core, to_core(piece))):
                code = side
                for step in range(3):
                    code = code * 2 + bit(side, step)
                at.append((code * 2) ^ flips)
                pieces.append(one)
        outs = place_pieces(tall, jnp.stack(at), pieces, shapes, outs)
    more, feat_grad = extra
    first = first + more
    first_sum = first + to_core(first)
    d_w, d_bias, d_x, d_h, _ = outs
    return (
        new_states.reshape(batches, own, width),
        jnp.stack(state_grad),
        feat_grad,
        first_sum[:feat_count],
        first_sum[feat_count],
        d_w,
        d_bias.reshape(-1),
        d_x,
        d_h,
        first_sum[24:27].reshape(-1),
        first_sum[27:30].reshape(-1),
    )


def solution(mesh):
    spread = ("graph", "edge")
    rows = P(None, spread, None)
    edges = P(None, spread)
    feats = P(None, None, spread)
    in_specs = (rows, feats, edges, edges) + (P(),) * 8 + (rows,)
    out_specs = (rows, rows, feats) + (P(),) * 8
    return jax.shard_map(
        body,
        mesh=mesh,
        in_specs=in_specs,
        out_specs=out_specs,
        check_vma=False,
    )
```

```python
import functools

import jax
import jax.numpy as jnp
from jax import lax
from jax.experimental import pallas as pl
from jax.experimental.pallas import tpu as pltpu
from jax.sharding import PartitionSpec as P

F32 = jnp.float32
BF16 = jnp.bfloat16
LANES = 128
PIECE = 4
GROUP = 12
MIB = 1024 * 1024


def dot(first, second, dims=((1,), (0,))):
    return lax.dot_general(first, second, (dims, ((), ())), preferred_element_type=F32)


def dot_nt(first, second):
    return dot(first, second, ((1,), (1,)))


def row_ids(shape):
    return lax.broadcasted_iota(jnp.int32, shape, 0)


def col_ids(shape):
    return lax.broadcasted_iota(jnp.int32, shape, 1)


def full_call(kernel, out_shape, scratch=(), limit=16, **more):
    return pl.pallas_call(
        kernel,
        out_shape=out_shape,
        scratch_shapes=scratch,
        compiler_params=pltpu.CompilerParams(vmem_limit_bytes=limit * MIB),
        **more,
    )


def ranks_of(owner, owners):
    hits = (row_ids((owners, owner.shape[1])) == owner).astype(F32)
    before = (row_ids((LANES, LANES)) < col_ids((LANES, LANES))).astype(BF16)
    seen = jnp.zeros((owners, 1), F32)
    ranks = []
    for start in range(0, owner.shape[1], LANES):
        part = hits[:, start : start + LANES]
        place = dot(part.astype(BF16), before) + seen
        ranks.append(jnp.sum(part * place, axis=0, keepdims=True))
        seen = seen + jnp.sum(part, axis=1, keepdims=True)
    return hits, jnp.concatenate(ranks, axis=1)


def route_kernel(own_rows, src_ref, dst_ref, feat_ref, out_ref):
    owners, rows, cap = out_ref.shape
    batches, feats, edges = feat_ref.shape
    shift = own_rows.bit_length() - 1
    marks = [jnp.zeros((16, cap), F32)] * owners
    for batch in range(batches):
        source, target = src_ref[batch : batch + 1], dst_ref[batch : batch + 1]
        owner = source >> shift
        hits, rank = ranks_of(owner, owners)
        spots = (row_ids((cap, edges)) == rank.astype(jnp.int32)).astype(BF16)
        line = row_ids((16, edges)) - 3 * batch
        first = owner << shift
        extra = jnp.where(line == 0, source - first, jnp.where(line == 1, target - first, 1))
        extra = jnp.where((line >= 0) & (line < 3), extra, 0).astype(F32)
        load = jnp.concatenate([feat_ref[batch].astype(F32), extra], axis=0)
        masked = [(load * hits[part : part + 1]).astype(BF16) for part in range(owners)]
        out = dot_nt(jnp.concatenate(masked, axis=0), spots)
        for part in range(owners):
            tile = out[part * (feats + 16) : (part + 1) * (feats + 16)]
            out_ref[part, batch * feats : (batch + 1) * feats] = tile[:feats].astype(BF16)
            marks[part] = marks[part] + tile[feats:]
    for part in range(owners):
        out_ref[part, batches * feats :] = marks[part].astype(BF16)


def unroute_kernel(own_rows, src_ref, back_ref, out_ref):
    owners, batches, rows, cap = back_ref.shape
    edges = src_ref.shape[1]
    shift = own_rows.bit_length() - 1
    for batch in range(batches):
        hits, rank = ranks_of(src_ref[batch : batch + 1] >> shift, owners)
        spots = (row_ids((cap, edges)) == rank.astype(jnp.int32)).astype(BF16)
        parts = [back_ref[part, batch] for part in range(owners)]
        spread = dot(jnp.concatenate(parts, axis=0), spots)
        total = jnp.zeros((rows, edges), F32)
        for part in range(owners):
            total = total + spread[part * rows : (part + 1) * rows] * hits[part : part + 1]
        out_ref[batch] = total.astype(BF16)


def edge_piece(batches, order_ref, edge_ref, piece, batch):
    some = [edge_ref[order_ref[batch, PIECE * piece + k]] for k in range(PIECE)]
    block = jnp.concatenate(some, axis=1)
    feats, marks = block[batch * 16 : (batch + 1) * 16], block[batches * 16 :].astype(F32)
    source = marks[3 * batch : 3 * batch + 1].astype(jnp.int32)
    target = marks[3 * batch + 1 : 3 * batch + 2].astype(jnp.int32)
    held = marks[3 * batch + 2 : 3 * batch + 3]
    code = ((target >> 3) & 3) * 128 + (target >> 5) * 64 + source
    code = jnp.where(held > 0.5, code, -1)
    pairs = (row_ids((512, block.shape[1])) == code).astype(BF16)
    low = row_ids((8, block.shape[1])) == (target & 7)
    return feats, held, pairs, low


def order_blocks(batches, edge_ref, order_ref):
    blocks = edge_ref.shape[0]
    for batch in range(batches):
        front, back = jnp.int32(0), jnp.int32(blocks - 1)
        row = 3 * batch + 2
        for block in range(blocks):
            marks = edge_ref[block, batches * 16 :].astype(F32)
            held = jnp.max(marks[row : row + 1]) > 0.5
            order_ref[batch, jnp.where(held, front, back)] = jnp.int32(block)
            step = held.astype(jnp.int32)
            front, back = front + step, back - (1 - step)
        order_ref[batch, blocks] = front


def first_layer(w_in_ref, b_in_ref):
    bias = jnp.broadcast_to(b_in_ref[...].reshape(1, -1), (8, b_in_ref.shape[0]))
    return w_in_ref[...].astype(F32).T.astype(BF16), bias.T[:, :1]


def gates_of(mail_low, level, w_x, w_h, b_x, b_h):
    width = level.shape[1]
    from_mail = dot(mail_low, w_x[...]) + b_x[...].reshape(1, -1)
    from_state = dot(level, w_h[...]) + b_h[...].reshape(1, -1)
    reset = jax.nn.sigmoid(from_mail[:, :width] + from_state[:, :width])
    update = jax.nn.sigmoid(from_mail[:, width : 2 * width] + from_state[:, width : 2 * width])
    state_part = from_state[:, 2 * width :]
    candidate = jnp.tanh(from_mail[:, 2 * width :] + reset * state_part)
    return reset, update, candidate, state_part


def doubled(level):
    blank = jnp.zeros_like(level)
    return jnp.concatenate(
        [jnp.concatenate([level, blank], axis=1), jnp.concatenate([blank, level], axis=1)], axis=0
    )


def bias_blocks(bias_ref, tail_ref):
    tail_ref[...] = jnp.zeros_like(tail_ref)
    high = bias_ref[...].astype(BF16)
    tail_ref[0] = high
    tail_ref[1] = (bias_ref[...] - high.astype(F32)).astype(BF16)


def turned(tile):
    size = tile.shape[1]
    eye = (row_ids((size, size)) == col_ids((size, size))).astype(F32).astype(BF16)
    return dot_nt(eye, tile).astype(BF16)


def weights_of(w_ref, tail_ref, number):
    units = w_ref.shape[0]
    blocks = []
    for unit in range(number * GROUP, (number + 1) * GROUP):
        blocks.append(w_ref[unit] if unit < units else tail_ref[unit - units])
    return jnp.concatenate(blocks, axis=1)


def pulled_rows(pulled, half):
    rows = []
    for start in range(0, pulled.shape[1], LANES):
        tile = pulled[:, start : start + LANES]
        rows.append(jnp.concatenate([tile[:half], tile[half:]], axis=1))
    return jnp.concatenate(rows, axis=0)


def main_kernel(
    where_ref,
    edge_ref,
    state_ref,
    cot_ref,
    w_in_ref,
    b_in_ref,
    w_far,
    bias_ref,
    w_x,
    w_h,
    b_x,
    b_h,
    new_ref,
    kept_first,
    kept_last,
    given_first,
    given_last,
    g_far,
    level_ref,
    dm_ref,
    base_ref,
    order_ref,
    rows_ref,
    hid_ref,
    acc_ref,
    g_ref,
    p_ref,
    w_ref,
    tail_ref,
    sum_ref,
    sum_sems,
    sems,
):
    fetch = pltpu.make_async_copy(w_far, w_ref, sems.at[0])
    fetch.start()
    blocks = edge_ref.shape[0]
    batches = g_ref.shape[0]
    hidden_units = hid_ref.shape[0]
    units = acc_ref.shape[0] // 8
    own = state_ref.shape[0] // batches
    half = own // 2
    span = GROUP * half
    wide = GROUP * LANES
    chunks = units // GROUP
    order_blocks(batches, edge_ref, order_ref)
    bias_blocks(bias_ref, tail_ref)
    w_in, b_in = first_layer(w_in_ref, b_in_ref)

    for batch in range(batches):
        acc_ref[...] = jnp.zeros_like(acc_ref)

        def add_piece(piece, carry):
            feats, held, pairs, low = edge_piece(batches, order_ref, edge_ref, piece, batch)
            pre = dot(w_in, feats) + b_in
            hid_ref[...] = (pre * jax.nn.sigmoid(pre)).astype(BF16).astype(F32)
            ones = jnp.where(low, 1.0, 0.0)
            parts = []
            for unit in range(0, hidden_units, 2):
                two = [jnp.where(low, hid_ref[unit + k : unit + k + 1], 0.0) for k in range(2)]
                parts.append(jnp.concatenate(two, axis=0).astype(BF16))
            parts.append(jnp.concatenate([ones, ones], axis=0).astype(BF16))
            parts.append(jnp.zeros((8 * (units - hidden_units - 2), pre.shape[1]), BF16))
            acc_ref[...] += dot_nt(jnp.concatenate(parts, axis=0), pairs)
            return carry

        lax.fori_loop(0, (order_ref[batch, blocks] + PIECE - 1) // PIECE, add_piece, 0)

        def place(step, carry):
            for four in range(3):
                rows = []
                for k in range(4):
                    for part in range(4):
                        start = pl.multiple_of(step * 96 + four * 32 + k * 8, 8)
                        rows.append(acc_ref[pl.ds(start, 8), part * LANES : (part + 1) * LANES])
                at = pl.ds(pl.multiple_of((step * 3 + four) * LANES, LANES), LANES)
                g_ref[batch, at, :] = jnp.concatenate(rows, axis=0).astype(BF16)
            return carry

        lax.fori_loop(0, units // 12, place, 0)

    def forward(step, level):
        two = [doubled(level[batch * own : (batch + 1) * own]) for batch in range(batches)]
        mail = jnp.zeros((batches * own, LANES), F32)
        base = step * batches * own
        for number in range(chunks):
            for batch in range(batches):
                out = dot(g_ref[batch, number * span : (number + 1) * span, :], two[batch])
                out = out.astype(BF16)
                for unit in range(GROUP):
                    lane = number * wide + unit * LANES
                    for part in range(2):
                        row = base + batch * own + part * half
                        p_ref[row : row + half, lane : lane + LANES] = out[
                            unit * half : (unit + 1) * half, part * LANES : (part + 1) * LANES
                        ]
            rows = p_ref[base : base + batches * own, number * wide : (number + 1) * wide]
            mail = mail + dot_nt(rows, weights_of(w_ref, tail_ref, number))
        return mail

    def backward(d_mail):
        sums = [jnp.zeros((LANES, 2 * LANES), F32) for batch in range(batches)]
        for number in range(chunks):
            pulled = dot(d_mail, weights_of(w_ref, tail_ref, number)).astype(BF16)
            at = slice(number * span, (number + 1) * span)
            for batch in range(batches):
                tall = pulled_rows(pulled[batch * own : (batch + 1) * own], half)
                sums[batch] = sums[batch] + dot(turned(g_ref[batch, at, :]), tall)
        return jnp.concatenate([one[:own, :LANES] + one[own:, LANES:] for one in sums], axis=0)

    weights = (w_x, w_h, b_x, b_h)
    level_zero = state_ref[...]
    state_zero = level_zero.astype(F32)
    leave = pltpu.make_async_copy(g_ref, g_far, sems.at[1])
    leave.start()
    fetch.wait()
    mail_zero = forward(0, level_zero).astype(BF16)
    gates_zero = gates_of(mail_zero, level_zero, *weights)
    state_one = (1.0 - gates_zero[1]) * gates_zero[2] + gates_zero[1] * state_zero
    level_one = state_one.astype(BF16)
    mail_one = forward(1, level_one).astype(BF16)
    gates_one = gates_of(mail_one, level_one, *weights)
    new_ref[...] = ((1.0 - gates_one[1]) * gates_one[2] + gates_one[1] * state_one).astype(BF16)

    def gru_back(d_next, gates, current):
        reset, update, candidate, state_part = gates
        d_cand = d_next * (1.0 - update) * (1.0 - candidate * candidate)
        d_reset = d_cand * state_part * reset * (1.0 - reset)
        d_update = d_next * (current - candidate) * update * (1.0 - update)
        dg_mail = jnp.concatenate([d_reset, d_update, d_cand], axis=1).astype(BF16)
        dg_state = jnp.concatenate([d_reset, d_update, d_cand * reset], axis=1).astype(BF16)
        d_mail = dot_nt(dg_mail, w_x[...]).astype(BF16)
        d_current = d_next * update + dot_nt(dg_state, w_h[...])
        return dg_mail, dg_state, d_mail, d_current

    dgm_one, dgs_one, dm_one, d_state = gru_back(cot_ref[...].astype(F32), gates_one, state_one)
    d_state = d_state + backward(dm_one)
    dgm_zero, dgs_zero, dm_zero, d_state = gru_back(d_state, gates_zero, state_zero)
    base_ref[...] = d_state
    level_ref[...] = jnp.concatenate([level_zero, level_one], axis=1)
    dm_ref[...] = jnp.concatenate([dm_zero, dm_one], axis=1)

    def both(first, second):
        return jnp.concatenate([first.astype(F32), second.astype(F32)], axis=0)

    dms = both(dm_zero, dm_one).T
    mails, levels = both(mail_zero, mail_one), both(level_zero, level_one)
    dgm, dgs = both(dgm_zero, dgm_one), both(dgs_zero, dgs_one)
    width = dgm.shape[1]
    rows_ref[...] = jnp.zeros_like(rows_ref)
    for k, one in enumerate((dgm, dgs)):
        total = jnp.sum(one, axis=0, keepdims=True)
        for part in range(3):
            row = 24 + 3 * k + part
            rows_ref[row : row + 1, :] = total[:, part * LANES : (part + 1) * LANES]
    small = jnp.concatenate(
        [
            dot(dms.astype(BF16), p_ref[:, hidden_units * LANES : (hidden_units + 1) * LANES]),
            dot(mails.T.astype(BF16), dgm.astype(BF16)),
            dot(levels.T.astype(BF16), dgs.astype(BF16)),
            jnp.zeros((2 * own, LANES), F32),
        ],
        axis=1,
    )

    def sorted_rows(value):
        rows = value.shape[0] // 2
        upper, lower = value[:rows], value[rows:]
        halves = [jnp.where(where_ref[0] == k, upper, lower) for k in range(2)]
        parts = []
        for k, one in enumerate(halves):
            first, second = one[: rows // 2], one[rows // 2 :]
            parts += [jnp.where(where_ref[1 + k] == side, second, first) for side in range(2)]
        return jnp.concatenate(parts, axis=0).astype(BF16)

    dms, small = sorted_rows(dms), sorted_rows(small)
    rows_in, groups, tall, wide_out = kept_first.shape
    taken = wide_out - 2 * LANES
    moves = []
    for group in range(groups):
        out = dot(dms, p_ref[:, group * taken : (group + 1) * taken]).astype(BF16)
        extra = small[:, group * 2 * LANES : (group + 1) * 2 * LANES]
        for k, ref in enumerate((given_first, kept_first, given_last, kept_last)):
            for row in range(rows_in):
                at = ((2, 0, 3, 1)[k] * rows_in + row) * tall
                sum_ref[k, row, group, :, :taken] = out[at : at + tall]
                sum_ref[k, row, group, :, taken:] = extra[at : at + tall]
                moves.append(
                    pltpu.make_async_copy(
                        sum_ref.at[k, row, group], ref.at[row, group], sum_sems.at[k, row, group]
                    )
                )
                moves[-1].start()
    for move in moves:
        move.wait()
    leave.wait()


def edge_kernel(
    batch,
    order_ref,
    edge_ref,
    g_far,
    level_ref,
    dm_ref,
    base_ref,
    w_in_ref,
    b_in_ref,
    w_far,
    bias_ref,
    before_ref,
    feat_before,
    grad_ref,
    feat_ref,
    win_ref,
    tail_ref,
    dg_ref,
    w_ref,
    g_ref,
    sems,
):
    blocks = edge_ref.shape[0]
    batches = order_ref.shape[0]
    hidden_units = w_in_ref.shape[1]
    chunks = (hidden_units + tail_ref.shape[0]) // GROUP
    own, width = grad_ref.shape
    half = own // 2
    fetches = []
    for number in range(chunks):
        some = pl.ds(number * GROUP, min(GROUP, hidden_units - number * GROUP))
        rows = pl.ds(number * GROUP * half, GROUP * half)
        fetches += [
            pltpu.make_async_copy(w_far.at[some], w_ref.at[some], sems.at[number, 0]),
            pltpu.make_async_copy(
                g_far.at[batch, rows], g_ref.at[rows], sems.at[number, 1]
            ),
        ]
    for fetch in fetches:
        fetch.start()
    mine = slice(batch * own, (batch + 1) * own)
    bias_blocks(bias_ref, tail_ref)

    pulls = [dm_ref[mine, step * width : (step + 1) * width] for step in range(2)]
    levels = [doubled(level_ref[mine, step * width : (step + 1) * width]) for step in range(2)]
    levels = jnp.concatenate(levels, axis=1)
    total = jnp.zeros((2 * own, 2 * width), F32)
    both = jnp.concatenate(pulls, axis=0)
    for number in range(chunks):
        fetches[2 * number].wait()
        fetches[2 * number + 1].wait()
        pulled = dot(both, weights_of(w_ref, tail_ref, number)).astype(BF16)
        talls = [pulled_rows(pulled[k * own : (k + 1) * own], half) for k in range(2)]
        at = slice(number * GROUP * half, (number + 1) * GROUP * half)
        total = total + dot(turned(g_ref[at, :]), talls[0])
        d_pair = dot_nt(jnp.concatenate(talls, axis=1), levels)
        for unit in range(0, GROUP, 2):
            row = (number * GROUP + unit) * 8
            for part in range(half // 8):
                pair = [
                    d_pair[(unit + k) * half + part * 8 : (unit + k) * half + part * 8 + 8]
                    for k in range(2)
                ]
                dg_ref[row : row + 16, part * LANES : (part + 1) * LANES] = jnp.concatenate(
                    pair, axis=0
                ).astype(BF16)
    grad = base_ref[mine] + total[:own, :width] + total[own:, width:]
    grad_ref[...] = grad.astype(BF16)

    w_in, b_in = first_layer(w_in_ref, b_in_ref)
    fold = (col_ids((hidden_units, 8 * hidden_units)) >> 3) == row_ids(
        (hidden_units, 8 * hidden_units)
    )
    fold = fold.astype(F32).astype(BF16)
    feat_ref[...] = jnp.zeros_like(feat_ref)
    if batch > 0:
        feat_ref[:, : batch * 16] = feat_before[...]

    def one_piece(piece, sums):
        feats, held, pairs, low = edge_piece(batches, order_ref, edge_ref, piece, batch)
        pre = dot(w_in, feats) + b_in
        sig = jax.nn.sigmoid(pre)
        spread = dot(dg_ref[: 8 * hidden_units], pairs)
        spread = spread.reshape(hidden_units, 8, pre.shape[1])
        spread = jnp.where(low[None], spread, 0.0).reshape(8 * hidden_units, pre.shape[1])
        d_hidden = dot(fold, spread.astype(BF16))
        d_pre = (d_hidden * sig * (1.0 + pre * (1.0 - sig))).astype(BF16)
        out = dot(w_in_ref[...], d_pre).astype(BF16)
        for k in range(PIECE):
            at = order_ref[batch, PIECE * piece + k]
            feat_ref[at, batch * 16 :] = out[:, k * LANES : (k + 1) * LANES]
        ones = jnp.where(row_ids((16, pre.shape[1])) == 0, held, 0.0).astype(BF16)
        return sums + dot_nt(jnp.concatenate([feats, ones], axis=0), d_pre)

    win_ref[...] = lax.fori_loop(
        0, (order_ref[batch, blocks] + PIECE - 1) // PIECE, one_piece, before_ref[...]
    )


def add_kernel(first_ref, second_ref, out_ref):
    out_ref[...] = (first_ref[...].astype(F32) + second_ref[...].astype(F32)).astype(BF16)


def copy_kernel(in_ref, out_ref):
    out_ref[...] = in_ref[...]


def rows_kernel(first_ref, second_ref, out_ref, rows_ref):
    tall, wide = first_ref.shape
    main = wide // LANES - 2
    total = first_ref[...].astype(F32) + second_ref[...].astype(F32)
    for block in range(main):
        rows_ref[pl.ds(block, tall, stride=main), :] = total[:, block * LANES : (block + 1) * LANES]
    for k in range(2):
        start = tall * (main + k)
        rows_ref[start : start + tall, :] = total[:, (main + k) * LANES : (main + k + 1) * LANES]
    out_ref[0] = rows_ref[...].astype(BF16)


def rows_of(first, second):
    tall, wide = first.shape
    shape = (tall * (wide // LANES), LANES)
    return full_call(
        rows_kernel,
        jax.ShapeDtypeStruct((1,) + shape, BF16),
        (pltpu.VMEM(shape, F32),),
        cost_estimate=cost(1),
    )(first, second)


def place_kernel(tall, count, carried, *refs):
    at_ref, pieces = refs[0], refs[1 : 1 + count]
    outs = refs[1 + count + carried : 6 + count + carried]
    big_ref, little_ref, sems = refs[6 + count + carried :]
    d_w, d_bias, d_x, d_h, d_rest = outs
    waits = []
    slot = 0
    for k, piece in enumerate(pieces):
        chunks, rows_in, lanes = piece.shape
        main = rows_in // tall - 2
        for chunk in range(chunks):
            code = at_ref[k] ^ (2 * chunk)
            line, part = code >> 2, code & 3
            at = pl.ds(pl.multiple_of(line * tall, 8), tall)
            rows = piece[chunk].astype(F32)
            for row in range(tall):
                big_ref[slot, :, row * lanes : (row + 1) * lanes] = rows[row * main : (row + 1) * main]
            copy = pltpu.make_async_copy(
                big_ref.at[slot],
                d_w.at[
                    pl.ds(pl.multiple_of(part * main, 8), main),
                    pl.ds(pl.multiple_of(line * (tall * lanes), LANES), tall * lanes),
                ],
                sems.at[slot, 0],
            )
            copy.start()
            waits.append(copy)

            for side in range(2):
                start = tall * (main + side)
                little_ref[slot, side] = rows[start : start + tall]

                def move(target, lane):
                    lane = jnp.maximum(lane, 0) * lanes
                    to = pl.ds(pl.multiple_of(jnp.minimum(lane, target.shape[1] - lanes), LANES), lanes)
                    return pltpu.make_async_copy(
                        little_ref.at[slot, side], target.at[at, to], sems.at[slot, 1 + side]
                    )

                block = 2 * part + side
                to_x, to_h = move(d_x, block - 1), move(d_h, block - 4)
                alone = move((d_bias, d_rest)[side], 0)
                lone = block == 7 * side
                pl.when(lone)(alone.start)
                pl.when((block > 0) & (block < 4))(to_x.start)
                pl.when((block > 3) & (block < 7))(to_h.start)
                waits.append(alone)
            slot += 1
    for copy in waits:
        copy.wait()


def cost(micros):
    return pl.CostEstimate(
        flops=int(micros * 1e9), bytes_accessed=int(micros * 3e6), transcendentals=0
    )


def place_pieces(tall, at, pieces, shapes, before=()):
    count = len(pieces)
    chunks, rows_in, lanes = pieces[0].shape
    slots = count * chunks
    vmem = pl.BlockSpec(memory_space=pltpu.VMEM)
    hbm = pl.BlockSpec(memory_space=pl.ANY)
    return pl.pallas_call(
        functools.partial(place_kernel, tall, count, len(before)),
        out_shape=shapes,
        in_specs=[pl.BlockSpec(memory_space=pltpu.SMEM)] + [vmem] * count + [hbm] * len(before),
        out_specs=[hbm] * len(shapes),
        scratch_shapes=(
            pltpu.VMEM((slots, rows_in // tall - 2, tall * lanes), F32),
            pltpu.VMEM((slots, 2, tall, lanes), F32),
            pltpu.SemaphoreType.DMA((slots, 3)),
        ),
        input_output_aliases={1 + count + k: k for k in range(len(before))},
        cost_estimate=cost(slots / 4),
        compiler_params=pltpu.CompilerParams(vmem_limit_bytes=16 * MIB),
    )(at, *pieces, *before)


def body(
    states,
    edge_feats,
    source_index,
    target_index,
    w_edge_in,
    b_edge_in,
    w_edge_out,
    b_edge_out,
    w_input,
    w_hidden,
    b_input,
    b_hidden,
    cotangent,
):
    batches, own, width = states.shape
    edges = source_index.shape[1]
    owners = lax.axis_size("edge")
    cap = max(2, 2 * edges // owners)
    feat_count, units = w_edge_in.shape

    sent = full_call(
        functools.partial(route_kernel, own),
        jax.ShapeDtypeStruct((owners, batches * feat_count + 16, cap), BF16),
        limit=60,
    )(source_index, target_index, edge_feats)
    edge_data = lax.all_to_all(sent, "edge", 0, 0, tiled=True)
    merge = max(1, LANES // cap)
    if merge > 1:
        edge_data = edge_data.reshape(owners // merge, merge, -1, cap).transpose(0, 2, 1, 3)
        edge_data = edge_data.reshape(owners // merge, -1, merge * cap)

    w_mats = w_edge_out.reshape(units, width, width)
    padded = (units + 2 + GROUP - 1) // GROUP * GROUP

    tall = width // 8
    pairs = own // 2
    blocks = edge_data.shape[0]
    core = lax.axis_index("graph")
    spot = lax.axis_index("edge")
    orders = ((0, 1, 2, 3), (2, 0, 1, 3))

    def bit(side, step):
        first, second = [(spot >> orders[k][step]) & 1 for k in range(2)]
        return jnp.where(side == 0, first, second)

    where = jnp.stack([core, bit(core, 0), bit(1 - core, 0)])
    smem = pl.BlockSpec(memory_space=pltpu.SMEM)
    vmem = pl.BlockSpec(memory_space=pltpu.VMEM)
    far = pl.BlockSpec(memory_space=pltpu.HBM)
    bias = b_edge_out.reshape(width, width)
    quarter = jax.ShapeDtypeStruct((2, 4, tall, (units // 4 + 2) * width), BF16)
    new_states, *sums, g_pairs, levels, d_mails, base, order, first = full_call(
        main_kernel,
        (
            jax.ShapeDtypeStruct((batches * own, width), BF16),
            *[quarter] * 4,
            jax.ShapeDtypeStruct((batches, padded * pairs, LANES), BF16),
            jax.ShapeDtypeStruct((batches * own, 2 * width), BF16),
            jax.ShapeDtypeStruct((batches * own, 2 * width), BF16),
            jax.ShapeDtypeStruct((batches * own, width), F32),
            jax.ShapeDtypeStruct((batches, blocks + 1), jnp.int32),
            jax.ShapeDtypeStruct((32, width), F32),
        ),
        (
            pltpu.VMEM((units, PIECE * LANES), F32),
            pltpu.VMEM((padded * 8, 512), F32),
            pltpu.VMEM((batches, padded * pairs, LANES), BF16),
            pltpu.VMEM((2 * batches * own, padded * width), BF16),
            pltpu.VMEM((units, width, width), BF16),
            pltpu.VMEM((padded - units, width, width), BF16),
            pltpu.VMEM((4,) + quarter.shape, BF16),
            pltpu.SemaphoreType.DMA((4,) + quarter.shape[:2]),
            pltpu.SemaphoreType.DMA((2,)),
        ),
        limit=60,
        in_specs=[smem] + [vmem] * 5 + [far] + [vmem] * 5,
        out_specs=[vmem] + [far] * 5 + [vmem] * 3 + [smem, vmem],
    )(
        where,
        edge_data,
        states.reshape(batches * own, width),
        cotangent.reshape(batches * own, width),
        w_edge_in,
        b_edge_in,
        w_mats,
        bias,
        w_input,
        w_hidden,
        b_input,
        b_hidden,
    )

    cores = lax.axis_size("graph")

    def to_core(value):
        return lax.ppermute(value, "graph", [(0, 1), (1, 0)])

    def swap(value, masks):
        moves = []
        for side in range(cores):
            first = side * owners
            moves += [(first + k, first + (k ^ masks[side])) for k in range(owners)]
        return lax.ppermute(value, ("graph", "edge"), moves)

    def swap_step(value, step):
        return swap(value, [1 << orders[side][step] for side in range(cores)])

    def pick(value, number):
        return lax.dynamic_index_in_dim(value, number, 0, False)

    def added(terms):
        return sum(one.astype(F32) for one in terms)

    def after(value, *others):
        return lax.optimization_barrier((value, *others))[0]

    def edge_grads(batch, pairs_in, first, feats):
        return full_call(
            functools.partial(edge_kernel, batch),
            (
                jax.ShapeDtypeStruct((own, width), BF16),
                jax.ShapeDtypeStruct((blocks, (batch + 1) * feat_count, LANES), BF16),
                jax.ShapeDtypeStruct((32, units), F32),
            ),
            (
                pltpu.VMEM((padded - units, width, width), BF16),
                pltpu.VMEM((padded * 8, 512), BF16),
                pltpu.VMEM((units, width, width), BF16),
                pltpu.VMEM((padded * pairs, LANES), BF16),
                pltpu.SemaphoreType.DMA((padded // GROUP, 2)),
            ),
            limit=60,
            in_specs=[smem, vmem, far] + [vmem] * 5 + [far] + [vmem] * 3,
            cost_estimate=cost(9),
        )(
            order, edge_data, pairs_in, levels, d_mails, base,
            w_edge_in, b_edge_in, w_mats, bias, first, feats,
        )

    def both(big, small, step):
        return lax.optimization_barrier((swap_step(big, step), swap_step(small, step)))

    kept_first, kept_last, given_first, given_last = sums
    got_first, got_last = to_core(given_first), to_core(given_last)
    kept_first = full_call(
        copy_kernel, jax.ShapeDtypeStruct(kept_first.shape, BF16), cost_estimate=cost(1)
    )(kept_first)
    give = full_call(
        add_kernel, jax.ShapeDtypeStruct(kept_first.shape, BF16), cost_estimate=cost(1)
    )(kept_first, got_first)
    terms = [kept_last, got_last]
    state_grad, d_feats = [], b_edge_in
    for step in range(3):
        if step > 0:
            number = bit(core, step)
            give = added([pick(one, 1 - number) for one in terms]).astype(BF16)
            terms = [pick(one, number) for one in terms]
        if step == 2:
            got, small = both(give, first, step)
            first = first + small
        else:
            got = swap_step(give, step)
        if step < batches:
            grad, d_feats, first = edge_grads(step, after(g_pairs, give), first, d_feats)
            got = after(got, first)
            state_grad.append(grad)
        terms.append(got)
        if step == 0:
            terms = [one.reshape((2, 2, 2) + one.shape[2:]) for one in terms]
    totals = [added([pick(one, 0) for one in terms]).astype(BF16)]
    terms[-1] = after(terms[-1], totals[0])
    totals.append(added([pick(one, 1) for one in terms]).astype(BF16))
    for extra in range(3, owners.bit_length() - 1):
        masks = [1 << extra] * cores
        small = swap(first, masks)
        gots = [swap(one, masks) for one in totals]
        if extra < owners.bit_length() - 2:
            first = first + small
            totals = [added([one, got]).astype(BF16) for one, got in zip(totals, gots)]

    helds, nears, acrosses = [], [], []
    for part in range(2):
        held = rows_of(totals[part], gots[part])
        if part == 0:
            got = swap_step(held, 2)
            gots[1] = after(gots[1], got)
        else:
            got, small = lax.optimization_barrier((swap_step(held, 2), small))
            first = first + small
        held = jnp.concatenate([held, got], axis=0)
        acrosses.append(swap_step(held, 0))
        if part == 0:
            near = swap_step(held, 1)
        else:
            near, small = both(held, first, 1)
            first = first + small
        helds.append(held)
        nears.append(near)
    back = d_feats
    if merge > 1:
        back = back.reshape(blocks, -1, merge, cap).transpose(0, 2, 1, 3)
    back = after(back.reshape(owners, -1, cap), helds[1])
    back = lax.all_to_all(back, "edge", 0, 0, tiled=True)
    nears = [after(nears[0], helds[1]), after(nears[1], back)]
    more = swap_step(first, 0)
    lasts = [swap_step(near, 0) for near in nears]

    feat_grad = full_call(
        functools.partial(unroute_kernel, own),
        jax.ShapeDtypeStruct((batches, feat_count, edges), BF16),
        cost_estimate=cost(3),
    )(source_index, back.reshape(owners, batches, feat_count, cap))

    shapes = tuple(
        jax.ShapeDtypeStruct(shape, F32)
        for shape in (
            (units, width * width),
            (width, width),
            (width, 3 * width),
            (width, 3 * width),
            (width, width),
        )
    )
    outs = ()
    waves = (
        ((helds[0], 0), (helds[1], 1)),
        ((nears[0], 4), (acrosses[0], 8)),
        ((nears[1], 5), (acrosses[1], 9), (lasts[0], 12)),
        ((lasts[1], 13),),
    )
    for number, wave in enumerate(waves):
        at, pieces = [], []
        extra = (more, feat_grad) if number == 3 else ()
        ready = lax.optimization_barrier((outs, tuple(piece for piece, _ in wave), extra))
        outs, wave, extra = ready[0], zip(ready[1], [flips for _, flips in wave]), ready[2]
        for piece, flips in wave:
            for side, one in ((core, piece), (1 - core, to_core(piece))):
                code = side
                for step in range(3):
                    code = code * 2 + bit(side, step)
                at.append((code * 2) ^ flips)
                pieces.append(one)
        outs = place_pieces(tall, jnp.stack(at), pieces, shapes, outs)
    more, feat_grad = extra
    first = first + more
    first_sum = first + to_core(first)
    d_w, d_bias, d_x, d_h, _ = outs
    return (
        new_states.reshape(batches, own, width),
        jnp.stack(state_grad),
        feat_grad,
        first_sum[:feat_count],
        first_sum[feat_count],
        d_w,
        d_bias.reshape(-1),
        d_x,
        d_h,
        first_sum[24:27].reshape(-1),
        first_sum[27:30].reshape(-1),
    )


def solution(mesh):
    spread = ("graph", "edge")
    rows = P(None, spread, None)
    edges = P(None, spread)
    feats = P(None, None, spread)
    in_specs = (rows, feats, edges, edges) + (P(),) * 8 + (rows,)
    out_specs = (rows, rows, feats) + (P(),) * 8
    return jax.shard_map(
        body,
        mesh=mesh,
        in_specs=in_specs,
        out_specs=out_specs,
        check_vma=False,
    )
```

```python
import functools

import jax
import jax.numpy as jnp
from jax import lax
from jax.experimental import pallas as pl
from jax.experimental.pallas import tpu as pltpu
from jax.sharding import PartitionSpec as P

F32 = jnp.float32
BF16 = jnp.bfloat16
LANES = 128
PIECE = 4
GROUP = 12
MIB = 1024 * 1024


def dot(first, second, dims=((1,), (0,))):
    return lax.dot_general(first, second, (dims, ((), ())), preferred_element_type=F32)


def dot_nt(first, second):
    return dot(first, second, ((1,), (1,)))


def row_ids(shape):
    return lax.broadcasted_iota(jnp.int32, shape, 0)


def col_ids(shape):
    return lax.broadcasted_iota(jnp.int32, shape, 1)


def full_call(kernel, out_shape, scratch=(), limit=16, **more):
    return pl.pallas_call(
        kernel,
        out_shape=out_shape,
        scratch_shapes=scratch,
        compiler_params=pltpu.CompilerParams(vmem_limit_bytes=limit * MIB),
        **more,
    )


def ranks_of(owner, owners):
    hits = (row_ids((owners, owner.shape[1])) == owner).astype(F32)
    before = (row_ids((LANES, LANES)) < col_ids((LANES, LANES))).astype(BF16)
    seen = jnp.zeros((owners, 1), F32)
    ranks = []
    for start in range(0, owner.shape[1], LANES):
        part = hits[:, start : start + LANES]
        place = dot(part.astype(BF16), before) + seen
        ranks.append(jnp.sum(part * place, axis=0, keepdims=True))
        seen = seen + jnp.sum(part, axis=1, keepdims=True)
    return hits, jnp.concatenate(ranks, axis=1)


def route_kernel(own_rows, src_ref, dst_ref, feat_ref, out_ref):
    owners, rows, cap = out_ref.shape
    batches, feats, edges = feat_ref.shape
    shift = own_rows.bit_length() - 1
    marks = [jnp.zeros((16, cap), F32)] * owners
    for batch in range(batches):
        source, target = src_ref[batch : batch + 1], dst_ref[batch : batch + 1]
        owner = source >> shift
        hits, rank = ranks_of(owner, owners)
        spots = (row_ids((cap, edges)) == rank.astype(jnp.int32)).astype(BF16)
        line = row_ids((16, edges)) - 3 * batch
        first = owner << shift
        extra = jnp.where(line == 0, source - first, jnp.where(line == 1, target - first, 1))
        extra = jnp.where((line >= 0) & (line < 3), extra, 0).astype(F32)
        load = jnp.concatenate([feat_ref[batch].astype(F32), extra], axis=0)
        masked = [(load * hits[part : part + 1]).astype(BF16) for part in range(owners)]
        out = dot_nt(jnp.concatenate(masked, axis=0), spots)
        for part in range(owners):
            tile = out[part * (feats + 16) : (part + 1) * (feats + 16)]
            out_ref[part, batch * feats : (batch + 1) * feats] = tile[:feats].astype(BF16)
            marks[part] = marks[part] + tile[feats:]
    for part in range(owners):
        out_ref[part, batches * feats :] = marks[part].astype(BF16)


def unroute_kernel(own_rows, src_ref, back_ref, out_ref):
    owners, batches, rows, cap = back_ref.shape
    edges = src_ref.shape[1]
    shift = own_rows.bit_length() - 1
    for batch in range(batches):
        hits, rank = ranks_of(src_ref[batch : batch + 1] >> shift, owners)
        spots = (row_ids((cap, edges)) == rank.astype(jnp.int32)).astype(BF16)
        parts = [back_ref[part, batch] for part in range(owners)]
        spread = dot(jnp.concatenate(parts, axis=0), spots)
        total = jnp.zeros((rows, edges), F32)
        for part in range(owners):
            total = total + spread[part * rows : (part + 1) * rows] * hits[part : part + 1]
        out_ref[batch] = total.astype(BF16)


def edge_piece(batches, order_ref, edge_ref, piece, batch):
    some = [edge_ref[order_ref[batch, PIECE * piece + k]] for k in range(PIECE)]
    block = jnp.concatenate(some, axis=1)
    feats, marks = block[batch * 16 : (batch + 1) * 16], block[batches * 16 :].astype(F32)
    source = marks[3 * batch : 3 * batch + 1].astype(jnp.int32)
    target = marks[3 * batch + 1 : 3 * batch + 2].astype(jnp.int32)
    held = marks[3 * batch + 2 : 3 * batch + 3]
    code = ((target >> 3) & 3) * 128 + (target >> 5) * 64 + source
    code = jnp.where(held > 0.5, code, -1)
    pairs = (row_ids((512, block.shape[1])) == code).astype(BF16)
    low = row_ids((8, block.shape[1])) == (target & 7)
    return feats, held, pairs, low


def order_blocks(batches, edge_ref, order_ref):
    blocks = edge_ref.shape[0]
    for batch in range(batches):
        front, back = jnp.int32(0), jnp.int32(blocks - 1)
        row = 3 * batch + 2
        for block in range(blocks):
            marks = edge_ref[block, batches * 16 :].astype(F32)
            held = jnp.max(marks[row : row + 1]) > 0.5
            order_ref[batch, jnp.where(held, front, back)] = jnp.int32(block)
            step = held.astype(jnp.int32)
            front, back = front + step, back - (1 - step)
        order_ref[batch, blocks] = front


def first_layer(w_in_ref, b_in_ref):
    bias = jnp.broadcast_to(b_in_ref[...].reshape(1, -1), (8, b_in_ref.shape[0]))
    return w_in_ref[...].astype(F32).T.astype(BF16), bias.T[:, :1]


def gates_of(mail_low, level, w_x, w_h, b_x, b_h):
    width = level.shape[1]
    from_mail = dot(mail_low, w_x[...]) + b_x[...].reshape(1, -1)
    from_state = dot(level, w_h[...]) + b_h[...].reshape(1, -1)
    reset = jax.nn.sigmoid(from_mail[:, :width] + from_state[:, :width])
    update = jax.nn.sigmoid(from_mail[:, width : 2 * width] + from_state[:, width : 2 * width])
    state_part = from_state[:, 2 * width :]
    candidate = jnp.tanh(from_mail[:, 2 * width :] + reset * state_part)
    return reset, update, candidate, state_part


def doubled(level):
    blank = jnp.zeros_like(level)
    return jnp.concatenate(
        [jnp.concatenate([level, blank], axis=1), jnp.concatenate([blank, level], axis=1)], axis=0
    )


def bias_blocks(bias_ref, tail_ref):
    tail_ref[...] = jnp.zeros_like(tail_ref)
    high = bias_ref[...].astype(BF16)
    tail_ref[0] = high
    tail_ref[1] = (bias_ref[...] - high.astype(F32)).astype(BF16)


def turned(tile):
    size = tile.shape[1]
    eye = (row_ids((size, size)) == col_ids((size, size))).astype(F32).astype(BF16)
    return dot_nt(eye, tile).astype(BF16)


def weights_of(w_ref, tail_ref, number):
    units = w_ref.shape[0]
    blocks = []
    for unit in range(number * GROUP, (number + 1) * GROUP):
        blocks.append(w_ref[unit] if unit < units else tail_ref[unit - units])
    return jnp.concatenate(blocks, axis=1)


def pulled_rows(pulled, half):
    rows = []
    for start in range(0, pulled.shape[1], LANES):
        tile = pulled[:, start : start + LANES]
        rows.append(jnp.concatenate([tile[:half], tile[half:]], axis=1))
    return jnp.concatenate(rows, axis=0)


def main_kernel(
    where_ref,
    edge_ref,
    state_ref,
    cot_ref,
    w_in_ref,
    b_in_ref,
    w_far,
    bias_ref,
    w_x,
    w_h,
    b_x,
    b_h,
    new_ref,
    kept_first,
    kept_last,
    given_first,
    given_last,
    g_far,
    level_ref,
    dm_ref,
    base_ref,
    order_ref,
    rows_ref,
    hid_ref,
    acc_ref,
    g_ref,
    p_ref,
    w_ref,
    tail_ref,
    sum_ref,
    sum_sems,
    sems,
):
    fetch = pltpu.make_async_copy(w_far, w_ref, sems.at[0])
    fetch.start()
    blocks = edge_ref.shape[0]
    batches = g_ref.shape[0]
    hidden_units = hid_ref.shape[0]
    units = acc_ref.shape[0] // 8
    own = state_ref.shape[0] // batches
    half = own // 2
    span = GROUP * half
    wide = GROUP * LANES
    chunks = units // GROUP
    order_blocks(batches, edge_ref, order_ref)
    bias_blocks(bias_ref, tail_ref)
    w_in, b_in = first_layer(w_in_ref, b_in_ref)

    for batch in range(batches):
        acc_ref[...] = jnp.zeros_like(acc_ref)

        def add_piece(piece, carry):
            feats, held, pairs, low = edge_piece(batches, order_ref, edge_ref, piece, batch)
            pre = dot(w_in, feats) + b_in
            hid_ref[...] = (pre * jax.nn.sigmoid(pre)).astype(BF16).astype(F32)
            ones = jnp.where(low, 1.0, 0.0)
            parts = []
            for unit in range(0, hidden_units, 2):
                two = [jnp.where(low, hid_ref[unit + k : unit + k + 1], 0.0) for k in range(2)]
                parts.append(jnp.concatenate(two, axis=0).astype(BF16))
            parts.append(jnp.concatenate([ones, ones], axis=0).astype(BF16))
            parts.append(jnp.zeros((8 * (units - hidden_units - 2), pre.shape[1]), BF16))
            acc_ref[...] += dot_nt(jnp.concatenate(parts, axis=0), pairs)
            return carry

        lax.fori_loop(0, (order_ref[batch, blocks] + PIECE - 1) // PIECE, add_piece, 0)

        def place(step, carry):
            for four in range(3):
                rows = []
                for k in range(4):
                    for part in range(4):
                        start = pl.multiple_of(step * 96 + four * 32 + k * 8, 8)
                        rows.append(acc_ref[pl.ds(start, 8), part * LANES : (part + 1) * LANES])
                at = pl.ds(pl.multiple_of((step * 3 + four) * LANES, LANES), LANES)
                g_ref[batch, at, :] = jnp.concatenate(rows, axis=0).astype(BF16)
            return carry

        lax.fori_loop(0, units // 12, place, 0)

    def forward(step, level):
        two = [doubled(level[batch * own : (batch + 1) * own]) for batch in range(batches)]
        mail = jnp.zeros((batches * own, LANES), F32)
        base = step * batches * own
        for number in range(chunks):
            for batch in range(batches):
                out = dot(g_ref[batch, number * span : (number + 1) * span, :], two[batch])
                out = out.astype(BF16)
                for unit in range(GROUP):
                    lane = number * wide + unit * LANES
                    for part in range(2):
                        row = base + batch * own + part * half
                        p_ref[row : row + half, lane : lane + LANES] = out[
                            unit * half : (unit + 1) * half, part * LANES : (part + 1) * LANES
                        ]
            rows = p_ref[base : base + batches * own, number * wide : (number + 1) * wide]
            mail = mail + dot_nt(rows, weights_of(w_ref, tail_ref, number))
        return mail

    def backward(d_mail):
        sums = [jnp.zeros((LANES, 2 * LANES), F32) for batch in range(batches)]
        for number in range(chunks):
            pulled = dot(d_mail, weights_of(w_ref, tail_ref, number)).astype(BF16)
            at = slice(number * span, (number + 1) * span)
            for batch in range(batches):
                tall = pulled_rows(pulled[batch * own : (batch + 1) * own], half)
                sums[batch] = sums[batch] + dot(turned(g_ref[batch, at, :]), tall)
        return jnp.concatenate([one[:own, :LANES] + one[own:, LANES:] for one in sums], axis=0)

    weights = (w_x, w_h, b_x, b_h)
    level_zero = state_ref[...]
    state_zero = level_zero.astype(F32)
    leave = pltpu.make_async_copy(g_ref, g_far, sems.at[1])
    leave.start()
    fetch.wait()
    mail_zero = forward(0, level_zero).astype(BF16)
    gates_zero = gates_of(mail_zero, level_zero, *weights)
    state_one = (1.0 - gates_zero[1]) * gates_zero[2] + gates_zero[1] * state_zero
    level_one = state_one.astype(BF16)
    mail_one = forward(1, level_one).astype(BF16)
    gates_one = gates_of(mail_one, level_one, *weights)
    new_ref[...] = ((1.0 - gates_one[1]) * gates_one[2] + gates_one[1] * state_one).astype(BF16)

    def gru_back(d_next, gates, current):
        reset, update, candidate, state_part = gates
        d_cand = d_next * (1.0 - update) * (1.0 - candidate * candidate)
        d_reset = d_cand * state_part * reset * (1.0 - reset)
        d_update = d_next * (current - candidate) * update * (1.0 - update)
        dg_mail = jnp.concatenate([d_reset, d_update, d_cand], axis=1).astype(BF16)
        dg_state = jnp.concatenate([d_reset, d_update, d_cand * reset], axis=1).astype(BF16)
        d_mail = dot_nt(dg_mail, w_x[...]).astype(BF16)
        d_current = d_next * update + dot_nt(dg_state, w_h[...])
        return dg_mail, dg_state, d_mail, d_current

    dgm_one, dgs_one, dm_one, d_state = gru_back(cot_ref[...].astype(F32), gates_one, state_one)
    d_state = d_state + backward(dm_one)
    dgm_zero, dgs_zero, dm_zero, d_state = gru_back(d_state, gates_zero, state_zero)
    base_ref[...] = d_state
    level_ref[...] = jnp.concatenate([level_zero, level_one], axis=1)
    dm_ref[...] = jnp.concatenate([dm_zero, dm_one], axis=1)

    def both(first, second):
        return jnp.concatenate([first.astype(F32), second.astype(F32)], axis=0)

    dms = both(dm_zero, dm_one).T
    mails, levels = both(mail_zero, mail_one), both(level_zero, level_one)
    dgm, dgs = both(dgm_zero, dgm_one), both(dgs_zero, dgs_one)
    width = dgm.shape[1]
    rows_ref[...] = jnp.zeros_like(rows_ref)
    for k, one in enumerate((dgm, dgs)):
        total = jnp.sum(one, axis=0, keepdims=True)
        for part in range(3):
            row = 24 + 3 * k + part
            rows_ref[row : row + 1, :] = total[:, part * LANES : (part + 1) * LANES]
    small = jnp.concatenate(
        [
            dot(dms.astype(BF16), p_ref[:, hidden_units * LANES : (hidden_units + 1) * LANES]),
            dot(mails.T.astype(BF16), dgm.astype(BF16)),
            dot(levels.T.astype(BF16), dgs.astype(BF16)),
            jnp.zeros((2 * own, LANES), F32),
        ],
        axis=1,
    )

    def sorted_rows(value):
        rows = value.shape[0] // 2
        upper, lower = value[:rows], value[rows:]
        halves = [jnp.where(where_ref[0] == k, upper, lower) for k in range(2)]
        parts = []
        for k, one in enumerate(halves):
            first, second = one[: rows // 2], one[rows // 2 :]
            parts += [jnp.where(where_ref[1 + k] == side, second, first) for side in range(2)]
        return jnp.concatenate(parts, axis=0).astype(BF16)

    dms, small = sorted_rows(dms), sorted_rows(small)
    rows_in, groups, tall, wide_out = kept_first.shape
    taken = wide_out - 2 * LANES
    moves = []
    for group in range(groups):
        out = dot(dms, p_ref[:, group * taken : (group + 1) * taken]).astype(BF16)
        extra = small[:, group * 2 * LANES : (group + 1) * 2 * LANES]
        for k, ref in enumerate((given_first, kept_first, given_last, kept_last)):
            for row in range(rows_in):
                at = ((2, 0, 3, 1)[k] * rows_in + row) * tall
                sum_ref[k, row, group, :, :taken] = out[at : at + tall]
                sum_ref[k, row, group, :, taken:] = extra[at : at + tall]
                moves.append(
                    pltpu.make_async_copy(
                        sum_ref.at[k, row, group], ref.at[row, group], sum_sems.at[k, row, group]
                    )
                )
                moves[-1].start()
    for move in moves:
        move.wait()
    leave.wait()


def edge_kernel(
    batch,
    order_ref,
    edge_ref,
    g_far,
    level_ref,
    dm_ref,
    base_ref,
    w_in_ref,
    b_in_ref,
    w_far,
    bias_ref,
    before_ref,
    feat_before,
    grad_ref,
    feat_ref,
    win_ref,
    tail_ref,
    dg_ref,
    w_ref,
    g_ref,
    sems,
):
    blocks = edge_ref.shape[0]
    batches = order_ref.shape[0]
    hidden_units = w_in_ref.shape[1]
    chunks = (hidden_units + tail_ref.shape[0]) // GROUP
    own, width = grad_ref.shape
    half = own // 2
    fetches = []
    for number in range(chunks):
        some = pl.ds(number * GROUP, min(GROUP, hidden_units - number * GROUP))
        rows = pl.ds(number * GROUP * half, GROUP * half)
        fetches += [
            pltpu.make_async_copy(w_far.at[some], w_ref.at[some], sems.at[number, 0]),
            pltpu.make_async_copy(
                g_far.at[batch, rows], g_ref.at[rows], sems.at[number, 1]
            ),
        ]
    for fetch in fetches:
        fetch.start()
    mine = slice(batch * own, (batch + 1) * own)
    bias_blocks(bias_ref, tail_ref)

    pulls = [dm_ref[mine, step * width : (step + 1) * width] for step in range(2)]
    levels = [doubled(level_ref[mine, step * width : (step + 1) * width]) for step in range(2)]
    levels = jnp.concatenate(levels, axis=1)
    total = jnp.zeros((2 * own, 2 * width), F32)
    both = jnp.concatenate(pulls, axis=0)
    for number in range(chunks):
        fetches[2 * number].wait()
        fetches[2 * number + 1].wait()
        pulled = dot(both, weights_of(w_ref, tail_ref, number)).astype(BF16)
        talls = [pulled_rows(pulled[k * own : (k + 1) * own], half) for k in range(2)]
        at = slice(number * GROUP * half, (number + 1) * GROUP * half)
        total = total + dot(turned(g_ref[at, :]), talls[0])
        d_pair = dot_nt(jnp.concatenate(talls, axis=1), levels)
        for unit in range(0, GROUP, 2):
            row = (number * GROUP + unit) * 8
            for part in range(half // 8):
                pair = [
                    d_pair[(unit + k) * half + part * 8 : (unit + k) * half + part * 8 + 8]
                    for k in range(2)
                ]
                dg_ref[row : row + 16, part * LANES : (part + 1) * LANES] = jnp.concatenate(
                    pair, axis=0
                ).astype(BF16)
    grad = base_ref[mine] + total[:own, :width] + total[own:, width:]
    grad_ref[...] = grad.astype(BF16)

    w_in, b_in = first_layer(w_in_ref, b_in_ref)
    fold = (col_ids((hidden_units, 8 * hidden_units)) >> 3) == row_ids(
        (hidden_units, 8 * hidden_units)
    )
    fold = fold.astype(F32).astype(BF16)
    feat_ref[...] = jnp.zeros_like(feat_ref)
    if batch > 0:
        feat_ref[:, : batch * 16] = feat_before[...]

    def one_piece(piece, sums):
        feats, held, pairs, low = edge_piece(batches, order_ref, edge_ref, piece, batch)
        pre = dot(w_in, feats) + b_in
        sig = jax.nn.sigmoid(pre)
        spread = dot(dg_ref[: 8 * hidden_units], pairs)
        spread = spread.reshape(hidden_units, 8, pre.shape[1])
        spread = jnp.where(low[None], spread, 0.0).reshape(8 * hidden_units, pre.shape[1])
        d_hidden = dot(fold, spread.astype(BF16))
        d_pre = (d_hidden * sig * (1.0 + pre * (1.0 - sig))).astype(BF16)
        out = dot(w_in_ref[...], d_pre).astype(BF16)
        for k in range(PIECE):
            at = order_ref[batch, PIECE * piece + k]
            feat_ref[at, batch * 16 :] = out[:, k * LANES : (k + 1) * LANES]
        ones = jnp.where(row_ids((16, pre.shape[1])) == 0, held, 0.0).astype(BF16)
        return sums + dot_nt(jnp.concatenate([feats, ones], axis=0), d_pre)

    win_ref[...] = lax.fori_loop(
        0, (order_ref[batch, blocks] + PIECE - 1) // PIECE, one_piece, before_ref[...]
    )


def add_kernel(first_ref, second_ref, out_ref):
    out_ref[...] = (first_ref[...].astype(F32) + second_ref[...].astype(F32)).astype(BF16)


def copy_kernel(in_ref, out_ref):
    out_ref[...] = in_ref[...]


def rows_kernel(first_ref, second_ref, out_ref, rows_ref):
    parts, tall, wide = first_ref.shape
    main = wide // LANES - 2
    for part in range(parts):
        total = first_ref[part].astype(F32) + second_ref[part].astype(F32)
        for block in range(main):
            rows_ref[pl.ds(block, tall, stride=main), :] = total[
                :, block * LANES : (block + 1) * LANES
            ]
        for k in range(2):
            start = tall * (main + k)
            rows_ref[start : start + tall, :] = total[:, (main + k) * LANES : (main + k + 1) * LANES]
        out_ref[part] = rows_ref[...].astype(BF16)


def rows_of(first, second):
    parts, tall, wide = first.shape
    shape = (tall * (wide // LANES), LANES)
    return full_call(
        rows_kernel,
        jax.ShapeDtypeStruct((parts,) + shape, BF16),
        (pltpu.VMEM(shape, F32),),
        cost_estimate=cost(1),
    )(first, second)


def place_kernel(tall, count, carried, *refs):
    at_ref, pieces = refs[0], refs[1 : 1 + count]
    outs = refs[1 + count + carried : 6 + count + carried]
    big_ref, little_ref, sems = refs[6 + count + carried :]
    d_w, d_bias, d_x, d_h, d_rest = outs
    waits = []
    slot = 0
    for k, piece in enumerate(pieces):
        chunks, rows_in, lanes = piece.shape
        main = rows_in // tall - 2
        for chunk in range(chunks):
            code = at_ref[k] ^ chunk
            line, part = code >> 2, code & 3
            at = pl.ds(pl.multiple_of(line * tall, 8), tall)
            rows = piece[chunk].astype(F32)
            for row in range(tall):
                big_ref[slot, :, row * lanes : (row + 1) * lanes] = rows[row * main : (row + 1) * main]
            copy = pltpu.make_async_copy(
                big_ref.at[slot],
                d_w.at[
                    pl.ds(pl.multiple_of(part * main, 8), main),
                    pl.ds(pl.multiple_of(line * (tall * lanes), LANES), tall * lanes),
                ],
                sems.at[slot, 0],
            )
            copy.start()
            waits.append(copy)

            for side in range(2):
                start = tall * (main + side)
                little_ref[slot, side] = rows[start : start + tall]

                def move(target, lane):
                    lane = jnp.maximum(lane, 0) * lanes
                    to = pl.ds(pl.multiple_of(jnp.minimum(lane, target.shape[1] - lanes), LANES), lanes)
                    return pltpu.make_async_copy(
                        little_ref.at[slot, side], target.at[at, to], sems.at[slot, 1 + side]
                    )

                block = 2 * part + side
                to_x, to_h = move(d_x, block - 1), move(d_h, block - 4)
                alone = move((d_bias, d_rest)[side], 0)
                lone = block == 7 * side
                pl.when(lone)(alone.start)
                pl.when((block > 0) & (block < 4))(to_x.start)
                pl.when((block > 3) & (block < 7))(to_h.start)
                waits.append(alone)
            slot += 1
    for copy in waits:
        copy.wait()


def cost(micros):
    return pl.CostEstimate(
        flops=int(micros * 1e9), bytes_accessed=int(micros * 3e6), transcendentals=0
    )


def place_pieces(tall, at, pieces, shapes, before=()):
    count = len(pieces)
    chunks, rows_in, lanes = pieces[0].shape
    slots = count * chunks
    vmem = pl.BlockSpec(memory_space=pltpu.VMEM)
    hbm = pl.BlockSpec(memory_space=pl.ANY)
    return pl.pallas_call(
        functools.partial(place_kernel, tall, count, len(before)),
        out_shape=shapes,
        in_specs=[pl.BlockSpec(memory_space=pltpu.SMEM)] + [vmem] * count + [hbm] * len(before),
        out_specs=[hbm] * len(shapes),
        scratch_shapes=(
            pltpu.VMEM((slots, rows_in // tall - 2, tall * lanes), F32),
            pltpu.VMEM((slots, 2, tall, lanes), F32),
            pltpu.SemaphoreType.DMA((slots, 3)),
        ),
        input_output_aliases={1 + count + k: k for k in range(len(before))},
        cost_estimate=cost(0.1),
        compiler_params=pltpu.CompilerParams(vmem_limit_bytes=16 * MIB),
    )(at, *pieces, *before)


def body(
    states,
    edge_feats,
    source_index,
    target_index,
    w_edge_in,
    b_edge_in,
    w_edge_out,
    b_edge_out,
    w_input,
    w_hidden,
    b_input,
    b_hidden,
    cotangent,
):
    batches, own, width = states.shape
    edges = source_index.shape[1]
    owners = lax.axis_size("edge")
    cap = max(2, 2 * edges // owners)
    feat_count, units = w_edge_in.shape

    sent = full_call(
        functools.partial(route_kernel, own),
        jax.ShapeDtypeStruct((owners, batches * feat_count + 16, cap), BF16),
        limit=60,
    )(source_index, target_index, edge_feats)
    edge_data = lax.all_to_all(sent, "edge", 0, 0, tiled=True)
    merge = max(1, LANES // cap)
    if merge > 1:
        edge_data = edge_data.reshape(owners // merge, merge, -1, cap).transpose(0, 2, 1, 3)
        edge_data = edge_data.reshape(owners // merge, -1, merge * cap)

    w_mats = w_edge_out.reshape(units, width, width)
    padded = (units + 2 + GROUP - 1) // GROUP * GROUP

    tall = width // 8
    pairs = own // 2
    blocks = edge_data.shape[0]
    core = lax.axis_index("graph")
    spot = lax.axis_index("edge")
    orders = ((0, 1, 2, 3), (2, 0, 1, 3))

    def bit(side, step):
        first, second = [(spot >> orders[k][step]) & 1 for k in range(2)]
        return jnp.where(side == 0, first, second)

    where = jnp.stack([core, bit(core, 0), bit(1 - core, 0)])
    smem = pl.BlockSpec(memory_space=pltpu.SMEM)
    vmem = pl.BlockSpec(memory_space=pltpu.VMEM)
    far = pl.BlockSpec(memory_space=pltpu.HBM)
    bias = b_edge_out.reshape(width, width)
    quarter = jax.ShapeDtypeStruct((2, 4, tall, (units // 4 + 2) * width), BF16)
    new_states, *sums, g_pairs, levels, d_mails, base, order, first = full_call(
        main_kernel,
        (
            jax.ShapeDtypeStruct((batches * own, width), BF16),
            *[quarter] * 4,
            jax.ShapeDtypeStruct((batches, padded * pairs, LANES), BF16),
            jax.ShapeDtypeStruct((batches * own, 2 * width), BF16),
            jax.ShapeDtypeStruct((batches * own, 2 * width), BF16),
            jax.ShapeDtypeStruct((batches * own, width), F32),
            jax.ShapeDtypeStruct((batches, blocks + 1), jnp.int32),
            jax.ShapeDtypeStruct((32, width), F32),
        ),
        (
            pltpu.VMEM((units, PIECE * LANES), F32),
            pltpu.VMEM((padded * 8, 512), F32),
            pltpu.VMEM((batches, padded * pairs, LANES), BF16),
            pltpu.VMEM((2 * batches * own, padded * width), BF16),
            pltpu.VMEM((units, width, width), BF16),
            pltpu.VMEM((padded - units, width, width), BF16),
            pltpu.VMEM((4,) + quarter.shape, BF16),
            pltpu.SemaphoreType.DMA((4,) + quarter.shape[:2]),
            pltpu.SemaphoreType.DMA((2,)),
        ),
        limit=60,
        in_specs=[smem] + [vmem] * 5 + [far] + [vmem] * 5,
        out_specs=[vmem] + [far] * 5 + [vmem] * 3 + [smem, vmem],
    )(
        where,
        edge_data,
        states.reshape(batches * own, width),
        cotangent.reshape(batches * own, width),
        w_edge_in,
        b_edge_in,
        w_mats,
        bias,
        w_input,
        w_hidden,
        b_input,
        b_hidden,
    )

    cores = lax.axis_size("graph")

    def to_core(value):
        return lax.ppermute(value, "graph", [(0, 1), (1, 0)])

    def swap(value, masks):
        moves = []
        for side in range(cores):
            first = side * owners
            moves += [(first + k, first + (k ^ masks[side])) for k in range(owners)]
        return lax.ppermute(value, ("graph", "edge"), moves)

    def swap_step(value, step):
        return swap(value, [1 << orders[side][step] for side in range(cores)])

    def pick(value, number):
        return lax.dynamic_index_in_dim(value, number, 0, False)

    def added(terms):
        return sum(one.astype(F32) for one in terms)

    def after(value, *others):
        return lax.optimization_barrier((value, *others))[0]

    def edge_grads(batch, pairs_in, first, feats):
        return full_call(
            functools.partial(edge_kernel, batch),
            (
                jax.ShapeDtypeStruct((own, width), BF16),
                jax.ShapeDtypeStruct((blocks, (batch + 1) * feat_count, LANES), BF16),
                jax.ShapeDtypeStruct((32, units), F32),
            ),
            (
                pltpu.VMEM((padded - units, width, width), BF16),
                pltpu.VMEM((padded * 8, 512), BF16),
                pltpu.VMEM((units, width, width), BF16),
                pltpu.VMEM((padded * pairs, LANES), BF16),
                pltpu.SemaphoreType.DMA((padded // GROUP, 2)),
            ),
            limit=60,
            in_specs=[smem, vmem, far] + [vmem] * 5 + [far] + [vmem] * 3,
            cost_estimate=cost(9),
        )(
            order, edge_data, pairs_in, levels, d_mails, base,
            w_edge_in, b_edge_in, w_mats, bias, first, feats,
        )

    def both(big, small, step):
        return lax.optimization_barrier((swap_step(big, step), swap_step(small, step)))

    kept_first, kept_last, given_first, given_last = sums
    got_first, got_last = to_core(given_first), to_core(given_last)
    kept_first = full_call(
        copy_kernel, jax.ShapeDtypeStruct(kept_first.shape, BF16), cost_estimate=cost(1)
    )(kept_first)
    give = full_call(
        add_kernel, jax.ShapeDtypeStruct(kept_first.shape, BF16), cost_estimate=cost(1)
    )(kept_first, got_first)
    terms = [kept_last, got_last]
    state_grad, d_feats = [], b_edge_in
    for step in range(3):
        if step > 0:
            number = bit(core, step)
            give = added([pick(one, 1 - number) for one in terms]).astype(BF16)
            terms = [pick(one, number) for one in terms]
        if step == 2:
            got, small = both(give, first, step)
            first = first + small
        else:
            got = swap_step(give, step)
        if step < batches:
            grad, d_feats, first = edge_grads(step, after(g_pairs, give), first, d_feats)
            got = after(got, first)
            state_grad.append(grad)
        terms.append(got)
        if step == 0:
            terms = [one.reshape((2, 2, 2) + one.shape[2:]) for one in terms]
    total = added(terms).astype(BF16)
    for extra in range(3, owners.bit_length() - 1):
        masks = [1 << extra] * cores
        got, small = swap(total, masks), swap(first, masks)
        if extra < owners.bit_length() - 2:
            first = first + small
        if extra < owners.bit_length() - 2:
            total = added([total, got]).astype(BF16)
    held = rows_of(total, got)

    got, small = lax.optimization_barrier((swap_step(held, 2), small))
    first = first + small
    held = jnp.concatenate([held, got], axis=0)
    across = swap_step(held, 0)
    back = d_feats
    if merge > 1:
        back = back.reshape(blocks, -1, merge, cap).transpose(0, 2, 1, 3)
    back = after(back.reshape(owners, -1, cap), held)
    back = lax.all_to_all(back, "edge", 0, 0, tiled=True)

    near, more = both(held, first, 1)
    first = first + more
    last, more = swap_step(near, 0), swap_step(first, 0)
    near = after(near, back)

    feat_grad = full_call(
        functools.partial(unroute_kernel, own),
        jax.ShapeDtypeStruct((batches, feat_count, edges), BF16),
        cost_estimate=cost(0.1),
    )(source_index, back.reshape(owners, batches, feat_count, cap))

    shapes = tuple(
        jax.ShapeDtypeStruct(shape, F32)
        for shape in (
            (units, width * width),
            (width, width),
            (width, 3 * width),
            (width, 3 * width),
            (width, width),
        )
    )
    outs = ()
    for wave in (((held, 0),), ((near, 4), (across, 8)), ((last, 12),)):
        at, pieces = [], []
        extra = (more, feat_grad) if wave[0][0] is last else ()
        ready = lax.optimization_barrier((outs, tuple(piece for piece, _ in wave), extra))
        outs, wave, extra = ready[0], zip(ready[1], [flips for _, flips in wave]), ready[2]
        for piece, flips in wave:
            for side, one in ((core, piece), (1 - core, to_core(piece))):
                code = side
                for step in range(3):
                    code = code * 2 + bit(side, step)
                at.append((code * 2) ^ flips)
                pieces.append(one)
        outs = place_pieces(tall, jnp.stack(at), pieces, shapes, outs)
    more, feat_grad = extra
    first = first + more
    first_sum = first + to_core(first)
    d_w, d_bias, d_x, d_h, _ = outs
    return (
        new_states.reshape(batches, own, width),
        jnp.stack(state_grad),
        feat_grad,
        first_sum[:feat_count],
        first_sum[feat_count],
        d_w,
        d_bias.reshape(-1),
        d_x,
        d_h,
        first_sum[24:27].reshape(-1),
        first_sum[27:30].reshape(-1),
    )


def solution(mesh):
    spread = ("graph", "edge")
    rows = P(None, spread, None)
    edges = P(None, spread)
    feats = P(None, None, spread)
    in_specs = (rows, feats, edges, edges) + (P(),) * 8 + (rows,)
    out_specs = (rows, rows, feats) + (P(),) * 8
    return jax.shard_map(
        body,
        mesh=mesh,
        in_specs=in_specs,
        out_specs=out_specs,
        check_vma=False,
    )
```

```python
import functools

import jax
import jax.numpy as jnp
from jax import lax
from jax.experimental import pallas as pl
from jax.experimental.pallas import tpu as pltpu
from jax.sharding import PartitionSpec as P

F32 = jnp.float32
BF16 = jnp.bfloat16
LANES = 128
PIECE = 4
GROUP = 12
MIB = 1024 * 1024


def dot(first, second, dims=((1,), (0,))):
    return lax.dot_general(first, second, (dims, ((), ())), preferred_element_type=F32)


def dot_nt(first, second):
    return dot(first, second, ((1,), (1,)))


def row_ids(shape):
    return lax.broadcasted_iota(jnp.int32, shape, 0)


def col_ids(shape):
    return lax.broadcasted_iota(jnp.int32, shape, 1)


def full_call(kernel, out_shape, scratch=(), limit=16, **more):
    return pl.pallas_call(
        kernel,
        out_shape=out_shape,
        scratch_shapes=scratch,
        compiler_params=pltpu.CompilerParams(vmem_limit_bytes=limit * MIB),
        **more,
    )


def ranks_of(owner, owners):
    hits = (row_ids((owners, owner.shape[1])) == owner).astype(F32)
    before = (row_ids((LANES, LANES)) < col_ids((LANES, LANES))).astype(BF16)
    seen = jnp.zeros((owners, 1), F32)
    ranks = []
    for start in range(0, owner.shape[1], LANES):
        part = hits[:, start : start + LANES]
        place = dot(part.astype(BF16), before) + seen
        ranks.append(jnp.sum(part * place, axis=0, keepdims=True))
        seen = seen + jnp.sum(part, axis=1, keepdims=True)
    return hits, jnp.concatenate(ranks, axis=1)


def route_kernel(own_rows, src_ref, dst_ref, feat_ref, out_ref):
    owners, rows, cap = out_ref.shape
    batches, feats, edges = feat_ref.shape
    shift = own_rows.bit_length() - 1
    marks = [jnp.zeros((16, cap), F32)] * owners
    for batch in range(batches):
        source, target = src_ref[batch : batch + 1], dst_ref[batch : batch + 1]
        owner = source >> shift
        hits, rank = ranks_of(owner, owners)
        spots = (row_ids((cap, edges)) == rank.astype(jnp.int32)).astype(BF16)
        line = row_ids((16, edges)) - 3 * batch
        first = owner << shift
        extra = jnp.where(line == 0, source - first, jnp.where(line == 1, target - first, 1))
        extra = jnp.where((line >= 0) & (line < 3), extra, 0).astype(F32)
        load = jnp.concatenate([feat_ref[batch].astype(F32), extra], axis=0)
        masked = [(load * hits[part : part + 1]).astype(BF16) for part in range(owners)]
        out = dot_nt(jnp.concatenate(masked, axis=0), spots)
        for part in range(owners):
            tile = out[part * (feats + 16) : (part + 1) * (feats + 16)]
            out_ref[part, batch * feats : (batch + 1) * feats] = tile[:feats].astype(BF16)
            marks[part] = marks[part] + tile[feats:]
    for part in range(owners):
        out_ref[part, batches * feats :] = marks[part].astype(BF16)


def unroute_kernel(own_rows, src_ref, back_ref, out_ref):
    owners, batches, rows, cap = back_ref.shape
    edges = src_ref.shape[1]
    shift = own_rows.bit_length() - 1
    for batch in range(batches):
        hits, rank = ranks_of(src_ref[batch : batch + 1] >> shift, owners)
        spots = (row_ids((cap, edges)) == rank.astype(jnp.int32)).astype(BF16)
        parts = [back_ref[part, batch] for part in range(owners)]
        spread = dot(jnp.concatenate(parts, axis=0), spots)
        total = jnp.zeros((rows, edges), F32)
        for part in range(owners):
            total = total + spread[part * rows : (part + 1) * rows] * hits[part : part + 1]
        out_ref[batch] = total.astype(BF16)


def edge_piece(batches, order_ref, edge_ref, piece, batch):
    some = [edge_ref[order_ref[batch, PIECE * piece + k]] for k in range(PIECE)]
    block = jnp.concatenate(some, axis=1)
    feats, marks = block[batch * 16 : (batch + 1) * 16], block[batches * 16 :].astype(F32)
    source = marks[3 * batch : 3 * batch + 1].astype(jnp.int32)
    target = marks[3 * batch + 1 : 3 * batch + 2].astype(jnp.int32)
    held = marks[3 * batch + 2 : 3 * batch + 3]
    code = ((target >> 3) & 3) * 128 + (target >> 5) * 64 + source
    code = jnp.where(held > 0.5, code, -1)
    pairs = (row_ids((512, block.shape[1])) == code).astype(BF16)
    low = row_ids((8, block.shape[1])) == (target & 7)
    return feats, held, pairs, low


def order_blocks(batches, edge_ref, order_ref):
    blocks = edge_ref.shape[0]
    for batch in range(batches):
        front, back = jnp.int32(0), jnp.int32(blocks - 1)
        row = 3 * batch + 2
        for block in range(blocks):
            marks = edge_ref[block, batches * 16 :].astype(F32)
            held = jnp.max(marks[row : row + 1]) > 0.5
            order_ref[batch, jnp.where(held, front, back)] = jnp.int32(block)
            step = held.astype(jnp.int32)
            front, back = front + step, back - (1 - step)
        order_ref[batch, blocks] = front


def first_layer(w_in_ref, b_in_ref):
    bias = jnp.broadcast_to(b_in_ref[...].reshape(1, -1), (8, b_in_ref.shape[0]))
    return w_in_ref[...].astype(F32).T.astype(BF16), bias.T[:, :1]


def gates_of(mail_low, level, w_x, w_h, b_x, b_h):
    width = level.shape[1]
    from_mail = dot(mail_low, w_x[...]) + b_x[...].reshape(1, -1)
    from_state = dot(level, w_h[...]) + b_h[...].reshape(1, -1)
    reset = jax.nn.sigmoid(from_mail[:, :width] + from_state[:, :width])
    update = jax.nn.sigmoid(from_mail[:, width : 2 * width] + from_state[:, width : 2 * width])
    state_part = from_state[:, 2 * width :]
    candidate = jnp.tanh(from_mail[:, 2 * width :] + reset * state_part)
    return reset, update, candidate, state_part


def doubled(level):
    blank = jnp.zeros_like(level)
    return jnp.concatenate(
        [jnp.concatenate([level, blank], axis=1), jnp.concatenate([blank, level], axis=1)], axis=0
    )


def bias_blocks(bias_ref, tail_ref):
    tail_ref[...] = jnp.zeros_like(tail_ref)
    high = bias_ref[...].astype(BF16)
    tail_ref[0] = high
    tail_ref[1] = (bias_ref[...] - high.astype(F32)).astype(BF16)


def turned(tile):
    size = tile.shape[1]
    eye = (row_ids((size, size)) == col_ids((size, size))).astype(F32).astype(BF16)
    return dot_nt(eye, tile).astype(BF16)


def weights_of(w_ref, tail_ref, number):
    units = w_ref.shape[0]
    blocks = []
    for unit in range(number * GROUP, (number + 1) * GROUP):
        blocks.append(w_ref[unit] if unit < units else tail_ref[unit - units])
    return jnp.concatenate(blocks, axis=1)


def pulled_rows(pulled, half):
    rows = []
    for start in range(0, pulled.shape[1], LANES):
        tile = pulled[:, start : start + LANES]
        rows.append(jnp.concatenate([tile[:half], tile[half:]], axis=1))
    return jnp.concatenate(rows, axis=0)


def main_kernel(
    where_ref,
    edge_ref,
    state_ref,
    cot_ref,
    w_in_ref,
    b_in_ref,
    w_far,
    bias_ref,
    w_x,
    w_h,
    b_x,
    b_h,
    new_ref,
    kept_first,
    kept_last,
    given_first,
    given_last,
    g_far,
    level_ref,
    dm_ref,
    base_ref,
    order_ref,
    rows_ref,
    hid_ref,
    acc_ref,
    g_ref,
    p_ref,
    w_ref,
    tail_ref,
    sum_ref,
    sum_sems,
    sems,
):
    fetch = pltpu.make_async_copy(w_far, w_ref, sems.at[0])
    fetch.start()
    blocks = edge_ref.shape[0]
    batches = g_ref.shape[0]
    hidden_units = hid_ref.shape[0]
    units = acc_ref.shape[0] // 8
    own = state_ref.shape[0] // batches
    half = own // 2
    span = GROUP * half
    wide = GROUP * LANES
    chunks = units // GROUP
    order_blocks(batches, edge_ref, order_ref)
    bias_blocks(bias_ref, tail_ref)
    w_in, b_in = first_layer(w_in_ref, b_in_ref)

    for batch in range(batches):
        acc_ref[...] = jnp.zeros_like(acc_ref)

        def add_piece(piece, carry):
            feats, held, pairs, low = edge_piece(batches, order_ref, edge_ref, piece, batch)
            pre = dot(w_in, feats) + b_in
            hid_ref[...] = (pre * jax.nn.sigmoid(pre)).astype(BF16).astype(F32)
            ones = jnp.where(low, 1.0, 0.0)
            parts = []
            for unit in range(0, hidden_units, 2):
                two = [jnp.where(low, hid_ref[unit + k : unit + k + 1], 0.0) for k in range(2)]
                parts.append(jnp.concatenate(two, axis=0).astype(BF16))
            parts.append(jnp.concatenate([ones, ones], axis=0).astype(BF16))
            parts.append(jnp.zeros((8 * (units - hidden_units - 2), pre.shape[1]), BF16))
            acc_ref[...] += dot_nt(jnp.concatenate(parts, axis=0), pairs)
            return carry

        lax.fori_loop(0, (order_ref[batch, blocks] + PIECE - 1) // PIECE, add_piece, 0)

        def place(step, carry):
            for four in range(3):
                rows = []
                for k in range(4):
                    for part in range(4):
                        start = pl.multiple_of(step * 96 + four * 32 + k * 8, 8)
                        rows.append(acc_ref[pl.ds(start, 8), part * LANES : (part + 1) * LANES])
                at = pl.ds(pl.multiple_of((step * 3 + four) * LANES, LANES), LANES)
                g_ref[batch, at, :] = jnp.concatenate(rows, axis=0).astype(BF16)
            return carry

        lax.fori_loop(0, units // 12, place, 0)

    def forward(step, level):
        two = [doubled(level[batch * own : (batch + 1) * own]) for batch in range(batches)]
        mail = jnp.zeros((batches * own, LANES), F32)
        base = step * batches * own
        for number in range(chunks):
            for batch in range(batches):
                out = dot(g_ref[batch, number * span : (number + 1) * span, :], two[batch])
                out = out.astype(BF16)
                for unit in range(GROUP):
                    lane = number * wide + unit * LANES
                    for part in range(2):
                        row = base + batch * own + part * half
                        p_ref[row : row + half, lane : lane + LANES] = out[
                            unit * half : (unit + 1) * half, part * LANES : (part + 1) * LANES
                        ]
            rows = p_ref[base : base + batches * own, number * wide : (number + 1) * wide]
            mail = mail + dot_nt(rows, weights_of(w_ref, tail_ref, number))
        return mail

    def backward(d_mail):
        sums = [jnp.zeros((LANES, 2 * LANES), F32) for batch in range(batches)]
        for number in range(chunks):
            pulled = dot(d_mail, weights_of(w_ref, tail_ref, number)).astype(BF16)
            at = slice(number * span, (number + 1) * span)
            for batch in range(batches):
                tall = pulled_rows(pulled[batch * own : (batch + 1) * own], half)
                sums[batch] = sums[batch] + dot(turned(g_ref[batch, at, :]), tall)
        return jnp.concatenate([one[:own, :LANES] + one[own:, LANES:] for one in sums], axis=0)

    weights = (w_x, w_h, b_x, b_h)
    level_zero = state_ref[...]
    state_zero = level_zero.astype(F32)
    leave = pltpu.make_async_copy(g_ref, g_far, sems.at[1])
    leave.start()
    fetch.wait()
    mail_zero = forward(0, level_zero).astype(BF16)
    gates_zero = gates_of(mail_zero, level_zero, *weights)
    state_one = (1.0 - gates_zero[1]) * gates_zero[2] + gates_zero[1] * state_zero
    level_one = state_one.astype(BF16)
    mail_one = forward(1, level_one).astype(BF16)
    gates_one = gates_of(mail_one, level_one, *weights)
    new_ref[...] = ((1.0 - gates_one[1]) * gates_one[2] + gates_one[1] * state_one).astype(BF16)

    def gru_back(d_next, gates, current):
        reset, update, candidate, state_part = gates
        d_cand = d_next * (1.0 - update) * (1.0 - candidate * candidate)
        d_reset = d_cand * state_part * reset * (1.0 - reset)
        d_update = d_next * (current - candidate) * update * (1.0 - update)
        dg_mail = jnp.concatenate([d_reset, d_update, d_cand], axis=1).astype(BF16)
        dg_state = jnp.concatenate([d_reset, d_update, d_cand * reset], axis=1).astype(BF16)
        d_mail = dot_nt(dg_mail, w_x[...]).astype(BF16)
        d_current = d_next * update + dot_nt(dg_state, w_h[...])
        return dg_mail, dg_state, d_mail, d_current

    dgm_one, dgs_one, dm_one, d_state = gru_back(cot_ref[...].astype(F32), gates_one, state_one)
    d_state = d_state + backward(dm_one)
    dgm_zero, dgs_zero, dm_zero, d_state = gru_back(d_state, gates_zero, state_zero)
    base_ref[...] = d_state
    level_ref[...] = jnp.concatenate([level_zero, level_one], axis=1)
    dm_ref[...] = jnp.concatenate([dm_zero, dm_one], axis=1)

    def both(first, second):
        return jnp.concatenate([first.astype(F32), second.astype(F32)], axis=0)

    dms = both(dm_zero, dm_one).T
    mails, levels = both(mail_zero, mail_one), both(level_zero, level_one)
    dgm, dgs = both(dgm_zero, dgm_one), both(dgs_zero, dgs_one)
    width = dgm.shape[1]
    rows_ref[...] = jnp.zeros_like(rows_ref)
    for k, one in enumerate((dgm, dgs)):
        total = jnp.sum(one, axis=0, keepdims=True)
        for part in range(3):
            row = 24 + 3 * k + part
            rows_ref[row : row + 1, :] = total[:, part * LANES : (part + 1) * LANES]
    small = jnp.concatenate(
        [
            dot(dms.astype(BF16), p_ref[:, hidden_units * LANES : (hidden_units + 1) * LANES]),
            dot(mails.T.astype(BF16), dgm.astype(BF16)),
            dot(levels.T.astype(BF16), dgs.astype(BF16)),
            jnp.zeros((2 * own, LANES), F32),
        ],
        axis=1,
    )

    def sorted_rows(value):
        rows = value.shape[0] // 2
        upper, lower = value[:rows], value[rows:]
        halves = [jnp.where(where_ref[0] == k, upper, lower) for k in range(2)]
        parts = []
        for k, one in enumerate(halves):
            first, second = one[: rows // 2], one[rows // 2 :]
            parts += [jnp.where(where_ref[1 + k] == side, second, first) for side in range(2)]
        return jnp.concatenate(parts, axis=0).astype(BF16)

    dms, small = sorted_rows(dms), sorted_rows(small)
    rows_in, groups, tall, wide_out = kept_first.shape
    taken = wide_out - 2 * LANES
    moves = []
    for group in range(groups):
        out = dot(dms, p_ref[:, group * taken : (group + 1) * taken]).astype(BF16)
        extra = small[:, group * 2 * LANES : (group + 1) * 2 * LANES]
        for k, ref in enumerate((given_first, kept_first, given_last, kept_last)):
            for row in range(rows_in):
                at = ((2, 0, 3, 1)[k] * rows_in + row) * tall
                sum_ref[k, row, group, :, :taken] = out[at : at + tall]
                sum_ref[k, row, group, :, taken:] = extra[at : at + tall]
                moves.append(
                    pltpu.make_async_copy(
                        sum_ref.at[k, row, group], ref.at[row, group], sum_sems.at[k, row, group]
                    )
                )
                moves[-1].start()
    for move in moves:
        move.wait()
    leave.wait()


def edge_sums(batch, batches, order_ref, edge_ref, dg_ref, w_in_ref, b_in_ref, feat_ref, before):
    blocks = edge_ref.shape[0]
    hidden_units = w_in_ref.shape[1]
    w_in, b_in = first_layer(w_in_ref, b_in_ref)
    fold = (col_ids((hidden_units, 8 * hidden_units)) >> 3) == row_ids(
        (hidden_units, 8 * hidden_units)
    )
    fold = fold.astype(F32).astype(BF16)

    def one_piece(piece, sums):
        feats, held, pairs, low = edge_piece(batches, order_ref, edge_ref, piece, batch)
        pre = dot(w_in, feats) + b_in
        sig = jax.nn.sigmoid(pre)
        spread = dot(dg_ref[: 8 * hidden_units], pairs)
        spread = spread.reshape(hidden_units, 8, pre.shape[1])
        spread = jnp.where(low[None], spread, 0.0).reshape(8 * hidden_units, pre.shape[1])
        d_hidden = dot(fold, spread.astype(BF16))
        d_pre = (d_hidden * sig * (1.0 + pre * (1.0 - sig))).astype(BF16)
        out = dot(w_in_ref[...], d_pre).astype(BF16)
        for k in range(PIECE):
            at = order_ref[batch, PIECE * piece + k]
            feat_ref[at, batch * 16 : (batch + 1) * 16] = out[:, k * LANES : (k + 1) * LANES]
        ones = jnp.where(row_ids((16, pre.shape[1])) == 0, held, 0.0).astype(BF16)
        return sums + dot_nt(jnp.concatenate([feats, ones], axis=0), d_pre)

    return lax.fori_loop(0, (order_ref[batch, blocks] + PIECE - 1) // PIECE, one_piece, before)


def back_kernel(
    order_ref,
    edge_ref,
    g_far,
    level_ref,
    dm_ref,
    base_ref,
    w_in_ref,
    b_in_ref,
    w_far,
    bias_ref,
    before_ref,
    grad_ref,
    feat_ref,
    dg_ref,
    win_ref,
    tail_ref,
    dg_first,
    w_ref,
    g_ref,
    sems,
):
    batches, own, width = grad_ref.shape
    hidden_units = w_in_ref.shape[1]
    chunks = (hidden_units + tail_ref.shape[0]) // GROUP
    half = own // 2
    fetches = []
    for number in range(chunks):
        some = pl.ds(number * GROUP, min(GROUP, hidden_units - number * GROUP))
        rows = pl.ds(number * GROUP * half, GROUP * half)
        fetches += [
            pltpu.make_async_copy(w_far.at[some], w_ref.at[some], sems.at[number, 0]),
            pltpu.make_async_copy(g_far.at[:, rows], g_ref.at[:, rows], sems.at[number, 1]),
        ]
    for fetch in fetches:
        fetch.start()
    bias_blocks(bias_ref, tail_ref)
    feat_ref[...] = jnp.zeros_like(feat_ref)

    pulls, levels = [], []
    for batch in range(batches):
        mine = slice(batch * own, (batch + 1) * own)
        pulls += [dm_ref[mine, step * width : (step + 1) * width] for step in range(2)]
        both = [doubled(level_ref[mine, step * width : (step + 1) * width]) for step in range(2)]
        levels.append(jnp.concatenate(both, axis=1))
    pulls = jnp.concatenate(pulls, axis=0)
    totals = [jnp.zeros((2 * own, 2 * width), F32) for batch in range(batches)]
    for number in range(chunks):
        fetches[2 * number].wait()
        fetches[2 * number + 1].wait()
        pulled = dot(pulls, weights_of(w_ref, tail_ref, number)).astype(BF16)
        at = slice(number * GROUP * half, (number + 1) * GROUP * half)
        for batch in range(batches):
            target = dg_ref if batch else dg_first
            talls = [
                pulled_rows(pulled[(2 * batch + k) * own : (2 * batch + k + 1) * own], half)
                for k in range(2)
            ]
            totals[batch] = totals[batch] + dot(turned(g_ref[batch, at, :]), talls[0])
            d_pair = dot_nt(jnp.concatenate(talls, axis=1), levels[batch])
            for unit in range(0, GROUP, 2):
                row = (number * GROUP + unit) * 8
                for part in range(half // 8):
                    pair = [
                        d_pair[(unit + k) * half + part * 8 : (unit + k) * half + part * 8 + 8]
                        for k in range(2)
                    ]
                    target[row : row + 16, part * LANES : (part + 1) * LANES] = jnp.concatenate(
                        pair, axis=0
                    ).astype(BF16)
    for batch in range(batches):
        grad = base_ref[batch * own : (batch + 1) * own] + totals[batch][:own, :width]
        grad_ref[batch] = (grad + totals[batch][own:, width:]).astype(BF16)
    win_ref[...] = edge_sums(
        0, batches, order_ref, edge_ref, dg_first, w_in_ref, b_in_ref, feat_ref, before_ref[...]
    )


def edge_kernel(
    order_ref, edge_ref, dg_ref, feat_in, w_in_ref, b_in_ref, before_ref, feat_ref, win_ref
):
    feat_ref[...] = feat_in[...]
    win_ref[...] = edge_sums(
        1,
        order_ref.shape[0],
        order_ref,
        edge_ref,
        dg_ref,
        w_in_ref,
        b_in_ref,
        feat_ref,
        before_ref[...],
    )


def add_kernel(first_ref, second_ref, out_ref):
    out_ref[...] = (first_ref[...].astype(F32) + second_ref[...].astype(F32)).astype(BF16)


def copy_kernel(in_ref, out_ref):
    out_ref[...] = in_ref[...]


def rows_kernel(first_ref, second_ref, out_ref, rows_ref):
    parts, tall, wide = first_ref.shape
    main = wide // LANES - 2
    for part in range(parts):
        total = first_ref[part].astype(F32) + second_ref[part].astype(F32)
        for block in range(main):
            rows_ref[pl.ds(block, tall, stride=main), :] = total[
                :, block * LANES : (block + 1) * LANES
            ]
        for k in range(2):
            start = tall * (main + k)
            rows_ref[start : start + tall, :] = total[:, (main + k) * LANES : (main + k + 1) * LANES]
        out_ref[part] = rows_ref[...].astype(BF16)


def rows_of(first, second):
    parts, tall, wide = first.shape
    shape = (tall * (wide // LANES), LANES)
    return full_call(
        rows_kernel,
        jax.ShapeDtypeStruct((parts,) + shape, BF16),
        (pltpu.VMEM(shape, F32),),
        cost_estimate=cost(1),
    )(first, second)


def place_kernel(tall, count, carried, *refs):
    at_ref, pieces = refs[0], refs[1 : 1 + count]
    outs = refs[1 + count + carried : 6 + count + carried]
    big_ref, little_ref, sems = refs[6 + count + carried :]
    d_w, d_bias, d_x, d_h, d_rest = outs
    waits = []
    slot = 0
    for k, piece in enumerate(pieces):
        chunks, rows_in, lanes = piece.shape
        main = rows_in // tall - 2
        for chunk in range(chunks):
            code = at_ref[k] ^ chunk
            line, part = code >> 2, code & 3
            at = pl.ds(pl.multiple_of(line * tall, 8), tall)
            rows = piece[chunk].astype(F32)
            for row in range(tall):
                big_ref[slot, :, row * lanes : (row + 1) * lanes] = rows[row * main : (row + 1) * main]
            copy = pltpu.make_async_copy(
                big_ref.at[slot],
                d_w.at[
                    pl.ds(pl.multiple_of(part * main, 8), main),
                    pl.ds(pl.multiple_of(line * (tall * lanes), LANES), tall * lanes),
                ],
                sems.at[slot, 0],
            )
            copy.start()
            waits.append(copy)

            for side in range(2):
                start = tall * (main + side)
                little_ref[slot, side] = rows[start : start + tall]

                def move(target, lane):
                    lane = jnp.maximum(lane, 0) * lanes
                    to = pl.ds(pl.multiple_of(jnp.minimum(lane, target.shape[1] - lanes), LANES), lanes)
                    return pltpu.make_async_copy(
                        little_ref.at[slot, side], target.at[at, to], sems.at[slot, 1 + side]
                    )

                block = 2 * part + side
                to_x, to_h = move(d_x, block - 1), move(d_h, block - 4)
                alone = move((d_bias, d_rest)[side], 0)
                lone = block == 7 * side
                pl.when(lone)(alone.start)
                pl.when((block > 0) & (block < 4))(to_x.start)
                pl.when((block > 3) & (block < 7))(to_h.start)
                waits.append(alone)
            slot += 1
    for copy in waits:
        copy.wait()


def cost(micros):
    return pl.CostEstimate(
        flops=int(micros * 1e9), bytes_accessed=int(micros * 3e6), transcendentals=0
    )


def place_pieces(tall, at, pieces, shapes, before=()):
    count = len(pieces)
    chunks, rows_in, lanes = pieces[0].shape
    slots = count * chunks
    vmem = pl.BlockSpec(memory_space=pltpu.VMEM)
    hbm = pl.BlockSpec(memory_space=pl.ANY)
    return pl.pallas_call(
        functools.partial(place_kernel, tall, count, len(before)),
        out_shape=shapes,
        in_specs=[pl.BlockSpec(memory_space=pltpu.SMEM)] + [vmem] * count + [hbm] * len(before),
        out_specs=[hbm] * len(shapes),
        scratch_shapes=(
            pltpu.VMEM((slots, rows_in // tall - 2, tall * lanes), F32),
            pltpu.VMEM((slots, 2, tall, lanes), F32),
            pltpu.SemaphoreType.DMA((slots, 3)),
        ),
        input_output_aliases={1 + count + k: k for k in range(len(before))},
        cost_estimate=cost(0.1),
        compiler_params=pltpu.CompilerParams(vmem_limit_bytes=16 * MIB),
    )(at, *pieces, *before)


def body(
    states,
    edge_feats,
    source_index,
    target_index,
    w_edge_in,
    b_edge_in,
    w_edge_out,
    b_edge_out,
    w_input,
    w_hidden,
    b_input,
    b_hidden,
    cotangent,
):
    batches, own, width = states.shape
    edges = source_index.shape[1]
    owners = lax.axis_size("edge")
    cap = max(2, 2 * edges // owners)
    feat_count, units = w_edge_in.shape

    sent = full_call(
        functools.partial(route_kernel, own),
        jax.ShapeDtypeStruct((owners, batches * feat_count + 16, cap), BF16),
        limit=60,
    )(source_index, target_index, edge_feats)
    edge_data = lax.all_to_all(sent, "edge", 0, 0, tiled=True)
    merge = max(1, LANES // cap)
    if merge > 1:
        edge_data = edge_data.reshape(owners // merge, merge, -1, cap).transpose(0, 2, 1, 3)
        edge_data = edge_data.reshape(owners // merge, -1, merge * cap)

    w_mats = w_edge_out.reshape(units, width, width)
    padded = (units + 2 + GROUP - 1) // GROUP * GROUP

    tall = width // 8
    pairs = own // 2
    blocks = edge_data.shape[0]
    core = lax.axis_index("graph")
    spot = lax.axis_index("edge")
    orders = ((0, 1, 2, 3), (2, 0, 1, 3))

    def bit(side, step):
        first, second = [(spot >> orders[k][step]) & 1 for k in range(2)]
        return jnp.where(side == 0, first, second)

    where = jnp.stack([core, bit(core, 0), bit(1 - core, 0)])
    smem = pl.BlockSpec(memory_space=pltpu.SMEM)
    vmem = pl.BlockSpec(memory_space=pltpu.VMEM)
    far = pl.BlockSpec(memory_space=pltpu.HBM)
    bias = b_edge_out.reshape(width, width)
    quarter = jax.ShapeDtypeStruct((2, 4, tall, (units // 4 + 2) * width), BF16)
    new_states, *sums, g_pairs, levels, d_mails, base, order, first = full_call(
        main_kernel,
        (
            jax.ShapeDtypeStruct((batches * own, width), BF16),
            *[quarter] * 4,
            jax.ShapeDtypeStruct((batches, padded * pairs, LANES), BF16),
            jax.ShapeDtypeStruct((batches * own, 2 * width), BF16),
            jax.ShapeDtypeStruct((batches * own, 2 * width), BF16),
            jax.ShapeDtypeStruct((batches * own, width), F32),
            jax.ShapeDtypeStruct((batches, blocks + 1), jnp.int32),
            jax.ShapeDtypeStruct((32, width), F32),
        ),
        (
            pltpu.VMEM((units, PIECE * LANES), F32),
            pltpu.VMEM((padded * 8, 512), F32),
            pltpu.VMEM((batches, padded * pairs, LANES), BF16),
            pltpu.VMEM((2 * batches * own, padded * width), BF16),
            pltpu.VMEM((units, width, width), BF16),
            pltpu.VMEM((padded - units, width, width), BF16),
            pltpu.VMEM((4,) + quarter.shape, BF16),
            pltpu.SemaphoreType.DMA((4,) + quarter.shape[:2]),
            pltpu.SemaphoreType.DMA((2,)),
        ),
        limit=60,
        in_specs=[smem] + [vmem] * 5 + [far] + [vmem] * 5,
        out_specs=[vmem] + [far] * 5 + [vmem] * 3 + [smem, vmem],
    )(
        where,
        edge_data,
        states.reshape(batches * own, width),
        cotangent.reshape(batches * own, width),
        w_edge_in,
        b_edge_in,
        w_mats,
        bias,
        w_input,
        w_hidden,
        b_input,
        b_hidden,
    )

    cores = lax.axis_size("graph")

    def to_core(value):
        return lax.ppermute(value, "graph", [(0, 1), (1, 0)])

    def swap(value, masks):
        moves = []
        for side in range(cores):
            first = side * owners
            moves += [(first + k, first + (k ^ masks[side])) for k in range(owners)]
        return lax.ppermute(value, ("graph", "edge"), moves)

    def swap_step(value, step):
        return swap(value, [1 << orders[side][step] for side in range(cores)])

    def pick(value, number):
        return lax.dynamic_index_in_dim(value, number, 0, False)

    def added(terms):
        return sum(one.astype(F32) for one in terms)

    def after(value, *others):
        return lax.optimization_barrier((value, *others))[0]

    feat_shape = jax.ShapeDtypeStruct((blocks, batches * feat_count, LANES), BF16)
    win_shape = jax.ShapeDtypeStruct((32, units), F32)

    def first_grads(pairs_in):
        return full_call(
            back_kernel,
            (
                jax.ShapeDtypeStruct((batches, own, width), BF16),
                feat_shape,
                jax.ShapeDtypeStruct((padded * 8, 512), BF16),
                win_shape,
            ),
            (
                pltpu.VMEM((padded - units, width, width), BF16),
                pltpu.VMEM((padded * 8, 512), BF16),
                pltpu.VMEM((units, width, width), BF16),
                pltpu.VMEM((batches, padded * pairs, LANES), BF16),
                pltpu.SemaphoreType.DMA((padded // GROUP, 2)),
            ),
            limit=60,
            in_specs=[smem, vmem, far] + [vmem] * 5 + [far] + [vmem] * 2,
            cost_estimate=cost(12),
        )(
            order, edge_data, pairs_in, levels, d_mails, base,
            w_edge_in, b_edge_in, w_mats, bias, first,
        )

    def second_grads(d_pairs, feats, before):
        return full_call(
            edge_kernel,
            (feat_shape, win_shape),
            in_specs=[smem] + [vmem] * 6,
            cost_estimate=cost(5),
        )(order, edge_data, d_pairs, feats, w_edge_in, b_edge_in, before)

    def added_at(big, small, flip):
        big, more = lax.optimization_barrier((big, swap(small, [flip] * cores)))
        return big, small + more

    kept_first, kept_last, given_first, given_last = sums
    got_first, got_last = to_core(given_first), to_core(given_last)
    kept_first = full_call(
        copy_kernel, jax.ShapeDtypeStruct(kept_first.shape, BF16), cost_estimate=cost(1)
    )(kept_first)
    give = full_call(
        add_kernel, jax.ShapeDtypeStruct(kept_first.shape, BF16), cost_estimate=cost(1)
    )(kept_first, got_first)
    terms = [kept_last, got_last]
    for step in range(3):
        if step > 0:
            number = bit(core, step)
            give = added([pick(one, 1 - number) for one in terms]).astype(BF16)
            terms = [pick(one, number) for one in terms]
        got = swap_step(give, step)
        if step == 0:
            state_grad, d_feats, d_pairs, first = first_grads(after(g_pairs, give))
            got = after(got, first)
        if step == 1:
            d_feats, first = second_grads(after(d_pairs, give), d_feats, first)
            got = after(got, first)
        if step == 2:
            got, first = added_at(got, first, 4)
        terms.append(got)
        if step == 0:
            terms = [one.reshape((2, 2, 2) + one.shape[2:]) for one in terms]
    total = added(terms).astype(BF16)
    for extra in range(3, owners.bit_length() - 1):
        got = swap(total, [1 << extra] * cores)
        if extra > 3:
            got, first = added_at(got, first, 1 << extra)
        if extra < owners.bit_length() - 2:
            total = added([total, got]).astype(BF16)
    first = first + swap(first, [1] * cores)
    got, first = added_at(got, first, 2)
    held = rows_of(total, got)

    got, first = added_at(swap_step(held, 2), first, 8)
    held = jnp.concatenate([held, got], axis=0)
    across = swap_step(held, 0)
    back = d_feats
    if merge > 1:
        back = back.reshape(blocks, -1, merge, cap).transpose(0, 2, 1, 3)
    back = after(back.reshape(owners, -1, cap), held)
    back = lax.all_to_all(back, "edge", 0, 0, tiled=True)

    near = swap_step(held, 1)
    near, more = lax.optimization_barrier((near, to_core(first)))
    first = first + more
    last = swap_step(near, 0)
    near = after(near, back)
    small_outs = (
        first[:feat_count],
        first[feat_count],
        first[24:27].reshape(-1),
        first[27:30].reshape(-1),
    )

    feat_grad = full_call(
        functools.partial(unroute_kernel, own),
        jax.ShapeDtypeStruct((batches, feat_count, edges), BF16),
        cost_estimate=cost(0.1),
    )(source_index, back.reshape(owners, batches, feat_count, cap))

    shapes = tuple(
        jax.ShapeDtypeStruct(shape, F32)
        for shape in (
            (units, width * width),
            (width, width),
            (width, 3 * width),
            (width, 3 * width),
            (width, width),
        )
    )
    outs = ()
    def place(outs, pieces):
        at = []
        for _, side, flips in pieces:
            code = side
            for step in range(3):
                code = code * 2 + bit(side, step)
            at.append((code * 2) ^ flips)
        return place_pieces(tall, jnp.stack(at), [one for one, _, _ in pieces], shapes, outs)

    outs = place((), [(held, core, 0), (to_core(held), 1 - core, 0)])
    outs, near, across = lax.optimization_barrier((outs, near, across))
    outs = place(
        outs,
        [
            (near, core, 4),
            (to_core(near), 1 - core, 4),
            (across, core, 8),
            (to_core(across), 1 - core, 8),
        ],
    )
    outs, last, feat_grad, small_outs = lax.optimization_barrier(
        (outs, last, feat_grad, small_outs)
    )
    other = to_core(last)
    outs = place(outs, [(last, core, 12)])
    outs = place(outs, [(other, 1 - core, 12)])
    d_w, d_bias, d_x, d_h, _ = outs
    return (
        new_states.reshape(batches, own, width),
        state_grad,
        feat_grad,
        small_outs[0],
        small_outs[1],
        d_w,
        d_bias.reshape(-1),
        d_x,
        d_h,
        small_outs[2],
        small_outs[3],
    )


def solution(mesh):
    spread = ("graph", "edge")
    rows = P(None, spread, None)
    edges = P(None, spread)
    feats = P(None, None, spread)
    in_specs = (rows, feats, edges, edges) + (P(),) * 8 + (rows,)
    out_specs = (rows, rows, feats) + (P(),) * 8
    return jax.shard_map(
        body,
        mesh=mesh,
        in_specs=in_specs,
        out_specs=out_specs,
        check_vma=False,
    )
```

```python
import functools

import jax
import jax.numpy as jnp
from jax import lax
from jax.experimental import pallas as pl
from jax.experimental.pallas import tpu as pltpu
from jax.sharding import PartitionSpec as P

F32 = jnp.float32
BF16 = jnp.bfloat16
LANES = 128
PIECE = 4
GROUP = 12
MIB = 1024 * 1024


def dot(first, second, dims=((1,), (0,))):
    return lax.dot_general(first, second, (dims, ((), ())), preferred_element_type=F32)


def dot_nt(first, second):
    return dot(first, second, ((1,), (1,)))


def row_ids(shape):
    return lax.broadcasted_iota(jnp.int32, shape, 0)


def col_ids(shape):
    return lax.broadcasted_iota(jnp.int32, shape, 1)


def full_call(kernel, out_shape, scratch=(), limit=16, **more):
    return pl.pallas_call(
        kernel,
        out_shape=out_shape,
        scratch_shapes=scratch,
        compiler_params=pltpu.CompilerParams(vmem_limit_bytes=limit * MIB),
        **more,
    )


def ranks_of(owner, owners):
    hits = (row_ids((owners, owner.shape[1])) == owner).astype(F32)
    before = (row_ids((LANES, LANES)) < col_ids((LANES, LANES))).astype(BF16)
    seen = jnp.zeros((owners, 1), F32)
    ranks = []
    for start in range(0, owner.shape[1], LANES):
        part = hits[:, start : start + LANES]
        place = dot(part.astype(BF16), before) + seen
        ranks.append(jnp.sum(part * place, axis=0, keepdims=True))
        seen = seen + jnp.sum(part, axis=1, keepdims=True)
    return hits, jnp.concatenate(ranks, axis=1)


def route_kernel(own_rows, src_ref, dst_ref, feat_ref, out_ref):
    owners, rows, cap = out_ref.shape
    batches, feats, edges = feat_ref.shape
    shift = own_rows.bit_length() - 1
    marks = [jnp.zeros((16, cap), F32)] * owners
    for batch in range(batches):
        source, target = src_ref[batch : batch + 1], dst_ref[batch : batch + 1]
        owner = source >> shift
        hits, rank = ranks_of(owner, owners)
        spots = (row_ids((cap, edges)) == rank.astype(jnp.int32)).astype(BF16)
        line = row_ids((16, edges)) - 3 * batch
        first = owner << shift
        extra = jnp.where(line == 0, source - first, jnp.where(line == 1, target - first, 1))
        extra = jnp.where((line >= 0) & (line < 3), extra, 0).astype(F32)
        load = jnp.concatenate([feat_ref[batch].astype(F32), extra], axis=0)
        masked = [(load * hits[part : part + 1]).astype(BF16) for part in range(owners)]
        out = dot_nt(jnp.concatenate(masked, axis=0), spots)
        for part in range(owners):
            tile = out[part * (feats + 16) : (part + 1) * (feats + 16)]
            out_ref[part, batch * feats : (batch + 1) * feats] = tile[:feats].astype(BF16)
            marks[part] = marks[part] + tile[feats:]
    for part in range(owners):
        out_ref[part, batches * feats :] = marks[part].astype(BF16)


def unroute_kernel(own_rows, src_ref, back_ref, out_ref):
    owners, batches, rows, cap = back_ref.shape
    edges = src_ref.shape[1]
    shift = own_rows.bit_length() - 1
    for batch in range(batches):
        hits, rank = ranks_of(src_ref[batch : batch + 1] >> shift, owners)
        spots = (row_ids((cap, edges)) == rank.astype(jnp.int32)).astype(BF16)
        parts = [back_ref[part, batch] for part in range(owners)]
        spread = dot(jnp.concatenate(parts, axis=0), spots)
        total = jnp.zeros((rows, edges), F32)
        for part in range(owners):
            total = total + spread[part * rows : (part + 1) * rows] * hits[part : part + 1]
        out_ref[batch] = total.astype(BF16)


def edge_piece(batches, order_ref, edge_ref, piece, batch):
    some = [edge_ref[order_ref[batch, PIECE * piece + k]] for k in range(PIECE)]
    block = jnp.concatenate(some, axis=1)
    feats, marks = block[batch * 16 : (batch + 1) * 16], block[batches * 16 :].astype(F32)
    source = marks[3 * batch : 3 * batch + 1].astype(jnp.int32)
    target = marks[3 * batch + 1 : 3 * batch + 2].astype(jnp.int32)
    held = marks[3 * batch + 2 : 3 * batch + 3]
    code = ((target >> 3) & 3) * 128 + (target >> 5) * 64 + source
    code = jnp.where(held > 0.5, code, -1)
    pairs = (row_ids((512, block.shape[1])) == code).astype(BF16)
    low = row_ids((8, block.shape[1])) == (target & 7)
    return feats, held, pairs, low


def order_blocks(batches, edge_ref, order_ref):
    blocks = edge_ref.shape[0]
    for batch in range(batches):
        front, back = jnp.int32(0), jnp.int32(blocks - 1)
        row = 3 * batch + 2
        for block in range(blocks):
            marks = edge_ref[block, batches * 16 :].astype(F32)
            held = jnp.max(marks[row : row + 1]) > 0.5
            order_ref[batch, jnp.where(held, front, back)] = jnp.int32(block)
            step = held.astype(jnp.int32)
            front, back = front + step, back - (1 - step)
        order_ref[batch, blocks] = front


def first_layer(w_in_ref, b_in_ref):
    bias = jnp.broadcast_to(b_in_ref[...].reshape(1, -1), (8, b_in_ref.shape[0]))
    return w_in_ref[...].astype(F32).T.astype(BF16), bias.T[:, :1]


def gates_of(mail_low, level, w_x, w_h, b_x, b_h):
    width = level.shape[1]
    from_mail = dot(mail_low, w_x[...]) + b_x[...].reshape(1, -1)
    from_state = dot(level, w_h[...]) + b_h[...].reshape(1, -1)
    reset = jax.nn.sigmoid(from_mail[:, :width] + from_state[:, :width])
    update = jax.nn.sigmoid(from_mail[:, width : 2 * width] + from_state[:, width : 2 * width])
    state_part = from_state[:, 2 * width :]
    candidate = jnp.tanh(from_mail[:, 2 * width :] + reset * state_part)
    return reset, update, candidate, state_part


def doubled(level):
    blank = jnp.zeros_like(level)
    return jnp.concatenate(
        [jnp.concatenate([level, blank], axis=1), jnp.concatenate([blank, level], axis=1)], axis=0
    )


def bias_blocks(bias_ref, tail_ref):
    tail_ref[...] = jnp.zeros_like(tail_ref)
    high = bias_ref[...].astype(BF16)
    tail_ref[0] = high
    tail_ref[1] = (bias_ref[...] - high.astype(F32)).astype(BF16)


def turned(tile):
    size = tile.shape[1]
    eye = (row_ids((size, size)) == col_ids((size, size))).astype(F32).astype(BF16)
    return dot_nt(eye, tile).astype(BF16)


def weights_of(w_ref, tail_ref, number):
    units = w_ref.shape[0]
    blocks = []
    for unit in range(number * GROUP, (number + 1) * GROUP):
        blocks.append(w_ref[unit] if unit < units else tail_ref[unit - units])
    return jnp.concatenate(blocks, axis=1)


def pulled_rows(pulled, half):
    rows = []
    for start in range(0, pulled.shape[1], LANES):
        tile = pulled[:, start : start + LANES]
        rows.append(jnp.concatenate([tile[:half], tile[half:]], axis=1))
    return jnp.concatenate(rows, axis=0)


def main_kernel(
    where_ref,
    edge_ref,
    state_ref,
    cot_ref,
    w_in_ref,
    b_in_ref,
    w_far,
    bias_ref,
    w_x,
    w_h,
    b_x,
    b_h,
    new_ref,
    kept_first,
    kept_last,
    given_first,
    given_last,
    g_far,
    level_ref,
    dm_ref,
    base_ref,
    order_ref,
    rows_ref,
    hid_ref,
    acc_ref,
    g_ref,
    p_ref,
    w_ref,
    tail_ref,
    sum_ref,
    sum_sems,
    sems,
):
    fetch = pltpu.make_async_copy(w_far, w_ref, sems.at[0])
    fetch.start()
    blocks = edge_ref.shape[0]
    batches = g_ref.shape[0]
    hidden_units = hid_ref.shape[0]
    units = acc_ref.shape[0] // 8
    own = state_ref.shape[0] // batches
    half = own // 2
    span = GROUP * half
    wide = GROUP * LANES
    chunks = units // GROUP
    order_blocks(batches, edge_ref, order_ref)
    bias_blocks(bias_ref, tail_ref)
    w_in, b_in = first_layer(w_in_ref, b_in_ref)

    for batch in range(batches):
        acc_ref[...] = jnp.zeros_like(acc_ref)

        def add_piece(piece, carry):
            feats, held, pairs, low = edge_piece(batches, order_ref, edge_ref, piece, batch)
            pre = dot(w_in, feats) + b_in
            hid_ref[...] = (pre * jax.nn.sigmoid(pre)).astype(BF16).astype(F32)
            ones = jnp.where(low, 1.0, 0.0)
            parts = []
            for unit in range(0, hidden_units, 2):
                two = [jnp.where(low, hid_ref[unit + k : unit + k + 1], 0.0) for k in range(2)]
                parts.append(jnp.concatenate(two, axis=0).astype(BF16))
            parts.append(jnp.concatenate([ones, ones], axis=0).astype(BF16))
            parts.append(jnp.zeros((8 * (units - hidden_units - 2), pre.shape[1]), BF16))
            acc_ref[...] += dot_nt(jnp.concatenate(parts, axis=0), pairs)
            return carry

        lax.fori_loop(0, (order_ref[batch, blocks] + PIECE - 1) // PIECE, add_piece, 0)

        def place(step, carry):
            for four in range(3):
                rows = []
                for k in range(4):
                    for part in range(4):
                        start = pl.multiple_of(step * 96 + four * 32 + k * 8, 8)
                        rows.append(acc_ref[pl.ds(start, 8), part * LANES : (part + 1) * LANES])
                at = pl.ds(pl.multiple_of((step * 3 + four) * LANES, LANES), LANES)
                g_ref[batch, at, :] = jnp.concatenate(rows, axis=0).astype(BF16)
            return carry

        lax.fori_loop(0, units // 12, place, 0)

    def forward(step, level):
        two = [doubled(level[batch * own : (batch + 1) * own]) for batch in range(batches)]
        mail = jnp.zeros((batches * own, LANES), F32)
        base = step * batches * own
        for number in range(chunks):
            for batch in range(batches):
                out = dot(g_ref[batch, number * span : (number + 1) * span, :], two[batch])
                out = out.astype(BF16)
                for unit in range(GROUP):
                    lane = number * wide + unit * LANES
                    for part in range(2):
                        row = base + batch * own + part * half
                        p_ref[row : row + half, lane : lane + LANES] = out[
                            unit * half : (unit + 1) * half, part * LANES : (part + 1) * LANES
                        ]
            rows = p_ref[base : base + batches * own, number * wide : (number + 1) * wide]
            mail = mail + dot_nt(rows, weights_of(w_ref, tail_ref, number))
        return mail

    def backward(d_mail):
        sums = [jnp.zeros((LANES, 2 * LANES), F32) for batch in range(batches)]
        for number in range(chunks):
            pulled = dot(d_mail, weights_of(w_ref, tail_ref, number)).astype(BF16)
            at = slice(number * span, (number + 1) * span)
            for batch in range(batches):
                tall = pulled_rows(pulled[batch * own : (batch + 1) * own], half)
                sums[batch] = sums[batch] + dot(turned(g_ref[batch, at, :]), tall)
        return jnp.concatenate([one[:own, :LANES] + one[own:, LANES:] for one in sums], axis=0)

    weights = (w_x, w_h, b_x, b_h)
    level_zero = state_ref[...]
    state_zero = level_zero.astype(F32)
    leave = pltpu.make_async_copy(g_ref, g_far, sems.at[1])
    leave.start()
    fetch.wait()
    mail_zero = forward(0, level_zero).astype(BF16)
    gates_zero = gates_of(mail_zero, level_zero, *weights)
    state_one = (1.0 - gates_zero[1]) * gates_zero[2] + gates_zero[1] * state_zero
    level_one = state_one.astype(BF16)
    mail_one = forward(1, level_one).astype(BF16)
    gates_one = gates_of(mail_one, level_one, *weights)
    new_ref[...] = ((1.0 - gates_one[1]) * gates_one[2] + gates_one[1] * state_one).astype(BF16)

    def gru_back(d_next, gates, current):
        reset, update, candidate, state_part = gates
        d_cand = d_next * (1.0 - update) * (1.0 - candidate * candidate)
        d_reset = d_cand * state_part * reset * (1.0 - reset)
        d_update = d_next * (current - candidate) * update * (1.0 - update)
        dg_mail = jnp.concatenate([d_reset, d_update, d_cand], axis=1).astype(BF16)
        dg_state = jnp.concatenate([d_reset, d_update, d_cand * reset], axis=1).astype(BF16)
        d_mail = dot_nt(dg_mail, w_x[...]).astype(BF16)
        d_current = d_next * update + dot_nt(dg_state, w_h[...])
        return dg_mail, dg_state, d_mail, d_current

    dgm_one, dgs_one, dm_one, d_state = gru_back(cot_ref[...].astype(F32), gates_one, state_one)
    d_state = d_state + backward(dm_one)
    dgm_zero, dgs_zero, dm_zero, d_state = gru_back(d_state, gates_zero, state_zero)
    base_ref[...] = d_state
    level_ref[...] = jnp.concatenate([level_zero, level_one], axis=1)
    dm_ref[...] = jnp.concatenate([dm_zero, dm_one], axis=1)

    def both(first, second):
        return jnp.concatenate([first.astype(F32), second.astype(F32)], axis=0)

    dms = both(dm_zero, dm_one).T
    mails, levels = both(mail_zero, mail_one), both(level_zero, level_one)
    dgm, dgs = both(dgm_zero, dgm_one), both(dgs_zero, dgs_one)
    width = dgm.shape[1]
    rows_ref[...] = jnp.zeros_like(rows_ref)
    for k, one in enumerate((dgm, dgs)):
        total = jnp.sum(one, axis=0, keepdims=True)
        for part in range(3):
            row = 24 + 3 * k + part
            rows_ref[row : row + 1, :] = total[:, part * LANES : (part + 1) * LANES]
    small = jnp.concatenate(
        [
            dot(dms.astype(BF16), p_ref[:, hidden_units * LANES : (hidden_units + 1) * LANES]),
            dot(mails.T.astype(BF16), dgm.astype(BF16)),
            dot(levels.T.astype(BF16), dgs.astype(BF16)),
            jnp.zeros((2 * own, LANES), F32),
        ],
        axis=1,
    )

    def sorted_rows(value):
        rows = value.shape[0] // 2
        upper, lower = value[:rows], value[rows:]
        halves = [jnp.where(where_ref[0] == k, upper, lower) for k in range(2)]
        parts = []
        for k, one in enumerate(halves):
            first, second = one[: rows // 2], one[rows // 2 :]
            parts += [jnp.where(where_ref[1 + k] == side, second, first) for side in range(2)]
        return jnp.concatenate(parts, axis=0).astype(BF16)

    dms, small = sorted_rows(dms), sorted_rows(small)
    rows_in, groups, tall, wide_out = kept_first.shape
    taken = wide_out - 2 * LANES
    moves = []
    for group in range(groups):
        out = dot(dms, p_ref[:, group * taken : (group + 1) * taken]).astype(BF16)
        extra = small[:, group * 2 * LANES : (group + 1) * 2 * LANES]
        for k, ref in enumerate((given_first, kept_first, given_last, kept_last)):
            for row in range(rows_in):
                at = ((2, 0, 3, 1)[k] * rows_in + row) * tall
                sum_ref[k, row, group, :, :taken] = out[at : at + tall]
                sum_ref[k, row, group, :, taken:] = extra[at : at + tall]
                moves.append(
                    pltpu.make_async_copy(
                        sum_ref.at[k, row, group], ref.at[row, group], sum_sems.at[k, row, group]
                    )
                )
                moves[-1].start()
    for move in moves:
        move.wait()
    leave.wait()


def edge_sums(batch, batches, order_ref, edge_ref, dg_ref, w_in_ref, b_in_ref, feat_ref, before):
    blocks = edge_ref.shape[0]
    hidden_units = w_in_ref.shape[1]
    w_in, b_in = first_layer(w_in_ref, b_in_ref)
    fold = (col_ids((hidden_units, 8 * hidden_units)) >> 3) == row_ids(
        (hidden_units, 8 * hidden_units)
    )
    fold = fold.astype(F32).astype(BF16)

    def one_piece(piece, sums):
        feats, held, pairs, low = edge_piece(batches, order_ref, edge_ref, piece, batch)
        pre = dot(w_in, feats) + b_in
        sig = jax.nn.sigmoid(pre)
        spread = dot(dg_ref[batch, : 8 * hidden_units], pairs)
        spread = spread.reshape(hidden_units, 8, pre.shape[1])
        spread = jnp.where(low[None], spread, 0.0).reshape(8 * hidden_units, pre.shape[1])
        d_hidden = dot(fold, spread.astype(BF16))
        d_pre = (d_hidden * sig * (1.0 + pre * (1.0 - sig))).astype(BF16)
        out = dot(w_in_ref[...], d_pre).astype(BF16)
        for k in range(PIECE):
            at = order_ref[batch, PIECE * piece + k]
            feat_ref[at, batch * 16 : (batch + 1) * 16] = out[:, k * LANES : (k + 1) * LANES]
        ones = jnp.where(row_ids((16, pre.shape[1])) == 0, held, 0.0).astype(BF16)
        return sums + dot_nt(jnp.concatenate([feats, ones], axis=0), d_pre)

    return lax.fori_loop(0, (order_ref[batch, blocks] + PIECE - 1) // PIECE, one_piece, before)


def back_kernel(
    g_far,
    level_ref,
    dm_ref,
    base_ref,
    w_far,
    bias_ref,
    grad_ref,
    dg_ref,
    tail_ref,
    w_ref,
    g_ref,
    sems,
):
    batches, own, width = grad_ref.shape
    hidden_units = w_ref.shape[0]
    chunks = (hidden_units + tail_ref.shape[0]) // GROUP
    half = own // 2
    fetches = []
    for number in range(chunks):
        some = pl.ds(number * GROUP, min(GROUP, hidden_units - number * GROUP))
        rows = pl.ds(number * GROUP * half, GROUP * half)
        fetches += [
            pltpu.make_async_copy(w_far.at[some], w_ref.at[some], sems.at[number, 0]),
            pltpu.make_async_copy(g_far.at[:, rows], g_ref.at[:, rows], sems.at[number, 1]),
        ]
    for fetch in fetches:
        fetch.start()
    bias_blocks(bias_ref, tail_ref)

    pulls, levels = [], []
    for batch in range(batches):
        mine = slice(batch * own, (batch + 1) * own)
        pulls += [dm_ref[mine, step * width : (step + 1) * width] for step in range(2)]
        both = [doubled(level_ref[mine, step * width : (step + 1) * width]) for step in range(2)]
        levels.append(jnp.concatenate(both, axis=1))
    pulls = jnp.concatenate(pulls, axis=0)
    totals = [jnp.zeros((2 * own, 2 * width), F32) for batch in range(batches)]
    for number in range(chunks):
        fetches[2 * number].wait()
        fetches[2 * number + 1].wait()
        pulled = dot(pulls, weights_of(w_ref, tail_ref, number)).astype(BF16)
        at = slice(number * GROUP * half, (number + 1) * GROUP * half)
        for batch in range(batches):
            talls = [
                pulled_rows(pulled[(2 * batch + k) * own : (2 * batch + k + 1) * own], half)
                for k in range(2)
            ]
            totals[batch] = totals[batch] + dot(turned(g_ref[batch, at, :]), talls[0])
            d_pair = dot_nt(jnp.concatenate(talls, axis=1), levels[batch])
            for unit in range(0, GROUP, 2):
                row = (number * GROUP + unit) * 8
                for part in range(half // 8):
                    pair = [
                        d_pair[(unit + k) * half + part * 8 : (unit + k) * half + part * 8 + 8]
                        for k in range(2)
                    ]
                    dg_ref[batch, row : row + 16, part * LANES : (part + 1) * LANES] = jnp.concatenate(
                        pair, axis=0
                    ).astype(BF16)
    for batch in range(batches):
        grad = base_ref[batch * own : (batch + 1) * own] + totals[batch][:own, :width]
        grad_ref[batch] = (grad + totals[batch][own:, width:]).astype(BF16)


def edge_kernel(order_ref, edge_ref, dg_ref, w_in_ref, b_in_ref, before_ref, feat_ref, win_ref):
    batches = order_ref.shape[0]
    feat_ref[...] = jnp.zeros_like(feat_ref)
    sums = before_ref[...]
    for batch in range(batches):
        sums = edge_sums(
            batch, batches, order_ref, edge_ref, dg_ref, w_in_ref, b_in_ref, feat_ref, sums
        )
    win_ref[...] = sums


def add_kernel(first_ref, second_ref, out_ref):
    out_ref[...] = (first_ref[...].astype(F32) + second_ref[...].astype(F32)).astype(BF16)


def copy_kernel(in_ref, out_ref):
    out_ref[...] = in_ref[...]


def rows_kernel(first_ref, second_ref, out_ref, rows_ref):
    parts, tall, wide = first_ref.shape
    main = wide // LANES - 2
    for part in range(parts):
        total = first_ref[part].astype(F32) + second_ref[part].astype(F32)
        for block in range(main):
            rows_ref[pl.ds(block, tall, stride=main), :] = total[
                :, block * LANES : (block + 1) * LANES
            ]
        for k in range(2):
            start = tall * (main + k)
            rows_ref[start : start + tall, :] = total[:, (main + k) * LANES : (main + k + 1) * LANES]
        out_ref[part] = rows_ref[...].astype(BF16)


def rows_of(first, second):
    parts, tall, wide = first.shape
    shape = (tall * (wide // LANES), LANES)
    return full_call(
        rows_kernel,
        jax.ShapeDtypeStruct((parts,) + shape, BF16),
        (pltpu.VMEM(shape, F32),),
        cost_estimate=cost(1),
    )(first, second)


def place_kernel(tall, count, carried, *refs):
    at_ref, pieces = refs[0], refs[1 : 1 + count]
    outs = refs[1 + count + carried : 6 + count + carried]
    big_ref, little_ref, sems = refs[6 + count + carried :]
    d_w, d_bias, d_x, d_h, d_rest = outs
    waits = []
    slot = 0
    for k, piece in enumerate(pieces):
        chunks, rows_in, lanes = piece.shape
        main = rows_in // tall - 2
        for chunk in range(chunks):
            code = at_ref[k] ^ chunk
            line, part = code >> 2, code & 3
            at = pl.ds(pl.multiple_of(line * tall, 8), tall)
            rows = piece[chunk].astype(F32)
            for row in range(tall):
                big_ref[slot, :, row * lanes : (row + 1) * lanes] = rows[row * main : (row + 1) * main]
            copy = pltpu.make_async_copy(
                big_ref.at[slot],
                d_w.at[
                    pl.ds(pl.multiple_of(part * main, 8), main),
                    pl.ds(pl.multiple_of(line * (tall * lanes), LANES), tall * lanes),
                ],
                sems.at[slot, 0],
            )
            copy.start()
            waits.append(copy)

            for side in range(2):
                start = tall * (main + side)
                little_ref[slot, side] = rows[start : start + tall]

                def move(target, lane):
                    lane = jnp.maximum(lane, 0) * lanes
                    to = pl.ds(pl.multiple_of(jnp.minimum(lane, target.shape[1] - lanes), LANES), lanes)
                    return pltpu.make_async_copy(
                        little_ref.at[slot, side], target.at[at, to], sems.at[slot, 1 + side]
                    )

                block = 2 * part + side
                to_x, to_h = move(d_x, block - 1), move(d_h, block - 4)
                alone = move((d_bias, d_rest)[side], 0)
                lone = block == 7 * side
                pl.when(lone)(alone.start)
                pl.when((block > 0) & (block < 4))(to_x.start)
                pl.when((block > 3) & (block < 7))(to_h.start)
                waits.append(alone)
            slot += 1
    for copy in waits:
        copy.wait()


def cost(micros):
    return pl.CostEstimate(
        flops=int(micros * 1e9), bytes_accessed=int(micros * 3e6), transcendentals=0
    )


def place_pieces(tall, at, pieces, shapes, before=()):
    count = len(pieces)
    chunks, rows_in, lanes = pieces[0].shape
    slots = count * chunks
    vmem = pl.BlockSpec(memory_space=pltpu.VMEM)
    hbm = pl.BlockSpec(memory_space=pl.ANY)
    return pl.pallas_call(
        functools.partial(place_kernel, tall, count, len(before)),
        out_shape=shapes,
        in_specs=[pl.BlockSpec(memory_space=pltpu.SMEM)] + [vmem] * count + [hbm] * len(before),
        out_specs=[hbm] * len(shapes),
        scratch_shapes=(
            pltpu.VMEM((slots, rows_in // tall - 2, tall * lanes), F32),
            pltpu.VMEM((slots, 2, tall, lanes), F32),
            pltpu.SemaphoreType.DMA((slots, 3)),
        ),
        input_output_aliases={1 + count + k: k for k in range(len(before))},
        cost_estimate=cost(0.1),
        compiler_params=pltpu.CompilerParams(vmem_limit_bytes=16 * MIB),
    )(at, *pieces, *before)


def body(
    states,
    edge_feats,
    source_index,
    target_index,
    w_edge_in,
    b_edge_in,
    w_edge_out,
    b_edge_out,
    w_input,
    w_hidden,
    b_input,
    b_hidden,
    cotangent,
):
    batches, own, width = states.shape
    edges = source_index.shape[1]
    owners = lax.axis_size("edge")
    cap = max(2, 2 * edges // owners)
    feat_count, units = w_edge_in.shape

    sent = full_call(
        functools.partial(route_kernel, own),
        jax.ShapeDtypeStruct((owners, batches * feat_count + 16, cap), BF16),
        limit=60,
    )(source_index, target_index, edge_feats)
    edge_data = lax.all_to_all(sent, "edge", 0, 0, tiled=True)
    merge = max(1, LANES // cap)
    if merge > 1:
        edge_data = edge_data.reshape(owners // merge, merge, -1, cap).transpose(0, 2, 1, 3)
        edge_data = edge_data.reshape(owners // merge, -1, merge * cap)

    w_mats = w_edge_out.reshape(units, width, width)
    padded = (units + 2 + GROUP - 1) // GROUP * GROUP

    tall = width // 8
    pairs = own // 2
    blocks = edge_data.shape[0]
    core = lax.axis_index("graph")
    spot = lax.axis_index("edge")
    orders = ((0, 1, 2, 3), (2, 0, 1, 3))

    def bit(side, step):
        first, second = [(spot >> orders[k][step]) & 1 for k in range(2)]
        return jnp.where(side == 0, first, second)

    where = jnp.stack([core, bit(core, 0), bit(1 - core, 0)])
    smem = pl.BlockSpec(memory_space=pltpu.SMEM)
    vmem = pl.BlockSpec(memory_space=pltpu.VMEM)
    far = pl.BlockSpec(memory_space=pltpu.HBM)
    bias = b_edge_out.reshape(width, width)
    quarter = jax.ShapeDtypeStruct((2, 4, tall, (units // 4 + 2) * width), BF16)
    new_states, *sums, g_pairs, levels, d_mails, base, order, first = full_call(
        main_kernel,
        (
            jax.ShapeDtypeStruct((batches * own, width), BF16),
            *[quarter] * 4,
            jax.ShapeDtypeStruct((batches, padded * pairs, LANES), BF16),
            jax.ShapeDtypeStruct((batches * own, 2 * width), BF16),
            jax.ShapeDtypeStruct((batches * own, 2 * width), BF16),
            jax.ShapeDtypeStruct((batches * own, width), F32),
            jax.ShapeDtypeStruct((batches, blocks + 1), jnp.int32),
            jax.ShapeDtypeStruct((32, width), F32),
        ),
        (
            pltpu.VMEM((units, PIECE * LANES), F32),
            pltpu.VMEM((padded * 8, 512), F32),
            pltpu.VMEM((batches, padded * pairs, LANES), BF16),
            pltpu.VMEM((2 * batches * own, padded * width), BF16),
            pltpu.VMEM((units, width, width), BF16),
            pltpu.VMEM((padded - units, width, width), BF16),
            pltpu.VMEM((4,) + quarter.shape, BF16),
            pltpu.SemaphoreType.DMA((4,) + quarter.shape[:2]),
            pltpu.SemaphoreType.DMA((2,)),
        ),
        limit=60,
        in_specs=[smem] + [vmem] * 5 + [far] + [vmem] * 5,
        out_specs=[vmem] + [far] * 5 + [vmem] * 3 + [smem, vmem],
    )(
        where,
        edge_data,
        states.reshape(batches * own, width),
        cotangent.reshape(batches * own, width),
        w_edge_in,
        b_edge_in,
        w_mats,
        bias,
        w_input,
        w_hidden,
        b_input,
        b_hidden,
    )

    cores = lax.axis_size("graph")

    def to_core(value):
        return lax.ppermute(value, "graph", [(0, 1), (1, 0)])

    def swap(value, masks):
        moves = []
        for side in range(cores):
            first = side * owners
            moves += [(first + k, first + (k ^ masks[side])) for k in range(owners)]
        return lax.ppermute(value, ("graph", "edge"), moves)

    def swap_step(value, step):
        return swap(value, [1 << orders[side][step] for side in range(cores)])

    def pick(value, number):
        return lax.dynamic_index_in_dim(value, number, 0, False)

    def added(terms):
        return sum(one.astype(F32) for one in terms)

    def after(value, *others):
        return lax.optimization_barrier((value, *others))[0]

    def first_grads(pairs_in):
        return full_call(
            back_kernel,
            (
                jax.ShapeDtypeStruct((batches, own, width), BF16),
                jax.ShapeDtypeStruct((batches, padded * 8, 512), BF16),
            ),
            (
                pltpu.VMEM((padded - units, width, width), BF16),
                pltpu.VMEM((units, width, width), BF16),
                pltpu.VMEM((batches, padded * pairs, LANES), BF16),
                pltpu.SemaphoreType.DMA((padded // GROUP, 2)),
            ),
            limit=60,
            in_specs=[far] + [vmem] * 3 + [far, vmem],
            cost_estimate=cost(12),
        )(pairs_in, levels, d_mails, base, w_mats, bias)

    def second_grads(d_pairs):
        return full_call(
            edge_kernel,
            (
                jax.ShapeDtypeStruct((blocks, batches * feat_count, LANES), BF16),
                jax.ShapeDtypeStruct((32, units), F32),
            ),
            limit=60,
            in_specs=[smem] + [vmem] * 5,
            cost_estimate=cost(9),
        )(order, edge_data, d_pairs, w_edge_in, b_edge_in, first)

    def added_at(big, small, flip):
        big, more = lax.optimization_barrier((big, swap(small, [flip] * cores)))
        return big, small + more

    kept_first, kept_last, given_first, given_last = sums
    got_first, got_last = to_core(given_first), to_core(given_last)
    kept_first = full_call(
        copy_kernel, jax.ShapeDtypeStruct(kept_first.shape, BF16), cost_estimate=cost(1)
    )(kept_first)
    give = full_call(
        add_kernel, jax.ShapeDtypeStruct(kept_first.shape, BF16), cost_estimate=cost(1)
    )(kept_first, got_first)
    terms = [kept_last, got_last]
    for step in range(3):
        if step > 0:
            number = bit(core, step)
            give = added([pick(one, 1 - number) for one in terms]).astype(BF16)
            terms = [pick(one, number) for one in terms]
        got = swap_step(give, step)
        if step == 0:
            state_grad, d_pairs = first_grads(after(g_pairs, give))
            got = after(got, state_grad)
        if step == 1:
            d_feats, first = second_grads(after(d_pairs, give))
            got = after(got, first)
        if step == 2:
            got, first = added_at(got, first, 4)
        terms.append(got)
        if step == 0:
            terms = [one.reshape((2, 2, 2) + one.shape[2:]) for one in terms]
    total = added(terms).astype(BF16)
    for extra in range(3, owners.bit_length() - 1):
        got = swap(total, [1 << extra] * cores)
        if extra > 3:
            got, first = added_at(got, first, 1 << extra)
        if extra < owners.bit_length() - 2:
            total = added([total, got]).astype(BF16)
    first = first + swap(first, [1] * cores)
    got, first = added_at(got, first, 2)
    held = rows_of(total, got)

    got, first = added_at(swap_step(held, 2), first, 8)
    held = jnp.concatenate([held, got], axis=0)
    across = swap_step(held, 0)
    back = d_feats
    if merge > 1:
        back = back.reshape(blocks, -1, merge, cap).transpose(0, 2, 1, 3)
    back = after(back.reshape(owners, -1, cap), held)
    back = lax.all_to_all(back, "edge", 0, 0, tiled=True)

    near = swap_step(held, 1)
    near, more = lax.optimization_barrier((near, to_core(first)))
    first = first + more
    last = swap_step(near, 0)
    near = after(near, back)
    small_outs = (
        first[:feat_count],
        first[feat_count],
        first[24:27].reshape(-1),
        first[27:30].reshape(-1),
    )

    feat_grad = full_call(
        functools.partial(unroute_kernel, own),
        jax.ShapeDtypeStruct((batches, feat_count, edges), BF16),
        cost_estimate=cost(0.1),
    )(source_index, back.reshape(owners, batches, feat_count, cap))

    shapes = tuple(
        jax.ShapeDtypeStruct(shape, F32)
        for shape in (
            (units, width * width),
            (width, width),
            (width, 3 * width),
            (width, 3 * width),
            (width, width),
        )
    )
    outs = ()
    def place(outs, pieces):
        at = []
        for _, side, flips in pieces:
            code = side
            for step in range(3):
                code = code * 2 + bit(side, step)
            at.append((code * 2) ^ flips)
        return place_pieces(tall, jnp.stack(at), [one for one, _, _ in pieces], shapes, outs)

    outs = place((), [(held, core, 0), (to_core(held), 1 - core, 0)])
    outs, near, across = lax.optimization_barrier((outs, near, across))
    outs = place(
        outs,
        [
            (near, core, 4),
            (to_core(near), 1 - core, 4),
            (across, core, 8),
            (to_core(across), 1 - core, 8),
        ],
    )
    outs, last, feat_grad, small_outs = lax.optimization_barrier(
        (outs, last, feat_grad, small_outs)
    )
    other = to_core(last)
    outs = place(outs, [(last, core, 12)])
    outs = place(outs, [(other, 1 - core, 12)])
    d_w, d_bias, d_x, d_h, _ = outs
    return (
        new_states.reshape(batches, own, width),
        state_grad,
        feat_grad,
        small_outs[0],
        small_outs[1],
        d_w,
        d_bias.reshape(-1),
        d_x,
        d_h,
        small_outs[2],
        small_outs[3],
    )


def solution(mesh):
    spread = ("graph", "edge")
    rows = P(None, spread, None)
    edges = P(None, spread)
    feats = P(None, None, spread)
    in_specs = (rows, feats, edges, edges) + (P(),) * 8 + (rows,)
    out_specs = (rows, rows, feats) + (P(),) * 8
    return jax.shard_map(
        body,
        mesh=mesh,
        in_specs=in_specs,
        out_specs=out_specs,
        check_vma=False,
    )
```

```python
import functools

import jax
import jax.numpy as jnp
from jax import lax
from jax.experimental import pallas as pl
from jax.experimental.pallas import tpu as pltpu
from jax.sharding import PartitionSpec as P

F32 = jnp.float32
BF16 = jnp.bfloat16
LANES = 128
PIECE = 4
GROUP = 12
MIB = 1024 * 1024


def dot(first, second, dims=((1,), (0,))):
    return lax.dot_general(first, second, (dims, ((), ())), preferred_element_type=F32)


def dot_nt(first, second):
    return dot(first, second, ((1,), (1,)))


def row_ids(shape):
    return lax.broadcasted_iota(jnp.int32, shape, 0)


def col_ids(shape):
    return lax.broadcasted_iota(jnp.int32, shape, 1)


def full_call(kernel, out_shape, scratch=(), limit=16, **more):
    return pl.pallas_call(
        kernel,
        out_shape=out_shape,
        scratch_shapes=scratch,
        compiler_params=pltpu.CompilerParams(vmem_limit_bytes=limit * MIB),
        **more,
    )


def ranks_of(owner, owners):
    hits = (row_ids((owners, owner.shape[1])) == owner).astype(F32)
    before = (row_ids((LANES, LANES)) < col_ids((LANES, LANES))).astype(BF16)
    seen = jnp.zeros((owners, 1), F32)
    ranks = []
    for start in range(0, owner.shape[1], LANES):
        part = hits[:, start : start + LANES]
        place = dot(part.astype(BF16), before) + seen
        ranks.append(jnp.sum(part * place, axis=0, keepdims=True))
        seen = seen + jnp.sum(part, axis=1, keepdims=True)
    return hits, jnp.concatenate(ranks, axis=1)


def route_kernel(own_rows, src_ref, dst_ref, feat_ref, out_ref):
    owners, rows, cap = out_ref.shape
    batches, feats, edges = feat_ref.shape
    shift = own_rows.bit_length() - 1
    marks = [jnp.zeros((16, cap), F32)] * owners
    for batch in range(batches):
        source, target = src_ref[batch : batch + 1], dst_ref[batch : batch + 1]
        owner = source >> shift
        hits, rank = ranks_of(owner, owners)
        spots = (row_ids((cap, edges)) == rank.astype(jnp.int32)).astype(BF16)
        line = row_ids((16, edges)) - 3 * batch
        first = owner << shift
        extra = jnp.where(line == 0, source - first, jnp.where(line == 1, target - first, 1))
        extra = jnp.where((line >= 0) & (line < 3), extra, 0).astype(F32)
        load = jnp.concatenate([feat_ref[batch].astype(F32), extra], axis=0)
        masked = [(load * hits[part : part + 1]).astype(BF16) for part in range(owners)]
        out = dot_nt(jnp.concatenate(masked, axis=0), spots)
        for part in range(owners):
            tile = out[part * (feats + 16) : (part + 1) * (feats + 16)]
            out_ref[part, batch * feats : (batch + 1) * feats] = tile[:feats].astype(BF16)
            marks[part] = marks[part] + tile[feats:]
    for part in range(owners):
        out_ref[part, batches * feats :] = marks[part].astype(BF16)


def unroute_kernel(own_rows, src_ref, back_ref, out_ref):
    owners, batches, rows, cap = back_ref.shape
    edges = src_ref.shape[1]
    shift = own_rows.bit_length() - 1
    for batch in range(batches):
        hits, rank = ranks_of(src_ref[batch : batch + 1] >> shift, owners)
        spots = (row_ids((cap, edges)) == rank.astype(jnp.int32)).astype(BF16)
        parts = [back_ref[part, batch] for part in range(owners)]
        spread = dot(jnp.concatenate(parts, axis=0), spots)
        total = jnp.zeros((rows, edges), F32)
        for part in range(owners):
            total = total + spread[part * rows : (part + 1) * rows] * hits[part : part + 1]
        out_ref[batch] = total.astype(BF16)


def edge_piece(batches, order_ref, edge_ref, piece, batch):
    some = [edge_ref[order_ref[batch, PIECE * piece + k]] for k in range(PIECE)]
    block = jnp.concatenate(some, axis=1)
    feats, marks = block[batch * 16 : (batch + 1) * 16], block[batches * 16 :].astype(F32)
    source = marks[3 * batch : 3 * batch + 1].astype(jnp.int32)
    target = marks[3 * batch + 1 : 3 * batch + 2].astype(jnp.int32)
    held = marks[3 * batch + 2 : 3 * batch + 3]
    code = ((target >> 3) & 3) * 128 + (target >> 5) * 64 + source
    code = jnp.where(held > 0.5, code, -1)
    pairs = (row_ids((512, block.shape[1])) == code).astype(BF16)
    low = row_ids((8, block.shape[1])) == (target & 7)
    return feats, held, pairs, low


def order_blocks(batches, edge_ref, order_ref):
    blocks = edge_ref.shape[0]
    for batch in range(batches):
        front, back = jnp.int32(0), jnp.int32(blocks - 1)
        row = 3 * batch + 2
        for block in range(blocks):
            marks = edge_ref[block, batches * 16 :].astype(F32)
            held = jnp.max(marks[row : row + 1]) > 0.5
            order_ref[batch, jnp.where(held, front, back)] = jnp.int32(block)
            step = held.astype(jnp.int32)
            front, back = front + step, back - (1 - step)
        order_ref[batch, blocks] = front


def first_layer(w_in_ref, b_in_ref):
    bias = jnp.broadcast_to(b_in_ref[...].reshape(1, -1), (8, b_in_ref.shape[0]))
    return w_in_ref[...].astype(F32).T.astype(BF16), bias.T[:, :1]


def gates_of(mail_low, level, w_x, w_h, b_x, b_h):
    width = level.shape[1]
    from_mail = dot(mail_low, w_x[...]) + b_x[...].reshape(1, -1)
    from_state = dot(level, w_h[...]) + b_h[...].reshape(1, -1)
    reset = jax.nn.sigmoid(from_mail[:, :width] + from_state[:, :width])
    update = jax.nn.sigmoid(from_mail[:, width : 2 * width] + from_state[:, width : 2 * width])
    state_part = from_state[:, 2 * width :]
    candidate = jnp.tanh(from_mail[:, 2 * width :] + reset * state_part)
    return reset, update, candidate, state_part


def doubled(level):
    blank = jnp.zeros_like(level)
    return jnp.concatenate(
        [jnp.concatenate([level, blank], axis=1), jnp.concatenate([blank, level], axis=1)], axis=0
    )


def bias_blocks(bias_ref, tail_ref):
    tail_ref[...] = jnp.zeros_like(tail_ref)
    high = bias_ref[...].astype(BF16)
    tail_ref[0] = high
    tail_ref[1] = (bias_ref[...] - high.astype(F32)).astype(BF16)


def turned(tile):
    size = tile.shape[1]
    eye = (row_ids((size, size)) == col_ids((size, size))).astype(F32).astype(BF16)
    return dot_nt(eye, tile).astype(BF16)


def weights_of(w_ref, tail_ref, number):
    units = w_ref.shape[0]
    blocks = []
    for unit in range(number * GROUP, (number + 1) * GROUP):
        blocks.append(w_ref[unit] if unit < units else tail_ref[unit - units])
    return jnp.concatenate(blocks, axis=1)


def pulled_rows(pulled, half):
    rows = []
    for start in range(0, pulled.shape[1], LANES):
        tile = pulled[:, start : start + LANES]
        rows.append(jnp.concatenate([tile[:half], tile[half:]], axis=1))
    return jnp.concatenate(rows, axis=0)


def main_kernel(
    where_ref,
    edge_ref,
    state_ref,
    cot_ref,
    w_in_ref,
    b_in_ref,
    w_far,
    bias_ref,
    w_x,
    w_h,
    b_x,
    b_h,
    new_ref,
    kept_first,
    kept_last,
    given_first,
    given_last,
    g_far,
    level_ref,
    dm_ref,
    base_ref,
    order_ref,
    rows_ref,
    hid_ref,
    acc_ref,
    g_ref,
    p_ref,
    w_ref,
    tail_ref,
    sum_ref,
    sum_sems,
    sems,
):
    fetch = pltpu.make_async_copy(w_far, w_ref, sems.at[0])
    fetch.start()
    blocks = edge_ref.shape[0]
    batches = g_ref.shape[0]
    hidden_units = hid_ref.shape[0]
    units = acc_ref.shape[0] // 8
    own = state_ref.shape[0] // batches
    half = own // 2
    span = GROUP * half
    wide = GROUP * LANES
    chunks = units // GROUP
    order_blocks(batches, edge_ref, order_ref)
    bias_blocks(bias_ref, tail_ref)
    w_in, b_in = first_layer(w_in_ref, b_in_ref)

    for batch in range(batches):
        acc_ref[...] = jnp.zeros_like(acc_ref)

        def add_piece(piece, carry):
            feats, held, pairs, low = edge_piece(batches, order_ref, edge_ref, piece, batch)
            pre = dot(w_in, feats) + b_in
            hid_ref[...] = (pre * jax.nn.sigmoid(pre)).astype(BF16).astype(F32)
            ones = jnp.where(low, 1.0, 0.0)
            parts = []
            for unit in range(0, hidden_units, 2):
                two = [jnp.where(low, hid_ref[unit + k : unit + k + 1], 0.0) for k in range(2)]
                parts.append(jnp.concatenate(two, axis=0).astype(BF16))
            parts.append(jnp.concatenate([ones, ones], axis=0).astype(BF16))
            parts.append(jnp.zeros((8 * (units - hidden_units - 2), pre.shape[1]), BF16))
            acc_ref[...] += dot_nt(jnp.concatenate(parts, axis=0), pairs)
            return carry

        lax.fori_loop(0, (order_ref[batch, blocks] + PIECE - 1) // PIECE, add_piece, 0)

        def place(step, carry):
            for four in range(3):
                rows = []
                for k in range(4):
                    for part in range(4):
                        start = pl.multiple_of(step * 96 + four * 32 + k * 8, 8)
                        rows.append(acc_ref[pl.ds(start, 8), part * LANES : (part + 1) * LANES])
                at = pl.ds(pl.multiple_of((step * 3 + four) * LANES, LANES), LANES)
                g_ref[batch, at, :] = jnp.concatenate(rows, axis=0).astype(BF16)
            return carry

        lax.fori_loop(0, units // 12, place, 0)

    def forward(step, level):
        two = [doubled(level[batch * own : (batch + 1) * own]) for batch in range(batches)]
        mail = jnp.zeros((batches * own, LANES), F32)
        base = step * batches * own
        for number in range(chunks):
            for batch in range(batches):
                out = dot(g_ref[batch, number * span : (number + 1) * span, :], two[batch])
                out = out.astype(BF16)
                for unit in range(GROUP):
                    lane = number * wide + unit * LANES
                    for part in range(2):
                        row = base + batch * own + part * half
                        p_ref[row : row + half, lane : lane + LANES] = out[
                            unit * half : (unit + 1) * half, part * LANES : (part + 1) * LANES
                        ]
            rows = p_ref[base : base + batches * own, number * wide : (number + 1) * wide]
            mail = mail + dot_nt(rows, weights_of(w_ref, tail_ref, number))
        return mail

    def backward(d_mail):
        sums = [jnp.zeros((LANES, 2 * LANES), F32) for batch in range(batches)]
        for number in range(chunks):
            pulled = dot(d_mail, weights_of(w_ref, tail_ref, number)).astype(BF16)
            at = slice(number * span, (number + 1) * span)
            for batch in range(batches):
                tall = pulled_rows(pulled[batch * own : (batch + 1) * own], half)
                sums[batch] = sums[batch] + dot(turned(g_ref[batch, at, :]), tall)
        return jnp.concatenate([one[:own, :LANES] + one[own:, LANES:] for one in sums], axis=0)

    weights = (w_x, w_h, b_x, b_h)
    level_zero = state_ref[...]
    state_zero = level_zero.astype(F32)
    leave = pltpu.make_async_copy(g_ref, g_far, sems.at[1])
    leave.start()
    fetch.wait()
    mail_zero = forward(0, level_zero).astype(BF16)
    gates_zero = gates_of(mail_zero, level_zero, *weights)
    state_one = (1.0 - gates_zero[1]) * gates_zero[2] + gates_zero[1] * state_zero
    level_one = state_one.astype(BF16)
    mail_one = forward(1, level_one).astype(BF16)
    gates_one = gates_of(mail_one, level_one, *weights)
    new_ref[...] = ((1.0 - gates_one[1]) * gates_one[2] + gates_one[1] * state_one).astype(BF16)

    def gru_back(d_next, gates, current):
        reset, update, candidate, state_part = gates
        d_cand = d_next * (1.0 - update) * (1.0 - candidate * candidate)
        d_reset = d_cand * state_part * reset * (1.0 - reset)
        d_update = d_next * (current - candidate) * update * (1.0 - update)
        dg_mail = jnp.concatenate([d_reset, d_update, d_cand], axis=1).astype(BF16)
        dg_state = jnp.concatenate([d_reset, d_update, d_cand * reset], axis=1).astype(BF16)
        d_mail = dot_nt(dg_mail, w_x[...]).astype(BF16)
        d_current = d_next * update + dot_nt(dg_state, w_h[...])
        return dg_mail, dg_state, d_mail, d_current

    dgm_one, dgs_one, dm_one, d_state = gru_back(cot_ref[...].astype(F32), gates_one, state_one)
    d_state = d_state + backward(dm_one)
    dgm_zero, dgs_zero, dm_zero, d_state = gru_back(d_state, gates_zero, state_zero)
    base_ref[...] = d_state
    level_ref[...] = jnp.concatenate([level_zero, level_one], axis=1)
    dm_ref[...] = jnp.concatenate([dm_zero, dm_one], axis=1)

    def both(first, second):
        return jnp.concatenate([first.astype(F32), second.astype(F32)], axis=0)

    dms = both(dm_zero, dm_one).T
    mails, levels = both(mail_zero, mail_one), both(level_zero, level_one)
    dgm, dgs = both(dgm_zero, dgm_one), both(dgs_zero, dgs_one)
    width = dgm.shape[1]
    rows_ref[...] = jnp.zeros_like(rows_ref)
    for k, one in enumerate((dgm, dgs)):
        total = jnp.sum(one, axis=0, keepdims=True)
        for part in range(3):
            row = 24 + 3 * k + part
            rows_ref[row : row + 1, :] = total[:, part * LANES : (part + 1) * LANES]
    small = jnp.concatenate(
        [
            dot(dms.astype(BF16), p_ref[:, hidden_units * LANES : (hidden_units + 1) * LANES]),
            dot(mails.T.astype(BF16), dgm.astype(BF16)),
            dot(levels.T.astype(BF16), dgs.astype(BF16)),
            jnp.zeros((2 * own, LANES), F32),
        ],
        axis=1,
    )

    def sorted_rows(value):
        rows = value.shape[0] // 2
        upper, lower = value[:rows], value[rows:]
        halves = [jnp.where(where_ref[0] == k, upper, lower) for k in range(2)]
        parts = []
        for k, one in enumerate(halves):
            first, second = one[: rows // 2], one[rows // 2 :]
            parts += [jnp.where(where_ref[1 + k] == side, second, first) for side in range(2)]
        return jnp.concatenate(parts, axis=0).astype(BF16)

    dms, small = sorted_rows(dms), sorted_rows(small)
    rows_in, groups, tall, wide_out = kept_first.shape
    taken = wide_out - 2 * LANES
    moves = []
    for group in range(groups):
        out = dot(dms, p_ref[:, group * taken : (group + 1) * taken]).astype(BF16)
        extra = small[:, group * 2 * LANES : (group + 1) * 2 * LANES]
        for k, ref in enumerate((given_first, kept_first, given_last, kept_last)):
            for row in range(rows_in):
                at = ((2, 0, 3, 1)[k] * rows_in + row) * tall
                sum_ref[k, row, group, :, :taken] = out[at : at + tall]
                sum_ref[k, row, group, :, taken:] = extra[at : at + tall]
                moves.append(
                    pltpu.make_async_copy(
                        sum_ref.at[k, row, group], ref.at[row, group], sum_sems.at[k, row, group]
                    )
                )
                moves[-1].start()
    for move in moves:
        move.wait()
    leave.wait()


def edge_sums(batch, batches, order_ref, edge_ref, dg_ref, w_in_ref, b_in_ref, feat_ref, before):
    blocks = edge_ref.shape[0]
    hidden_units = w_in_ref.shape[1]
    w_in, b_in = first_layer(w_in_ref, b_in_ref)
    fold = (col_ids((hidden_units, 8 * hidden_units)) >> 3) == row_ids(
        (hidden_units, 8 * hidden_units)
    )
    fold = fold.astype(F32).astype(BF16)

    def one_piece(piece, sums):
        feats, held, pairs, low = edge_piece(batches, order_ref, edge_ref, piece, batch)
        pre = dot(w_in, feats) + b_in
        sig = jax.nn.sigmoid(pre)
        spread = dot(dg_ref[batch, : 8 * hidden_units], pairs)
        spread = spread.reshape(hidden_units, 8, pre.shape[1])
        spread = jnp.where(low[None], spread, 0.0).reshape(8 * hidden_units, pre.shape[1])
        d_hidden = dot(fold, spread.astype(BF16))
        d_pre = (d_hidden * sig * (1.0 + pre * (1.0 - sig))).astype(BF16)
        out = dot(w_in_ref[...], d_pre).astype(BF16)
        for k in range(PIECE):
            at = order_ref[batch, PIECE * piece + k]
            feat_ref[at, batch * 16 : (batch + 1) * 16] = out[:, k * LANES : (k + 1) * LANES]
        ones = jnp.where(row_ids((16, pre.shape[1])) == 0, held, 0.0).astype(BF16)
        return sums + dot_nt(jnp.concatenate([feats, ones], axis=0), d_pre)

    return lax.fori_loop(0, (order_ref[batch, blocks] + PIECE - 1) // PIECE, one_piece, before)


def back_kernel(
    g_far,
    level_ref,
    dm_ref,
    base_ref,
    w_far,
    bias_ref,
    grad_ref,
    dg_ref,
    tail_ref,
    w_ref,
    g_ref,
    sems,
):
    batches, own, width = grad_ref.shape
    hidden_units = w_ref.shape[0]
    chunks = (hidden_units + tail_ref.shape[0]) // GROUP
    half = own // 2
    fetches = []
    for number in range(chunks):
        some = pl.ds(number * GROUP, min(GROUP, hidden_units - number * GROUP))
        rows = pl.ds(number * GROUP * half, GROUP * half)
        fetches += [
            pltpu.make_async_copy(w_far.at[some], w_ref.at[some], sems.at[number, 0]),
            pltpu.make_async_copy(g_far.at[:, rows], g_ref.at[:, rows], sems.at[number, 1]),
        ]
    for fetch in fetches:
        fetch.start()
    bias_blocks(bias_ref, tail_ref)

    pulls, levels = [], []
    for batch in range(batches):
        mine = slice(batch * own, (batch + 1) * own)
        pulls += [dm_ref[mine, step * width : (step + 1) * width] for step in range(2)]
        both = [doubled(level_ref[mine, step * width : (step + 1) * width]) for step in range(2)]
        levels.append(jnp.concatenate(both, axis=1))
    pulls = jnp.concatenate(pulls, axis=0)
    totals = [jnp.zeros((2 * own, 2 * width), F32) for batch in range(batches)]
    for number in range(chunks):
        fetches[2 * number].wait()
        fetches[2 * number + 1].wait()
        pulled = dot(pulls, weights_of(w_ref, tail_ref, number)).astype(BF16)
        at = slice(number * GROUP * half, (number + 1) * GROUP * half)
        for batch in range(batches):
            talls = [
                pulled_rows(pulled[(2 * batch + k) * own : (2 * batch + k + 1) * own], half)
                for k in range(2)
            ]
            totals[batch] = totals[batch] + dot(turned(g_ref[batch, at, :]), talls[0])
            d_pair = dot_nt(jnp.concatenate(talls, axis=1), levels[batch])
            for unit in range(0, GROUP, 2):
                row = (number * GROUP + unit) * 8
                for part in range(half // 8):
                    pair = [
                        d_pair[(unit + k) * half + part * 8 : (unit + k) * half + part * 8 + 8]
                        for k in range(2)
                    ]
                    dg_ref[batch, row : row + 16, part * LANES : (part + 1) * LANES] = jnp.concatenate(
                        pair, axis=0
                    ).astype(BF16)
    for batch in range(batches):
        grad = base_ref[batch * own : (batch + 1) * own] + totals[batch][:own, :width]
        grad_ref[batch] = (grad + totals[batch][own:, width:]).astype(BF16)


def edge_kernel(order_ref, edge_ref, dg_ref, w_in_ref, b_in_ref, before_ref, feat_ref, win_ref):
    batches = order_ref.shape[0]
    feat_ref[...] = jnp.zeros_like(feat_ref)
    sums = before_ref[...]
    for batch in range(batches):
        sums = edge_sums(
            batch, batches, order_ref, edge_ref, dg_ref, w_in_ref, b_in_ref, feat_ref, sums
        )
    win_ref[...] = sums


def add_kernel(first_ref, second_ref, out_ref):
    out_ref[...] = (first_ref[...].astype(F32) + second_ref[...].astype(F32)).astype(BF16)


def copy_kernel(in_ref, out_ref):
    out_ref[...] = in_ref[...]


def rows_kernel(first_ref, second_ref, out_ref, rows_ref):
    parts, tall, wide = first_ref.shape
    main = wide // LANES - 2
    for part in range(parts):
        total = first_ref[part].astype(F32) + second_ref[part].astype(F32)
        for block in range(main):
            rows_ref[pl.ds(block, tall, stride=main), :] = total[
                :, block * LANES : (block + 1) * LANES
            ]
        for k in range(2):
            start = tall * (main + k)
            rows_ref[start : start + tall, :] = total[:, (main + k) * LANES : (main + k + 1) * LANES]
        out_ref[part] = rows_ref[...].astype(BF16)


def rows_of(first, second):
    parts, tall, wide = first.shape
    shape = (tall * (wide // LANES), LANES)
    return full_call(
        rows_kernel,
        jax.ShapeDtypeStruct((parts,) + shape, BF16),
        (pltpu.VMEM(shape, F32),),
        cost_estimate=cost(1),
    )(first, second)


def place_kernel(tall, count, carried, *refs):
    at_ref, pieces = refs[0], refs[1 : 1 + count]
    outs = refs[1 + count + carried : 6 + count + carried]
    big_ref, little_ref, sems = refs[6 + count + carried :]
    d_w, d_bias, d_x, d_h, d_rest = outs
    waits = []
    slot = 0
    for k, piece in enumerate(pieces):
        chunks, rows_in, lanes = piece.shape
        main = rows_in // tall - 2
        for chunk in range(chunks):
            code = at_ref[k] ^ chunk
            line, part = code >> 2, code & 3
            at = pl.ds(pl.multiple_of(line * tall, 8), tall)
            rows = piece[chunk].astype(F32)
            for row in range(tall):
                big_ref[slot, :, row * lanes : (row + 1) * lanes] = rows[row * main : (row + 1) * main]
            copy = pltpu.make_async_copy(
                big_ref.at[slot],
                d_w.at[
                    pl.ds(pl.multiple_of(part * main, 8), main),
                    pl.ds(pl.multiple_of(line * (tall * lanes), LANES), tall * lanes),
                ],
                sems.at[slot, 0],
            )
            copy.start()
            waits.append(copy)

            for side in range(2):
                start = tall * (main + side)
                little_ref[slot, side] = rows[start : start + tall]

                def move(target, lane):
                    lane = jnp.maximum(lane, 0) * lanes
                    to = pl.ds(pl.multiple_of(jnp.minimum(lane, target.shape[1] - lanes), LANES), lanes)
                    return pltpu.make_async_copy(
                        little_ref.at[slot, side], target.at[at, to], sems.at[slot, 1 + side]
                    )

                block = 2 * part + side
                to_x, to_h = move(d_x, block - 1), move(d_h, block - 4)
                alone = move((d_bias, d_rest)[side], 0)
                lone = block == 7 * side
                pl.when(lone)(alone.start)
                pl.when((block > 0) & (block < 4))(to_x.start)
                pl.when((block > 3) & (block < 7))(to_h.start)
                waits.append(alone)
            slot += 1
    for copy in waits:
        copy.wait()


def cost(micros):
    return pl.CostEstimate(
        flops=int(micros * 1e9), bytes_accessed=int(micros * 3e6), transcendentals=0
    )


def place_pieces(tall, at, pieces, shapes, before=()):
    count = len(pieces)
    chunks, rows_in, lanes = pieces[0].shape
    slots = count * chunks
    vmem = pl.BlockSpec(memory_space=pltpu.VMEM)
    hbm = pl.BlockSpec(memory_space=pl.ANY)
    return pl.pallas_call(
        functools.partial(place_kernel, tall, count, len(before)),
        out_shape=shapes,
        in_specs=[pl.BlockSpec(memory_space=pltpu.SMEM)] + [vmem] * count + [hbm] * len(before),
        out_specs=[hbm] * len(shapes),
        scratch_shapes=(
            pltpu.VMEM((slots, rows_in // tall - 2, tall * lanes), F32),
            pltpu.VMEM((slots, 2, tall, lanes), F32),
            pltpu.SemaphoreType.DMA((slots, 3)),
        ),
        input_output_aliases={1 + count + k: k for k in range(len(before))},
        cost_estimate=cost(slots / 4),
        compiler_params=pltpu.CompilerParams(vmem_limit_bytes=16 * MIB),
    )(at, *pieces, *before)


def body(
    states,
    edge_feats,
    source_index,
    target_index,
    w_edge_in,
    b_edge_in,
    w_edge_out,
    b_edge_out,
    w_input,
    w_hidden,
    b_input,
    b_hidden,
    cotangent,
):
    batches, own, width = states.shape
    edges = source_index.shape[1]
    owners = lax.axis_size("edge")
    cap = max(2, 2 * edges // owners)
    feat_count, units = w_edge_in.shape

    sent = full_call(
        functools.partial(route_kernel, own),
        jax.ShapeDtypeStruct((owners, batches * feat_count + 16, cap), BF16),
        limit=60,
    )(source_index, target_index, edge_feats)
    edge_data = lax.all_to_all(sent, "edge", 0, 0, tiled=True)
    merge = max(1, LANES // cap)
    if merge > 1:
        edge_data = edge_data.reshape(owners // merge, merge, -1, cap).transpose(0, 2, 1, 3)
        edge_data = edge_data.reshape(owners // merge, -1, merge * cap)

    w_mats = w_edge_out.reshape(units, width, width)
    padded = (units + 2 + GROUP - 1) // GROUP * GROUP

    tall = width // 8
    pairs = own // 2
    blocks = edge_data.shape[0]
    core = lax.axis_index("graph")
    spot = lax.axis_index("edge")
    orders = ((0, 1, 2, 3), (2, 0, 1, 3))

    def bit(side, step):
        first, second = [(spot >> orders[k][step]) & 1 for k in range(2)]
        return jnp.where(side == 0, first, second)

    where = jnp.stack([core, bit(core, 0), bit(1 - core, 0)])
    smem = pl.BlockSpec(memory_space=pltpu.SMEM)
    vmem = pl.BlockSpec(memory_space=pltpu.VMEM)
    far = pl.BlockSpec(memory_space=pltpu.HBM)
    bias = b_edge_out.reshape(width, width)
    quarter = jax.ShapeDtypeStruct((2, 4, tall, (units // 4 + 2) * width), BF16)
    new_states, *sums, g_pairs, levels, d_mails, base, order, first = full_call(
        main_kernel,
        (
            jax.ShapeDtypeStruct((batches * own, width), BF16),
            *[quarter] * 4,
            jax.ShapeDtypeStruct((batches, padded * pairs, LANES), BF16),
            jax.ShapeDtypeStruct((batches * own, 2 * width), BF16),
            jax.ShapeDtypeStruct((batches * own, 2 * width), BF16),
            jax.ShapeDtypeStruct((batches * own, width), F32),
            jax.ShapeDtypeStruct((batches, blocks + 1), jnp.int32),
            jax.ShapeDtypeStruct((32, width), F32),
        ),
        (
            pltpu.VMEM((units, PIECE * LANES), F32),
            pltpu.VMEM((padded * 8, 512), F32),
            pltpu.VMEM((batches, padded * pairs, LANES), BF16),
            pltpu.VMEM((2 * batches * own, padded * width), BF16),
            pltpu.VMEM((units, width, width), BF16),
            pltpu.VMEM((padded - units, width, width), BF16),
            pltpu.VMEM((4,) + quarter.shape, BF16),
            pltpu.SemaphoreType.DMA((4,) + quarter.shape[:2]),
            pltpu.SemaphoreType.DMA((2,)),
        ),
        limit=60,
        in_specs=[smem] + [vmem] * 5 + [far] + [vmem] * 5,
        out_specs=[vmem] + [far] * 5 + [vmem] * 3 + [smem, vmem],
    )(
        where,
        edge_data,
        states.reshape(batches * own, width),
        cotangent.reshape(batches * own, width),
        w_edge_in,
        b_edge_in,
        w_mats,
        bias,
        w_input,
        w_hidden,
        b_input,
        b_hidden,
    )

    cores = lax.axis_size("graph")

    def to_core(value):
        return lax.ppermute(value, "graph", [(0, 1), (1, 0)])

    def swap(value, masks):
        moves = []
        for side in range(cores):
            first = side * owners
            moves += [(first + k, first + (k ^ masks[side])) for k in range(owners)]
        return lax.ppermute(value, ("graph", "edge"), moves)

    def swap_step(value, step):
        return swap(value, [1 << orders[side][step] for side in range(cores)])

    def pick(value, number):
        return lax.dynamic_index_in_dim(value, number, 0, False)

    def added(terms):
        return sum(one.astype(F32) for one in terms)

    def after(value, *others):
        return lax.optimization_barrier((value, *others))[0]

    def first_grads(pairs_in):
        return full_call(
            back_kernel,
            (
                jax.ShapeDtypeStruct((batches, own, width), BF16),
                jax.ShapeDtypeStruct((batches, padded * 8, 512), BF16),
            ),
            (
                pltpu.VMEM((padded - units, width, width), BF16),
                pltpu.VMEM((units, width, width), BF16),
                pltpu.VMEM((batches, padded * pairs, LANES), BF16),
                pltpu.SemaphoreType.DMA((padded // GROUP, 2)),
            ),
            limit=60,
            in_specs=[far] + [vmem] * 3 + [far, vmem],
            cost_estimate=cost(12),
        )(pairs_in, levels, d_mails, base, w_mats, bias)

    def second_grads(d_pairs):
        return full_call(
            edge_kernel,
            (
                jax.ShapeDtypeStruct((blocks, batches * feat_count, LANES), BF16),
                jax.ShapeDtypeStruct((32, units), F32),
            ),
            limit=60,
            in_specs=[smem] + [vmem] * 5,
            cost_estimate=cost(9),
        )(order, edge_data, d_pairs, w_edge_in, b_edge_in, first)

    def added_at(big, small, flip):
        big, more = lax.optimization_barrier((big, swap(small, [flip] * cores)))
        return big, small + more

    kept_first, kept_last, given_first, given_last = sums
    got_first, got_last = to_core(given_first), to_core(given_last)
    kept_first = full_call(
        copy_kernel, jax.ShapeDtypeStruct(kept_first.shape, BF16), cost_estimate=cost(1)
    )(kept_first)
    give = full_call(
        add_kernel, jax.ShapeDtypeStruct(kept_first.shape, BF16), cost_estimate=cost(1)
    )(kept_first, got_first)
    terms = [kept_last, got_last]
    for step in range(3):
        if step > 0:
            number = bit(core, step)
            give = added([pick(one, 1 - number) for one in terms]).astype(BF16)
            terms = [pick(one, number) for one in terms]
        got = swap_step(give, step)
        if step == 0:
            state_grad, d_pairs = first_grads(after(g_pairs, give))
            got = after(got, state_grad)
        if step == 1:
            d_feats, first = second_grads(after(d_pairs, give))
            got = after(got, first)
        if step == 2:
            got, first = added_at(got, first, 4)
        terms.append(got)
        if step == 0:
            terms = [one.reshape((2, 2, 2) + one.shape[2:]) for one in terms]
    total = added(terms).astype(BF16)
    for extra in range(3, owners.bit_length() - 1):
        got = swap(total, [1 << extra] * cores)
        if extra > 3:
            got, first = added_at(got, first, 1 << extra)
        if extra < owners.bit_length() - 2:
            total = added([total, got]).astype(BF16)
    first = first + swap(first, [1] * cores)
    got, first = added_at(got, first, 2)
    held = rows_of(total, got)

    got, first = added_at(swap_step(held, 2), first, 8)
    held = jnp.concatenate([held, got], axis=0)
    across = swap_step(held, 0)
    back = d_feats
    if merge > 1:
        back = back.reshape(blocks, -1, merge, cap).transpose(0, 2, 1, 3)
    back = after(back.reshape(owners, -1, cap), held)
    back = lax.all_to_all(back, "edge", 0, 0, tiled=True)

    shapes = tuple(
        jax.ShapeDtypeStruct(shape, F32)
        for shape in (
            (units, width * width),
            (width, width),
            (width, 3 * width),
            (width, 3 * width),
            (width, width),
        )
    )
    outs = ()
    def place(outs, pieces):
        at = []
        for _, side, flips in pieces:
            code = side
            for step in range(3):
                code = code * 2 + bit(side, step)
            at.append((code * 2) ^ flips)
        return place_pieces(tall, jnp.stack(at), [one for one, _, _ in pieces], shapes, outs)

    outs = place((), [(held, core, 0), (to_core(held), 1 - core, 0)])
    outs, near, more = lax.optimization_barrier((outs, swap_step(held, 1), to_core(first)))
    first = first + more
    small_outs = (
        first[:feat_count],
        first[feat_count],
        first[24:27].reshape(-1),
        first[27:30].reshape(-1),
    )
    last = swap_step(near, 0)
    outs, near_other, across_other, back = lax.optimization_barrier(
        (outs, to_core(near), to_core(across), back)
    )
    feat_grad = full_call(
        functools.partial(unroute_kernel, own),
        jax.ShapeDtypeStruct((batches, feat_count, edges), BF16),
        cost_estimate=cost(1.4),
    )(source_index, back.reshape(owners, batches, feat_count, cap))
    outs = place(
        outs,
        [
            (near, core, 4),
            (near_other, 1 - core, 4),
            (across, core, 8),
            (across_other, 1 - core, 8),
        ],
    )
    outs, last, feat_grad, small_outs = lax.optimization_barrier(
        (outs, last, feat_grad, small_outs)
    )
    other = to_core(last)
    outs = place(outs, [(last, core, 12)])
    outs = place(outs, [(other, 1 - core, 12)])
    d_w, d_bias, d_x, d_h, _ = outs
    return (
        new_states.reshape(batches, own, width),
        state_grad,
        feat_grad,
        small_outs[0],
        small_outs[1],
        d_w,
        d_bias.reshape(-1),
        d_x,
        d_h,
        small_outs[2],
        small_outs[3],
    )


def solution(mesh):
    spread = ("graph", "edge")
    rows = P(None, spread, None)
    edges = P(None, spread)
    feats = P(None, None, spread)
    in_specs = (rows, feats, edges, edges) + (P(),) * 8 + (rows,)
    out_specs = (rows, rows, feats) + (P(),) * 8
    return jax.shard_map(
        body,
        mesh=mesh,
        in_specs=in_specs,
        out_specs=out_specs,
        check_vma=False,
    )
```

```python
import functools

import jax
import jax.numpy as jnp
from jax import lax
from jax.experimental import pallas as pl
from jax.experimental.pallas import tpu as pltpu
from jax.sharding import PartitionSpec as P

F32 = jnp.float32
BF16 = jnp.bfloat16
LANES = 128
PIECE = 4
GROUP = 12
MIB = 1024 * 1024


def dot(first, second, dims=((1,), (0,))):
    return lax.dot_general(first, second, (dims, ((), ())), preferred_element_type=F32)


def dot_nt(first, second):
    return dot(first, second, ((1,), (1,)))


def row_ids(shape):
    return lax.broadcasted_iota(jnp.int32, shape, 0)


def col_ids(shape):
    return lax.broadcasted_iota(jnp.int32, shape, 1)


def full_call(kernel, out_shape, scratch=(), limit=16, **more):
    return pl.pallas_call(
        kernel,
        out_shape=out_shape,
        scratch_shapes=scratch,
        compiler_params=pltpu.CompilerParams(vmem_limit_bytes=limit * MIB),
        **more,
    )


def ranks_of(owner, owners):
    hits = (row_ids((owners, owner.shape[1])) == owner).astype(F32)
    before = (row_ids((LANES, LANES)) < col_ids((LANES, LANES))).astype(BF16)
    seen = jnp.zeros((owners, 1), F32)
    ranks = []
    for start in range(0, owner.shape[1], LANES):
        part = hits[:, start : start + LANES]
        place = dot(part.astype(BF16), before) + seen
        ranks.append(jnp.sum(part * place, axis=0, keepdims=True))
        seen = seen + jnp.sum(part, axis=1, keepdims=True)
    return hits, jnp.concatenate(ranks, axis=1)


def route_kernel(own_rows, src_ref, dst_ref, feat_ref, out_ref):
    owners, rows, cap = out_ref.shape
    batches, feats, edges = feat_ref.shape
    shift = own_rows.bit_length() - 1
    marks = [jnp.zeros((16, cap), F32)] * owners
    for batch in range(batches):
        source, target = src_ref[batch : batch + 1], dst_ref[batch : batch + 1]
        owner = source >> shift
        hits, rank = ranks_of(owner, owners)
        spots = (row_ids((cap, edges)) == rank.astype(jnp.int32)).astype(BF16)
        line = row_ids((16, edges)) - 3 * batch
        first = owner << shift
        extra = jnp.where(line == 0, source - first, jnp.where(line == 1, target - first, 1))
        extra = jnp.where((line >= 0) & (line < 3), extra, 0).astype(F32)
        load = jnp.concatenate([feat_ref[batch].astype(F32), extra], axis=0)
        masked = [(load * hits[part : part + 1]).astype(BF16) for part in range(owners)]
        out = dot_nt(jnp.concatenate(masked, axis=0), spots)
        for part in range(owners):
            tile = out[part * (feats + 16) : (part + 1) * (feats + 16)]
            out_ref[part, batch * feats : (batch + 1) * feats] = tile[:feats].astype(BF16)
            marks[part] = marks[part] + tile[feats:]
    for part in range(owners):
        out_ref[part, batches * feats :] = marks[part].astype(BF16)


def unroute_kernel(own_rows, src_ref, back_ref, out_ref):
    owners, batches, rows, cap = back_ref.shape
    edges = src_ref.shape[1]
    shift = own_rows.bit_length() - 1
    for batch in range(batches):
        hits, rank = ranks_of(src_ref[batch : batch + 1] >> shift, owners)
        spots = (row_ids((cap, edges)) == rank.astype(jnp.int32)).astype(BF16)
        parts = [back_ref[part, batch] for part in range(owners)]
        spread = dot(jnp.concatenate(parts, axis=0), spots)
        total = jnp.zeros((rows, edges), F32)
        for part in range(owners):
            total = total + spread[part * rows : (part + 1) * rows] * hits[part : part + 1]
        out_ref[batch] = total.astype(BF16)


def edge_piece(batches, order_ref, edge_ref, piece, batch):
    some = [edge_ref[order_ref[batch, PIECE * piece + k]] for k in range(PIECE)]
    block = jnp.concatenate(some, axis=1)
    feats, marks = block[batch * 16 : (batch + 1) * 16], block[batches * 16 :].astype(F32)
    source = marks[3 * batch : 3 * batch + 1].astype(jnp.int32)
    target = marks[3 * batch + 1 : 3 * batch + 2].astype(jnp.int32)
    held = marks[3 * batch + 2 : 3 * batch + 3]
    code = ((target >> 3) & 3) * 128 + (target >> 5) * 64 + source
    code = jnp.where(held > 0.5, code, -1)
    pairs = (row_ids((512, block.shape[1])) == code).astype(BF16)
    low = row_ids((8, block.shape[1])) == (target & 7)
    return feats, held, pairs, low


def order_blocks(batches, edge_ref, order_ref):
    blocks = edge_ref.shape[0]
    for batch in range(batches):
        front, back = jnp.int32(0), jnp.int32(blocks - 1)
        row = 3 * batch + 2
        for block in range(blocks):
            marks = edge_ref[block, batches * 16 :].astype(F32)
            held = jnp.max(marks[row : row + 1]) > 0.5
            order_ref[batch, jnp.where(held, front, back)] = jnp.int32(block)
            step = held.astype(jnp.int32)
            front, back = front + step, back - (1 - step)
        order_ref[batch, blocks] = front


def first_layer(w_in_ref, b_in_ref):
    bias = jnp.broadcast_to(b_in_ref[...].reshape(1, -1), (8, b_in_ref.shape[0]))
    return w_in_ref[...].astype(F32).T.astype(BF16), bias.T[:, :1]


def gates_of(mail_low, level, w_x, w_h, b_x, b_h):
    width = level.shape[1]
    from_mail = dot(mail_low, w_x[...]) + b_x[...].reshape(1, -1)
    from_state = dot(level, w_h[...]) + b_h[...].reshape(1, -1)
    reset = jax.nn.sigmoid(from_mail[:, :width] + from_state[:, :width])
    update = jax.nn.sigmoid(from_mail[:, width : 2 * width] + from_state[:, width : 2 * width])
    state_part = from_state[:, 2 * width :]
    candidate = jnp.tanh(from_mail[:, 2 * width :] + reset * state_part)
    return reset, update, candidate, state_part


def doubled(level):
    blank = jnp.zeros_like(level)
    return jnp.concatenate(
        [jnp.concatenate([level, blank], axis=1), jnp.concatenate([blank, level], axis=1)], axis=0
    )


def bias_blocks(bias_ref, tail_ref):
    tail_ref[...] = jnp.zeros_like(tail_ref)
    high = bias_ref[...].astype(BF16)
    tail_ref[0] = high
    tail_ref[1] = (bias_ref[...] - high.astype(F32)).astype(BF16)


def turned(tile):
    size = tile.shape[1]
    eye = (row_ids((size, size)) == col_ids((size, size))).astype(F32).astype(BF16)
    return dot_nt(eye, tile).astype(BF16)


def weights_of(w_ref, tail_ref, number):
    units = w_ref.shape[0]
    blocks = []
    for unit in range(number * GROUP, (number + 1) * GROUP):
        blocks.append(w_ref[unit] if unit < units else tail_ref[unit - units])
    return jnp.concatenate(blocks, axis=1)


def pulled_rows(pulled, half):
    rows = []
    for start in range(0, pulled.shape[1], LANES):
        tile = pulled[:, start : start + LANES]
        rows.append(jnp.concatenate([tile[:half], tile[half:]], axis=1))
    return jnp.concatenate(rows, axis=0)


def main_kernel(
    where_ref,
    edge_ref,
    state_ref,
    cot_ref,
    w_in_ref,
    b_in_ref,
    w_far,
    bias_ref,
    w_x,
    w_h,
    b_x,
    b_h,
    new_ref,
    kept_first,
    kept_last,
    given_first,
    given_last,
    g_far,
    level_ref,
    dm_ref,
    base_ref,
    order_ref,
    rows_ref,
    hid_ref,
    acc_ref,
    g_ref,
    p_ref,
    w_ref,
    tail_ref,
    sum_ref,
    sum_sems,
    sems,
):
    fetch = pltpu.make_async_copy(w_far, w_ref, sems.at[0])
    fetch.start()
    blocks = edge_ref.shape[0]
    batches = g_ref.shape[0]
    hidden_units = hid_ref.shape[0]
    units = acc_ref.shape[0] // 8
    own = state_ref.shape[0] // batches
    half = own // 2
    span = GROUP * half
    wide = GROUP * LANES
    chunks = units // GROUP
    order_blocks(batches, edge_ref, order_ref)
    bias_blocks(bias_ref, tail_ref)
    w_in, b_in = first_layer(w_in_ref, b_in_ref)

    for batch in range(batches):
        acc_ref[...] = jnp.zeros_like(acc_ref)

        def add_piece(piece, carry):
            feats, held, pairs, low = edge_piece(batches, order_ref, edge_ref, piece, batch)
            pre = dot(w_in, feats) + b_in
            hid_ref[...] = (pre * jax.nn.sigmoid(pre)).astype(BF16).astype(F32)
            ones = jnp.where(low, 1.0, 0.0)
            parts = []
            for unit in range(0, hidden_units, 2):
                two = [jnp.where(low, hid_ref[unit + k : unit + k + 1], 0.0) for k in range(2)]
                parts.append(jnp.concatenate(two, axis=0).astype(BF16))
            parts.append(jnp.concatenate([ones, ones], axis=0).astype(BF16))
            parts.append(jnp.zeros((8 * (units - hidden_units - 2), pre.shape[1]), BF16))
            acc_ref[...] += dot_nt(jnp.concatenate(parts, axis=0), pairs)
            return carry

        lax.fori_loop(0, (order_ref[batch, blocks] + PIECE - 1) // PIECE, add_piece, 0)

        def place(step, carry):
            for four in range(3):
                rows = []
                for k in range(4):
                    for part in range(4):
                        start = pl.multiple_of(step * 96 + four * 32 + k * 8, 8)
                        rows.append(acc_ref[pl.ds(start, 8), part * LANES : (part + 1) * LANES])
                at = pl.ds(pl.multiple_of((step * 3 + four) * LANES, LANES), LANES)
                g_ref[batch, at, :] = jnp.concatenate(rows, axis=0).astype(BF16)
            return carry

        lax.fori_loop(0, units // 12, place, 0)

    def forward(step, level):
        two = [doubled(level[batch * own : (batch + 1) * own]) for batch in range(batches)]
        mail = jnp.zeros((batches * own, LANES), F32)
        base = step * batches * own
        for number in range(chunks):
            for batch in range(batches):
                out = dot(g_ref[batch, number * span : (number + 1) * span, :], two[batch])
                out = out.astype(BF16)
                for unit in range(GROUP):
                    lane = number * wide + unit * LANES
                    for part in range(2):
                        row = base + batch * own + part * half
                        p_ref[row : row + half, lane : lane + LANES] = out[
                            unit * half : (unit + 1) * half, part * LANES : (part + 1) * LANES
                        ]
            rows = p_ref[base : base + batches * own, number * wide : (number + 1) * wide]
            mail = mail + dot_nt(rows, weights_of(w_ref, tail_ref, number))
        return mail

    def backward(d_mail):
        sums = [jnp.zeros((LANES, 2 * LANES), F32) for batch in range(batches)]
        for number in range(chunks):
            pulled = dot(d_mail, weights_of(w_ref, tail_ref, number)).astype(BF16)
            at = slice(number * span, (number + 1) * span)
            for batch in range(batches):
                tall = pulled_rows(pulled[batch * own : (batch + 1) * own], half)
                sums[batch] = sums[batch] + dot(turned(g_ref[batch, at, :]), tall)
        return jnp.concatenate([one[:own, :LANES] + one[own:, LANES:] for one in sums], axis=0)

    weights = (w_x, w_h, b_x, b_h)
    level_zero = state_ref[...]
    state_zero = level_zero.astype(F32)
    leave = pltpu.make_async_copy(g_ref, g_far, sems.at[1])
    leave.start()
    fetch.wait()
    mail_zero = forward(0, level_zero).astype(BF16)
    gates_zero = gates_of(mail_zero, level_zero, *weights)
    state_one = (1.0 - gates_zero[1]) * gates_zero[2] + gates_zero[1] * state_zero
    level_one = state_one.astype(BF16)
    mail_one = forward(1, level_one).astype(BF16)
    gates_one = gates_of(mail_one, level_one, *weights)
    new_ref[...] = ((1.0 - gates_one[1]) * gates_one[2] + gates_one[1] * state_one).astype(BF16)

    def gru_back(d_next, gates, current):
        reset, update, candidate, state_part = gates
        d_cand = d_next * (1.0 - update) * (1.0 - candidate * candidate)
        d_reset = d_cand * state_part * reset * (1.0 - reset)
        d_update = d_next * (current - candidate) * update * (1.0 - update)
        dg_mail = jnp.concatenate([d_reset, d_update, d_cand], axis=1).astype(BF16)
        dg_state = jnp.concatenate([d_reset, d_update, d_cand * reset], axis=1).astype(BF16)
        d_mail = dot_nt(dg_mail, w_x[...]).astype(BF16)
        d_current = d_next * update + dot_nt(dg_state, w_h[...])
        return dg_mail, dg_state, d_mail, d_current

    dgm_one, dgs_one, dm_one, d_state = gru_back(cot_ref[...].astype(F32), gates_one, state_one)
    d_state = d_state + backward(dm_one)
    dgm_zero, dgs_zero, dm_zero, d_state = gru_back(d_state, gates_zero, state_zero)
    base_ref[...] = d_state
    level_ref[...] = jnp.concatenate([level_zero, level_one], axis=1)
    dm_ref[...] = jnp.concatenate([dm_zero, dm_one], axis=1)

    def both(first, second):
        return jnp.concatenate([first.astype(F32), second.astype(F32)], axis=0)

    dms = both(dm_zero, dm_one).T
    mails, levels = both(mail_zero, mail_one), both(level_zero, level_one)
    dgm, dgs = both(dgm_zero, dgm_one), both(dgs_zero, dgs_one)
    width = dgm.shape[1]
    rows_ref[...] = jnp.zeros_like(rows_ref)
    for k, one in enumerate((dgm, dgs)):
        total = jnp.sum(one, axis=0, keepdims=True)
        for part in range(3):
            row = 24 + 3 * k + part
            rows_ref[row : row + 1, :] = total[:, part * LANES : (part + 1) * LANES]
    small = jnp.concatenate(
        [
            dot(dms.astype(BF16), p_ref[:, hidden_units * LANES : (hidden_units + 1) * LANES]),
            dot(mails.T.astype(BF16), dgm.astype(BF16)),
            dot(levels.T.astype(BF16), dgs.astype(BF16)),
            jnp.zeros((2 * own, LANES), F32),
        ],
        axis=1,
    )

    def sorted_rows(value):
        rows = value.shape[0] // 2
        upper, lower = value[:rows], value[rows:]
        halves = [jnp.where(where_ref[0] == k, upper, lower) for k in range(2)]
        parts = []
        for k, one in enumerate(halves):
            first, second = one[: rows // 2], one[rows // 2 :]
            parts += [jnp.where(where_ref[1 + k] == side, second, first) for side in range(2)]
        return jnp.concatenate(parts, axis=0).astype(BF16)

    dms, small = sorted_rows(dms), sorted_rows(small)
    rows_in, groups, tall, wide_out = kept_first.shape
    taken = wide_out - 2 * LANES
    moves = []
    for group in range(groups):
        out = dot(dms, p_ref[:, group * taken : (group + 1) * taken]).astype(BF16)
        extra = small[:, group * 2 * LANES : (group + 1) * 2 * LANES]
        for k, ref in enumerate((given_first, kept_first, given_last, kept_last)):
            for row in range(rows_in):
                at = ((2, 0, 3, 1)[k] * rows_in + row) * tall
                sum_ref[k, row, group, :, :taken] = out[at : at + tall]
                sum_ref[k, row, group, :, taken:] = extra[at : at + tall]
                moves.append(
                    pltpu.make_async_copy(
                        sum_ref.at[k, row, group], ref.at[row, group], sum_sems.at[k, row, group]
                    )
                )
                moves[-1].start()
    for move in moves:
        move.wait()
    leave.wait()


def edge_sums(batch, batches, order_ref, edge_ref, dg_ref, w_in_ref, b_in_ref, feat_ref, before):
    blocks = edge_ref.shape[0]
    hidden_units = w_in_ref.shape[1]
    w_in, b_in = first_layer(w_in_ref, b_in_ref)
    fold = (col_ids((hidden_units, 8 * hidden_units)) >> 3) == row_ids(
        (hidden_units, 8 * hidden_units)
    )
    fold = fold.astype(F32).astype(BF16)

    def one_piece(piece, sums):
        feats, held, pairs, low = edge_piece(batches, order_ref, edge_ref, piece, batch)
        pre = dot(w_in, feats) + b_in
        sig = jax.nn.sigmoid(pre)
        spread = dot(dg_ref[batch, : 8 * hidden_units], pairs)
        spread = spread.reshape(hidden_units, 8, pre.shape[1])
        spread = jnp.where(low[None], spread, 0.0).reshape(8 * hidden_units, pre.shape[1])
        d_hidden = dot(fold, spread.astype(BF16))
        d_pre = (d_hidden * sig * (1.0 + pre * (1.0 - sig))).astype(BF16)
        out = dot(w_in_ref[...], d_pre).astype(BF16)
        for k in range(PIECE):
            at = order_ref[batch, PIECE * piece + k]
            feat_ref[at, batch * 16 : (batch + 1) * 16] = out[:, k * LANES : (k + 1) * LANES]
        ones = jnp.where(row_ids((16, pre.shape[1])) == 0, held, 0.0).astype(BF16)
        return sums + dot_nt(jnp.concatenate([feats, ones], axis=0), d_pre)

    return lax.fori_loop(0, (order_ref[batch, blocks] + PIECE - 1) // PIECE, one_piece, before)


def back_kernel(
    g_far,
    level_ref,
    dm_ref,
    base_ref,
    w_far,
    bias_ref,
    grad_ref,
    dg_ref,
    tail_ref,
    w_ref,
    g_ref,
    sems,
):
    batches, own, width = grad_ref.shape
    hidden_units = w_ref.shape[0]
    chunks = (hidden_units + tail_ref.shape[0]) // GROUP
    half = own // 2
    fetches = []
    for number in range(chunks):
        some = pl.ds(number * GROUP, min(GROUP, hidden_units - number * GROUP))
        rows = pl.ds(number * GROUP * half, GROUP * half)
        fetches += [
            pltpu.make_async_copy(w_far.at[some], w_ref.at[some], sems.at[number, 0]),
            pltpu.make_async_copy(g_far.at[:, rows], g_ref.at[:, rows], sems.at[number, 1]),
        ]
    for fetch in fetches:
        fetch.start()
    bias_blocks(bias_ref, tail_ref)

    pulls, levels = [], []
    for batch in range(batches):
        mine = slice(batch * own, (batch + 1) * own)
        pulls += [dm_ref[mine, step * width : (step + 1) * width] for step in range(2)]
        both = [doubled(level_ref[mine, step * width : (step + 1) * width]) for step in range(2)]
        levels.append(jnp.concatenate(both, axis=1))
    pulls = jnp.concatenate(pulls, axis=0)
    totals = [jnp.zeros((2 * own, 2 * width), F32) for batch in range(batches)]
    for number in range(chunks):
        fetches[2 * number].wait()
        fetches[2 * number + 1].wait()
        pulled = dot(pulls, weights_of(w_ref, tail_ref, number)).astype(BF16)
        at = slice(number * GROUP * half, (number + 1) * GROUP * half)
        for batch in range(batches):
            talls = [
                pulled_rows(pulled[(2 * batch + k) * own : (2 * batch + k + 1) * own], half)
                for k in range(2)
            ]
            totals[batch] = totals[batch] + dot(turned(g_ref[batch, at, :]), talls[0])
            d_pair = dot_nt(jnp.concatenate(talls, axis=1), levels[batch])
            for unit in range(0, GROUP, 2):
                row = (number * GROUP + unit) * 8
                for part in range(half // 8):
                    pair = [
                        d_pair[(unit + k) * half + part * 8 : (unit + k) * half + part * 8 + 8]
                        for k in range(2)
                    ]
                    dg_ref[batch, row : row + 16, part * LANES : (part + 1) * LANES] = jnp.concatenate(
                        pair, axis=0
                    ).astype(BF16)
    for batch in range(batches):
        grad = base_ref[batch * own : (batch + 1) * own] + totals[batch][:own, :width]
        grad_ref[batch] = (grad + totals[batch][own:, width:]).astype(BF16)


def edge_kernel(order_ref, edge_ref, dg_ref, w_in_ref, b_in_ref, before_ref, feat_ref, win_ref):
    batches = order_ref.shape[0]
    feat_ref[...] = jnp.zeros_like(feat_ref)
    sums = before_ref[...]
    for batch in range(batches):
        sums = edge_sums(
            batch, batches, order_ref, edge_ref, dg_ref, w_in_ref, b_in_ref, feat_ref, sums
        )
    win_ref[...] = sums


def add_kernel(first_ref, second_ref, out_ref):
    out_ref[...] = (first_ref[...].astype(F32) + second_ref[...].astype(F32)).astype(BF16)


def copy_kernel(in_ref, out_ref):
    out_ref[...] = in_ref[...]


def rows_kernel(first_ref, second_ref, out_ref, rows_ref):
    parts, tall, wide = first_ref.shape
    main = wide // LANES - 2
    for part in range(parts):
        total = first_ref[part].astype(F32) + second_ref[part].astype(F32)
        for block in range(main):
            rows_ref[pl.ds(block, tall, stride=main), :] = total[
                :, block * LANES : (block + 1) * LANES
            ]
        for k in range(2):
            start = tall * (main + k)
            rows_ref[start : start + tall, :] = total[:, (main + k) * LANES : (main + k + 1) * LANES]
        out_ref[part] = rows_ref[...].astype(BF16)


def rows_of(first, second):
    parts, tall, wide = first.shape
    shape = (tall * (wide // LANES), LANES)
    return full_call(
        rows_kernel,
        jax.ShapeDtypeStruct((parts,) + shape, BF16),
        (pltpu.VMEM(shape, F32),),
        cost_estimate=cost(1),
    )(first, second)


def place_kernel(tall, count, carried, *refs):
    at_ref, pieces = refs[0], refs[1 : 1 + count]
    outs = refs[1 + count + carried : 6 + count + carried]
    big_ref, little_ref, sems = refs[6 + count + carried :]
    d_w, d_bias, d_x, d_h, d_rest = outs
    waits = []
    slot = 0
    for k, piece in enumerate(pieces):
        chunks, rows_in, lanes = piece.shape
        main = rows_in // tall - 2
        for chunk in range(chunks):
            code = at_ref[k] ^ chunk
            line, part = code >> 2, code & 3
            at = pl.ds(pl.multiple_of(line * tall, 8), tall)
            rows = piece[chunk].astype(F32)
            for row in range(tall):
                big_ref[slot, :, row * lanes : (row + 1) * lanes] = rows[row * main : (row + 1) * main]
            copy = pltpu.make_async_copy(
                big_ref.at[slot],
                d_w.at[
                    pl.ds(pl.multiple_of(part * main, 8), main),
                    pl.ds(pl.multiple_of(line * (tall * lanes), LANES), tall * lanes),
                ],
                sems.at[slot, 0],
            )
            copy.start()
            waits.append(copy)

            for side in range(2):
                start = tall * (main + side)
                little_ref[slot, side] = rows[start : start + tall]

                def move(target, lane):
                    lane = jnp.maximum(lane, 0) * lanes
                    to = pl.ds(pl.multiple_of(jnp.minimum(lane, target.shape[1] - lanes), LANES), lanes)
                    return pltpu.make_async_copy(
                        little_ref.at[slot, side], target.at[at, to], sems.at[slot, 1 + side]
                    )

                block = 2 * part + side
                to_x, to_h = move(d_x, block - 1), move(d_h, block - 4)
                alone = move((d_bias, d_rest)[side], 0)
                lone = block == 7 * side
                pl.when(lone)(alone.start)
                pl.when((block > 0) & (block < 4))(to_x.start)
                pl.when((block > 3) & (block < 7))(to_h.start)
                waits.append(alone)
            slot += 1
    for copy in waits:
        copy.wait()


def cost(micros):
    return pl.CostEstimate(
        flops=int(micros * 1e9), bytes_accessed=int(micros * 3e6), transcendentals=0
    )


def place_pieces(tall, at, pieces, shapes, before=()):
    count = len(pieces)
    chunks, rows_in, lanes = pieces[0].shape
    slots = count * chunks
    vmem = pl.BlockSpec(memory_space=pltpu.VMEM)
    hbm = pl.BlockSpec(memory_space=pl.ANY)
    return pl.pallas_call(
        functools.partial(place_kernel, tall, count, len(before)),
        out_shape=shapes,
        in_specs=[pl.BlockSpec(memory_space=pltpu.SMEM)] + [vmem] * count + [hbm] * len(before),
        out_specs=[hbm] * len(shapes),
        scratch_shapes=(
            pltpu.VMEM((slots, rows_in // tall - 2, tall * lanes), F32),
            pltpu.VMEM((slots, 2, tall, lanes), F32),
            pltpu.SemaphoreType.DMA((slots, 3)),
        ),
        input_output_aliases={1 + count + k: k for k in range(len(before))},
        cost_estimate=cost(slots / 4),
        compiler_params=pltpu.CompilerParams(vmem_limit_bytes=16 * MIB),
    )(at, *pieces, *before)


def body(
    states,
    edge_feats,
    source_index,
    target_index,
    w_edge_in,
    b_edge_in,
    w_edge_out,
    b_edge_out,
    w_input,
    w_hidden,
    b_input,
    b_hidden,
    cotangent,
):
    batches, own, width = states.shape
    edges = source_index.shape[1]
    owners = lax.axis_size("edge")
    cap = max(2, 2 * edges // owners)
    feat_count, units = w_edge_in.shape

    sent = full_call(
        functools.partial(route_kernel, own),
        jax.ShapeDtypeStruct((owners, batches * feat_count + 16, cap), BF16),
        limit=60,
    )(source_index, target_index, edge_feats)
    edge_data = lax.all_to_all(sent, "edge", 0, 0, tiled=True)
    merge = max(1, LANES // cap)
    if merge > 1:
        edge_data = edge_data.reshape(owners // merge, merge, -1, cap).transpose(0, 2, 1, 3)
        edge_data = edge_data.reshape(owners // merge, -1, merge * cap)

    w_mats = w_edge_out.reshape(units, width, width)
    padded = (units + 2 + GROUP - 1) // GROUP * GROUP

    tall = width // 8
    pairs = own // 2
    blocks = edge_data.shape[0]
    core = lax.axis_index("graph")
    spot = lax.axis_index("edge")
    orders = ((0, 1, 2, 3), (2, 0, 1, 3))

    def bit(side, step):
        first, second = [(spot >> orders[k][step]) & 1 for k in range(2)]
        return jnp.where(side == 0, first, second)

    where = jnp.stack([core, bit(core, 0), bit(1 - core, 0)])
    smem = pl.BlockSpec(memory_space=pltpu.SMEM)
    vmem = pl.BlockSpec(memory_space=pltpu.VMEM)
    far = pl.BlockSpec(memory_space=pltpu.HBM)
    bias = b_edge_out.reshape(width, width)
    quarter = jax.ShapeDtypeStruct((2, 4, tall, (units // 4 + 2) * width), BF16)
    new_states, *sums, g_pairs, levels, d_mails, base, order, first = full_call(
        main_kernel,
        (
            jax.ShapeDtypeStruct((batches * own, width), BF16),
            *[quarter] * 4,
            jax.ShapeDtypeStruct((batches, padded * pairs, LANES), BF16),
            jax.ShapeDtypeStruct((batches * own, 2 * width), BF16),
            jax.ShapeDtypeStruct((batches * own, 2 * width), BF16),
            jax.ShapeDtypeStruct((batches * own, width), F32),
            jax.ShapeDtypeStruct((batches, blocks + 1), jnp.int32),
            jax.ShapeDtypeStruct((32, width), F32),
        ),
        (
            pltpu.VMEM((units, PIECE * LANES), F32),
            pltpu.VMEM((padded * 8, 512), F32),
            pltpu.VMEM((batches, padded * pairs, LANES), BF16),
            pltpu.VMEM((2 * batches * own, padded * width), BF16),
            pltpu.VMEM((units, width, width), BF16),
            pltpu.VMEM((padded - units, width, width), BF16),
            pltpu.VMEM((4,) + quarter.shape, BF16),
            pltpu.SemaphoreType.DMA((4,) + quarter.shape[:2]),
            pltpu.SemaphoreType.DMA((2,)),
        ),
        limit=60,
        in_specs=[smem] + [vmem] * 5 + [far] + [vmem] * 5,
        out_specs=[vmem] + [far] * 5 + [vmem] * 3 + [smem, vmem],
    )(
        where,
        edge_data,
        states.reshape(batches * own, width),
        cotangent.reshape(batches * own, width),
        w_edge_in,
        b_edge_in,
        w_mats,
        bias,
        w_input,
        w_hidden,
        b_input,
        b_hidden,
    )

    cores = lax.axis_size("graph")

    def to_core(value):
        return lax.ppermute(value, "graph", [(0, 1), (1, 0)])

    def swap(value, masks):
        moves = []
        for side in range(cores):
            first = side * owners
            moves += [(first + k, first + (k ^ masks[side])) for k in range(owners)]
        return lax.ppermute(value, ("graph", "edge"), moves)

    def swap_step(value, step):
        return swap(value, [1 << orders[side][step] for side in range(cores)])

    def pick(value, number):
        return lax.dynamic_index_in_dim(value, number, 0, False)

    def added(terms):
        return sum(one.astype(F32) for one in terms)

    def after(value, *others):
        return lax.optimization_barrier((value, *others))[0]

    def first_grads(pairs_in):
        return full_call(
            back_kernel,
            (
                jax.ShapeDtypeStruct((batches, own, width), BF16),
                jax.ShapeDtypeStruct((batches, padded * 8, 512), BF16),
            ),
            (
                pltpu.VMEM((padded - units, width, width), BF16),
                pltpu.VMEM((units, width, width), BF16),
                pltpu.VMEM((batches, padded * pairs, LANES), BF16),
                pltpu.SemaphoreType.DMA((padded // GROUP, 2)),
            ),
            limit=60,
            in_specs=[far] + [vmem] * 3 + [far, vmem],
            cost_estimate=cost(12),
        )(pairs_in, levels, d_mails, base, w_mats, bias)

    def second_grads(d_pairs):
        return full_call(
            edge_kernel,
            (
                jax.ShapeDtypeStruct((blocks, batches * feat_count, LANES), BF16),
                jax.ShapeDtypeStruct((32, units), F32),
            ),
            limit=60,
            in_specs=[smem] + [vmem] * 5,
            cost_estimate=cost(9),
        )(order, edge_data, d_pairs, w_edge_in, b_edge_in, first)

    def added_at(big, small, flip):
        big, more = lax.optimization_barrier((big, swap(small, [flip] * cores)))
        return big, small + more

    kept_first, kept_last, given_first, given_last = sums
    got_first, got_last = to_core(given_first), to_core(given_last)
    kept_first = full_call(
        copy_kernel, jax.ShapeDtypeStruct(kept_first.shape, BF16), cost_estimate=cost(1)
    )(kept_first)
    give = full_call(
        add_kernel, jax.ShapeDtypeStruct(kept_first.shape, BF16), cost_estimate=cost(1)
    )(kept_first, got_first)
    terms = [kept_last, got_last]
    for step in range(3):
        if step > 0:
            number = bit(core, step)
            give = added([pick(one, 1 - number) for one in terms]).astype(BF16)
            terms = [pick(one, number) for one in terms]
        got = swap_step(give, step)
        if step == 0:
            state_grad, d_pairs = first_grads(after(g_pairs, give))
            got = after(got, state_grad)
        if step == 1:
            d_feats, first = second_grads(after(d_pairs, give))
            got = after(got, first)
        if step == 2:
            got, first = added_at(got, first, 4)
        terms.append(got)
        if step == 0:
            terms = [one.reshape((2, 2, 2) + one.shape[2:]) for one in terms]
    total = added(terms).astype(BF16)
    for extra in range(3, owners.bit_length() - 1):
        got = swap(total, [1 << extra] * cores)
        if extra > 3:
            got, first = added_at(got, first, 1 << extra)
        if extra < owners.bit_length() - 2:
            total = added([total, got]).astype(BF16)
    first = first + swap(first, [1] * cores)
    got, first = added_at(got, first, 2)
    held = rows_of(total, got)

    got, first = added_at(swap_step(held, 2), first, 8)
    held = jnp.concatenate([held, got], axis=0)
    across = swap_step(held, 0)
    back = d_feats
    if merge > 1:
        back = back.reshape(blocks, -1, merge, cap).transpose(0, 2, 1, 3)
    back = after(back.reshape(owners, -1, cap), held)
    back = lax.all_to_all(back, "edge", 0, 0, tiled=True)

    shapes = tuple(
        jax.ShapeDtypeStruct(shape, F32)
        for shape in (
            (units, width * width),
            (width, width),
            (width, 3 * width),
            (width, 3 * width),
            (width, width),
        )
    )
    outs = ()
    def place(outs, pieces):
        at = []
        for _, side, flips in pieces:
            code = side
            for step in range(3):
                code = code * 2 + bit(side, step)
            at.append((code * 2) ^ flips)
        return place_pieces(tall, jnp.stack(at), [one for one, _, _ in pieces], shapes, outs)

    outs = place((), [(held, core, 0), (to_core(held), 1 - core, 0)])
    outs, near, more = lax.optimization_barrier((outs, swap_step(held, 1), to_core(first)))
    first = first + more
    small_outs = (
        first[:feat_count],
        first[feat_count],
        first[24:27].reshape(-1),
        first[27:30].reshape(-1),
    )
    last = swap_step(near, 0)
    outs, near, across, back = lax.optimization_barrier((outs, near, across, back))
    near_other, across_other = to_core(near), to_core(across)
    feat_grad = full_call(
        functools.partial(unroute_kernel, own),
        jax.ShapeDtypeStruct((batches, feat_count, edges), BF16),
        cost_estimate=cost(1.4),
    )(source_index, back.reshape(owners, batches, feat_count, cap))
    outs = place(
        outs,
        [
            (near, core, 4),
            (near_other, 1 - core, 4),
            (across, core, 8),
            (across_other, 1 - core, 8),
        ],
    )
    outs, last, feat_grad, small_outs = lax.optimization_barrier(
        (outs, last, feat_grad, small_outs)
    )
    other = to_core(last)
    outs = place(outs, [(last, core, 12)])
    outs = place(outs, [(other, 1 - core, 12)])
    d_w, d_bias, d_x, d_h, _ = outs
    return (
        new_states.reshape(batches, own, width),
        state_grad,
        feat_grad,
        small_outs[0],
        small_outs[1],
        d_w,
        d_bias.reshape(-1),
        d_x,
        d_h,
        small_outs[2],
        small_outs[3],
    )


def solution(mesh):
    spread = ("graph", "edge")
    rows = P(None, spread, None)
    edges = P(None, spread)
    feats = P(None, None, spread)
    in_specs = (rows, feats, edges, edges) + (P(),) * 8 + (rows,)
    out_specs = (rows, rows, feats) + (P(),) * 8
    return jax.shard_map(
        body,
        mesh=mesh,
        in_specs=in_specs,
        out_specs=out_specs,
        check_vma=False,
    )
```

```python
import functools

import jax
import jax.numpy as jnp
from jax import lax
from jax.experimental import pallas as pl
from jax.experimental.pallas import tpu as pltpu
from jax.sharding import PartitionSpec as P

F32 = jnp.float32
BF16 = jnp.bfloat16
LANES = 128
PIECE = 4
GROUP = 12
MIB = 1024 * 1024


def dot(first, second, dims=((1,), (0,))):
    return lax.dot_general(first, second, (dims, ((), ())), preferred_element_type=F32)


def dot_nt(first, second):
    return dot(first, second, ((1,), (1,)))


def row_ids(shape):
    return lax.broadcasted_iota(jnp.int32, shape, 0)


def col_ids(shape):
    return lax.broadcasted_iota(jnp.int32, shape, 1)


def full_call(kernel, out_shape, scratch=(), limit=16, **more):
    return pl.pallas_call(
        kernel,
        out_shape=out_shape,
        scratch_shapes=scratch,
        compiler_params=pltpu.CompilerParams(vmem_limit_bytes=limit * MIB),
        **more,
    )


def ranks_of(owner, owners):
    hits = (row_ids((owners, owner.shape[1])) == owner).astype(F32)
    before = (row_ids((LANES, LANES)) < col_ids((LANES, LANES))).astype(BF16)
    seen = jnp.zeros((owners, 1), F32)
    ranks = []
    for start in range(0, owner.shape[1], LANES):
        part = hits[:, start : start + LANES]
        place = dot(part.astype(BF16), before) + seen
        ranks.append(jnp.sum(part * place, axis=0, keepdims=True))
        seen = seen + jnp.sum(part, axis=1, keepdims=True)
    return hits, jnp.concatenate(ranks, axis=1)


def route_kernel(own_rows, src_ref, dst_ref, feat_ref, out_ref):
    owners, rows, cap = out_ref.shape
    batches, feats, edges = feat_ref.shape
    shift = own_rows.bit_length() - 1
    marks = [jnp.zeros((16, cap), F32)] * owners
    for batch in range(batches):
        source, target = src_ref[batch : batch + 1], dst_ref[batch : batch + 1]
        owner = source >> shift
        hits, rank = ranks_of(owner, owners)
        spots = (row_ids((cap, edges)) == rank.astype(jnp.int32)).astype(BF16)
        line = row_ids((16, edges)) - 3 * batch
        first = owner << shift
        extra = jnp.where(line == 0, source - first, jnp.where(line == 1, target - first, 1))
        extra = jnp.where((line >= 0) & (line < 3), extra, 0).astype(F32)
        load = jnp.concatenate([feat_ref[batch].astype(F32), extra], axis=0)
        masked = [(load * hits[part : part + 1]).astype(BF16) for part in range(owners)]
        out = dot_nt(jnp.concatenate(masked, axis=0), spots)
        for part in range(owners):
            tile = out[part * (feats + 16) : (part + 1) * (feats + 16)]
            out_ref[part, batch * feats : (batch + 1) * feats] = tile[:feats].astype(BF16)
            marks[part] = marks[part] + tile[feats:]
    for part in range(owners):
        out_ref[part, batches * feats :] = marks[part].astype(BF16)


def unroute_kernel(own_rows, src_ref, back_ref, out_ref):
    owners, batches, rows, cap = back_ref.shape
    edges = src_ref.shape[1]
    shift = own_rows.bit_length() - 1
    for batch in range(batches):
        hits, rank = ranks_of(src_ref[batch : batch + 1] >> shift, owners)
        spots = (row_ids((cap, edges)) == rank.astype(jnp.int32)).astype(BF16)
        parts = [back_ref[part, batch] for part in range(owners)]
        spread = dot(jnp.concatenate(parts, axis=0), spots)
        total = jnp.zeros((rows, edges), F32)
        for part in range(owners):
            total = total + spread[part * rows : (part + 1) * rows] * hits[part : part + 1]
        out_ref[batch] = total.astype(BF16)


def edge_piece(batches, order_ref, edge_ref, piece, batch):
    some = [edge_ref[order_ref[batch, PIECE * piece + k]] for k in range(PIECE)]
    block = jnp.concatenate(some, axis=1)
    feats, marks = block[batch * 16 : (batch + 1) * 16], block[batches * 16 :].astype(F32)
    source = marks[3 * batch : 3 * batch + 1].astype(jnp.int32)
    target = marks[3 * batch + 1 : 3 * batch + 2].astype(jnp.int32)
    held = marks[3 * batch + 2 : 3 * batch + 3]
    code = ((target >> 3) & 3) * 128 + (target >> 5) * 64 + source
    code = jnp.where(held > 0.5, code, -1)
    pairs = (row_ids((512, block.shape[1])) == code).astype(BF16)
    low = row_ids((8, block.shape[1])) == (target & 7)
    return feats, held, pairs, low


def order_blocks(batches, edge_ref, order_ref):
    blocks = edge_ref.shape[0]
    for batch in range(batches):
        front, back = jnp.int32(0), jnp.int32(blocks - 1)
        row = 3 * batch + 2
        for block in range(blocks):
            marks = edge_ref[block, batches * 16 :].astype(F32)
            held = jnp.max(marks[row : row + 1]) > 0.5
            order_ref[batch, jnp.where(held, front, back)] = jnp.int32(block)
            step = held.astype(jnp.int32)
            front, back = front + step, back - (1 - step)
        order_ref[batch, blocks] = front


def first_layer(w_in_ref, b_in_ref):
    bias = jnp.broadcast_to(b_in_ref[...].reshape(1, -1), (8, b_in_ref.shape[0]))
    return w_in_ref[...].astype(F32).T.astype(BF16), bias.T[:, :1]


def gates_of(mail_low, level, w_x, w_h, b_x, b_h):
    width = level.shape[1]
    from_mail = dot(mail_low, w_x[...]) + b_x[...].reshape(1, -1)
    from_state = dot(level, w_h[...]) + b_h[...].reshape(1, -1)
    reset = jax.nn.sigmoid(from_mail[:, :width] + from_state[:, :width])
    update = jax.nn.sigmoid(from_mail[:, width : 2 * width] + from_state[:, width : 2 * width])
    state_part = from_state[:, 2 * width :]
    candidate = jnp.tanh(from_mail[:, 2 * width :] + reset * state_part)
    return reset, update, candidate, state_part


def doubled(level):
    blank = jnp.zeros_like(level)
    return jnp.concatenate(
        [jnp.concatenate([level, blank], axis=1), jnp.concatenate([blank, level], axis=1)], axis=0
    )


def bias_blocks(bias_ref, tail_ref):
    tail_ref[...] = jnp.zeros_like(tail_ref)
    high = bias_ref[...].astype(BF16)
    tail_ref[0] = high
    tail_ref[1] = (bias_ref[...] - high.astype(F32)).astype(BF16)


def turned(tile):
    size = tile.shape[1]
    eye = (row_ids((size, size)) == col_ids((size, size))).astype(F32).astype(BF16)
    return dot_nt(eye, tile).astype(BF16)


def weights_of(w_ref, tail_ref, number):
    units = w_ref.shape[0]
    blocks = []
    for unit in range(number * GROUP, (number + 1) * GROUP):
        blocks.append(w_ref[unit] if unit < units else tail_ref[unit - units])
    return jnp.concatenate(blocks, axis=1)


def pulled_rows(pulled, half):
    rows = []
    for start in range(0, pulled.shape[1], LANES):
        tile = pulled[:, start : start + LANES]
        rows.append(jnp.concatenate([tile[:half], tile[half:]], axis=1))
    return jnp.concatenate(rows, axis=0)


def main_kernel(
    where_ref,
    edge_ref,
    state_ref,
    cot_ref,
    w_in_ref,
    b_in_ref,
    w_far,
    bias_ref,
    w_x,
    w_h,
    b_x,
    b_h,
    new_ref,
    kept_first,
    kept_last,
    given_first,
    given_last,
    g_far,
    level_ref,
    dm_ref,
    base_ref,
    order_ref,
    rows_ref,
    hid_ref,
    acc_ref,
    g_ref,
    p_ref,
    w_ref,
    tail_ref,
    sum_ref,
    sum_sems,
    sems,
):
    fetch = pltpu.make_async_copy(w_far, w_ref, sems.at[0])
    fetch.start()
    blocks = edge_ref.shape[0]
    batches = g_ref.shape[0]
    hidden_units = hid_ref.shape[0]
    units = acc_ref.shape[0] // 8
    own = state_ref.shape[0] // batches
    half = own // 2
    span = GROUP * half
    wide = GROUP * LANES
    chunks = units // GROUP
    order_blocks(batches, edge_ref, order_ref)
    bias_blocks(bias_ref, tail_ref)
    w_in, b_in = first_layer(w_in_ref, b_in_ref)

    for batch in range(batches):
        acc_ref[...] = jnp.zeros_like(acc_ref)

        def add_piece(piece, carry):
            feats, held, pairs, low = edge_piece(batches, order_ref, edge_ref, piece, batch)
            pre = dot(w_in, feats) + b_in
            hid_ref[...] = (pre * jax.nn.sigmoid(pre)).astype(BF16).astype(F32)
            ones = jnp.where(low, 1.0, 0.0)
            parts = []
            for unit in range(0, hidden_units, 2):
                two = [jnp.where(low, hid_ref[unit + k : unit + k + 1], 0.0) for k in range(2)]
                parts.append(jnp.concatenate(two, axis=0).astype(BF16))
            parts.append(jnp.concatenate([ones, ones], axis=0).astype(BF16))
            parts.append(jnp.zeros((8 * (units - hidden_units - 2), pre.shape[1]), BF16))
            acc_ref[...] += dot_nt(jnp.concatenate(parts, axis=0), pairs)
            return carry

        lax.fori_loop(0, (order_ref[batch, blocks] + PIECE - 1) // PIECE, add_piece, 0)

        def place(step, carry):
            for four in range(3):
                rows = []
                for k in range(4):
                    for part in range(4):
                        start = pl.multiple_of(step * 96 + four * 32 + k * 8, 8)
                        rows.append(acc_ref[pl.ds(start, 8), part * LANES : (part + 1) * LANES])
                at = pl.ds(pl.multiple_of((step * 3 + four) * LANES, LANES), LANES)
                g_ref[batch, at, :] = jnp.concatenate(rows, axis=0).astype(BF16)
            return carry

        lax.fori_loop(0, units // 12, place, 0)

    def forward(step, level):
        two = [doubled(level[batch * own : (batch + 1) * own]) for batch in range(batches)]
        mail = jnp.zeros((batches * own, LANES), F32)
        base = step * batches * own
        for number in range(chunks):
            for batch in range(batches):
                out = dot(g_ref[batch, number * span : (number + 1) * span, :], two[batch])
                out = out.astype(BF16)
                for unit in range(GROUP):
                    lane = number * wide + unit * LANES
                    for part in range(2):
                        row = base + batch * own + part * half
                        p_ref[row : row + half, lane : lane + LANES] = out[
                            unit * half : (unit + 1) * half, part * LANES : (part + 1) * LANES
                        ]
            rows = p_ref[base : base + batches * own, number * wide : (number + 1) * wide]
            mail = mail + dot_nt(rows, weights_of(w_ref, tail_ref, number))
        return mail

    def backward(d_mail):
        sums = [jnp.zeros((LANES, 2 * LANES), F32) for batch in range(batches)]
        for number in range(chunks):
            pulled = dot(d_mail, weights_of(w_ref, tail_ref, number)).astype(BF16)
            at = slice(number * span, (number + 1) * span)
            for batch in range(batches):
                tall = pulled_rows(pulled[batch * own : (batch + 1) * own], half)
                sums[batch] = sums[batch] + dot(turned(g_ref[batch, at, :]), tall)
        return jnp.concatenate([one[:own, :LANES] + one[own:, LANES:] for one in sums], axis=0)

    weights = (w_x, w_h, b_x, b_h)
    level_zero = state_ref[...]
    state_zero = level_zero.astype(F32)
    leave = pltpu.make_async_copy(g_ref, g_far, sems.at[1])
    leave.start()
    fetch.wait()
    mail_zero = forward(0, level_zero).astype(BF16)
    gates_zero = gates_of(mail_zero, level_zero, *weights)
    state_one = (1.0 - gates_zero[1]) * gates_zero[2] + gates_zero[1] * state_zero
    level_one = state_one.astype(BF16)
    mail_one = forward(1, level_one).astype(BF16)
    gates_one = gates_of(mail_one, level_one, *weights)
    new_ref[...] = ((1.0 - gates_one[1]) * gates_one[2] + gates_one[1] * state_one).astype(BF16)

    def gru_back(d_next, gates, current):
        reset, update, candidate, state_part = gates
        d_cand = d_next * (1.0 - update) * (1.0 - candidate * candidate)
        d_reset = d_cand * state_part * reset * (1.0 - reset)
        d_update = d_next * (current - candidate) * update * (1.0 - update)
        dg_mail = jnp.concatenate([d_reset, d_update, d_cand], axis=1).astype(BF16)
        dg_state = jnp.concatenate([d_reset, d_update, d_cand * reset], axis=1).astype(BF16)
        d_mail = dot_nt(dg_mail, w_x[...]).astype(BF16)
        d_current = d_next * update + dot_nt(dg_state, w_h[...])
        return dg_mail, dg_state, d_mail, d_current

    dgm_one, dgs_one, dm_one, d_state = gru_back(cot_ref[...].astype(F32), gates_one, state_one)
    d_state = d_state + backward(dm_one)
    dgm_zero, dgs_zero, dm_zero, d_state = gru_back(d_state, gates_zero, state_zero)
    base_ref[...] = d_state
    level_ref[...] = jnp.concatenate([level_zero, level_one], axis=1)
    dm_ref[...] = jnp.concatenate([dm_zero, dm_one], axis=1)

    def both(first, second):
        return jnp.concatenate([first.astype(F32), second.astype(F32)], axis=0)

    dms = both(dm_zero, dm_one).T
    mails, levels = both(mail_zero, mail_one), both(level_zero, level_one)
    dgm, dgs = both(dgm_zero, dgm_one), both(dgs_zero, dgs_one)
    width = dgm.shape[1]
    rows_ref[...] = jnp.zeros_like(rows_ref)
    for k, one in enumerate((dgm, dgs)):
        total = jnp.sum(one, axis=0, keepdims=True)
        for part in range(3):
            row = 24 + 3 * k + part
            rows_ref[row : row + 1, :] = total[:, part * LANES : (part + 1) * LANES]
    small = jnp.concatenate(
        [
            dot(dms.astype(BF16), p_ref[:, hidden_units * LANES : (hidden_units + 1) * LANES]),
            dot(mails.T.astype(BF16), dgm.astype(BF16)),
            dot(levels.T.astype(BF16), dgs.astype(BF16)),
            jnp.zeros((2 * own, LANES), F32),
        ],
        axis=1,
    )

    def sorted_rows(value):
        rows = value.shape[0] // 2
        upper, lower = value[:rows], value[rows:]
        halves = [jnp.where(where_ref[0] == k, upper, lower) for k in range(2)]
        parts = []
        for k, one in enumerate(halves):
            first, second = one[: rows // 2], one[rows // 2 :]
            parts += [jnp.where(where_ref[1 + k] == side, second, first) for side in range(2)]
        return jnp.concatenate(parts, axis=0).astype(BF16)

    dms, small = sorted_rows(dms), sorted_rows(small)
    rows_in, groups, tall, wide_out = kept_first.shape
    taken = wide_out - 2 * LANES
    moves = []
    for group in range(groups):
        out = dot(dms, p_ref[:, group * taken : (group + 1) * taken]).astype(BF16)
        extra = small[:, group * 2 * LANES : (group + 1) * 2 * LANES]
        for k, ref in enumerate((given_first, kept_first, given_last, kept_last)):
            for row in range(rows_in):
                at = ((2, 0, 3, 1)[k] * rows_in + row) * tall
                sum_ref[k, row, group, :, :taken] = out[at : at + tall]
                sum_ref[k, row, group, :, taken:] = extra[at : at + tall]
                moves.append(
                    pltpu.make_async_copy(
                        sum_ref.at[k, row, group], ref.at[row, group], sum_sems.at[k, row, group]
                    )
                )
                moves[-1].start()
    for move in moves:
        move.wait()
    leave.wait()


def edge_sums(batch, batches, order_ref, edge_ref, dg_ref, w_in_ref, b_in_ref, feat_ref, before):
    blocks = edge_ref.shape[0]
    hidden_units = w_in_ref.shape[1]
    w_in, b_in = first_layer(w_in_ref, b_in_ref)
    fold = (col_ids((hidden_units, 8 * hidden_units)) >> 3) == row_ids(
        (hidden_units, 8 * hidden_units)
    )
    fold = fold.astype(F32).astype(BF16)

    def one_piece(piece, sums):
        feats, held, pairs, low = edge_piece(batches, order_ref, edge_ref, piece, batch)
        pre = dot(w_in, feats) + b_in
        sig = jax.nn.sigmoid(pre)
        spread = dot(dg_ref[batch, : 8 * hidden_units], pairs)
        spread = spread.reshape(hidden_units, 8, pre.shape[1])
        spread = jnp.where(low[None], spread, 0.0).reshape(8 * hidden_units, pre.shape[1])
        d_hidden = dot(fold, spread.astype(BF16))
        d_pre = (d_hidden * sig * (1.0 + pre * (1.0 - sig))).astype(BF16)
        out = dot(w_in_ref[...], d_pre).astype(BF16)
        for k in range(PIECE):
            at = order_ref[batch, PIECE * piece + k]
            feat_ref[at, batch * 16 : (batch + 1) * 16] = out[:, k * LANES : (k + 1) * LANES]
        ones = jnp.where(row_ids((16, pre.shape[1])) == 0, held, 0.0).astype(BF16)
        return sums + dot_nt(jnp.concatenate([feats, ones], axis=0), d_pre)

    return lax.fori_loop(0, (order_ref[batch, blocks] + PIECE - 1) // PIECE, one_piece, before)


def back_kernel(
    g_far,
    level_ref,
    dm_ref,
    base_ref,
    w_far,
    bias_ref,
    grad_ref,
    dg_ref,
    tail_ref,
    w_ref,
    g_ref,
    sems,
):
    batches, own, width = grad_ref.shape
    hidden_units = w_ref.shape[0]
    chunks = (hidden_units + tail_ref.shape[0]) // GROUP
    half = own // 2
    fetches = []
    for number in range(chunks):
        some = pl.ds(number * GROUP, min(GROUP, hidden_units - number * GROUP))
        rows = pl.ds(number * GROUP * half, GROUP * half)
        fetches += [
            pltpu.make_async_copy(w_far.at[some], w_ref.at[some], sems.at[number, 0]),
            pltpu.make_async_copy(g_far.at[:, rows], g_ref.at[:, rows], sems.at[number, 1]),
        ]
    for fetch in fetches:
        fetch.start()
    bias_blocks(bias_ref, tail_ref)

    pulls, levels = [], []
    for batch in range(batches):
        mine = slice(batch * own, (batch + 1) * own)
        pulls += [dm_ref[mine, step * width : (step + 1) * width] for step in range(2)]
        both = [doubled(level_ref[mine, step * width : (step + 1) * width]) for step in range(2)]
        levels.append(jnp.concatenate(both, axis=1))
    pulls = jnp.concatenate(pulls, axis=0)
    totals = [jnp.zeros((2 * own, 2 * width), F32) for batch in range(batches)]
    for number in range(chunks):
        fetches[2 * number].wait()
        fetches[2 * number + 1].wait()
        pulled = dot(pulls, weights_of(w_ref, tail_ref, number)).astype(BF16)
        at = slice(number * GROUP * half, (number + 1) * GROUP * half)
        for batch in range(batches):
            talls = [
                pulled_rows(pulled[(2 * batch + k) * own : (2 * batch + k + 1) * own], half)
                for k in range(2)
            ]
            totals[batch] = totals[batch] + dot(turned(g_ref[batch, at, :]), talls[0])
            d_pair = dot_nt(jnp.concatenate(talls, axis=1), levels[batch])
            for unit in range(0, GROUP, 2):
                row = (number * GROUP + unit) * 8
                for part in range(half // 8):
                    pair = [
                        d_pair[(unit + k) * half + part * 8 : (unit + k) * half + part * 8 + 8]
                        for k in range(2)
                    ]
                    dg_ref[batch, row : row + 16, part * LANES : (part + 1) * LANES] = jnp.concatenate(
                        pair, axis=0
                    ).astype(BF16)
    for batch in range(batches):
        grad = base_ref[batch * own : (batch + 1) * own] + totals[batch][:own, :width]
        grad_ref[batch] = (grad + totals[batch][own:, width:]).astype(BF16)


def edge_kernel(order_ref, edge_ref, dg_ref, w_in_ref, b_in_ref, before_ref, feat_ref, win_ref):
    batches = order_ref.shape[0]
    feat_ref[...] = jnp.zeros_like(feat_ref)
    sums = before_ref[...]
    for batch in range(batches):
        sums = edge_sums(
            batch, batches, order_ref, edge_ref, dg_ref, w_in_ref, b_in_ref, feat_ref, sums
        )
    win_ref[...] = sums


def add_kernel(first_ref, second_ref, out_ref):
    out_ref[...] = (first_ref[...].astype(F32) + second_ref[...].astype(F32)).astype(BF16)


def copy_kernel(in_ref, out_ref):
    out_ref[...] = in_ref[...]


def rows_kernel(first_ref, second_ref, out_ref, rows_ref):
    parts, tall, wide = first_ref.shape
    main = wide // LANES - 2
    for part in range(parts):
        total = first_ref[part].astype(F32) + second_ref[part].astype(F32)
        for block in range(main):
            rows_ref[pl.ds(block, tall, stride=main), :] = total[
                :, block * LANES : (block + 1) * LANES
            ]
        for k in range(2):
            start = tall * (main + k)
            rows_ref[start : start + tall, :] = total[:, (main + k) * LANES : (main + k + 1) * LANES]
        out_ref[part] = rows_ref[...].astype(BF16)


def rows_of(first, second):
    parts, tall, wide = first.shape
    shape = (tall * (wide // LANES), LANES)
    return full_call(
        rows_kernel,
        jax.ShapeDtypeStruct((parts,) + shape, BF16),
        (pltpu.VMEM(shape, F32),),
        cost_estimate=cost(1),
    )(first, second)


def place_kernel(tall, count, carried, *refs):
    at_ref, pieces = refs[0], refs[1 : 1 + count]
    outs = refs[1 + count + carried : 6 + count + carried]
    big_ref, little_ref, sems = refs[6 + count + carried :]
    d_w, d_bias, d_x, d_h, d_rest = outs
    waits = []
    slot = 0
    for k, piece in enumerate(pieces):
        chunks, rows_in, lanes = piece.shape
        main = rows_in // tall - 2
        for chunk in range(chunks):
            code = at_ref[k] ^ chunk
            line, part = code >> 2, code & 3
            at = pl.ds(pl.multiple_of(line * tall, 8), tall)
            rows = piece[chunk].astype(F32)
            for row in range(tall):
                big_ref[slot, :, row * lanes : (row + 1) * lanes] = rows[row * main : (row + 1) * main]
            copy = pltpu.make_async_copy(
                big_ref.at[slot],
                d_w.at[
                    pl.ds(pl.multiple_of(part * main, 8), main),
                    pl.ds(pl.multiple_of(line * (tall * lanes), LANES), tall * lanes),
                ],
                sems.at[slot, 0],
            )
            copy.start()
            waits.append(copy)

            for side in range(2):
                start = tall * (main + side)
                little_ref[slot, side] = rows[start : start + tall]

                def move(target, lane):
                    lane = jnp.maximum(lane, 0) * lanes
                    to = pl.ds(pl.multiple_of(jnp.minimum(lane, target.shape[1] - lanes), LANES), lanes)
                    return pltpu.make_async_copy(
                        little_ref.at[slot, side], target.at[at, to], sems.at[slot, 1 + side]
                    )

                block = 2 * part + side
                to_x, to_h = move(d_x, block - 1), move(d_h, block - 4)
                alone = move((d_bias, d_rest)[side], 0)
                lone = block == 7 * side
                pl.when(lone)(alone.start)
                pl.when((block > 0) & (block < 4))(to_x.start)
                pl.when((block > 3) & (block < 7))(to_h.start)
                waits.append(alone)
            slot += 1
    for copy in waits:
        copy.wait()


def cost(micros):
    return pl.CostEstimate(
        flops=int(micros * 1e9), bytes_accessed=int(micros * 3e6), transcendentals=0
    )


def place_pieces(tall, at, pieces, shapes, before=()):
    count = len(pieces)
    chunks, rows_in, lanes = pieces[0].shape
    slots = count * chunks
    vmem = pl.BlockSpec(memory_space=pltpu.VMEM)
    hbm = pl.BlockSpec(memory_space=pl.ANY)
    return pl.pallas_call(
        functools.partial(place_kernel, tall, count, len(before)),
        out_shape=shapes,
        in_specs=[pl.BlockSpec(memory_space=pltpu.SMEM)] + [vmem] * count + [hbm] * len(before),
        out_specs=[hbm] * len(shapes),
        scratch_shapes=(
            pltpu.VMEM((slots, rows_in // tall - 2, tall * lanes), F32),
            pltpu.VMEM((slots, 2, tall, lanes), F32),
            pltpu.SemaphoreType.DMA((slots, 3)),
        ),
        input_output_aliases={1 + count + k: k for k in range(len(before))},
        cost_estimate=cost(slots / 4),
        compiler_params=pltpu.CompilerParams(vmem_limit_bytes=16 * MIB),
    )(at, *pieces, *before)


def body(
    states,
    edge_feats,
    source_index,
    target_index,
    w_edge_in,
    b_edge_in,
    w_edge_out,
    b_edge_out,
    w_input,
    w_hidden,
    b_input,
    b_hidden,
    cotangent,
):
    batches, own, width = states.shape
    edges = source_index.shape[1]
    owners = lax.axis_size("edge")
    cap = max(2, 2 * edges // owners)
    feat_count, units = w_edge_in.shape

    sent = full_call(
        functools.partial(route_kernel, own),
        jax.ShapeDtypeStruct((owners, batches * feat_count + 16, cap), BF16),
        limit=60,
    )(source_index, target_index, edge_feats)
    edge_data = lax.all_to_all(sent, "edge", 0, 0, tiled=True)
    merge = max(1, LANES // cap)
    if merge > 1:
        edge_data = edge_data.reshape(owners // merge, merge, -1, cap).transpose(0, 2, 1, 3)
        edge_data = edge_data.reshape(owners // merge, -1, merge * cap)

    w_mats = w_edge_out.reshape(units, width, width)
    padded = (units + 2 + GROUP - 1) // GROUP * GROUP

    tall = width // 8
    pairs = own // 2
    blocks = edge_data.shape[0]
    core = lax.axis_index("graph")
    spot = lax.axis_index("edge")
    orders = ((0, 1, 2, 3), (2, 0, 1, 3))

    def bit(side, step):
        first, second = [(spot >> orders[k][step]) & 1 for k in range(2)]
        return jnp.where(side == 0, first, second)

    where = jnp.stack([core, bit(core, 0), bit(1 - core, 0)])
    smem = pl.BlockSpec(memory_space=pltpu.SMEM)
    vmem = pl.BlockSpec(memory_space=pltpu.VMEM)
    far = pl.BlockSpec(memory_space=pltpu.HBM)
    bias = b_edge_out.reshape(width, width)
    quarter = jax.ShapeDtypeStruct((2, 4, tall, (units // 4 + 2) * width), BF16)
    new_states, *sums, g_pairs, levels, d_mails, base, order, first = full_call(
        main_kernel,
        (
            jax.ShapeDtypeStruct((batches * own, width), BF16),
            *[quarter] * 4,
            jax.ShapeDtypeStruct((batches, padded * pairs, LANES), BF16),
            jax.ShapeDtypeStruct((batches * own, 2 * width), BF16),
            jax.ShapeDtypeStruct((batches * own, 2 * width), BF16),
            jax.ShapeDtypeStruct((batches * own, width), F32),
            jax.ShapeDtypeStruct((batches, blocks + 1), jnp.int32),
            jax.ShapeDtypeStruct((32, width), F32),
        ),
        (
            pltpu.VMEM((units, PIECE * LANES), F32),
            pltpu.VMEM((padded * 8, 512), F32),
            pltpu.VMEM((batches, padded * pairs, LANES), BF16),
            pltpu.VMEM((2 * batches * own, padded * width), BF16),
            pltpu.VMEM((units, width, width), BF16),
            pltpu.VMEM((padded - units, width, width), BF16),
            pltpu.VMEM((4,) + quarter.shape, BF16),
            pltpu.SemaphoreType.DMA((4,) + quarter.shape[:2]),
            pltpu.SemaphoreType.DMA((2,)),
        ),
        limit=60,
        in_specs=[smem] + [vmem] * 5 + [far] + [vmem] * 5,
        out_specs=[vmem] + [far] * 5 + [vmem] * 3 + [smem, vmem],
    )(
        where,
        edge_data,
        states.reshape(batches * own, width),
        cotangent.reshape(batches * own, width),
        w_edge_in,
        b_edge_in,
        w_mats,
        bias,
        w_input,
        w_hidden,
        b_input,
        b_hidden,
    )

    cores = lax.axis_size("graph")

    def to_core(value):
        return lax.ppermute(value, "graph", [(0, 1), (1, 0)])

    def swap(value, masks):
        moves = []
        for side in range(cores):
            first = side * owners
            moves += [(first + k, first + (k ^ masks[side])) for k in range(owners)]
        return lax.ppermute(value, ("graph", "edge"), moves)

    def swap_step(value, step):
        return swap(value, [1 << orders[side][step] for side in range(cores)])

    def pick(value, number):
        return lax.dynamic_index_in_dim(value, number, 0, False)

    def added(terms):
        return sum(one.astype(F32) for one in terms)

    def after(value, *others):
        return lax.optimization_barrier((value, *others))[0]

    def first_grads(pairs_in):
        return full_call(
            back_kernel,
            (
                jax.ShapeDtypeStruct((batches, own, width), BF16),
                jax.ShapeDtypeStruct((batches, padded * 8, 512), BF16),
            ),
            (
                pltpu.VMEM((padded - units, width, width), BF16),
                pltpu.VMEM((units, width, width), BF16),
                pltpu.VMEM((batches, padded * pairs, LANES), BF16),
                pltpu.SemaphoreType.DMA((padded // GROUP, 2)),
            ),
            limit=60,
            in_specs=[far] + [vmem] * 3 + [far, vmem],
            cost_estimate=cost(12),
        )(pairs_in, levels, d_mails, base, w_mats, bias)

    def second_grads(d_pairs):
        return full_call(
            edge_kernel,
            (
                jax.ShapeDtypeStruct((blocks, batches * feat_count, LANES), BF16),
                jax.ShapeDtypeStruct((32, units), F32),
            ),
            limit=60,
            in_specs=[smem] + [vmem] * 5,
            cost_estimate=cost(9),
        )(order, edge_data, d_pairs, w_edge_in, b_edge_in, first)

    bits = owners.bit_length() - 1

    def hop(first, feats, number):
        axis, side = bits - 1 - number, 1 - ((spot >> number) & 1)
        masks = [1 << number] * cores
        give = lax.dynamic_index_in_dim(feats, side, axis, False)
        return swap(first, masks), swap(give, masks), side, axis

    def ride(big, first, feats, number):
        more, got, side, axis = hop(first, feats, number)
        big, more, got = lax.optimization_barrier((big, more, got))
        return big, first + more, lax.dynamic_update_index_in_dim(feats, got, side, axis)

    kept_first, kept_last, given_first, given_last = sums
    got_first, got_last = to_core(given_first), to_core(given_last)
    kept_first = full_call(
        copy_kernel, jax.ShapeDtypeStruct(kept_first.shape, BF16), cost_estimate=cost(1)
    )(kept_first)
    give = full_call(
        add_kernel, jax.ShapeDtypeStruct(kept_first.shape, BF16), cost_estimate=cost(1)
    )(kept_first, got_first)
    terms = [kept_last, got_last]
    for step in range(3):
        if step > 0:
            number = bit(core, step)
            give = added([pick(one, 1 - number) for one in terms]).astype(BF16)
            terms = [pick(one, number) for one in terms]
        got = swap_step(give, step)
        if step == 0:
            state_grad, d_pairs = first_grads(after(g_pairs, give))
            got = after(got, state_grad)
        if step == 1:
            feats, first = second_grads(after(d_pairs, give))
            if merge > 1:
                feats = feats.reshape(blocks, -1, merge, cap).transpose(0, 2, 1, 3)
            feats = feats.reshape((2,) * bits + (batches * feat_count, cap))
            got = after(got, first)
        if step == 2:
            got, first, feats = ride(got, first, feats, 2)
        terms.append(got)
        if step == 0:
            terms = [one.reshape((2, 2, 2) + one.shape[2:]) for one in terms]
    total = added(terms).astype(BF16)
    first, feats = after(first, total), after(feats, total)
    for extra in range(3, owners.bit_length() - 1):
        got = swap(total, [1 << extra] * cores)
        if extra > 3:
            got, first, feats = ride(got, first, feats, extra)
        if extra < owners.bit_length() - 2:
            total = added([total, got]).astype(BF16)
    more, moved, side, axis = hop(first, feats, 0)
    feats = lax.dynamic_update_index_in_dim(feats, moved, side, axis)
    got, first, feats = ride(got, first + more, feats, 1)
    held = rows_of(total, got)

    got, first, feats = ride(swap_step(held, 2), first, feats, 3)
    held = jnp.concatenate([held, got], axis=0)
    across = swap_step(held, 0)
    shapes = tuple(
        jax.ShapeDtypeStruct(shape, F32)
        for shape in (
            (units, width * width),
            (width, width),
            (width, 3 * width),
            (width, 3 * width),
            (width, width),
        )
    )
    outs = ()
    def place(outs, pieces):
        at = []
        for _, side, flips in pieces:
            code = side
            for step in range(3):
                code = code * 2 + bit(side, step)
            at.append((code * 2) ^ flips)
        return place_pieces(tall, jnp.stack(at), [one for one, _, _ in pieces], shapes, outs)

    outs = place((), [(held, core, 0), (to_core(held), 1 - core, 0)])
    outs, near, more = lax.optimization_barrier((outs, swap_step(held, 1), to_core(first)))
    first = first + more
    small_outs = (
        first[:feat_count],
        first[feat_count],
        first[24:27].reshape(-1),
        first[27:30].reshape(-1),
    )
    last = swap_step(near, 0)
    near_other, across_other = to_core(near), to_core(across)
    feat_grad = full_call(
        functools.partial(unroute_kernel, own),
        jax.ShapeDtypeStruct((batches, feat_count, edges), BF16),
        cost_estimate=cost(1.4),
    )(source_index, feats.reshape(owners, batches, feat_count, cap))
    outs = place(
        outs,
        [
            (near, core, 4),
            (near_other, 1 - core, 4),
            (across, core, 8),
            (across_other, 1 - core, 8),
        ],
    )
    outs, last, feat_grad, small_outs = lax.optimization_barrier(
        (outs, last, feat_grad, small_outs)
    )
    other = to_core(last)
    outs = place(outs, [(last, core, 12)])
    outs = place(outs, [(other, 1 - core, 12)])
    d_w, d_bias, d_x, d_h, _ = outs
    return (
        new_states.reshape(batches, own, width),
        state_grad,
        feat_grad,
        small_outs[0],
        small_outs[1],
        d_w,
        d_bias.reshape(-1),
        d_x,
        d_h,
        small_outs[2],
        small_outs[3],
    )


def solution(mesh):
    spread = ("graph", "edge")
    rows = P(None, spread, None)
    edges = P(None, spread)
    feats = P(None, None, spread)
    in_specs = (rows, feats, edges, edges) + (P(),) * 8 + (rows,)
    out_specs = (rows, rows, feats) + (P(),) * 8
    return jax.shard_map(
        body,
        mesh=mesh,
        in_specs=in_specs,
        out_specs=out_specs,
        check_vma=False,
    )
```

```python
import functools

import jax
import jax.numpy as jnp
from jax import lax
from jax.experimental import pallas as pl
from jax.experimental.pallas import tpu as pltpu
from jax.sharding import PartitionSpec as P

F32 = jnp.float32
BF16 = jnp.bfloat16
LANES = 128
PIECE = 4
GROUP = 12
MIB = 1024 * 1024


def dot(first, second, dims=((1,), (0,))):
    return lax.dot_general(first, second, (dims, ((), ())), preferred_element_type=F32)


def dot_nt(first, second):
    return dot(first, second, ((1,), (1,)))


def row_ids(shape):
    return lax.broadcasted_iota(jnp.int32, shape, 0)


def col_ids(shape):
    return lax.broadcasted_iota(jnp.int32, shape, 1)


def full_call(kernel, out_shape, scratch=(), limit=16, **more):
    return pl.pallas_call(
        kernel,
        out_shape=out_shape,
        scratch_shapes=scratch,
        compiler_params=pltpu.CompilerParams(vmem_limit_bytes=limit * MIB),
        **more,
    )


def ranks_of(owner, owners):
    hits = (row_ids((owners, owner.shape[1])) == owner).astype(F32)
    before = (row_ids((LANES, LANES)) < col_ids((LANES, LANES))).astype(BF16)
    seen = jnp.zeros((owners, 1), F32)
    ranks = []
    for start in range(0, owner.shape[1], LANES):
        part = hits[:, start : start + LANES]
        place = dot(part.astype(BF16), before) + seen
        ranks.append(jnp.sum(part * place, axis=0, keepdims=True))
        seen = seen + jnp.sum(part, axis=1, keepdims=True)
    return hits, jnp.concatenate(ranks, axis=1)


def route_kernel(own_rows, src_ref, dst_ref, feat_ref, out_ref):
    owners, rows, cap = out_ref.shape
    batches, feats, edges = feat_ref.shape
    shift = own_rows.bit_length() - 1
    marks = [jnp.zeros((16, cap), F32)] * owners
    for batch in range(batches):
        source, target = src_ref[batch : batch + 1], dst_ref[batch : batch + 1]
        owner = source >> shift
        hits, rank = ranks_of(owner, owners)
        spots = (row_ids((cap, edges)) == rank.astype(jnp.int32)).astype(BF16)
        line = row_ids((16, edges)) - 3 * batch
        first = owner << shift
        extra = jnp.where(line == 0, source - first, jnp.where(line == 1, target - first, 1))
        extra = jnp.where((line >= 0) & (line < 3), extra, 0).astype(F32)
        load = jnp.concatenate([feat_ref[batch].astype(F32), extra], axis=0)
        masked = [(load * hits[part : part + 1]).astype(BF16) for part in range(owners)]
        out = dot_nt(jnp.concatenate(masked, axis=0), spots)
        for part in range(owners):
            tile = out[part * (feats + 16) : (part + 1) * (feats + 16)]
            out_ref[part, batch * feats : (batch + 1) * feats] = tile[:feats].astype(BF16)
            marks[part] = marks[part] + tile[feats:]
    for part in range(owners):
        out_ref[part, batches * feats :] = marks[part].astype(BF16)


def unroute_kernel(own_rows, src_ref, back_ref, out_ref):
    owners, batches, rows, cap = back_ref.shape
    edges = src_ref.shape[1]
    shift = own_rows.bit_length() - 1
    for batch in range(batches):
        hits, rank = ranks_of(src_ref[batch : batch + 1] >> shift, owners)
        spots = (row_ids((cap, edges)) == rank.astype(jnp.int32)).astype(BF16)
        parts = [back_ref[part, batch] for part in range(owners)]
        spread = dot(jnp.concatenate(parts, axis=0), spots)
        total = jnp.zeros((rows, edges), F32)
        for part in range(owners):
            total = total + spread[part * rows : (part + 1) * rows] * hits[part : part + 1]
        out_ref[batch] = total.astype(BF16)


def edge_piece(batches, order_ref, edge_ref, piece, batch):
    some = [edge_ref[order_ref[batch, PIECE * piece + k]] for k in range(PIECE)]
    block = jnp.concatenate(some, axis=1)
    feats, marks = block[batch * 16 : (batch + 1) * 16], block[batches * 16 :].astype(F32)
    source = marks[3 * batch : 3 * batch + 1].astype(jnp.int32)
    target = marks[3 * batch + 1 : 3 * batch + 2].astype(jnp.int32)
    held = marks[3 * batch + 2 : 3 * batch + 3]
    code = ((target >> 3) & 3) * 128 + (target >> 5) * 64 + source
    code = jnp.where(held > 0.5, code, -1)
    pairs = (row_ids((512, block.shape[1])) == code).astype(BF16)
    low = row_ids((8, block.shape[1])) == (target & 7)
    return feats, held, pairs, low


def order_blocks(batches, edge_ref, order_ref):
    blocks = edge_ref.shape[0]
    for batch in range(batches):
        front, back = jnp.int32(0), jnp.int32(blocks - 1)
        row = 3 * batch + 2
        for block in range(blocks):
            marks = edge_ref[block, batches * 16 :].astype(F32)
            held = jnp.max(marks[row : row + 1]) > 0.5
            order_ref[batch, jnp.where(held, front, back)] = jnp.int32(block)
            step = held.astype(jnp.int32)
            front, back = front + step, back - (1 - step)
        order_ref[batch, blocks] = front


def first_layer(w_in_ref, b_in_ref):
    bias = jnp.broadcast_to(b_in_ref[...].reshape(1, -1), (8, b_in_ref.shape[0]))
    return w_in_ref[...].astype(F32).T.astype(BF16), bias.T[:, :1]


def gates_of(mail_low, level, w_x, w_h, b_x, b_h):
    width = level.shape[1]
    from_mail = dot(mail_low, w_x[...]) + b_x[...].reshape(1, -1)
    from_state = dot(level, w_h[...]) + b_h[...].reshape(1, -1)
    reset = jax.nn.sigmoid(from_mail[:, :width] + from_state[:, :width])
    update = jax.nn.sigmoid(from_mail[:, width : 2 * width] + from_state[:, width : 2 * width])
    state_part = from_state[:, 2 * width :]
    candidate = jnp.tanh(from_mail[:, 2 * width :] + reset * state_part)
    return reset, update, candidate, state_part


def doubled(level):
    blank = jnp.zeros_like(level)
    return jnp.concatenate(
        [jnp.concatenate([level, blank], axis=1), jnp.concatenate([blank, level], axis=1)], axis=0
    )


def bias_blocks(bias_ref, tail_ref):
    tail_ref[...] = jnp.zeros_like(tail_ref)
    high = bias_ref[...].astype(BF16)
    tail_ref[0] = high
    tail_ref[1] = (bias_ref[...] - high.astype(F32)).astype(BF16)


def turned(tile):
    size = tile.shape[1]
    eye = (row_ids((size, size)) == col_ids((size, size))).astype(F32).astype(BF16)
    return dot_nt(eye, tile).astype(BF16)


def weights_of(w_ref, tail_ref, number):
    units = w_ref.shape[0]
    blocks = []
    for unit in range(number * GROUP, (number + 1) * GROUP):
        blocks.append(w_ref[unit] if unit < units else tail_ref[unit - units])
    return jnp.concatenate(blocks, axis=1)


def pulled_rows(pulled, half):
    rows = []
    for start in range(0, pulled.shape[1], LANES):
        tile = pulled[:, start : start + LANES]
        rows.append(jnp.concatenate([tile[:half], tile[half:]], axis=1))
    return jnp.concatenate(rows, axis=0)


def main_kernel(
    where_ref,
    edge_ref,
    state_ref,
    cot_ref,
    w_in_ref,
    b_in_ref,
    w_far,
    bias_ref,
    w_x,
    w_h,
    b_x,
    b_h,
    new_ref,
    kept_first,
    kept_last,
    given_first,
    given_last,
    g_far,
    level_ref,
    dm_ref,
    base_ref,
    order_ref,
    rows_ref,
    hid_ref,
    acc_ref,
    g_ref,
    p_ref,
    w_ref,
    tail_ref,
    sum_ref,
    sum_sems,
    sems,
):
    fetch = pltpu.make_async_copy(w_far, w_ref, sems.at[0])
    fetch.start()
    blocks = edge_ref.shape[0]
    batches = g_ref.shape[0]
    hidden_units = hid_ref.shape[0]
    units = acc_ref.shape[0] // 8
    own = state_ref.shape[0] // batches
    half = own // 2
    span = GROUP * half
    wide = GROUP * LANES
    chunks = units // GROUP
    order_blocks(batches, edge_ref, order_ref)
    bias_blocks(bias_ref, tail_ref)
    w_in, b_in = first_layer(w_in_ref, b_in_ref)

    for batch in range(batches):
        acc_ref[...] = jnp.zeros_like(acc_ref)

        def add_piece(piece, carry):
            feats, held, pairs, low = edge_piece(batches, order_ref, edge_ref, piece, batch)
            pre = dot(w_in, feats) + b_in
            hid_ref[...] = (pre * jax.nn.sigmoid(pre)).astype(BF16).astype(F32)
            ones = jnp.where(low, 1.0, 0.0)
            parts = []
            for unit in range(0, hidden_units, 2):
                two = [jnp.where(low, hid_ref[unit + k : unit + k + 1], 0.0) for k in range(2)]
                parts.append(jnp.concatenate(two, axis=0).astype(BF16))
            parts.append(jnp.concatenate([ones, ones], axis=0).astype(BF16))
            parts.append(jnp.zeros((8 * (units - hidden_units - 2), pre.shape[1]), BF16))
            acc_ref[...] += dot_nt(jnp.concatenate(parts, axis=0), pairs)
            return carry

        lax.fori_loop(0, (order_ref[batch, blocks] + PIECE - 1) // PIECE, add_piece, 0)

        def place(step, carry):
            for four in range(3):
                rows = []
                for k in range(4):
                    for part in range(4):
                        start = pl.multiple_of(step * 96 + four * 32 + k * 8, 8)
                        rows.append(acc_ref[pl.ds(start, 8), part * LANES : (part + 1) * LANES])
                at = pl.ds(pl.multiple_of((step * 3 + four) * LANES, LANES), LANES)
                g_ref[batch, at, :] = jnp.concatenate(rows, axis=0).astype(BF16)
            return carry

        lax.fori_loop(0, units // 12, place, 0)

    def forward(step, level):
        two = [doubled(level[batch * own : (batch + 1) * own]) for batch in range(batches)]
        mail = jnp.zeros((batches * own, LANES), F32)
        base = step * batches * own
        for number in range(chunks):
            for batch in range(batches):
                out = dot(g_ref[batch, number * span : (number + 1) * span, :], two[batch])
                out = out.astype(BF16)
                for unit in range(GROUP):
                    lane = number * wide + unit * LANES
                    for part in range(2):
                        row = base + batch * own + part * half
                        p_ref[row : row + half, lane : lane + LANES] = out[
                            unit * half : (unit + 1) * half, part * LANES : (part + 1) * LANES
                        ]
            rows = p_ref[base : base + batches * own, number * wide : (number + 1) * wide]
            mail = mail + dot_nt(rows, weights_of(w_ref, tail_ref, number))
        return mail

    def backward(d_mail):
        sums = [jnp.zeros((LANES, 2 * LANES), F32) for batch in range(batches)]
        for number in range(chunks):
            pulled = dot(d_mail, weights_of(w_ref, tail_ref, number)).astype(BF16)
            at = slice(number * span, (number + 1) * span)
            for batch in range(batches):
                tall = pulled_rows(pulled[batch * own : (batch + 1) * own], half)
                sums[batch] = sums[batch] + dot(turned(g_ref[batch, at, :]), tall)
        return jnp.concatenate([one[:own, :LANES] + one[own:, LANES:] for one in sums], axis=0)

    weights = (w_x, w_h, b_x, b_h)
    level_zero = state_ref[...]
    state_zero = level_zero.astype(F32)
    leave = pltpu.make_async_copy(g_ref, g_far, sems.at[1])
    leave.start()
    fetch.wait()
    mail_zero = forward(0, level_zero).astype(BF16)
    gates_zero = gates_of(mail_zero, level_zero, *weights)
    state_one = (1.0 - gates_zero[1]) * gates_zero[2] + gates_zero[1] * state_zero
    level_one = state_one.astype(BF16)
    mail_one = forward(1, level_one).astype(BF16)
    gates_one = gates_of(mail_one, level_one, *weights)
    new_ref[...] = ((1.0 - gates_one[1]) * gates_one[2] + gates_one[1] * state_one).astype(BF16)

    def gru_back(d_next, gates, current):
        reset, update, candidate, state_part = gates
        d_cand = d_next * (1.0 - update) * (1.0 - candidate * candidate)
        d_reset = d_cand * state_part * reset * (1.0 - reset)
        d_update = d_next * (current - candidate) * update * (1.0 - update)
        dg_mail = jnp.concatenate([d_reset, d_update, d_cand], axis=1).astype(BF16)
        dg_state = jnp.concatenate([d_reset, d_update, d_cand * reset], axis=1).astype(BF16)
        d_mail = dot_nt(dg_mail, w_x[...]).astype(BF16)
        d_current = d_next * update + dot_nt(dg_state, w_h[...])
        return dg_mail, dg_state, d_mail, d_current

    dgm_one, dgs_one, dm_one, d_state = gru_back(cot_ref[...].astype(F32), gates_one, state_one)
    d_state = d_state + backward(dm_one)
    dgm_zero, dgs_zero, dm_zero, d_state = gru_back(d_state, gates_zero, state_zero)
    base_ref[...] = d_state
    level_ref[...] = jnp.concatenate([level_zero, level_one], axis=1)
    dm_ref[...] = jnp.concatenate([dm_zero, dm_one], axis=1)

    def both(first, second):
        return jnp.concatenate([first.astype(F32), second.astype(F32)], axis=0)

    dms = both(dm_zero, dm_one).T
    mails, levels = both(mail_zero, mail_one), both(level_zero, level_one)
    dgm, dgs = both(dgm_zero, dgm_one), both(dgs_zero, dgs_one)
    width = dgm.shape[1]
    rows_ref[...] = jnp.zeros_like(rows_ref)
    for k, one in enumerate((dgm, dgs)):
        total = jnp.sum(one, axis=0, keepdims=True)
        for part in range(3):
            row = 24 + 3 * k + part
            rows_ref[row : row + 1, :] = total[:, part * LANES : (part + 1) * LANES]
    small = jnp.concatenate(
        [
            dot(dms.astype(BF16), p_ref[:, hidden_units * LANES : (hidden_units + 1) * LANES]),
            dot(mails.T.astype(BF16), dgm.astype(BF16)),
            dot(levels.T.astype(BF16), dgs.astype(BF16)),
            jnp.zeros((2 * own, LANES), F32),
        ],
        axis=1,
    )

    def sorted_rows(value):
        rows = value.shape[0] // 2
        upper, lower = value[:rows], value[rows:]
        halves = [jnp.where(where_ref[0] == k, upper, lower) for k in range(2)]
        parts = []
        for k, one in enumerate(halves):
            first, second = one[: rows // 2], one[rows // 2 :]
            parts += [jnp.where(where_ref[1 + k] == side, second, first) for side in range(2)]
        return jnp.concatenate(parts, axis=0).astype(BF16)

    dms, small = sorted_rows(dms), sorted_rows(small)
    rows_in, groups, tall, wide_out = kept_first.shape
    taken = wide_out - 2 * LANES
    moves = []
    for group in range(groups):
        out = dot(dms, p_ref[:, group * taken : (group + 1) * taken]).astype(BF16)
        extra = small[:, group * 2 * LANES : (group + 1) * 2 * LANES]
        for k, ref in enumerate((given_first, kept_first, given_last, kept_last)):
            for row in range(rows_in):
                at = ((2, 0, 3, 1)[k] * rows_in + row) * tall
                sum_ref[k, row, group, :, :taken] = out[at : at + tall]
                sum_ref[k, row, group, :, taken:] = extra[at : at + tall]
                moves.append(
                    pltpu.make_async_copy(
                        sum_ref.at[k, row, group], ref.at[row, group], sum_sems.at[k, row, group]
                    )
                )
                moves[-1].start()
    for move in moves:
        move.wait()
    leave.wait()


def edge_sums(batch, batches, order_ref, edge_ref, dg_ref, w_in_ref, b_in_ref, feat_ref, before):
    blocks = edge_ref.shape[0]
    hidden_units = w_in_ref.shape[1]
    w_in, b_in = first_layer(w_in_ref, b_in_ref)
    fold = (col_ids((hidden_units, 8 * hidden_units)) >> 3) == row_ids(
        (hidden_units, 8 * hidden_units)
    )
    fold = fold.astype(F32).astype(BF16)

    def one_piece(piece, sums):
        feats, held, pairs, low = edge_piece(batches, order_ref, edge_ref, piece, batch)
        pre = dot(w_in, feats) + b_in
        sig = jax.nn.sigmoid(pre)
        spread = dot(dg_ref[batch, : 8 * hidden_units], pairs)
        spread = spread.reshape(hidden_units, 8, pre.shape[1])
        spread = jnp.where(low[None], spread, 0.0).reshape(8 * hidden_units, pre.shape[1])
        d_hidden = dot(fold, spread.astype(BF16))
        d_pre = (d_hidden * sig * (1.0 + pre * (1.0 - sig))).astype(BF16)
        out = dot(w_in_ref[...], d_pre).astype(BF16)
        for k in range(PIECE):
            at = order_ref[batch, PIECE * piece + k]
            feat_ref[at, batch * 16 : (batch + 1) * 16] = out[:, k * LANES : (k + 1) * LANES]
        ones = jnp.where(row_ids((16, pre.shape[1])) == 0, held, 0.0).astype(BF16)
        return sums + dot_nt(jnp.concatenate([feats, ones], axis=0), d_pre)

    return lax.fori_loop(0, (order_ref[batch, blocks] + PIECE - 1) // PIECE, one_piece, before)


def back_kernel(
    g_far,
    level_ref,
    dm_ref,
    base_ref,
    w_far,
    bias_ref,
    grad_ref,
    dg_ref,
    tail_ref,
    w_ref,
    g_ref,
    sems,
):
    batches, own, width = grad_ref.shape
    hidden_units = w_ref.shape[0]
    chunks = (hidden_units + tail_ref.shape[0]) // GROUP
    half = own // 2
    fetches = []
    for number in range(chunks):
        some = pl.ds(number * GROUP, min(GROUP, hidden_units - number * GROUP))
        rows = pl.ds(number * GROUP * half, GROUP * half)
        fetches += [
            pltpu.make_async_copy(w_far.at[some], w_ref.at[some], sems.at[number, 0]),
            pltpu.make_async_copy(g_far.at[:, rows], g_ref.at[:, rows], sems.at[number, 1]),
        ]
    for fetch in fetches:
        fetch.start()
    bias_blocks(bias_ref, tail_ref)

    pulls, levels = [], []
    for batch in range(batches):
        mine = slice(batch * own, (batch + 1) * own)
        pulls += [dm_ref[mine, step * width : (step + 1) * width] for step in range(2)]
        both = [doubled(level_ref[mine, step * width : (step + 1) * width]) for step in range(2)]
        levels.append(jnp.concatenate(both, axis=1))
    pulls = jnp.concatenate(pulls, axis=0)
    totals = [jnp.zeros((2 * own, 2 * width), F32) for batch in range(batches)]
    for number in range(chunks):
        fetches[2 * number].wait()
        fetches[2 * number + 1].wait()
        pulled = dot(pulls, weights_of(w_ref, tail_ref, number)).astype(BF16)
        at = slice(number * GROUP * half, (number + 1) * GROUP * half)
        for batch in range(batches):
            talls = [
                pulled_rows(pulled[(2 * batch + k) * own : (2 * batch + k + 1) * own], half)
                for k in range(2)
            ]
            totals[batch] = totals[batch] + dot(turned(g_ref[batch, at, :]), talls[0])
            d_pair = dot_nt(jnp.concatenate(talls, axis=1), levels[batch])
            for unit in range(0, GROUP, 2):
                row = (number * GROUP + unit) * 8
                for part in range(half // 8):
                    pair = [
                        d_pair[(unit + k) * half + part * 8 : (unit + k) * half + part * 8 + 8]
                        for k in range(2)
                    ]
                    dg_ref[batch, row : row + 16, part * LANES : (part + 1) * LANES] = jnp.concatenate(
                        pair, axis=0
                    ).astype(BF16)
    for batch in range(batches):
        grad = base_ref[batch * own : (batch + 1) * own] + totals[batch][:own, :width]
        grad_ref[batch] = (grad + totals[batch][own:, width:]).astype(BF16)


def edge_kernel(order_ref, edge_ref, dg_ref, w_in_ref, b_in_ref, before_ref, feat_ref, win_ref):
    batches = order_ref.shape[0]
    feat_ref[...] = jnp.zeros_like(feat_ref)
    sums = before_ref[...]
    for batch in range(batches):
        sums = edge_sums(
            batch, batches, order_ref, edge_ref, dg_ref, w_in_ref, b_in_ref, feat_ref, sums
        )
    win_ref[...] = sums


def add_kernel(first_ref, second_ref, out_ref):
    out_ref[...] = (first_ref[...].astype(F32) + second_ref[...].astype(F32)).astype(BF16)


def copy_kernel(in_ref, out_ref):
    out_ref[...] = in_ref[...]


def rows_kernel(first_ref, second_ref, out_ref, rows_ref):
    parts, tall, wide = first_ref.shape
    main = wide // LANES - 2
    for part in range(parts):
        total = first_ref[part].astype(F32) + second_ref[part].astype(F32)
        for block in range(main):
            rows_ref[pl.ds(block, tall, stride=main), :] = total[
                :, block * LANES : (block + 1) * LANES
            ]
        for k in range(2):
            start = tall * (main + k)
            rows_ref[start : start + tall, :] = total[:, (main + k) * LANES : (main + k + 1) * LANES]
        out_ref[part] = rows_ref[...].astype(BF16)


def rows_of(first, second):
    parts, tall, wide = first.shape
    shape = (tall * (wide // LANES), LANES)
    return full_call(
        rows_kernel,
        jax.ShapeDtypeStruct((parts,) + shape, BF16),
        (pltpu.VMEM(shape, F32),),
        cost_estimate=cost(1),
    )(first, second)


def place_kernel(tall, count, carried, *refs):
    at_ref, pieces = refs[0], refs[1 : 1 + count]
    outs = refs[1 + count + carried : 6 + count + carried]
    big_ref, little_ref, sems = refs[6 + count + carried :]
    d_w, d_bias, d_x, d_h, d_rest = outs
    waits = []
    slot = 0
    for k, piece in enumerate(pieces):
        chunks, rows_in, lanes = piece.shape
        main = rows_in // tall - 2
        for chunk in range(chunks):
            code = at_ref[k] ^ chunk
            line, part = code >> 2, code & 3
            at = pl.ds(pl.multiple_of(line * tall, 8), tall)
            rows = piece[chunk].astype(F32)
            for row in range(tall):
                big_ref[slot, :, row * lanes : (row + 1) * lanes] = rows[row * main : (row + 1) * main]
            copy = pltpu.make_async_copy(
                big_ref.at[slot],
                d_w.at[
                    pl.ds(pl.multiple_of(part * main, 8), main),
                    pl.ds(pl.multiple_of(line * (tall * lanes), LANES), tall * lanes),
                ],
                sems.at[slot, 0],
            )
            copy.start()
            waits.append(copy)

            for side in range(2):
                start = tall * (main + side)
                little_ref[slot, side] = rows[start : start + tall]

                def move(target, lane):
                    lane = jnp.maximum(lane, 0) * lanes
                    to = pl.ds(pl.multiple_of(jnp.minimum(lane, target.shape[1] - lanes), LANES), lanes)
                    return pltpu.make_async_copy(
                        little_ref.at[slot, side], target.at[at, to], sems.at[slot, 1 + side]
                    )

                block = 2 * part + side
                to_x, to_h = move(d_x, block - 1), move(d_h, block - 4)
                alone = move((d_bias, d_rest)[side], 0)
                lone = block == 7 * side
                pl.when(lone)(alone.start)
                pl.when((block > 0) & (block < 4))(to_x.start)
                pl.when((block > 3) & (block < 7))(to_h.start)
                waits.append(alone)
            slot += 1
    for copy in waits:
        copy.wait()


def cost(micros):
    return pl.CostEstimate(
        flops=int(micros * 1e9), bytes_accessed=int(micros * 3e6), transcendentals=0
    )


def place_pieces(tall, at, pieces, shapes, before=()):
    count = len(pieces)
    chunks, rows_in, lanes = pieces[0].shape
    slots = count * chunks
    vmem = pl.BlockSpec(memory_space=pltpu.VMEM)
    hbm = pl.BlockSpec(memory_space=pl.ANY)
    return pl.pallas_call(
        functools.partial(place_kernel, tall, count, len(before)),
        out_shape=shapes,
        in_specs=[pl.BlockSpec(memory_space=pltpu.SMEM)] + [vmem] * count + [hbm] * len(before),
        out_specs=[hbm] * len(shapes),
        scratch_shapes=(
            pltpu.VMEM((slots, rows_in // tall - 2, tall * lanes), F32),
            pltpu.VMEM((slots, 2, tall, lanes), F32),
            pltpu.SemaphoreType.DMA((slots, 3)),
        ),
        input_output_aliases={1 + count + k: k for k in range(len(before))},
        cost_estimate=cost(slots / 4),
        compiler_params=pltpu.CompilerParams(vmem_limit_bytes=16 * MIB),
    )(at, *pieces, *before)


def body(
    states,
    edge_feats,
    source_index,
    target_index,
    w_edge_in,
    b_edge_in,
    w_edge_out,
    b_edge_out,
    w_input,
    w_hidden,
    b_input,
    b_hidden,
    cotangent,
):
    batches, own, width = states.shape
    edges = source_index.shape[1]
    owners = lax.axis_size("edge")
    cap = max(2, 2 * edges // owners)
    feat_count, units = w_edge_in.shape

    sent = full_call(
        functools.partial(route_kernel, own),
        jax.ShapeDtypeStruct((owners, batches * feat_count + 16, cap), BF16),
        limit=60,
    )(source_index, target_index, edge_feats)
    edge_data = lax.all_to_all(sent, "edge", 0, 0, tiled=True)
    merge = max(1, LANES // cap)
    if merge > 1:
        edge_data = edge_data.reshape(owners // merge, merge, -1, cap).transpose(0, 2, 1, 3)
        edge_data = edge_data.reshape(owners // merge, -1, merge * cap)

    w_mats = w_edge_out.reshape(units, width, width)
    padded = (units + 2 + GROUP - 1) // GROUP * GROUP

    tall = width // 8
    pairs = own // 2
    blocks = edge_data.shape[0]
    core = lax.axis_index("graph")
    spot = lax.axis_index("edge")
    orders = ((0, 1, 2, 3), (2, 0, 1, 3))

    def bit(side, step):
        first, second = [(spot >> orders[k][step]) & 1 for k in range(2)]
        return jnp.where(side == 0, first, second)

    where = jnp.stack([core, bit(core, 0), bit(1 - core, 0)])
    smem = pl.BlockSpec(memory_space=pltpu.SMEM)
    vmem = pl.BlockSpec(memory_space=pltpu.VMEM)
    far = pl.BlockSpec(memory_space=pltpu.HBM)
    bias = b_edge_out.reshape(width, width)
    quarter = jax.ShapeDtypeStruct((2, 4, tall, (units // 4 + 2) * width), BF16)
    new_states, *sums, g_pairs, levels, d_mails, base, order, first = full_call(
        main_kernel,
        (
            jax.ShapeDtypeStruct((batches * own, width), BF16),
            *[quarter] * 4,
            jax.ShapeDtypeStruct((batches, padded * pairs, LANES), BF16),
            jax.ShapeDtypeStruct((batches * own, 2 * width), BF16),
            jax.ShapeDtypeStruct((batches * own, 2 * width), BF16),
            jax.ShapeDtypeStruct((batches * own, width), F32),
            jax.ShapeDtypeStruct((batches, blocks + 1), jnp.int32),
            jax.ShapeDtypeStruct((32, width), F32),
        ),
        (
            pltpu.VMEM((units, PIECE * LANES), F32),
            pltpu.VMEM((padded * 8, 512), F32),
            pltpu.VMEM((batches, padded * pairs, LANES), BF16),
            pltpu.VMEM((2 * batches * own, padded * width), BF16),
            pltpu.VMEM((units, width, width), BF16),
            pltpu.VMEM((padded - units, width, width), BF16),
            pltpu.VMEM((4,) + quarter.shape, BF16),
            pltpu.SemaphoreType.DMA((4,) + quarter.shape[:2]),
            pltpu.SemaphoreType.DMA((2,)),
        ),
        limit=60,
        in_specs=[smem] + [vmem] * 5 + [far] + [vmem] * 5,
        out_specs=[vmem] + [far] * 5 + [vmem] * 3 + [smem, vmem],
    )(
        where,
        edge_data,
        states.reshape(batches * own, width),
        cotangent.reshape(batches * own, width),
        w_edge_in,
        b_edge_in,
        w_mats,
        bias,
        w_input,
        w_hidden,
        b_input,
        b_hidden,
    )

    cores = lax.axis_size("graph")

    def to_core(value):
        return lax.ppermute(value, "graph", [(0, 1), (1, 0)])

    def swap(value, masks):
        moves = []
        for side in range(cores):
            first = side * owners
            moves += [(first + k, first + (k ^ masks[side])) for k in range(owners)]
        return lax.ppermute(value, ("graph", "edge"), moves)

    def swap_step(value, step):
        return swap(value, [1 << orders[side][step] for side in range(cores)])

    def pick(value, number):
        return lax.dynamic_index_in_dim(value, number, 0, False)

    def added(terms):
        return sum(one.astype(F32) for one in terms)

    def after(value, *others):
        return lax.optimization_barrier((value, *others))[0]

    def first_grads(pairs_in):
        return full_call(
            back_kernel,
            (
                jax.ShapeDtypeStruct((batches, own, width), BF16),
                jax.ShapeDtypeStruct((batches, padded * 8, 512), BF16),
            ),
            (
                pltpu.VMEM((padded - units, width, width), BF16),
                pltpu.VMEM((units, width, width), BF16),
                pltpu.VMEM((batches, padded * pairs, LANES), BF16),
                pltpu.SemaphoreType.DMA((padded // GROUP, 2)),
            ),
            limit=60,
            in_specs=[far] + [vmem] * 3 + [far, vmem],
            cost_estimate=cost(12),
        )(pairs_in, levels, d_mails, base, w_mats, bias)

    def second_grads(d_pairs):
        return full_call(
            edge_kernel,
            (
                jax.ShapeDtypeStruct((blocks, batches * feat_count, LANES), BF16),
                jax.ShapeDtypeStruct((32, units), F32),
            ),
            limit=60,
            in_specs=[smem] + [vmem] * 5,
            cost_estimate=cost(9),
        )(order, edge_data, d_pairs, w_edge_in, b_edge_in, first)

    bits = owners.bit_length() - 1

    def added_at(big, first, number):
        big, more = lax.optimization_barrier((big, swap(first, [1 << number] * cores)))
        return big, first + more

    def give_half(feats, number):
        side = 1 - ((spot >> number) & 1)
        give = lax.dynamic_index_in_dim(feats, side, bits - 1 - number, False)
        return swap(give, [1 << number] * cores)

    def take_half(feats, got, number):
        side = 1 - ((spot >> number) & 1)
        return lax.dynamic_update_index_in_dim(feats, got, side, bits - 1 - number)

    kept_first, kept_last, given_first, given_last = sums
    got_first, got_last = to_core(given_first), to_core(given_last)
    kept_first = full_call(
        copy_kernel, jax.ShapeDtypeStruct(kept_first.shape, BF16), cost_estimate=cost(1)
    )(kept_first)
    give = full_call(
        add_kernel, jax.ShapeDtypeStruct(kept_first.shape, BF16), cost_estimate=cost(1)
    )(kept_first, got_first)
    terms = [kept_last, got_last]
    for step in range(3):
        if step > 0:
            number = bit(core, step)
            give = added([pick(one, 1 - number) for one in terms]).astype(BF16)
            terms = [pick(one, number) for one in terms]
        got = swap_step(give, step)
        if step == 0:
            state_grad, d_pairs = first_grads(after(g_pairs, give))
            got = after(got, state_grad)
        if step == 1:
            feats, first = second_grads(after(d_pairs, give))
            if merge > 1:
                feats = feats.reshape(blocks, -1, merge, cap).transpose(0, 2, 1, 3)
            feats = feats.reshape((2,) * bits + (batches * feat_count, cap))
            got = after(got, first)
        if step == 2:
            got, first = added_at(got, first, 2)
        terms.append(got)
        if step == 0:
            terms = [one.reshape((2, 2, 2) + one.shape[2:]) for one in terms]
    total = added(terms).astype(BF16)
    first, feats = after(first, total), after(feats, total)
    for extra in range(3, owners.bit_length() - 1):
        got = swap(total, [1 << extra] * cores)
        if extra > 3:
            got, first = added_at(got, first, extra)
            feats = take_half(feats, give_half(feats, extra), extra)
        if extra < owners.bit_length() - 2:
            total = added([total, got]).astype(BF16)
    first = first + swap(first, [1] * cores)
    feats = take_half(feats, give_half(feats, 0), 0)
    moved = give_half(feats, 1)
    got, first = added_at(got, first, 1)
    got, moved = lax.optimization_barrier((got, moved))
    feats = take_half(feats, moved, 1)
    held = rows_of(total, got)

    got, first = added_at(swap_step(held, 2), first, 3)
    held = jnp.concatenate([held, got], axis=0)
    across = swap_step(held, 0)
    shapes = tuple(
        jax.ShapeDtypeStruct(shape, F32)
        for shape in (
            (units, width * width),
            (width, width),
            (width, 3 * width),
            (width, 3 * width),
            (width, width),
        )
    )
    outs = ()
    def place(outs, pieces):
        at = []
        for _, side, flips in pieces:
            code = side
            for step in range(3):
                code = code * 2 + bit(side, step)
            at.append((code * 2) ^ flips)
        return place_pieces(tall, jnp.stack(at), [one for one, _, _ in pieces], shapes, outs)

    outs = place((), [(held, core, 0), (to_core(held), 1 - core, 0)])
    moved = give_half(after(feats, held), 2)
    outs, near, more, moved = lax.optimization_barrier(
        (outs, swap_step(held, 1), to_core(first), moved)
    )
    feats = take_half(feats, moved, 2)
    first = first + more
    last = swap_step(near, 0)
    moved = give_half(feats, 3)
    outs, near, across, moved, first = lax.optimization_barrier(
        (outs, near, across, moved, first)
    )
    feats = take_half(feats, moved, 3)
    small_outs = (
        first[:feat_count],
        first[feat_count],
        first[24:27].reshape(-1),
        first[27:30].reshape(-1),
    )
    near_other, across_other = to_core(near), to_core(across)
    feat_grad = full_call(
        functools.partial(unroute_kernel, own),
        jax.ShapeDtypeStruct((batches, feat_count, edges), BF16),
        cost_estimate=cost(1.4),
    )(source_index, feats.reshape(owners, batches, feat_count, cap))
    outs = place(
        outs,
        [
            (near, core, 4),
            (near_other, 1 - core, 4),
            (across, core, 8),
            (across_other, 1 - core, 8),
        ],
    )
    outs, last, feat_grad, small_outs = lax.optimization_barrier(
        (outs, last, feat_grad, small_outs)
    )
    other = to_core(last)
    outs = place(outs, [(last, core, 12)])
    outs = place(outs, [(other, 1 - core, 12)])
    d_w, d_bias, d_x, d_h, _ = outs
    return (
        new_states.reshape(batches, own, width),
        state_grad,
        feat_grad,
        small_outs[0],
        small_outs[1],
        d_w,
        d_bias.reshape(-1),
        d_x,
        d_h,
        small_outs[2],
        small_outs[3],
    )


def solution(mesh):
    spread = ("graph", "edge")
    rows = P(None, spread, None)
    edges = P(None, spread)
    feats = P(None, None, spread)
    in_specs = (rows, feats, edges, edges) + (P(),) * 8 + (rows,)
    out_specs = (rows, rows, feats) + (P(),) * 8
    return jax.shard_map(
        body,
        mesh=mesh,
        in_specs=in_specs,
        out_specs=out_specs,
        check_vma=False,
    )
```

```python
import functools

import jax
import jax.numpy as jnp
from jax import lax
from jax.experimental import pallas as pl
from jax.experimental.pallas import tpu as pltpu
from jax.sharding import PartitionSpec as P

F32 = jnp.float32
BF16 = jnp.bfloat16
LANES = 128
PIECE = 4
GROUP = 12
MIB = 1024 * 1024


def dot(first, second, dims=((1,), (0,))):
    return lax.dot_general(first, second, (dims, ((), ())), preferred_element_type=F32)


def dot_nt(first, second):
    return dot(first, second, ((1,), (1,)))


def row_ids(shape):
    return lax.broadcasted_iota(jnp.int32, shape, 0)


def col_ids(shape):
    return lax.broadcasted_iota(jnp.int32, shape, 1)


def full_call(kernel, out_shape, scratch=(), limit=16, **more):
    return pl.pallas_call(
        kernel,
        out_shape=out_shape,
        scratch_shapes=scratch,
        compiler_params=pltpu.CompilerParams(vmem_limit_bytes=limit * MIB),
        **more,
    )


def ranks_of(owner, owners):
    hits = (row_ids((owners, owner.shape[1])) == owner).astype(F32)
    before = (row_ids((LANES, LANES)) < col_ids((LANES, LANES))).astype(BF16)
    seen = jnp.zeros((owners, 1), F32)
    ranks = []
    for start in range(0, owner.shape[1], LANES):
        part = hits[:, start : start + LANES]
        place = dot(part.astype(BF16), before) + seen
        ranks.append(jnp.sum(part * place, axis=0, keepdims=True))
        seen = seen + jnp.sum(part, axis=1, keepdims=True)
    return hits, jnp.concatenate(ranks, axis=1)


def route_kernel(own_rows, src_ref, dst_ref, feat_ref, out_ref):
    owners, rows, cap = out_ref.shape
    batches, feats, edges = feat_ref.shape
    shift = own_rows.bit_length() - 1
    marks = [jnp.zeros((16, cap), F32)] * owners
    for batch in range(batches):
        source, target = src_ref[batch : batch + 1], dst_ref[batch : batch + 1]
        owner = source >> shift
        hits, rank = ranks_of(owner, owners)
        spots = (row_ids((cap, edges)) == rank.astype(jnp.int32)).astype(BF16)
        line = row_ids((16, edges)) - 3 * batch
        first = owner << shift
        extra = jnp.where(line == 0, source - first, jnp.where(line == 1, target - first, 1))
        extra = jnp.where((line >= 0) & (line < 3), extra, 0).astype(F32)
        load = jnp.concatenate([feat_ref[batch].astype(F32), extra], axis=0)
        masked = [(load * hits[part : part + 1]).astype(BF16) for part in range(owners)]
        out = dot_nt(jnp.concatenate(masked, axis=0), spots)
        for part in range(owners):
            tile = out[part * (feats + 16) : (part + 1) * (feats + 16)]
            out_ref[part, batch * feats : (batch + 1) * feats] = tile[:feats].astype(BF16)
            marks[part] = marks[part] + tile[feats:]
    for part in range(owners):
        out_ref[part, batches * feats :] = marks[part].astype(BF16)


def unroute_kernel(own_rows, src_ref, back_ref, out_ref):
    owners, batches, rows, cap = back_ref.shape
    edges = src_ref.shape[1]
    shift = own_rows.bit_length() - 1
    for batch in range(batches):
        hits, rank = ranks_of(src_ref[batch : batch + 1] >> shift, owners)
        spots = (row_ids((cap, edges)) == rank.astype(jnp.int32)).astype(BF16)
        parts = [back_ref[part, batch] for part in range(owners)]
        spread = dot(jnp.concatenate(parts, axis=0), spots)
        total = jnp.zeros((rows, edges), F32)
        for part in range(owners):
            total = total + spread[part * rows : (part + 1) * rows] * hits[part : part + 1]
        out_ref[batch] = total.astype(BF16)


def edge_piece(batches, order_ref, edge_ref, piece, batch):
    some = [edge_ref[order_ref[batch, PIECE * piece + k]] for k in range(PIECE)]
    block = jnp.concatenate(some, axis=1)
    feats, marks = block[batch * 16 : (batch + 1) * 16], block[batches * 16 :].astype(F32)
    source = marks[3 * batch : 3 * batch + 1].astype(jnp.int32)
    target = marks[3 * batch + 1 : 3 * batch + 2].astype(jnp.int32)
    held = marks[3 * batch + 2 : 3 * batch + 3]
    code = ((target >> 3) & 3) * 128 + (target >> 5) * 64 + source
    code = jnp.where(held > 0.5, code, -1)
    pairs = (row_ids((512, block.shape[1])) == code).astype(BF16)
    low = row_ids((8, block.shape[1])) == (target & 7)
    return feats, held, pairs, low


def order_blocks(batches, edge_ref, order_ref):
    blocks = edge_ref.shape[0]
    for batch in range(batches):
        front, back = jnp.int32(0), jnp.int32(blocks - 1)
        row = 3 * batch + 2
        for block in range(blocks):
            marks = edge_ref[block, batches * 16 :].astype(F32)
            held = jnp.max(marks[row : row + 1]) > 0.5
            order_ref[batch, jnp.where(held, front, back)] = jnp.int32(block)
            step = held.astype(jnp.int32)
            front, back = front + step, back - (1 - step)
        order_ref[batch, blocks] = front


def first_layer(w_in_ref, b_in_ref):
    bias = jnp.broadcast_to(b_in_ref[...].reshape(1, -1), (8, b_in_ref.shape[0]))
    return w_in_ref[...].astype(F32).T.astype(BF16), bias.T[:, :1]


def gates_of(mail_low, level, w_x, w_h, b_x, b_h):
    width = level.shape[1]
    from_mail = dot(mail_low, w_x[...]) + b_x[...].reshape(1, -1)
    from_state = dot(level, w_h[...]) + b_h[...].reshape(1, -1)
    reset = jax.nn.sigmoid(from_mail[:, :width] + from_state[:, :width])
    update = jax.nn.sigmoid(from_mail[:, width : 2 * width] + from_state[:, width : 2 * width])
    state_part = from_state[:, 2 * width :]
    candidate = jnp.tanh(from_mail[:, 2 * width :] + reset * state_part)
    return reset, update, candidate, state_part


def doubled(level):
    blank = jnp.zeros_like(level)
    return jnp.concatenate(
        [jnp.concatenate([level, blank], axis=1), jnp.concatenate([blank, level], axis=1)], axis=0
    )


def bias_blocks(bias_ref, tail_ref):
    tail_ref[...] = jnp.zeros_like(tail_ref)
    high = bias_ref[...].astype(BF16)
    tail_ref[0] = high
    tail_ref[1] = (bias_ref[...] - high.astype(F32)).astype(BF16)


def turned(tile):
    size = tile.shape[1]
    eye = (row_ids((size, size)) == col_ids((size, size))).astype(F32).astype(BF16)
    return dot_nt(eye, tile).astype(BF16)


def weights_of(w_ref, tail_ref, number):
    units = w_ref.shape[0]
    blocks = []
    for unit in range(number * GROUP, (number + 1) * GROUP):
        blocks.append(w_ref[unit] if unit < units else tail_ref[unit - units])
    return jnp.concatenate(blocks, axis=1)


def pulled_rows(pulled, half):
    rows = []
    for start in range(0, pulled.shape[1], LANES):
        tile = pulled[:, start : start + LANES]
        rows.append(jnp.concatenate([tile[:half], tile[half:]], axis=1))
    return jnp.concatenate(rows, axis=0)


def main_kernel(
    where_ref,
    edge_ref,
    state_ref,
    cot_ref,
    w_in_ref,
    b_in_ref,
    w_far,
    bias_ref,
    w_x,
    w_h,
    b_x,
    b_h,
    new_ref,
    kept_first,
    kept_last,
    given_first,
    given_last,
    g_far,
    level_ref,
    dm_ref,
    base_ref,
    order_ref,
    rows_ref,
    hid_ref,
    acc_ref,
    g_ref,
    p_ref,
    w_ref,
    tail_ref,
    sum_ref,
    sum_sems,
    sems,
):
    fetch = pltpu.make_async_copy(w_far, w_ref, sems.at[0])
    fetch.start()
    blocks = edge_ref.shape[0]
    batches = g_ref.shape[0]
    hidden_units = hid_ref.shape[0]
    units = acc_ref.shape[0] // 8
    own = state_ref.shape[0] // batches
    half = own // 2
    span = GROUP * half
    wide = GROUP * LANES
    chunks = units // GROUP
    order_blocks(batches, edge_ref, order_ref)
    bias_blocks(bias_ref, tail_ref)
    w_in, b_in = first_layer(w_in_ref, b_in_ref)

    for batch in range(batches):
        acc_ref[...] = jnp.zeros_like(acc_ref)

        def add_piece(piece, carry):
            feats, held, pairs, low = edge_piece(batches, order_ref, edge_ref, piece, batch)
            pre = dot(w_in, feats) + b_in
            hid_ref[...] = (pre * jax.nn.sigmoid(pre)).astype(BF16).astype(F32)
            ones = jnp.where(low, 1.0, 0.0)
            parts = []
            for unit in range(0, hidden_units, 2):
                two = [jnp.where(low, hid_ref[unit + k : unit + k + 1], 0.0) for k in range(2)]
                parts.append(jnp.concatenate(two, axis=0).astype(BF16))
            parts.append(jnp.concatenate([ones, ones], axis=0).astype(BF16))
            parts.append(jnp.zeros((8 * (units - hidden_units - 2), pre.shape[1]), BF16))
            acc_ref[...] += dot_nt(jnp.concatenate(parts, axis=0), pairs)
            return carry

        lax.fori_loop(0, (order_ref[batch, blocks] + PIECE - 1) // PIECE, add_piece, 0)

        def place(step, carry):
            for four in range(3):
                rows = []
                for k in range(4):
                    for part in range(4):
                        start = pl.multiple_of(step * 96 + four * 32 + k * 8, 8)
                        rows.append(acc_ref[pl.ds(start, 8), part * LANES : (part + 1) * LANES])
                at = pl.ds(pl.multiple_of((step * 3 + four) * LANES, LANES), LANES)
                g_ref[batch, at, :] = jnp.concatenate(rows, axis=0).astype(BF16)
            return carry

        lax.fori_loop(0, units // 12, place, 0)

    def forward(step, level):
        two = [doubled(level[batch * own : (batch + 1) * own]) for batch in range(batches)]
        mail = jnp.zeros((batches * own, LANES), F32)
        base = step * batches * own
        for number in range(chunks):
            for batch in range(batches):
                out = dot(g_ref[batch, number * span : (number + 1) * span, :], two[batch])
                out = out.astype(BF16)
                for unit in range(GROUP):
                    lane = number * wide + unit * LANES
                    for part in range(2):
                        row = base + batch * own + part * half
                        p_ref[row : row + half, lane : lane + LANES] = out[
                            unit * half : (unit + 1) * half, part * LANES : (part + 1) * LANES
                        ]
            rows = p_ref[base : base + batches * own, number * wide : (number + 1) * wide]
            mail = mail + dot_nt(rows, weights_of(w_ref, tail_ref, number))
        return mail

    def backward(d_mail):
        sums = [jnp.zeros((LANES, 2 * LANES), F32) for batch in range(batches)]
        for number in range(chunks):
            pulled = dot(d_mail, weights_of(w_ref, tail_ref, number)).astype(BF16)
            at = slice(number * span, (number + 1) * span)
            for batch in range(batches):
                tall = pulled_rows(pulled[batch * own : (batch + 1) * own], half)
                sums[batch] = sums[batch] + dot(turned(g_ref[batch, at, :]), tall)
        return jnp.concatenate([one[:own, :LANES] + one[own:, LANES:] for one in sums], axis=0)

    weights = (w_x, w_h, b_x, b_h)
    level_zero = state_ref[...]
    state_zero = level_zero.astype(F32)
    leave = pltpu.make_async_copy(g_ref, g_far, sems.at[1])
    leave.start()
    fetch.wait()
    mail_zero = forward(0, level_zero).astype(BF16)
    gates_zero = gates_of(mail_zero, level_zero, *weights)
    state_one = (1.0 - gates_zero[1]) * gates_zero[2] + gates_zero[1] * state_zero
    level_one = state_one.astype(BF16)
    mail_one = forward(1, level_one).astype(BF16)
    gates_one = gates_of(mail_one, level_one, *weights)
    new_ref[...] = ((1.0 - gates_one[1]) * gates_one[2] + gates_one[1] * state_one).astype(BF16)

    def gru_back(d_next, gates, current):
        reset, update, candidate, state_part = gates
        d_cand = d_next * (1.0 - update) * (1.0 - candidate * candidate)
        d_reset = d_cand * state_part * reset * (1.0 - reset)
        d_update = d_next * (current - candidate) * update * (1.0 - update)
        dg_mail = jnp.concatenate([d_reset, d_update, d_cand], axis=1).astype(BF16)
        dg_state = jnp.concatenate([d_reset, d_update, d_cand * reset], axis=1).astype(BF16)
        d_mail = dot_nt(dg_mail, w_x[...]).astype(BF16)
        d_current = d_next * update + dot_nt(dg_state, w_h[...])
        return dg_mail, dg_state, d_mail, d_current

    dgm_one, dgs_one, dm_one, d_state = gru_back(cot_ref[...].astype(F32), gates_one, state_one)
    d_state = d_state + backward(dm_one)
    dgm_zero, dgs_zero, dm_zero, d_state = gru_back(d_state, gates_zero, state_zero)
    base_ref[...] = d_state
    level_ref[...] = jnp.concatenate([level_zero, level_one], axis=1)
    dm_ref[...] = jnp.concatenate([dm_zero, dm_one], axis=1)

    def both(first, second):
        return jnp.concatenate([first.astype(F32), second.astype(F32)], axis=0)

    dms = both(dm_zero, dm_one).T
    mails, levels = both(mail_zero, mail_one), both(level_zero, level_one)
    dgm, dgs = both(dgm_zero, dgm_one), both(dgs_zero, dgs_one)
    width = dgm.shape[1]
    rows_ref[...] = jnp.zeros_like(rows_ref)
    for k, one in enumerate((dgm, dgs)):
        total = jnp.sum(one, axis=0, keepdims=True)
        for part in range(3):
            row = 24 + 3 * k + part
            rows_ref[row : row + 1, :] = total[:, part * LANES : (part + 1) * LANES]
    small = jnp.concatenate(
        [
            dot(dms.astype(BF16), p_ref[:, hidden_units * LANES : (hidden_units + 1) * LANES]),
            dot(mails.T.astype(BF16), dgm.astype(BF16)),
            dot(levels.T.astype(BF16), dgs.astype(BF16)),
            jnp.zeros((2 * own, LANES), F32),
        ],
        axis=1,
    )

    def sorted_rows(value):
        rows = value.shape[0] // 2
        upper, lower = value[:rows], value[rows:]
        halves = [jnp.where(where_ref[0] == k, upper, lower) for k in range(2)]
        parts = []
        for k, one in enumerate(halves):
            first, second = one[: rows // 2], one[rows // 2 :]
            parts += [jnp.where(where_ref[1 + k] == side, second, first) for side in range(2)]
        return jnp.concatenate(parts, axis=0).astype(BF16)

    dms, small = sorted_rows(dms), sorted_rows(small)
    rows_in, groups, tall, wide_out = kept_first.shape
    taken = wide_out - 2 * LANES
    moves = []
    for group in range(groups):
        out = dot(dms, p_ref[:, group * taken : (group + 1) * taken]).astype(BF16)
        extra = small[:, group * 2 * LANES : (group + 1) * 2 * LANES]
        for k, ref in enumerate((given_first, kept_first, given_last, kept_last)):
            for row in range(rows_in):
                at = ((2, 0, 3, 1)[k] * rows_in + row) * tall
                sum_ref[k, row, group, :, :taken] = out[at : at + tall]
                sum_ref[k, row, group, :, taken:] = extra[at : at + tall]
                moves.append(
                    pltpu.make_async_copy(
                        sum_ref.at[k, row, group], ref.at[row, group], sum_sems.at[k, row, group]
                    )
                )
                moves[-1].start()
    for move in moves:
        move.wait()
    leave.wait()


def edge_sums(batch, batches, order_ref, edge_ref, dg_ref, w_in_ref, b_in_ref, feat_ref, before):
    blocks = edge_ref.shape[0]
    hidden_units = w_in_ref.shape[1]
    w_in, b_in = first_layer(w_in_ref, b_in_ref)
    fold = (col_ids((hidden_units, 8 * hidden_units)) >> 3) == row_ids(
        (hidden_units, 8 * hidden_units)
    )
    fold = fold.astype(F32).astype(BF16)

    def one_piece(piece, sums):
        feats, held, pairs, low = edge_piece(batches, order_ref, edge_ref, piece, batch)
        pre = dot(w_in, feats) + b_in
        sig = jax.nn.sigmoid(pre)
        spread = dot(dg_ref[batch, : 8 * hidden_units], pairs)
        spread = spread.reshape(hidden_units, 8, pre.shape[1])
        spread = jnp.where(low[None], spread, 0.0).reshape(8 * hidden_units, pre.shape[1])
        d_hidden = dot(fold, spread.astype(BF16))
        d_pre = (d_hidden * sig * (1.0 + pre * (1.0 - sig))).astype(BF16)
        out = dot(w_in_ref[...], d_pre).astype(BF16)
        for k in range(PIECE):
            at = order_ref[batch, PIECE * piece + k]
            feat_ref[at, batch * 16 : (batch + 1) * 16] = out[:, k * LANES : (k + 1) * LANES]
        ones = jnp.where(row_ids((16, pre.shape[1])) == 0, held, 0.0).astype(BF16)
        return sums + dot_nt(jnp.concatenate([feats, ones], axis=0), d_pre)

    return lax.fori_loop(0, (order_ref[batch, blocks] + PIECE - 1) // PIECE, one_piece, before)


def back_kernel(
    g_far,
    level_ref,
    dm_ref,
    base_ref,
    w_far,
    bias_ref,
    grad_ref,
    dg_ref,
    tail_ref,
    w_ref,
    g_ref,
    sems,
):
    batches, own, width = grad_ref.shape
    hidden_units = w_ref.shape[0]
    chunks = (hidden_units + tail_ref.shape[0]) // GROUP
    half = own // 2
    fetches = []
    for number in range(chunks):
        some = pl.ds(number * GROUP, min(GROUP, hidden_units - number * GROUP))
        rows = pl.ds(number * GROUP * half, GROUP * half)
        fetches += [
            pltpu.make_async_copy(w_far.at[some], w_ref.at[some], sems.at[number, 0]),
            pltpu.make_async_copy(g_far.at[:, rows], g_ref.at[:, rows], sems.at[number, 1]),
        ]
    for fetch in fetches:
        fetch.start()
    bias_blocks(bias_ref, tail_ref)

    pulls, levels = [], []
    for batch in range(batches):
        mine = slice(batch * own, (batch + 1) * own)
        pulls += [dm_ref[mine, step * width : (step + 1) * width] for step in range(2)]
        both = [doubled(level_ref[mine, step * width : (step + 1) * width]) for step in range(2)]
        levels.append(jnp.concatenate(both, axis=1))
    pulls = jnp.concatenate(pulls, axis=0)
    totals = [jnp.zeros((2 * own, 2 * width), F32) for batch in range(batches)]
    for number in range(chunks):
        fetches[2 * number].wait()
        fetches[2 * number + 1].wait()
        pulled = dot(pulls, weights_of(w_ref, tail_ref, number)).astype(BF16)
        at = slice(number * GROUP * half, (number + 1) * GROUP * half)
        for batch in range(batches):
            talls = [
                pulled_rows(pulled[(2 * batch + k) * own : (2 * batch + k + 1) * own], half)
                for k in range(2)
            ]
            totals[batch] = totals[batch] + dot(turned(g_ref[batch, at, :]), talls[0])
            d_pair = dot_nt(jnp.concatenate(talls, axis=1), levels[batch])
            for unit in range(0, GROUP, 2):
                row = (number * GROUP + unit) * 8
                for part in range(half // 8):
                    pair = [
                        d_pair[(unit + k) * half + part * 8 : (unit + k) * half + part * 8 + 8]
                        for k in range(2)
                    ]
                    dg_ref[batch, row : row + 16, part * LANES : (part + 1) * LANES] = jnp.concatenate(
                        pair, axis=0
                    ).astype(BF16)
    for batch in range(batches):
        grad = base_ref[batch * own : (batch + 1) * own] + totals[batch][:own, :width]
        grad_ref[batch] = (grad + totals[batch][own:, width:]).astype(BF16)


def edge_kernel(order_ref, edge_ref, dg_ref, w_in_ref, b_in_ref, before_ref, feat_ref, win_ref):
    batches = order_ref.shape[0]
    feat_ref[...] = jnp.zeros_like(feat_ref)
    sums = before_ref[...]
    for batch in range(batches):
        sums = edge_sums(
            batch, batches, order_ref, edge_ref, dg_ref, w_in_ref, b_in_ref, feat_ref, sums
        )
    win_ref[...] = sums


def add_kernel(first_ref, second_ref, out_ref):
    out_ref[...] = (first_ref[...].astype(F32) + second_ref[...].astype(F32)).astype(BF16)


def copy_kernel(in_ref, out_ref):
    out_ref[...] = in_ref[...]


def rows_kernel(first_ref, second_ref, out_ref, rows_ref):
    parts, tall, wide = first_ref.shape
    main = wide // LANES - 2
    for part in range(parts):
        total = first_ref[part].astype(F32) + second_ref[part].astype(F32)
        for block in range(main):
            rows_ref[pl.ds(block, tall, stride=main), :] = total[
                :, block * LANES : (block + 1) * LANES
            ]
        for k in range(2):
            start = tall * (main + k)
            rows_ref[start : start + tall, :] = total[:, (main + k) * LANES : (main + k + 1) * LANES]
        out_ref[part] = rows_ref[...].astype(BF16)


def rows_of(first, second):
    parts, tall, wide = first.shape
    shape = (tall * (wide // LANES), LANES)
    return full_call(
        rows_kernel,
        jax.ShapeDtypeStruct((parts,) + shape, BF16),
        (pltpu.VMEM(shape, F32),),
        cost_estimate=cost(1),
    )(first, second)


def place_kernel(tall, count, carried, *refs):
    at_ref, pieces = refs[0], refs[1 : 1 + count]
    outs = refs[1 + count + carried : 6 + count + carried]
    big_ref, little_ref, sems = refs[6 + count + carried :]
    d_w, d_bias, d_x, d_h, d_rest = outs
    waits = []
    slot = 0
    for k, piece in enumerate(pieces):
        chunks, rows_in, lanes = piece.shape
        main = rows_in // tall - 2
        for chunk in range(chunks):
            code = at_ref[k] ^ chunk
            line, part = code >> 2, code & 3
            at = pl.ds(pl.multiple_of(line * tall, 8), tall)
            rows = piece[chunk].astype(F32)
            for row in range(tall):
                big_ref[slot, :, row * lanes : (row + 1) * lanes] = rows[row * main : (row + 1) * main]
            copy = pltpu.make_async_copy(
                big_ref.at[slot],
                d_w.at[
                    pl.ds(pl.multiple_of(part * main, 8), main),
                    pl.ds(pl.multiple_of(line * (tall * lanes), LANES), tall * lanes),
                ],
                sems.at[slot, 0],
            )
            copy.start()
            waits.append(copy)

            for side in range(2):
                start = tall * (main + side)
                little_ref[slot, side] = rows[start : start + tall]

                def move(target, lane):
                    lane = jnp.maximum(lane, 0) * lanes
                    to = pl.ds(pl.multiple_of(jnp.minimum(lane, target.shape[1] - lanes), LANES), lanes)
                    return pltpu.make_async_copy(
                        little_ref.at[slot, side], target.at[at, to], sems.at[slot, 1 + side]
                    )

                block = 2 * part + side
                to_x, to_h = move(d_x, block - 1), move(d_h, block - 4)
                alone = move((d_bias, d_rest)[side], 0)
                lone = block == 7 * side
                pl.when(lone)(alone.start)
                pl.when((block > 0) & (block < 4))(to_x.start)
                pl.when((block > 3) & (block < 7))(to_h.start)
                waits.append(alone)
            slot += 1
    for copy in waits:
        copy.wait()


def cost(micros):
    return pl.CostEstimate(
        flops=int(micros * 1e9), bytes_accessed=int(micros * 3e6), transcendentals=0
    )


def place_pieces(tall, at, pieces, shapes, before=()):
    count = len(pieces)
    chunks, rows_in, lanes = pieces[0].shape
    slots = count * chunks
    vmem = pl.BlockSpec(memory_space=pltpu.VMEM)
    hbm = pl.BlockSpec(memory_space=pl.ANY)
    return pl.pallas_call(
        functools.partial(place_kernel, tall, count, len(before)),
        out_shape=shapes,
        in_specs=[pl.BlockSpec(memory_space=pltpu.SMEM)] + [vmem] * count + [hbm] * len(before),
        out_specs=[hbm] * len(shapes),
        scratch_shapes=(
            pltpu.VMEM((slots, rows_in // tall - 2, tall * lanes), F32),
            pltpu.VMEM((slots, 2, tall, lanes), F32),
            pltpu.SemaphoreType.DMA((slots, 3)),
        ),
        input_output_aliases={1 + count + k: k for k in range(len(before))},
        cost_estimate=cost(slots / 4),
        compiler_params=pltpu.CompilerParams(vmem_limit_bytes=16 * MIB),
    )(at, *pieces, *before)


def body(
    states,
    edge_feats,
    source_index,
    target_index,
    w_edge_in,
    b_edge_in,
    w_edge_out,
    b_edge_out,
    w_input,
    w_hidden,
    b_input,
    b_hidden,
    cotangent,
):
    batches, own, width = states.shape
    edges = source_index.shape[1]
    owners = lax.axis_size("edge")
    cap = max(2, 2 * edges // owners)
    feat_count, units = w_edge_in.shape

    sent = full_call(
        functools.partial(route_kernel, own),
        jax.ShapeDtypeStruct((owners, batches * feat_count + 16, cap), BF16),
        limit=60,
    )(source_index, target_index, edge_feats)
    edge_data = lax.all_to_all(sent, "edge", 0, 0, tiled=True)
    merge = max(1, LANES // cap)
    if merge > 1:
        edge_data = edge_data.reshape(owners // merge, merge, -1, cap).transpose(0, 2, 1, 3)
        edge_data = edge_data.reshape(owners // merge, -1, merge * cap)

    w_mats = w_edge_out.reshape(units, width, width)
    padded = (units + 2 + GROUP - 1) // GROUP * GROUP

    tall = width // 8
    pairs = own // 2
    blocks = edge_data.shape[0]
    core = lax.axis_index("graph")
    spot = lax.axis_index("edge")
    orders = ((0, 1, 2, 3), (2, 0, 1, 3))

    def bit(side, step):
        first, second = [(spot >> orders[k][step]) & 1 for k in range(2)]
        return jnp.where(side == 0, first, second)

    where = jnp.stack([core, bit(core, 0), bit(1 - core, 0)])
    smem = pl.BlockSpec(memory_space=pltpu.SMEM)
    vmem = pl.BlockSpec(memory_space=pltpu.VMEM)
    far = pl.BlockSpec(memory_space=pltpu.HBM)
    bias = b_edge_out.reshape(width, width)
    quarter = jax.ShapeDtypeStruct((2, 4, tall, (units // 4 + 2) * width), BF16)
    new_states, *sums, g_pairs, levels, d_mails, base, order, first = full_call(
        main_kernel,
        (
            jax.ShapeDtypeStruct((batches * own, width), BF16),
            *[quarter] * 4,
            jax.ShapeDtypeStruct((batches, padded * pairs, LANES), BF16),
            jax.ShapeDtypeStruct((batches * own, 2 * width), BF16),
            jax.ShapeDtypeStruct((batches * own, 2 * width), BF16),
            jax.ShapeDtypeStruct((batches * own, width), F32),
            jax.ShapeDtypeStruct((batches, blocks + 1), jnp.int32),
            jax.ShapeDtypeStruct((32, width), F32),
        ),
        (
            pltpu.VMEM((units, PIECE * LANES), F32),
            pltpu.VMEM((padded * 8, 512), F32),
            pltpu.VMEM((batches, padded * pairs, LANES), BF16),
            pltpu.VMEM((2 * batches * own, padded * width), BF16),
            pltpu.VMEM((units, width, width), BF16),
            pltpu.VMEM((padded - units, width, width), BF16),
            pltpu.VMEM((4,) + quarter.shape, BF16),
            pltpu.SemaphoreType.DMA((4,) + quarter.shape[:2]),
            pltpu.SemaphoreType.DMA((2,)),
        ),
        limit=60,
        in_specs=[smem] + [vmem] * 5 + [far] + [vmem] * 5,
        out_specs=[vmem] + [far] * 5 + [vmem] * 3 + [smem, vmem],
    )(
        where,
        edge_data,
        states.reshape(batches * own, width),
        cotangent.reshape(batches * own, width),
        w_edge_in,
        b_edge_in,
        w_mats,
        bias,
        w_input,
        w_hidden,
        b_input,
        b_hidden,
    )

    cores = lax.axis_size("graph")

    def to_core(value):
        return lax.ppermute(value, "graph", [(0, 1), (1, 0)])

    def swap(value, masks):
        moves = []
        for side in range(cores):
            first = side * owners
            moves += [(first + k, first + (k ^ masks[side])) for k in range(owners)]
        return lax.ppermute(value, ("graph", "edge"), moves)

    def swap_step(value, step):
        return swap(value, [1 << orders[side][step] for side in range(cores)])

    def pick(value, number):
        return lax.dynamic_index_in_dim(value, number, 0, False)

    def added(terms):
        return sum(one.astype(F32) for one in terms)

    def after(value, *others):
        return lax.optimization_barrier((value, *others))[0]

    def first_grads(pairs_in):
        return full_call(
            back_kernel,
            (
                jax.ShapeDtypeStruct((batches, own, width), BF16),
                jax.ShapeDtypeStruct((batches, padded * 8, 512), BF16),
            ),
            (
                pltpu.VMEM((padded - units, width, width), BF16),
                pltpu.VMEM((units, width, width), BF16),
                pltpu.VMEM((batches, padded * pairs, LANES), BF16),
                pltpu.SemaphoreType.DMA((padded // GROUP, 2)),
            ),
            limit=60,
            in_specs=[far] + [vmem] * 3 + [far, vmem],
            cost_estimate=cost(12),
        )(pairs_in, levels, d_mails, base, w_mats, bias)

    def second_grads(d_pairs):
        return full_call(
            edge_kernel,
            (
                jax.ShapeDtypeStruct((blocks, batches * feat_count, LANES), BF16),
                jax.ShapeDtypeStruct((32, units), F32),
            ),
            limit=60,
            in_specs=[smem] + [vmem] * 5,
            cost_estimate=cost(9),
        )(order, edge_data, d_pairs, w_edge_in, b_edge_in, first)

    def added_at(big, small, flip):
        big, more = lax.optimization_barrier((big, swap(small, [flip] * cores)))
        return big, small + more

    kept_first, kept_last, given_first, given_last = sums
    got_first, got_last = to_core(given_first), to_core(given_last)
    kept_first = full_call(
        copy_kernel, jax.ShapeDtypeStruct(kept_first.shape, BF16), cost_estimate=cost(1)
    )(kept_first)
    give = full_call(
        add_kernel, jax.ShapeDtypeStruct(kept_first.shape, BF16), cost_estimate=cost(1)
    )(kept_first, got_first)
    terms = [kept_last, got_last]
    for step in range(3):
        if step > 0:
            number = bit(core, step)
            give = added([pick(one, 1 - number) for one in terms]).astype(BF16)
            terms = [pick(one, number) for one in terms]
        got = swap_step(give, step)
        if step == 0:
            state_grad, d_pairs = first_grads(after(g_pairs, give))
            got = after(got, state_grad)
        if step == 1:
            d_feats, first = second_grads(after(d_pairs, give))
            got = after(got, first)
        if step == 2:
            got, first = added_at(got, first, 4)
        terms.append(got)
        if step == 0:
            terms = [one.reshape((2, 2, 2) + one.shape[2:]) for one in terms]
    total = added(terms).astype(BF16)
    for extra in range(3, owners.bit_length() - 1):
        got = swap(total, [1 << extra] * cores)
        if extra > 3:
            got, first = added_at(got, first, 1 << extra)
        if extra < owners.bit_length() - 2:
            total = added([total, got]).astype(BF16)
    first = first + swap(first, [1] * cores)
    got, first = added_at(got, first, 2)
    held = rows_of(total, got)

    got, first = added_at(swap_step(held, 2), first, 8)
    held = jnp.concatenate([held, got], axis=0)
    across = swap_step(held, 0)
    back = d_feats
    if merge > 1:
        back = back.reshape(blocks, -1, merge, cap).transpose(0, 2, 1, 3)
    back = after(back.reshape(owners, -1, cap), held)
    back = lax.all_to_all(back, "edge", 0, 0, tiled=True)

    shapes = tuple(
        jax.ShapeDtypeStruct(shape, F32)
        for shape in (
            (units, width * width),
            (width, width),
            (width, 3 * width),
            (width, 3 * width),
            (width, width),
        )
    )
    outs = ()
    def place(outs, pieces):
        at = []
        for _, side, flips in pieces:
            code = side
            for step in range(3):
                code = code * 2 + bit(side, step)
            at.append((code * 2) ^ flips)
        return place_pieces(tall, jnp.stack(at), [one for one, _, _ in pieces], shapes, outs)

    outs = place((), [(held, core, 0), (to_core(held), 1 - core, 0)])
    outs, near, more = lax.optimization_barrier((outs, swap_step(held, 1), to_core(first)))
    first = first + more
    small_outs = (
        first[:feat_count],
        first[feat_count],
        first[24:27].reshape(-1),
        first[27:30].reshape(-1),
    )
    last = swap_step(near, 0)
    outs, near, across, back = lax.optimization_barrier((outs, near, across, back))
    near_other, across_other = to_core(near), to_core(across)
    feat_grad = full_call(
        functools.partial(unroute_kernel, own),
        jax.ShapeDtypeStruct((batches, feat_count, edges), BF16),
        cost_estimate=cost(1.4),
    )(source_index, back.reshape(owners, batches, feat_count, cap))
    ready = (outs, near_other, across_other, last, feat_grad, small_outs)
    ready = lax.optimization_barrier(ready)
    outs, near_other, across_other, last, feat_grad, small_outs = ready
    other = to_core(last)
    outs = place(
        outs,
        [
            (near, core, 4),
            (near_other, 1 - core, 4),
            (across, core, 8),
            (across_other, 1 - core, 8),
            (last, core, 12),
        ],
    )
    outs = place(outs, [(other, 1 - core, 12)])
    d_w, d_bias, d_x, d_h, _ = outs
    return (
        new_states.reshape(batches, own, width),
        state_grad,
        feat_grad,
        small_outs[0],
        small_outs[1],
        d_w,
        d_bias.reshape(-1),
        d_x,
        d_h,
        small_outs[2],
        small_outs[3],
    )


def solution(mesh):
    spread = ("graph", "edge")
    rows = P(None, spread, None)
    edges = P(None, spread)
    feats = P(None, None, spread)
    in_specs = (rows, feats, edges, edges) + (P(),) * 8 + (rows,)
    out_specs = (rows, rows, feats) + (P(),) * 8
    return jax.shard_map(
        body,
        mesh=mesh,
        in_specs=in_specs,
        out_specs=out_specs,
        check_vma=False,
    )
```

```python
import functools

import jax
import jax.numpy as jnp
from jax import lax
from jax.experimental import pallas as pl
from jax.experimental.pallas import tpu as pltpu
from jax.sharding import PartitionSpec as P

F32 = jnp.float32
BF16 = jnp.bfloat16
LANES = 128
PIECE = 4
GROUP = 12
MIB = 1024 * 1024


def dot(first, second, dims=((1,), (0,))):
    return lax.dot_general(first, second, (dims, ((), ())), preferred_element_type=F32)


def dot_nt(first, second):
    return dot(first, second, ((1,), (1,)))


def row_ids(shape):
    return lax.broadcasted_iota(jnp.int32, shape, 0)


def col_ids(shape):
    return lax.broadcasted_iota(jnp.int32, shape, 1)


def full_call(kernel, out_shape, scratch=(), limit=16, **more):
    return pl.pallas_call(
        kernel,
        out_shape=out_shape,
        scratch_shapes=scratch,
        compiler_params=pltpu.CompilerParams(vmem_limit_bytes=limit * MIB),
        **more,
    )


def ranks_of(owner, owners):
    hits = (row_ids((owners, owner.shape[1])) == owner).astype(F32)
    before = (row_ids((LANES, LANES)) < col_ids((LANES, LANES))).astype(BF16)
    seen = jnp.zeros((owners, 1), F32)
    ranks = []
    for start in range(0, owner.shape[1], LANES):
        part = hits[:, start : start + LANES]
        place = dot(part.astype(BF16), before) + seen
        ranks.append(jnp.sum(part * place, axis=0, keepdims=True))
        seen = seen + jnp.sum(part, axis=1, keepdims=True)
    return hits, jnp.concatenate(ranks, axis=1)


def route_kernel(own_rows, src_ref, dst_ref, feat_ref, out_ref):
    owners, rows, cap = out_ref.shape
    batches, feats, edges = feat_ref.shape
    shift = own_rows.bit_length() - 1
    marks = [jnp.zeros((16, cap), F32)] * owners
    for batch in range(batches):
        source, target = src_ref[batch : batch + 1], dst_ref[batch : batch + 1]
        owner = source >> shift
        hits, rank = ranks_of(owner, owners)
        spots = (row_ids((cap, edges)) == rank.astype(jnp.int32)).astype(BF16)
        line = row_ids((16, edges)) - 3 * batch
        first = owner << shift
        extra = jnp.where(line == 0, source - first, jnp.where(line == 1, target - first, 1))
        extra = jnp.where((line >= 0) & (line < 3), extra, 0).astype(F32)
        load = jnp.concatenate([feat_ref[batch].astype(F32), extra], axis=0)
        masked = [(load * hits[part : part + 1]).astype(BF16) for part in range(owners)]
        out = dot_nt(jnp.concatenate(masked, axis=0), spots)
        for part in range(owners):
            tile = out[part * (feats + 16) : (part + 1) * (feats + 16)]
            out_ref[part, batch * feats : (batch + 1) * feats] = tile[:feats].astype(BF16)
            marks[part] = marks[part] + tile[feats:]
    for part in range(owners):
        out_ref[part, batches * feats :] = marks[part].astype(BF16)


def unroute_kernel(own_rows, src_ref, back_ref, out_ref):
    owners, batches, rows, cap = back_ref.shape
    edges = src_ref.shape[1]
    shift = own_rows.bit_length() - 1
    for batch in range(batches):
        hits, rank = ranks_of(src_ref[batch : batch + 1] >> shift, owners)
        spots = (row_ids((cap, edges)) == rank.astype(jnp.int32)).astype(BF16)
        parts = [back_ref[part, batch] for part in range(owners)]
        spread = dot(jnp.concatenate(parts, axis=0), spots)
        total = jnp.zeros((rows, edges), F32)
        for part in range(owners):
            total = total + spread[part * rows : (part + 1) * rows] * hits[part : part + 1]
        out_ref[batch] = total.astype(BF16)


def edge_piece(batches, order_ref, edge_ref, piece, batch):
    some = [edge_ref[order_ref[batch, PIECE * piece + k]] for k in range(PIECE)]
    block = jnp.concatenate(some, axis=1)
    feats, marks = block[batch * 16 : (batch + 1) * 16], block[batches * 16 :].astype(F32)
    source = marks[3 * batch : 3 * batch + 1].astype(jnp.int32)
    target = marks[3 * batch + 1 : 3 * batch + 2].astype(jnp.int32)
    held = marks[3 * batch + 2 : 3 * batch + 3]
    code = ((target >> 3) & 3) * 128 + (target >> 5) * 64 + source
    code = jnp.where(held > 0.5, code, -1)
    pairs = (row_ids((512, block.shape[1])) == code).astype(BF16)
    low = row_ids((8, block.shape[1])) == (target & 7)
    return feats, held, pairs, low


def order_blocks(batches, edge_ref, order_ref):
    blocks = edge_ref.shape[0]
    for batch in range(batches):
        front, back = jnp.int32(0), jnp.int32(blocks - 1)
        row = 3 * batch + 2
        for block in range(blocks):
            marks = edge_ref[block, batches * 16 :].astype(F32)
            held = jnp.max(marks[row : row + 1]) > 0.5
            order_ref[batch, jnp.where(held, front, back)] = jnp.int32(block)
            step = held.astype(jnp.int32)
            front, back = front + step, back - (1 - step)
        order_ref[batch, blocks] = front


def first_layer(w_in_ref, b_in_ref):
    bias = jnp.broadcast_to(b_in_ref[...].reshape(1, -1), (8, b_in_ref.shape[0]))
    return w_in_ref[...].astype(F32).T.astype(BF16), bias.T[:, :1]


def gates_of(mail_low, level, w_x, w_h, b_x, b_h):
    width = level.shape[1]
    from_mail = dot(mail_low, w_x[...]) + b_x[...].reshape(1, -1)
    from_state = dot(level, w_h[...]) + b_h[...].reshape(1, -1)
    reset = jax.nn.sigmoid(from_mail[:, :width] + from_state[:, :width])
    update = jax.nn.sigmoid(from_mail[:, width : 2 * width] + from_state[:, width : 2 * width])
    state_part = from_state[:, 2 * width :]
    candidate = jnp.tanh(from_mail[:, 2 * width :] + reset * state_part)
    return reset, update, candidate, state_part


def doubled(level):
    blank = jnp.zeros_like(level)
    return jnp.concatenate(
        [jnp.concatenate([level, blank], axis=1), jnp.concatenate([blank, level], axis=1)], axis=0
    )


def bias_blocks(bias_ref, tail_ref):
    tail_ref[...] = jnp.zeros_like(tail_ref)
    high = bias_ref[...].astype(BF16)
    tail_ref[0] = high
    tail_ref[1] = (bias_ref[...] - high.astype(F32)).astype(BF16)


def turned(tile):
    size = tile.shape[1]
    eye = (row_ids((size, size)) == col_ids((size, size))).astype(F32).astype(BF16)
    return dot_nt(eye, tile).astype(BF16)


def weights_of(w_ref, tail_ref, number):
    units = w_ref.shape[0]
    blocks = []
    for unit in range(number * GROUP, (number + 1) * GROUP):
        blocks.append(w_ref[unit] if unit < units else tail_ref[unit - units])
    return jnp.concatenate(blocks, axis=1)


def pulled_rows(pulled, half):
    rows = []
    for start in range(0, pulled.shape[1], LANES):
        tile = pulled[:, start : start + LANES]
        rows.append(jnp.concatenate([tile[:half], tile[half:]], axis=1))
    return jnp.concatenate(rows, axis=0)


def main_kernel(
    where_ref,
    edge_ref,
    state_ref,
    cot_ref,
    w_in_ref,
    b_in_ref,
    w_far,
    bias_ref,
    w_x,
    w_h,
    b_x,
    b_h,
    new_ref,
    kept_first,
    kept_last,
    given_first,
    given_last,
    g_far,
    level_ref,
    dm_ref,
    base_ref,
    order_ref,
    rows_ref,
    hid_ref,
    acc_ref,
    g_ref,
    p_ref,
    w_ref,
    tail_ref,
    sum_ref,
    sum_sems,
    sems,
):
    fetch = pltpu.make_async_copy(w_far, w_ref, sems.at[0])
    fetch.start()
    blocks = edge_ref.shape[0]
    batches = g_ref.shape[0]
    hidden_units = hid_ref.shape[0]
    units = acc_ref.shape[0] // 8
    own = state_ref.shape[0] // batches
    half = own // 2
    span = GROUP * half
    wide = GROUP * LANES
    chunks = units // GROUP
    order_blocks(batches, edge_ref, order_ref)
    bias_blocks(bias_ref, tail_ref)
    w_in, b_in = first_layer(w_in_ref, b_in_ref)

    for batch in range(batches):
        acc_ref[...] = jnp.zeros_like(acc_ref)

        def add_piece(piece, carry):
            feats, held, pairs, low = edge_piece(batches, order_ref, edge_ref, piece, batch)
            pre = dot(w_in, feats) + b_in
            hid_ref[...] = (pre * jax.nn.sigmoid(pre)).astype(BF16).astype(F32)
            ones = jnp.where(low, 1.0, 0.0)
            parts = []
            for unit in range(0, hidden_units, 2):
                two = [jnp.where(low, hid_ref[unit + k : unit + k + 1], 0.0) for k in range(2)]
                parts.append(jnp.concatenate(two, axis=0).astype(BF16))
            parts.append(jnp.concatenate([ones, ones], axis=0).astype(BF16))
            parts.append(jnp.zeros((8 * (units - hidden_units - 2), pre.shape[1]), BF16))
            acc_ref[...] += dot_nt(jnp.concatenate(parts, axis=0), pairs)
            return carry

        lax.fori_loop(0, (order_ref[batch, blocks] + PIECE - 1) // PIECE, add_piece, 0)

        def place(step, carry):
            for four in range(3):
                rows = []
                for k in range(4):
                    for part in range(4):
                        start = pl.multiple_of(step * 96 + four * 32 + k * 8, 8)
                        rows.append(acc_ref[pl.ds(start, 8), part * LANES : (part + 1) * LANES])
                at = pl.ds(pl.multiple_of((step * 3 + four) * LANES, LANES), LANES)
                g_ref[batch, at, :] = jnp.concatenate(rows, axis=0).astype(BF16)
            return carry

        lax.fori_loop(0, units // 12, place, 0)

    def forward(step, level):
        two = [doubled(level[batch * own : (batch + 1) * own]) for batch in range(batches)]
        mail = jnp.zeros((batches * own, LANES), F32)
        base = step * batches * own
        for number in range(chunks):
            for batch in range(batches):
                out = dot(g_ref[batch, number * span : (number + 1) * span, :], two[batch])
                out = out.astype(BF16)
                for unit in range(GROUP):
                    lane = number * wide + unit * LANES
                    for part in range(2):
                        row = base + batch * own + part * half
                        p_ref[row : row + half, lane : lane + LANES] = out[
                            unit * half : (unit + 1) * half, part * LANES : (part + 1) * LANES
                        ]
            rows = p_ref[base : base + batches * own, number * wide : (number + 1) * wide]
            mail = mail + dot_nt(rows, weights_of(w_ref, tail_ref, number))
        return mail

    def backward(d_mail):
        sums = [jnp.zeros((LANES, 2 * LANES), F32) for batch in range(batches)]
        for number in range(chunks):
            pulled = dot(d_mail, weights_of(w_ref, tail_ref, number)).astype(BF16)
            at = slice(number * span, (number + 1) * span)
            for batch in range(batches):
                tall = pulled_rows(pulled[batch * own : (batch + 1) * own], half)
                sums[batch] = sums[batch] + dot(turned(g_ref[batch, at, :]), tall)
        return jnp.concatenate([one[:own, :LANES] + one[own:, LANES:] for one in sums], axis=0)

    weights = (w_x, w_h, b_x, b_h)
    level_zero = state_ref[...]
    state_zero = level_zero.astype(F32)
    leave = pltpu.make_async_copy(g_ref, g_far, sems.at[1])
    leave.start()
    fetch.wait()
    mail_zero = forward(0, level_zero).astype(BF16)
    gates_zero = gates_of(mail_zero, level_zero, *weights)
    state_one = (1.0 - gates_zero[1]) * gates_zero[2] + gates_zero[1] * state_zero
    level_one = state_one.astype(BF16)
    mail_one = forward(1, level_one).astype(BF16)
    gates_one = gates_of(mail_one, level_one, *weights)
    new_ref[...] = ((1.0 - gates_one[1]) * gates_one[2] + gates_one[1] * state_one).astype(BF16)

    def gru_back(d_next, gates, current):
        reset, update, candidate, state_part = gates
        d_cand = d_next * (1.0 - update) * (1.0 - candidate * candidate)
        d_reset = d_cand * state_part * reset * (1.0 - reset)
        d_update = d_next * (current - candidate) * update * (1.0 - update)
        dg_mail = jnp.concatenate([d_reset, d_update, d_cand], axis=1).astype(BF16)
        dg_state = jnp.concatenate([d_reset, d_update, d_cand * reset], axis=1).astype(BF16)
        d_mail = dot_nt(dg_mail, w_x[...]).astype(BF16)
        d_current = d_next * update + dot_nt(dg_state, w_h[...])
        return dg_mail, dg_state, d_mail, d_current

    dgm_one, dgs_one, dm_one, d_state = gru_back(cot_ref[...].astype(F32), gates_one, state_one)
    d_state = d_state + backward(dm_one)
    dgm_zero, dgs_zero, dm_zero, d_state = gru_back(d_state, gates_zero, state_zero)
    base_ref[...] = d_state
    level_ref[...] = jnp.concatenate([level_zero, level_one], axis=1)
    dm_ref[...] = jnp.concatenate([dm_zero, dm_one], axis=1)

    def both(first, second):
        return jnp.concatenate([first.astype(F32), second.astype(F32)], axis=0)

    dms = both(dm_zero, dm_one).T
    mails, levels = both(mail_zero, mail_one), both(level_zero, level_one)
    dgm, dgs = both(dgm_zero, dgm_one), both(dgs_zero, dgs_one)
    width = dgm.shape[1]
    rows_ref[...] = jnp.zeros_like(rows_ref)
    for k, one in enumerate((dgm, dgs)):
        total = jnp.sum(one, axis=0, keepdims=True)
        for part in range(3):
            row = 24 + 3 * k + part
            rows_ref[row : row + 1, :] = total[:, part * LANES : (part + 1) * LANES]
    small = jnp.concatenate(
        [
            dot(dms.astype(BF16), p_ref[:, hidden_units * LANES : (hidden_units + 1) * LANES]),
            dot(mails.T.astype(BF16), dgm.astype(BF16)),
            dot(levels.T.astype(BF16), dgs.astype(BF16)),
            jnp.zeros((2 * own, LANES), F32),
        ],
        axis=1,
    )

    def sorted_rows(value):
        rows = value.shape[0] // 2
        upper, lower = value[:rows], value[rows:]
        halves = [jnp.where(where_ref[0] == k, upper, lower) for k in range(2)]
        parts = []
        for k, one in enumerate(halves):
            first, second = one[: rows // 2], one[rows // 2 :]
            parts += [jnp.where(where_ref[1 + k] == side, second, first) for side in range(2)]
        return jnp.concatenate(parts, axis=0).astype(BF16)

    dms, small = sorted_rows(dms), sorted_rows(small)
    rows_in, groups, tall, wide_out = kept_first.shape
    taken = wide_out - 2 * LANES
    moves = []
    for group in range(groups):
        out = dot(dms, p_ref[:, group * taken : (group + 1) * taken]).astype(BF16)
        extra = small[:, group * 2 * LANES : (group + 1) * 2 * LANES]
        for k, ref in enumerate((given_first, kept_first, given_last, kept_last)):
            for row in range(rows_in):
                at = ((2, 0, 3, 1)[k] * rows_in + row) * tall
                sum_ref[k, row, group, :, :taken] = out[at : at + tall]
                sum_ref[k, row, group, :, taken:] = extra[at : at + tall]
                moves.append(
                    pltpu.make_async_copy(
                        sum_ref.at[k, row, group], ref.at[row, group], sum_sems.at[k, row, group]
                    )
                )
                moves[-1].start()
    for move in moves:
        move.wait()
    leave.wait()


def edge_sums(batch, batches, order_ref, edge_ref, dg_ref, w_in_ref, b_in_ref, feat_ref, before):
    blocks = edge_ref.shape[0]
    hidden_units = w_in_ref.shape[1]
    w_in, b_in = first_layer(w_in_ref, b_in_ref)
    fold = (col_ids((hidden_units, 8 * hidden_units)) >> 3) == row_ids(
        (hidden_units, 8 * hidden_units)
    )
    fold = fold.astype(F32).astype(BF16)

    def one_piece(piece, sums):
        feats, held, pairs, low = edge_piece(batches, order_ref, edge_ref, piece, batch)
        pre = dot(w_in, feats) + b_in
        sig = jax.nn.sigmoid(pre)
        spread = dot(dg_ref[batch, : 8 * hidden_units], pairs)
        spread = spread.reshape(hidden_units, 8, pre.shape[1])
        spread = jnp.where(low[None], spread, 0.0).reshape(8 * hidden_units, pre.shape[1])
        d_hidden = dot(fold, spread.astype(BF16))
        d_pre = (d_hidden * sig * (1.0 + pre * (1.0 - sig))).astype(BF16)
        out = dot(w_in_ref[...], d_pre).astype(BF16)
        for k in range(PIECE):
            at = order_ref[batch, PIECE * piece + k]
            feat_ref[at, batch * 16 : (batch + 1) * 16] = out[:, k * LANES : (k + 1) * LANES]
        ones = jnp.where(row_ids((16, pre.shape[1])) == 0, held, 0.0).astype(BF16)
        return sums + dot_nt(jnp.concatenate([feats, ones], axis=0), d_pre)

    return lax.fori_loop(0, (order_ref[batch, blocks] + PIECE - 1) // PIECE, one_piece, before)


def back_kernel(
    g_far,
    level_ref,
    dm_ref,
    base_ref,
    w_far,
    bias_ref,
    grad_ref,
    dg_ref,
    tail_ref,
    w_ref,
    g_ref,
    sems,
):
    batches, own, width = grad_ref.shape
    hidden_units = w_ref.shape[0]
    chunks = (hidden_units + tail_ref.shape[0]) // GROUP
    half = own // 2
    fetches = []
    for number in range(chunks):
        some = pl.ds(number * GROUP, min(GROUP, hidden_units - number * GROUP))
        rows = pl.ds(number * GROUP * half, GROUP * half)
        fetches += [
            pltpu.make_async_copy(w_far.at[some], w_ref.at[some], sems.at[number, 0]),
            pltpu.make_async_copy(g_far.at[:, rows], g_ref.at[:, rows], sems.at[number, 1]),
        ]
    for fetch in fetches:
        fetch.start()
    bias_blocks(bias_ref, tail_ref)

    pulls, levels = [], []
    for batch in range(batches):
        mine = slice(batch * own, (batch + 1) * own)
        pulls += [dm_ref[mine, step * width : (step + 1) * width] for step in range(2)]
        both = [doubled(level_ref[mine, step * width : (step + 1) * width]) for step in range(2)]
        levels.append(jnp.concatenate(both, axis=1))
    pulls = jnp.concatenate(pulls, axis=0)
    totals = [jnp.zeros((2 * own, 2 * width), F32) for batch in range(batches)]
    for number in range(chunks):
        fetches[2 * number].wait()
        fetches[2 * number + 1].wait()
        pulled = dot(pulls, weights_of(w_ref, tail_ref, number)).astype(BF16)
        at = slice(number * GROUP * half, (number + 1) * GROUP * half)
        for batch in range(batches):
            talls = [
                pulled_rows(pulled[(2 * batch + k) * own : (2 * batch + k + 1) * own], half)
                for k in range(2)
            ]
            totals[batch] = totals[batch] + dot(turned(g_ref[batch, at, :]), talls[0])
            d_pair = dot_nt(jnp.concatenate(talls, axis=1), levels[batch])
            for unit in range(0, GROUP, 2):
                row = (number * GROUP + unit) * 8
                for part in range(half // 8):
                    pair = [
                        d_pair[(unit + k) * half + part * 8 : (unit + k) * half + part * 8 + 8]
                        for k in range(2)
                    ]
                    dg_ref[batch, row : row + 16, part * LANES : (part + 1) * LANES] = jnp.concatenate(
                        pair, axis=0
                    ).astype(BF16)
    for batch in range(batches):
        grad = base_ref[batch * own : (batch + 1) * own] + totals[batch][:own, :width]
        grad_ref[batch] = (grad + totals[batch][own:, width:]).astype(BF16)


def edge_kernel(order_ref, edge_ref, dg_ref, w_in_ref, b_in_ref, before_ref, feat_ref, win_ref):
    batches = order_ref.shape[0]
    feat_ref[...] = jnp.zeros_like(feat_ref)
    sums = before_ref[...]
    for batch in range(batches):
        sums = edge_sums(
            batch, batches, order_ref, edge_ref, dg_ref, w_in_ref, b_in_ref, feat_ref, sums
        )
    win_ref[...] = sums


def add_kernel(first_ref, second_ref, out_ref):
    out_ref[...] = (first_ref[...].astype(F32) + second_ref[...].astype(F32)).astype(BF16)


def copy_kernel(in_ref, out_ref):
    out_ref[...] = in_ref[...]


def rows_kernel(first_ref, second_ref, out_ref, rows_ref):
    parts, tall, wide = first_ref.shape
    main = wide // LANES - 2
    for part in range(parts):
        total = first_ref[part].astype(F32) + second_ref[part].astype(F32)
        for block in range(main):
            rows_ref[pl.ds(block, tall, stride=main), :] = total[
                :, block * LANES : (block + 1) * LANES
            ]
        for k in range(2):
            start = tall * (main + k)
            rows_ref[start : start + tall, :] = total[:, (main + k) * LANES : (main + k + 1) * LANES]
        out_ref[part] = rows_ref[...].astype(BF16)


def rows_of(first, second):
    parts, tall, wide = first.shape
    shape = (tall * (wide // LANES), LANES)
    return full_call(
        rows_kernel,
        jax.ShapeDtypeStruct((parts,) + shape, BF16),
        (pltpu.VMEM(shape, F32),),
        cost_estimate=cost(1),
    )(first, second)


def place_kernel(tall, count, carried, *refs):
    at_ref, pieces = refs[0], refs[1 : 1 + count]
    outs = refs[1 + count + carried : 6 + count + carried]
    big_ref, little_ref, sems = refs[6 + count + carried :]
    d_w, d_bias, d_x, d_h, d_rest = outs
    waits = []
    slot = 0
    for k, piece in enumerate(pieces):
        chunks, rows_in, lanes = piece.shape
        main = rows_in // tall - 2
        for chunk in range(chunks):
            code = at_ref[k] ^ chunk
            line, part = code >> 2, code & 3
            at = pl.ds(pl.multiple_of(line * tall, 8), tall)
            rows = piece[chunk].astype(F32)
            for row in range(tall):
                big_ref[slot, :, row * lanes : (row + 1) * lanes] = rows[row * main : (row + 1) * main]
            copy = pltpu.make_async_copy(
                big_ref.at[slot],
                d_w.at[
                    pl.ds(pl.multiple_of(part * main, 8), main),
                    pl.ds(pl.multiple_of(line * (tall * lanes), LANES), tall * lanes),
                ],
                sems.at[slot, 0],
            )
            copy.start()
            waits.append(copy)

            for side in range(2):
                start = tall * (main + side)
                little_ref[slot, side] = rows[start : start + tall]

                def move(target, lane):
                    lane = jnp.maximum(lane, 0) * lanes
                    to = pl.ds(pl.multiple_of(jnp.minimum(lane, target.shape[1] - lanes), LANES), lanes)
                    return pltpu.make_async_copy(
                        little_ref.at[slot, side], target.at[at, to], sems.at[slot, 1 + side]
                    )

                block = 2 * part + side
                to_x, to_h = move(d_x, block - 1), move(d_h, block - 4)
                alone = move((d_bias, d_rest)[side], 0)
                lone = block == 7 * side
                pl.when(lone)(alone.start)
                pl.when((block > 0) & (block < 4))(to_x.start)
                pl.when((block > 3) & (block < 7))(to_h.start)
                waits.append(alone)
            slot += 1
    for copy in waits:
        copy.wait()


def cost(micros):
    return pl.CostEstimate(
        flops=int(micros * 1e9), bytes_accessed=int(micros * 3e6), transcendentals=0
    )


def place_pieces(tall, at, pieces, shapes, before=()):
    count = len(pieces)
    chunks, rows_in, lanes = pieces[0].shape
    slots = count * chunks
    vmem = pl.BlockSpec(memory_space=pltpu.VMEM)
    hbm = pl.BlockSpec(memory_space=pl.ANY)
    return pl.pallas_call(
        functools.partial(place_kernel, tall, count, len(before)),
        out_shape=shapes,
        in_specs=[pl.BlockSpec(memory_space=pltpu.SMEM)] + [vmem] * count + [hbm] * len(before),
        out_specs=[hbm] * len(shapes),
        scratch_shapes=(
            pltpu.VMEM((slots, rows_in // tall - 2, tall * lanes), F32),
            pltpu.VMEM((slots, 2, tall, lanes), F32),
            pltpu.SemaphoreType.DMA((slots, 3)),
        ),
        input_output_aliases={1 + count + k: k for k in range(len(before))},
        cost_estimate=cost(0.1),
        compiler_params=pltpu.CompilerParams(vmem_limit_bytes=16 * MIB),
    )(at, *pieces, *before)


def body(
    states,
    edge_feats,
    source_index,
    target_index,
    w_edge_in,
    b_edge_in,
    w_edge_out,
    b_edge_out,
    w_input,
    w_hidden,
    b_input,
    b_hidden,
    cotangent,
):
    batches, own, width = states.shape
    edges = source_index.shape[1]
    owners = lax.axis_size("edge")
    cap = max(2, 2 * edges // owners)
    feat_count, units = w_edge_in.shape

    sent = full_call(
        functools.partial(route_kernel, own),
        jax.ShapeDtypeStruct((owners, batches * feat_count + 16, cap), BF16),
        limit=60,
    )(source_index, target_index, edge_feats)
    edge_data = lax.all_to_all(sent, "edge", 0, 0, tiled=True)
    merge = max(1, LANES // cap)
    if merge > 1:
        edge_data = edge_data.reshape(owners // merge, merge, -1, cap).transpose(0, 2, 1, 3)
        edge_data = edge_data.reshape(owners // merge, -1, merge * cap)

    w_mats = w_edge_out.reshape(units, width, width)
    padded = (units + 2 + GROUP - 1) // GROUP * GROUP

    tall = width // 8
    pairs = own // 2
    blocks = edge_data.shape[0]
    core = lax.axis_index("graph")
    spot = lax.axis_index("edge")
    orders = ((0, 1, 2, 3), (2, 0, 1, 3))

    def bit(side, step):
        first, second = [(spot >> orders[k][step]) & 1 for k in range(2)]
        return jnp.where(side == 0, first, second)

    where = jnp.stack([core, bit(core, 0), bit(1 - core, 0)])
    smem = pl.BlockSpec(memory_space=pltpu.SMEM)
    vmem = pl.BlockSpec(memory_space=pltpu.VMEM)
    far = pl.BlockSpec(memory_space=pltpu.HBM)
    bias = b_edge_out.reshape(width, width)
    quarter = jax.ShapeDtypeStruct((2, 4, tall, (units // 4 + 2) * width), BF16)
    new_states, *sums, g_pairs, levels, d_mails, base, order, first = full_call(
        main_kernel,
        (
            jax.ShapeDtypeStruct((batches * own, width), BF16),
            *[quarter] * 4,
            jax.ShapeDtypeStruct((batches, padded * pairs, LANES), BF16),
            jax.ShapeDtypeStruct((batches * own, 2 * width), BF16),
            jax.ShapeDtypeStruct((batches * own, 2 * width), BF16),
            jax.ShapeDtypeStruct((batches * own, width), F32),
            jax.ShapeDtypeStruct((batches, blocks + 1), jnp.int32),
            jax.ShapeDtypeStruct((32, width), F32),
        ),
        (
            pltpu.VMEM((units, PIECE * LANES), F32),
            pltpu.VMEM((padded * 8, 512), F32),
            pltpu.VMEM((batches, padded * pairs, LANES), BF16),
            pltpu.VMEM((2 * batches * own, padded * width), BF16),
            pltpu.VMEM((units, width, width), BF16),
            pltpu.VMEM((padded - units, width, width), BF16),
            pltpu.VMEM((4,) + quarter.shape, BF16),
            pltpu.SemaphoreType.DMA((4,) + quarter.shape[:2]),
            pltpu.SemaphoreType.DMA((2,)),
        ),
        limit=60,
        in_specs=[smem] + [vmem] * 5 + [far] + [vmem] * 5,
        out_specs=[vmem] + [far] * 5 + [vmem] * 3 + [smem, vmem],
    )(
        where,
        edge_data,
        states.reshape(batches * own, width),
        cotangent.reshape(batches * own, width),
        w_edge_in,
        b_edge_in,
        w_mats,
        bias,
        w_input,
        w_hidden,
        b_input,
        b_hidden,
    )

    cores = lax.axis_size("graph")

    def to_core(value):
        return lax.ppermute(value, "graph", [(0, 1), (1, 0)])

    def swap(value, masks):
        moves = []
        for side in range(cores):
            first = side * owners
            moves += [(first + k, first + (k ^ masks[side])) for k in range(owners)]
        return lax.ppermute(value, ("graph", "edge"), moves)

    def swap_step(value, step):
        return swap(value, [1 << orders[side][step] for side in range(cores)])

    def pick(value, number):
        return lax.dynamic_index_in_dim(value, number, 0, False)

    def added(terms):
        return sum(one.astype(F32) for one in terms)

    def after(value, *others):
        return lax.optimization_barrier((value, *others))[0]

    def first_grads(pairs_in):
        return full_call(
            back_kernel,
            (
                jax.ShapeDtypeStruct((batches, own, width), BF16),
                jax.ShapeDtypeStruct((batches, padded * 8, 512), BF16),
            ),
            (
                pltpu.VMEM((padded - units, width, width), BF16),
                pltpu.VMEM((units, width, width), BF16),
                pltpu.VMEM((batches, padded * pairs, LANES), BF16),
                pltpu.SemaphoreType.DMA((padded // GROUP, 2)),
            ),
            limit=60,
            in_specs=[far] + [vmem] * 3 + [far, vmem],
            cost_estimate=cost(12),
        )(pairs_in, levels, d_mails, base, w_mats, bias)

    def second_grads(d_pairs):
        return full_call(
            edge_kernel,
            (
                jax.ShapeDtypeStruct((blocks, batches * feat_count, LANES), BF16),
                jax.ShapeDtypeStruct((32, units), F32),
            ),
            limit=60,
            in_specs=[smem] + [vmem] * 5,
            cost_estimate=cost(9),
        )(order, edge_data, d_pairs, w_edge_in, b_edge_in, first)

    def added_at(big, small, flip):
        big, more = lax.optimization_barrier((big, swap(small, [flip] * cores)))
        return big, small + more

    kept_first, kept_last, given_first, given_last = sums
    got_first, got_last = to_core(given_first), to_core(given_last)
    kept_first = full_call(
        copy_kernel, jax.ShapeDtypeStruct(kept_first.shape, BF16), cost_estimate=cost(1)
    )(kept_first)
    give = full_call(
        add_kernel, jax.ShapeDtypeStruct(kept_first.shape, BF16), cost_estimate=cost(1)
    )(kept_first, got_first)
    terms = [kept_last, got_last]
    for step in range(3):
        if step > 0:
            number = bit(core, step)
            give = added([pick(one, 1 - number) for one in terms]).astype(BF16)
            terms = [pick(one, number) for one in terms]
        got = swap_step(give, step)
        if step == 0:
            state_grad, d_pairs = first_grads(after(g_pairs, give))
            got = after(got, state_grad)
        if step == 1:
            d_feats, first = second_grads(after(d_pairs, give))
            got = after(got, first)
        terms.append(got)
        if step == 0:
            terms = [one.reshape((2, 2, 2) + one.shape[2:]) for one in terms]
    total = added(terms).astype(BF16)
    for extra in range(3, owners.bit_length() - 1):
        got = swap(total, [1 << extra] * cores)
        if extra > 3:
            got, first = added_at(got, first, 1 << extra)
        if extra < owners.bit_length() - 2:
            total = added([total, got]).astype(BF16)
    first = after(first, total)
    first = first + swap(first, [4] * cores)
    first = first + swap(first, [1] * cores)
    got, first = added_at(got, first, 2)
    held = rows_of(total, got)

    got, first = added_at(swap_step(held, 2), first, 8)
    held = jnp.concatenate([held, got], axis=0)
    across = swap_step(held, 0)
    back = d_feats
    if merge > 1:
        back = back.reshape(blocks, -1, merge, cap).transpose(0, 2, 1, 3)
    back = after(back.reshape(owners, -1, cap), held)
    back = lax.all_to_all(back, "edge", 0, 0, tiled=True)

    near = swap_step(held, 1)
    near, more = lax.optimization_barrier((near, to_core(first)))
    first = first + more
    last = swap_step(near, 0)
    near = after(near, back)
    small_outs = (
        first[:feat_count],
        first[feat_count],
        first[24:27].reshape(-1),
        first[27:30].reshape(-1),
    )

    feat_grad = full_call(
        functools.partial(unroute_kernel, own),
        jax.ShapeDtypeStruct((batches, feat_count, edges), BF16),
        cost_estimate=cost(0.1),
    )(source_index, back.reshape(owners, batches, feat_count, cap))

    shapes = tuple(
        jax.ShapeDtypeStruct(shape, F32)
        for shape in (
            (units, width * width),
            (width, width),
            (width, 3 * width),
            (width, 3 * width),
            (width, width),
        )
    )
    outs = ()
    def place(outs, pieces):
        at = []
        for _, side, flips in pieces:
            code = side
            for step in range(3):
                code = code * 2 + bit(side, step)
            at.append((code * 2) ^ flips)
        return place_pieces(tall, jnp.stack(at), [one for one, _, _ in pieces], shapes, outs)

    outs = place((), [(held, core, 0), (to_core(held), 1 - core, 0)])
    outs, near, across = lax.optimization_barrier((outs, near, across))
    outs = place(
        outs,
        [
            (near, core, 4),
            (to_core(near), 1 - core, 4),
            (across, core, 8),
            (to_core(across), 1 - core, 8),
        ],
    )
    outs, last, feat_grad, small_outs = lax.optimization_barrier(
        (outs, last, feat_grad, small_outs)
    )
    other = to_core(last)
    outs = place(outs, [(last, core, 12)])
    outs = place(outs, [(other, 1 - core, 12)])
    d_w, d_bias, d_x, d_h, _ = outs
    return (
        new_states.reshape(batches, own, width),
        state_grad,
        feat_grad,
        small_outs[0],
        small_outs[1],
        d_w,
        d_bias.reshape(-1),
        d_x,
        d_h,
        small_outs[2],
        small_outs[3],
    )


def solution(mesh):
    spread = ("graph", "edge")
    rows = P(None, spread, None)
    edges = P(None, spread)
    feats = P(None, None, spread)
    in_specs = (rows, feats, edges, edges) + (P(),) * 8 + (rows,)
    out_specs = (rows, rows, feats) + (P(),) * 8
    return jax.shard_map(
        body,
        mesh=mesh,
        in_specs=in_specs,
        out_specs=out_specs,
        check_vma=False,
    )
```

```python
import functools

import jax
import jax.numpy as jnp
from jax import lax
from jax.experimental import pallas as pl
from jax.experimental.pallas import tpu as pltpu
from jax.sharding import PartitionSpec as P

F32 = jnp.float32
BF16 = jnp.bfloat16
LANES = 128
PIECE = 4
GROUP = 22
MIB = 1024 * 1024


def dot(first, second, dims=((1,), (0,))):
    return lax.dot_general(first, second, (dims, ((), ())), preferred_element_type=F32)


def dot_nt(first, second):
    return dot(first, second, ((1,), (1,)))


def row_ids(shape):
    return lax.broadcasted_iota(jnp.int32, shape, 0)


def col_ids(shape):
    return lax.broadcasted_iota(jnp.int32, shape, 1)


def full_call(kernel, out_shape, scratch=(), limit=16, **more):
    return pl.pallas_call(
        kernel,
        out_shape=out_shape,
        scratch_shapes=scratch,
        compiler_params=pltpu.CompilerParams(vmem_limit_bytes=limit * MIB),
        **more,
    )


def ranks_of(owner, owners):
    hits = (row_ids((owners, owner.shape[1])) == owner).astype(F32)
    before = (row_ids((LANES, LANES)) < col_ids((LANES, LANES))).astype(BF16)
    seen = jnp.zeros((owners, 1), F32)
    ranks = []
    for start in range(0, owner.shape[1], LANES):
        part = hits[:, start : start + LANES]
        place = dot(part.astype(BF16), before) + seen
        ranks.append(jnp.sum(part * place, axis=0, keepdims=True))
        seen = seen + jnp.sum(part, axis=1, keepdims=True)
    return hits, jnp.concatenate(ranks, axis=1)


def route_kernel(own_rows, src_ref, dst_ref, feat_ref, out_ref):
    owners, rows, cap = out_ref.shape
    batches, feats, edges = feat_ref.shape
    shift = own_rows.bit_length() - 1
    marks = [jnp.zeros((16, cap), F32)] * owners
    for batch in range(batches):
        source, target = src_ref[batch : batch + 1], dst_ref[batch : batch + 1]
        owner = source >> shift
        hits, rank = ranks_of(owner, owners)
        spots = (row_ids((cap, edges)) == rank.astype(jnp.int32)).astype(BF16)
        line = row_ids((16, edges)) - 3 * batch
        first = owner << shift
        extra = jnp.where(line == 0, source - first, jnp.where(line == 1, target - first, 1))
        extra = jnp.where((line >= 0) & (line < 3), extra, 0).astype(F32)
        load = jnp.concatenate([feat_ref[batch].astype(F32), extra], axis=0)
        masked = [(load * hits[part : part + 1]).astype(BF16) for part in range(owners)]
        out = dot_nt(jnp.concatenate(masked, axis=0), spots)
        for part in range(owners):
            tile = out[part * (feats + 16) : (part + 1) * (feats + 16)]
            out_ref[part, batch * feats : (batch + 1) * feats] = tile[:feats].astype(BF16)
            marks[part] = marks[part] + tile[feats:]
    for part in range(owners):
        out_ref[part, batches * feats :] = marks[part].astype(BF16)


def unroute_kernel(own_rows, src_ref, back_ref, out_ref):
    owners, batches, rows, cap = back_ref.shape
    edges = src_ref.shape[1]
    shift = own_rows.bit_length() - 1
    for batch in range(batches):
        hits, rank = ranks_of(src_ref[batch : batch + 1] >> shift, owners)
        spots = (row_ids((cap, edges)) == rank.astype(jnp.int32)).astype(BF16)
        parts = [back_ref[part, batch] for part in range(owners)]
        spread = dot(jnp.concatenate(parts, axis=0), spots)
        total = jnp.zeros((rows, edges), F32)
        for part in range(owners):
            total = total + spread[part * rows : (part + 1) * rows] * hits[part : part + 1]
        out_ref[batch] = total.astype(BF16)


def edge_piece(batches, order_ref, edge_ref, piece, batch):
    some = [edge_ref[order_ref[batch, PIECE * piece + k]] for k in range(PIECE)]
    block = jnp.concatenate(some, axis=1)
    feats, marks = block[batch * 16 : (batch + 1) * 16], block[batches * 16 :].astype(F32)
    source = marks[3 * batch : 3 * batch + 1].astype(jnp.int32)
    target = marks[3 * batch + 1 : 3 * batch + 2].astype(jnp.int32)
    held = marks[3 * batch + 2 : 3 * batch + 3]
    code = ((target >> 3) & 3) * 128 + (target >> 5) * 64 + source
    code = jnp.where(held > 0.5, code, -1)
    pairs = (row_ids((512, block.shape[1])) == code).astype(BF16)
    low = row_ids((8, block.shape[1])) == (target & 7)
    return feats, held, pairs, low


def order_blocks(batches, edge_ref, order_ref):
    blocks = edge_ref.shape[0]
    for batch in range(batches):
        front, back = jnp.int32(0), jnp.int32(blocks - 1)
        row = 3 * batch + 2
        for block in range(blocks):
            marks = edge_ref[block, batches * 16 :].astype(F32)
            held = jnp.max(marks[row : row + 1]) > 0.5
            order_ref[batch, jnp.where(held, front, back)] = jnp.int32(block)
            step = held.astype(jnp.int32)
            front, back = front + step, back - (1 - step)
        order_ref[batch, blocks] = front


def first_layer(w_in_ref, b_in_ref):
    bias = jnp.broadcast_to(b_in_ref[...].reshape(1, -1), (8, b_in_ref.shape[0]))
    return w_in_ref[...].astype(F32).T.astype(BF16), bias.T[:, :1]


def gates_of(mail_low, level, w_x, w_h, b_x, b_h):
    width = level.shape[1]
    from_mail = dot(mail_low, w_x[...]) + b_x[...].reshape(1, -1)
    from_state = dot(level, w_h[...]) + b_h[...].reshape(1, -1)
    reset = jax.nn.sigmoid(from_mail[:, :width] + from_state[:, :width])
    update = jax.nn.sigmoid(from_mail[:, width : 2 * width] + from_state[:, width : 2 * width])
    state_part = from_state[:, 2 * width :]
    candidate = jnp.tanh(from_mail[:, 2 * width :] + reset * state_part)
    return reset, update, candidate, state_part


def doubled(level):
    blank = jnp.zeros_like(level)
    return jnp.concatenate(
        [jnp.concatenate([level, blank], axis=1), jnp.concatenate([blank, level], axis=1)], axis=0
    )


def bias_blocks(bias_ref, tail_ref):
    tail_ref[...] = jnp.zeros_like(tail_ref)
    high = bias_ref[...].astype(BF16)
    tail_ref[0] = high
    tail_ref[1] = (bias_ref[...] - high.astype(F32)).astype(BF16)


def turned(tile):
    size = tile.shape[1]
    eye = (row_ids((size, size)) == col_ids((size, size))).astype(F32).astype(BF16)
    return dot_nt(eye, tile).astype(BF16)


def weights_of(w_ref, tail_ref, number):
    units = w_ref.shape[0]
    blocks = []
    for unit in range(number * GROUP, (number + 1) * GROUP):
        blocks.append(w_ref[unit] if unit < units else tail_ref[unit - units])
    return jnp.concatenate(blocks, axis=1)


def pulled_rows(pulled, half):
    rows = []
    for start in range(0, pulled.shape[1], LANES):
        tile = pulled[:, start : start + LANES]
        rows.append(jnp.concatenate([tile[:half], tile[half:]], axis=1))
    return jnp.concatenate(rows, axis=0)


def main_kernel(
    where_ref,
    edge_ref,
    state_ref,
    cot_ref,
    w_in_ref,
    b_in_ref,
    w_far,
    bias_ref,
    w_x,
    w_h,
    b_x,
    b_h,
    new_ref,
    kept_first,
    kept_last,
    given_first,
    given_last,
    g_far,
    level_ref,
    dm_ref,
    base_ref,
    order_ref,
    rows_ref,
    hid_ref,
    acc_ref,
    g_ref,
    p_ref,
    w_ref,
    tail_ref,
    sum_ref,
    sum_sems,
    sems,
):
    fetch = pltpu.make_async_copy(w_far, w_ref, sems.at[0])
    fetch.start()
    blocks = edge_ref.shape[0]
    batches = g_ref.shape[0]
    hidden_units = hid_ref.shape[0]
    units = acc_ref.shape[0] // 8
    own = state_ref.shape[0] // batches
    half = own // 2
    span = GROUP * half
    wide = GROUP * LANES
    chunks = units // GROUP
    order_blocks(batches, edge_ref, order_ref)
    bias_blocks(bias_ref, tail_ref)
    w_in, b_in = first_layer(w_in_ref, b_in_ref)

    for batch in range(batches):
        acc_ref[...] = jnp.zeros_like(acc_ref)

        def add_piece(piece, carry):
            feats, held, pairs, low = edge_piece(batches, order_ref, edge_ref, piece, batch)
            pre = dot(w_in, feats) + b_in
            hid_ref[...] = (pre * jax.nn.sigmoid(pre)).astype(BF16).astype(F32)
            ones = jnp.where(low, 1.0, 0.0)
            parts = []
            for unit in range(0, hidden_units, 2):
                two = [jnp.where(low, hid_ref[unit + k : unit + k + 1], 0.0) for k in range(2)]
                parts.append(jnp.concatenate(two, axis=0).astype(BF16))
            parts.append(jnp.concatenate([ones, ones], axis=0).astype(BF16))
            parts.append(jnp.zeros((8 * (units - hidden_units - 2), pre.shape[1]), BF16))
            acc_ref[...] += dot_nt(jnp.concatenate(parts, axis=0), pairs)
            return carry

        lax.fori_loop(0, (order_ref[batch, blocks] + PIECE - 1) // PIECE, add_piece, 0)

        def place(step, carry):
            for four in range(3):
                rows = []
                for k in range(4):
                    for part in range(4):
                        start = pl.multiple_of(step * 96 + four * 32 + k * 8, 8)
                        rows.append(acc_ref[pl.ds(start, 8), part * LANES : (part + 1) * LANES])
                at = pl.ds(pl.multiple_of((step * 3 + four) * LANES, LANES), LANES)
                g_ref[batch, at, :] = jnp.concatenate(rows, axis=0).astype(BF16)
            return carry

        lax.fori_loop(0, units // 12, place, 0)

    def forward(step, level):
        two = [doubled(level[batch * own : (batch + 1) * own]) for batch in range(batches)]
        mail = jnp.zeros((batches * own, LANES), F32)
        base = step * batches * own
        for number in range(chunks):
            for batch in range(batches):
                out = dot(g_ref[batch, number * span : (number + 1) * span, :], two[batch])
                out = out.astype(BF16)
                for unit in range(GROUP):
                    lane = number * wide + unit * LANES
                    for part in range(2):
                        row = base + batch * own + part * half
                        p_ref[row : row + half, lane : lane + LANES] = out[
                            unit * half : (unit + 1) * half, part * LANES : (part + 1) * LANES
                        ]
            rows = p_ref[base : base + batches * own, number * wide : (number + 1) * wide]
            mail = mail + dot_nt(rows, weights_of(w_ref, tail_ref, number))
        return mail

    def backward(d_mail):
        sums = [jnp.zeros((LANES, 2 * LANES), F32) for batch in range(batches)]
        for number in range(chunks):
            pulled = dot(d_mail, weights_of(w_ref, tail_ref, number)).astype(BF16)
            at = slice(number * span, (number + 1) * span)
            for batch in range(batches):
                tall = pulled_rows(pulled[batch * own : (batch + 1) * own], half)
                sums[batch] = sums[batch] + dot(turned(g_ref[batch, at, :]), tall)
        return jnp.concatenate([one[:own, :LANES] + one[own:, LANES:] for one in sums], axis=0)

    weights = (w_x, w_h, b_x, b_h)
    level_zero = state_ref[...]
    state_zero = level_zero.astype(F32)
    leave = pltpu.make_async_copy(g_ref, g_far, sems.at[1])
    leave.start()
    fetch.wait()
    mail_zero = forward(0, level_zero).astype(BF16)
    gates_zero = gates_of(mail_zero, level_zero, *weights)
    state_one = (1.0 - gates_zero[1]) * gates_zero[2] + gates_zero[1] * state_zero
    level_one = state_one.astype(BF16)
    mail_one = forward(1, level_one).astype(BF16)
    gates_one = gates_of(mail_one, level_one, *weights)
    new_ref[...] = ((1.0 - gates_one[1]) * gates_one[2] + gates_one[1] * state_one).astype(BF16)

    def gru_back(d_next, gates, current):
        reset, update, candidate, state_part = gates
        d_cand = d_next * (1.0 - update) * (1.0 - candidate * candidate)
        d_reset = d_cand * state_part * reset * (1.0 - reset)
        d_update = d_next * (current - candidate) * update * (1.0 - update)
        dg_mail = jnp.concatenate([d_reset, d_update, d_cand], axis=1).astype(BF16)
        dg_state = jnp.concatenate([d_reset, d_update, d_cand * reset], axis=1).astype(BF16)
        d_mail = dot_nt(dg_mail, w_x[...]).astype(BF16)
        d_current = d_next * update + dot_nt(dg_state, w_h[...])
        return dg_mail, dg_state, d_mail, d_current

    dgm_one, dgs_one, dm_one, d_state = gru_back(cot_ref[...].astype(F32), gates_one, state_one)
    d_state = d_state + backward(dm_one)
    dgm_zero, dgs_zero, dm_zero, d_state = gru_back(d_state, gates_zero, state_zero)
    base_ref[...] = d_state
    level_ref[...] = jnp.concatenate([level_zero, level_one], axis=1)
    dm_ref[...] = jnp.concatenate([dm_zero, dm_one], axis=1)

    def both(first, second):
        return jnp.concatenate([first.astype(F32), second.astype(F32)], axis=0)

    dms = both(dm_zero, dm_one).T
    mails, levels = both(mail_zero, mail_one), both(level_zero, level_one)
    dgm, dgs = both(dgm_zero, dgm_one), both(dgs_zero, dgs_one)
    width = dgm.shape[1]
    rows_ref[...] = jnp.zeros_like(rows_ref)
    for k, one in enumerate((dgm, dgs)):
        total = jnp.sum(one, axis=0, keepdims=True)
        for part in range(3):
            row = 24 + 3 * k + part
            rows_ref[row : row + 1, :] = total[:, part * LANES : (part + 1) * LANES]
    small = jnp.concatenate(
        [
            dot(dms.astype(BF16), p_ref[:, hidden_units * LANES : (hidden_units + 1) * LANES]),
            dot(mails.T.astype(BF16), dgm.astype(BF16)),
            dot(levels.T.astype(BF16), dgs.astype(BF16)),
            jnp.zeros((2 * own, LANES), F32),
        ],
        axis=1,
    )

    def sorted_rows(value):
        rows = value.shape[0] // 2
        upper, lower = value[:rows], value[rows:]
        halves = [jnp.where(where_ref[0] == k, upper, lower) for k in range(2)]
        parts = []
        for k, one in enumerate(halves):
            first, second = one[: rows // 2], one[rows // 2 :]
            parts += [jnp.where(where_ref[1 + k] == side, second, first) for side in range(2)]
        return jnp.concatenate(parts, axis=0).astype(BF16)

    dms, small = sorted_rows(dms), sorted_rows(small)
    rows_in, groups, tall, wide_out = kept_first.shape
    taken = wide_out - 2 * LANES
    moves = []
    for group in range(groups):
        out = dot(dms, p_ref[:, group * taken : (group + 1) * taken]).astype(BF16)
        extra = small[:, group * 2 * LANES : (group + 1) * 2 * LANES]
        for k, ref in enumerate((given_first, kept_first, given_last, kept_last)):
            for row in range(rows_in):
                at = ((2, 0, 3, 1)[k] * rows_in + row) * tall
                sum_ref[k, row, group, :, :taken] = out[at : at + tall]
                sum_ref[k, row, group, :, taken:] = extra[at : at + tall]
                moves.append(
                    pltpu.make_async_copy(
                        sum_ref.at[k, row, group], ref.at[row, group], sum_sems.at[k, row, group]
                    )
                )
                moves[-1].start()
    for move in moves:
        move.wait()
    leave.wait()


def edge_sums(batch, batches, order_ref, edge_ref, dg_ref, w_in_ref, b_in_ref, feat_ref, before):
    blocks = edge_ref.shape[0]
    hidden_units = w_in_ref.shape[1]
    w_in, b_in = first_layer(w_in_ref, b_in_ref)
    fold = (col_ids((hidden_units, 8 * hidden_units)) >> 3) == row_ids(
        (hidden_units, 8 * hidden_units)
    )
    fold = fold.astype(F32).astype(BF16)

    def one_piece(piece, sums):
        feats, held, pairs, low = edge_piece(batches, order_ref, edge_ref, piece, batch)
        pre = dot(w_in, feats) + b_in
        sig = jax.nn.sigmoid(pre)
        spread = dot(dg_ref[batch, : 8 * hidden_units], pairs)
        spread = spread.reshape(hidden_units, 8, pre.shape[1])
        spread = jnp.where(low[None], spread, 0.0).reshape(8 * hidden_units, pre.shape[1])
        d_hidden = dot(fold, spread.astype(BF16))
        d_pre = (d_hidden * sig * (1.0 + pre * (1.0 - sig))).astype(BF16)
        out = dot(w_in_ref[...], d_pre).astype(BF16)
        for k in range(PIECE):
            at = order_ref[batch, PIECE * piece + k]
            feat_ref[at, batch * 16 : (batch + 1) * 16] = out[:, k * LANES : (k + 1) * LANES]
        ones = jnp.where(row_ids((16, pre.shape[1])) == 0, held, 0.0).astype(BF16)
        return sums + dot_nt(jnp.concatenate([feats, ones], axis=0), d_pre)

    return lax.fori_loop(0, (order_ref[batch, blocks] + PIECE - 1) // PIECE, one_piece, before)


def back_kernel(
    g_far,
    level_ref,
    dm_ref,
    base_ref,
    w_far,
    bias_ref,
    grad_ref,
    dg_ref,
    tail_ref,
    w_ref,
    g_ref,
    sems,
):
    batches, own, width = grad_ref.shape
    hidden_units = w_ref.shape[0]
    chunks = (hidden_units + tail_ref.shape[0]) // GROUP
    half = own // 2
    fetches = []
    for number in range(chunks):
        some = pl.ds(number * GROUP, min(GROUP, hidden_units - number * GROUP))
        rows = pl.ds(number * GROUP * half, GROUP * half)
        fetches += [
            pltpu.make_async_copy(w_far.at[some], w_ref.at[some], sems.at[number, 0]),
            pltpu.make_async_copy(g_far.at[:, rows], g_ref.at[:, rows], sems.at[number, 1]),
        ]
    for fetch in fetches:
        fetch.start()
    bias_blocks(bias_ref, tail_ref)

    pulls, levels = [], []
    for batch in range(batches):
        mine = slice(batch * own, (batch + 1) * own)
        pulls += [dm_ref[mine, step * width : (step + 1) * width] for step in range(2)]
        both = [doubled(level_ref[mine, step * width : (step + 1) * width]) for step in range(2)]
        levels.append(jnp.concatenate(both, axis=1))
    pulls = jnp.concatenate(pulls, axis=0)
    totals = [jnp.zeros((2 * own, 2 * width), F32) for batch in range(batches)]
    for number in range(chunks):
        fetches[2 * number].wait()
        fetches[2 * number + 1].wait()
        pulled = dot(pulls, weights_of(w_ref, tail_ref, number)).astype(BF16)
        at = slice(number * GROUP * half, (number + 1) * GROUP * half)
        for batch in range(batches):
            talls = [
                pulled_rows(pulled[(2 * batch + k) * own : (2 * batch + k + 1) * own], half)
                for k in range(2)
            ]
            totals[batch] = totals[batch] + dot(turned(g_ref[batch, at, :]), talls[0])
            d_pair = dot_nt(jnp.concatenate(talls, axis=1), levels[batch])
            for unit in range(0, GROUP, 2):
                row = (number * GROUP + unit) * 8
                for part in range(half // 8):
                    pair = [
                        d_pair[(unit + k) * half + part * 8 : (unit + k) * half + part * 8 + 8]
                        for k in range(2)
                    ]
                    dg_ref[batch, row : row + 16, part * LANES : (part + 1) * LANES] = jnp.concatenate(
                        pair, axis=0
                    ).astype(BF16)
    for batch in range(batches):
        grad = base_ref[batch * own : (batch + 1) * own] + totals[batch][:own, :width]
        grad_ref[batch] = (grad + totals[batch][own:, width:]).astype(BF16)


def edge_kernel(order_ref, edge_ref, dg_ref, w_in_ref, b_in_ref, before_ref, feat_ref, win_ref):
    batches = order_ref.shape[0]
    feat_ref[...] = jnp.zeros_like(feat_ref)
    sums = before_ref[...]
    for batch in range(batches):
        sums = edge_sums(
            batch, batches, order_ref, edge_ref, dg_ref, w_in_ref, b_in_ref, feat_ref, sums
        )
    win_ref[...] = sums


def add_kernel(first_ref, second_ref, out_ref):
    out_ref[...] = (first_ref[...].astype(F32) + second_ref[...].astype(F32)).astype(BF16)


def copy_kernel(in_ref, out_ref):
    out_ref[...] = in_ref[...]


def rows_kernel(first_ref, second_ref, out_ref, rows_ref):
    parts, tall, wide = first_ref.shape
    main = wide // LANES - 2
    for part in range(parts):
        total = first_ref[part].astype(F32) + second_ref[part].astype(F32)
        for block in range(main):
            rows_ref[pl.ds(block, tall, stride=main), :] = total[
                :, block * LANES : (block + 1) * LANES
            ]
        for k in range(2):
            start = tall * (main + k)
            rows_ref[start : start + tall, :] = total[:, (main + k) * LANES : (main + k + 1) * LANES]
        out_ref[part] = rows_ref[...].astype(BF16)


def rows_of(first, second):
    parts, tall, wide = first.shape
    shape = (tall * (wide // LANES), LANES)
    return full_call(
        rows_kernel,
        jax.ShapeDtypeStruct((parts,) + shape, BF16),
        (pltpu.VMEM(shape, F32),),
        cost_estimate=cost(1),
    )(first, second)


def place_kernel(tall, count, carried, *refs):
    at_ref, pieces = refs[0], refs[1 : 1 + count]
    outs = refs[1 + count + carried : 6 + count + carried]
    big_ref, little_ref, sems = refs[6 + count + carried :]
    d_w, d_bias, d_x, d_h, d_rest = outs
    waits = []
    slot = 0
    for k, piece in enumerate(pieces):
        chunks, rows_in, lanes = piece.shape
        main = rows_in // tall - 2
        for chunk in range(chunks):
            code = at_ref[k] ^ chunk
            line, part = code >> 2, code & 3
            at = pl.ds(pl.multiple_of(line * tall, 8), tall)
            rows = piece[chunk].astype(F32)
            for row in range(tall):
                big_ref[slot, :, row * lanes : (row + 1) * lanes] = rows[row * main : (row + 1) * main]
            copy = pltpu.make_async_copy(
                big_ref.at[slot],
                d_w.at[
                    pl.ds(pl.multiple_of(part * main, 8), main),
                    pl.ds(pl.multiple_of(line * (tall * lanes), LANES), tall * lanes),
                ],
                sems.at[slot, 0],
            )
            copy.start()
            waits.append(copy)

            for side in range(2):
                start = tall * (main + side)
                little_ref[slot, side] = rows[start : start + tall]

                def move(target, lane):
                    lane = jnp.maximum(lane, 0) * lanes
                    to = pl.ds(pl.multiple_of(jnp.minimum(lane, target.shape[1] - lanes), LANES), lanes)
                    return pltpu.make_async_copy(
                        little_ref.at[slot, side], target.at[at, to], sems.at[slot, 1 + side]
                    )

                block = 2 * part + side
                to_x, to_h = move(d_x, block - 1), move(d_h, block - 4)
                alone = move((d_bias, d_rest)[side], 0)
                lone = block == 7 * side
                pl.when(lone)(alone.start)
                pl.when((block > 0) & (block < 4))(to_x.start)
                pl.when((block > 3) & (block < 7))(to_h.start)
                waits.append(alone)
            slot += 1
    for copy in waits:
        copy.wait()


def cost(micros):
    return pl.CostEstimate(
        flops=int(micros * 1e9), bytes_accessed=int(micros * 3e6), transcendentals=0
    )


def place_pieces(tall, at, pieces, shapes, before=()):
    count = len(pieces)
    chunks, rows_in, lanes = pieces[0].shape
    slots = count * chunks
    vmem = pl.BlockSpec(memory_space=pltpu.VMEM)
    hbm = pl.BlockSpec(memory_space=pl.ANY)
    return pl.pallas_call(
        functools.partial(place_kernel, tall, count, len(before)),
        out_shape=shapes,
        in_specs=[pl.BlockSpec(memory_space=pltpu.SMEM)] + [vmem] * count + [hbm] * len(before),
        out_specs=[hbm] * len(shapes),
        scratch_shapes=(
            pltpu.VMEM((slots, rows_in // tall - 2, tall * lanes), F32),
            pltpu.VMEM((slots, 2, tall, lanes), F32),
            pltpu.SemaphoreType.DMA((slots, 3)),
        ),
        input_output_aliases={1 + count + k: k for k in range(len(before))},
        cost_estimate=cost(0.1),
        compiler_params=pltpu.CompilerParams(vmem_limit_bytes=16 * MIB),
    )(at, *pieces, *before)


def body(
    states,
    edge_feats,
    source_index,
    target_index,
    w_edge_in,
    b_edge_in,
    w_edge_out,
    b_edge_out,
    w_input,
    w_hidden,
    b_input,
    b_hidden,
    cotangent,
):
    batches, own, width = states.shape
    edges = source_index.shape[1]
    owners = lax.axis_size("edge")
    cap = max(2, 2 * edges // owners)
    feat_count, units = w_edge_in.shape

    sent = full_call(
        functools.partial(route_kernel, own),
        jax.ShapeDtypeStruct((owners, batches * feat_count + 16, cap), BF16),
        limit=60,
    )(source_index, target_index, edge_feats)
    edge_data = lax.all_to_all(sent, "edge", 0, 0, tiled=True)
    merge = max(1, LANES // cap)
    if merge > 1:
        edge_data = edge_data.reshape(owners // merge, merge, -1, cap).transpose(0, 2, 1, 3)
        edge_data = edge_data.reshape(owners // merge, -1, merge * cap)

    w_mats = w_edge_out.reshape(units, width, width)
    padded = (units + 2 + GROUP - 1) // GROUP * GROUP

    tall = width // 8
    pairs = own // 2
    blocks = edge_data.shape[0]
    core = lax.axis_index("graph")
    spot = lax.axis_index("edge")
    orders = ((0, 1, 2, 3), (2, 0, 1, 3))

    def bit(side, step):
        first, second = [(spot >> orders[k][step]) & 1 for k in range(2)]
        return jnp.where(side == 0, first, second)

    where = jnp.stack([core, bit(core, 0), bit(1 - core, 0)])
    smem = pl.BlockSpec(memory_space=pltpu.SMEM)
    vmem = pl.BlockSpec(memory_space=pltpu.VMEM)
    far = pl.BlockSpec(memory_space=pltpu.HBM)
    bias = b_edge_out.reshape(width, width)
    quarter = jax.ShapeDtypeStruct((2, 4, tall, (units // 4 + 2) * width), BF16)
    new_states, *sums, g_pairs, levels, d_mails, base, order, first = full_call(
        main_kernel,
        (
            jax.ShapeDtypeStruct((batches * own, width), BF16),
            *[quarter] * 4,
            jax.ShapeDtypeStruct((batches, padded * pairs, LANES), BF16),
            jax.ShapeDtypeStruct((batches * own, 2 * width), BF16),
            jax.ShapeDtypeStruct((batches * own, 2 * width), BF16),
            jax.ShapeDtypeStruct((batches * own, width), F32),
            jax.ShapeDtypeStruct((batches, blocks + 1), jnp.int32),
            jax.ShapeDtypeStruct((32, width), F32),
        ),
        (
            pltpu.VMEM((units, PIECE * LANES), F32),
            pltpu.VMEM((padded * 8, 512), F32),
            pltpu.VMEM((batches, padded * pairs, LANES), BF16),
            pltpu.VMEM((2 * batches * own, padded * width), BF16),
            pltpu.VMEM((units, width, width), BF16),
            pltpu.VMEM((padded - units, width, width), BF16),
            pltpu.VMEM((4,) + quarter.shape, BF16),
            pltpu.SemaphoreType.DMA((4,) + quarter.shape[:2]),
            pltpu.SemaphoreType.DMA((2,)),
        ),
        limit=60,
        in_specs=[smem] + [vmem] * 5 + [far] + [vmem] * 5,
        out_specs=[vmem] + [far] * 5 + [vmem] * 3 + [smem, vmem],
    )(
        where,
        edge_data,
        states.reshape(batches * own, width),
        cotangent.reshape(batches * own, width),
        w_edge_in,
        b_edge_in,
        w_mats,
        bias,
        w_input,
        w_hidden,
        b_input,
        b_hidden,
    )

    cores = lax.axis_size("graph")

    def to_core(value):
        return lax.ppermute(value, "graph", [(0, 1), (1, 0)])

    def swap(value, masks):
        moves = []
        for side in range(cores):
            first = side * owners
            moves += [(first + k, first + (k ^ masks[side])) for k in range(owners)]
        return lax.ppermute(value, ("graph", "edge"), moves)

    def swap_step(value, step):
        return swap(value, [1 << orders[side][step] for side in range(cores)])

    def pick(value, number):
        return lax.dynamic_index_in_dim(value, number, 0, False)

    def added(terms):
        return sum(one.astype(F32) for one in terms)

    def after(value, *others):
        return lax.optimization_barrier((value, *others))[0]

    def first_grads(pairs_in):
        return full_call(
            back_kernel,
            (
                jax.ShapeDtypeStruct((batches, own, width), BF16),
                jax.ShapeDtypeStruct((batches, padded * 8, 512), BF16),
            ),
            (
                pltpu.VMEM((padded - units, width, width), BF16),
                pltpu.VMEM((units, width, width), BF16),
                pltpu.VMEM((batches, padded * pairs, LANES), BF16),
                pltpu.SemaphoreType.DMA((padded // GROUP, 2)),
            ),
            limit=60,
            in_specs=[far] + [vmem] * 3 + [far, vmem],
            cost_estimate=cost(12),
        )(pairs_in, levels, d_mails, base, w_mats, bias)

    def second_grads(d_pairs):
        return full_call(
            edge_kernel,
            (
                jax.ShapeDtypeStruct((blocks, batches * feat_count, LANES), BF16),
                jax.ShapeDtypeStruct((32, units), F32),
            ),
            limit=60,
            in_specs=[smem] + [vmem] * 5,
            cost_estimate=cost(9),
        )(order, edge_data, d_pairs, w_edge_in, b_edge_in, first)

    def added_at(big, small, flip):
        big, more = lax.optimization_barrier((big, swap(small, [flip] * cores)))
        return big, small + more

    kept_first, kept_last, given_first, given_last = sums
    got_first, got_last = to_core(given_first), to_core(given_last)
    kept_first = full_call(
        copy_kernel, jax.ShapeDtypeStruct(kept_first.shape, BF16), cost_estimate=cost(1)
    )(kept_first)
    give = full_call(
        add_kernel, jax.ShapeDtypeStruct(kept_first.shape, BF16), cost_estimate=cost(1)
    )(kept_first, got_first)
    terms = [kept_last, got_last]
    for step in range(3):
        if step > 0:
            number = bit(core, step)
            give = added([pick(one, 1 - number) for one in terms]).astype(BF16)
            terms = [pick(one, number) for one in terms]
        got = swap_step(give, step)
        if step == 0:
            state_grad, d_pairs = first_grads(after(g_pairs, give))
            got = after(got, state_grad)
        if step == 1:
            d_feats, first = second_grads(after(d_pairs, give))
            got = after(got, first)
        if step == 2:
            got, first = added_at(got, first, 4)
        terms.append(got)
        if step == 0:
            terms = [one.reshape((2, 2, 2) + one.shape[2:]) for one in terms]
    total = added(terms).astype(BF16)
    for extra in range(3, owners.bit_length() - 1):
        got = swap(total, [1 << extra] * cores)
        if extra > 3:
            got, first = added_at(got, first, 1 << extra)
        if extra < owners.bit_length() - 2:
            total = added([total, got]).astype(BF16)
    first = first + swap(first, [1] * cores)
    got, first = added_at(got, first, 2)
    held = rows_of(total, got)

    got, first = added_at(swap_step(held, 2), first, 8)
    held = jnp.concatenate([held, got], axis=0)
    across = swap_step(held, 0)
    back = d_feats
    if merge > 1:
        back = back.reshape(blocks, -1, merge, cap).transpose(0, 2, 1, 3)
    back = after(back.reshape(owners, -1, cap), held)
    back = lax.all_to_all(back, "edge", 0, 0, tiled=True)

    near = swap_step(held, 1)
    near, more = lax.optimization_barrier((near, to_core(first)))
    first = first + more
    last = swap_step(near, 0)
    near = after(near, back)
    small_outs = (
        first[:feat_count],
        first[feat_count],
        first[24:27].reshape(-1),
        first[27:30].reshape(-1),
    )

    feat_grad = full_call(
        functools.partial(unroute_kernel, own),
        jax.ShapeDtypeStruct((batches, feat_count, edges), BF16),
        cost_estimate=cost(0.1),
    )(source_index, back.reshape(owners, batches, feat_count, cap))

    shapes = tuple(
        jax.ShapeDtypeStruct(shape, F32)
        for shape in (
            (units, width * width),
            (width, width),
            (width, 3 * width),
            (width, 3 * width),
            (width, width),
        )
    )
    outs = ()
    def place(outs, pieces):
        at = []
        for _, side, flips in pieces:
            code = side
            for step in range(3):
                code = code * 2 + bit(side, step)
            at.append((code * 2) ^ flips)
        return place_pieces(tall, jnp.stack(at), [one for one, _, _ in pieces], shapes, outs)

    outs = place((), [(held, core, 0), (to_core(held), 1 - core, 0)])
    outs, near, across = lax.optimization_barrier((outs, near, across))
    outs = place(
        outs,
        [
            (near, core, 4),
            (to_core(near), 1 - core, 4),
            (across, core, 8),
            (to_core(across), 1 - core, 8),
        ],
    )
    outs, last, feat_grad, small_outs = lax.optimization_barrier(
        (outs, last, feat_grad, small_outs)
    )
    other = to_core(last)
    outs = place(outs, [(last, core, 12)])
    outs = place(outs, [(other, 1 - core, 12)])
    d_w, d_bias, d_x, d_h, _ = outs
    return (
        new_states.reshape(batches, own, width),
        state_grad,
        feat_grad,
        small_outs[0],
        small_outs[1],
        d_w,
        d_bias.reshape(-1),
        d_x,
        d_h,
        small_outs[2],
        small_outs[3],
    )


def solution(mesh):
    spread = ("graph", "edge")
    rows = P(None, spread, None)
    edges = P(None, spread)
    feats = P(None, None, spread)
    in_specs = (rows, feats, edges, edges) + (P(),) * 8 + (rows,)
    out_specs = (rows, rows, feats) + (P(),) * 8
    return jax.shard_map(
        body,
        mesh=mesh,
        in_specs=in_specs,
        out_specs=out_specs,
        check_vma=False,
    )
```
